32 devices in a mesh: seq: 16 (over z, y, core), req: 2 (over x).
Axes of the slice: x: 2, y: 2, z: 4, core: 2. Of those that a mesh axis runs over, the one named last changes fastest.
Arguments:
- hidden_in: bfloat16 [32, 4, 2048], P('req'), may hold values from -6 to 6
- attn_gain: float32 [2048], replicated, may hold values from 0.5 to 1.5
- q_gain: float32 [256], replicated, may hold values from 0.5 to 1.5
- k_gain: float32 [256], replicated, may hold values from 0.5 to 1.5
- post_attn_gain: float32 [2048], replicated, may hold values from 0.5 to 1.5
- ffn_gain: float32 [2048], replicated, may hold values from 0.5 to 1.5
- post_ffn_gain: float32 [2048], replicated, may hold values from 0.5 to 1.5
- w_qkv: bfloat16 [2048, 3072], P('seq', 'req'), may hold values from -0.125 to 0.125
- w_out: bfloat16 [2048, 2048], P('seq', 'req'), may hold values from -0.125 to 0.125
- w_gate: bfloat16 [2048, 8192], P('req', 'seq'), may hold values from -0.125 to 0.125
- w_up: bfloat16 [2048, 8192], P('req', 'seq'), may hold values from -0.125 to 0.125
- w_down: bfloat16 [8192, 2048], P('seq', 'req'), may hold values from -0.0625 to 0.0625
- prompt_keys: bfloat16 [4, 2048, 512], P('req', 'seq')
- prompt_values: bfloat16 [4, 2048, 512], P('req', 'seq'), may hold values from -6 to 6
- tail_keys: bfloat16 [2, 4096, 512], P('req', 'seq')
- tail_values: bfloat16 [2, 4096, 512], P('req', 'seq'), may hold values from -6 to 6
- group_of: int32 [32], P('req'), may hold values from 0 to 3, as said below
- prompt_lengths: int32 [4], P('req'), may hold values from 1 to 2048
- tail_lengths: int32 [32], P('req'), may hold values from 1 to 256
- page_table: int32 [2, 256], P('req'), may hold values from 0 to 255, each once within a row
Outputs:
- layer_out: bfloat16 [32, 4, 2048], P('req')
The draws below stay inside these ranges and needn't reach their ends.
Inputs may be any that keep to these rules, and one draw needn't show every extreme that they name: `group_of`: request i belongs to one of the 2 groups i // 16 * 2 to i // 16 * 2 + 1 of its own block of requests. `page_table`: each row lists every pool page of its index of req once; entry j * 16 + p is the pool page of page p of the j-th request of that block.
All inputs are finite; a program needn't handle non-finite values.
Results may differ from the reference program's by a relative error of at most 0.012.
The reference program's roundings to bfloat16 on the way count: a program that leaves them out, or rounds other values in their place, can miss the bound.
Values may be sent and summed in bfloat16 or wider, within the bound.
No kernel may reach another device: no remote copies, remote signals or barrier semaphores. Data moves between devices by JAX's collectives and lax.ppermute only.
A program may use at most 128 MiB of HBM per device.

```python
import jax
import jax.numpy as jnp
from jax import lax

D = 2048
H = 8
KV = 2
HD = 256
FF = 8192
REQ_DEV = 16
STEPS = 4
GROUPS_DEV = 2
PROMPT_DEV = 128
PAGE = 16
SLOTS = 16
QKV = 3072
REQUESTS = 32
GROUPS = 4
PROMPT_MAX = 2048
POOL = 4096
TAIL_PAGES = 16
N_SEQ = 16
N_REQ = 2


def scaled_keys(key, shape):
    base = jax.random.normal(key, shape, jnp.float32)
    return 0.25 * base


def draw_prompt_keys(key, part):
    return scaled_keys(key, (GROUPS, PROMPT_MAX, KV * HD)).astype(jnp.bfloat16)


def draw_tail_keys(key, part):
    return scaled_keys(key, (N_REQ, POOL, KV * HD)).astype(jnp.bfloat16)


def draw_group_of(key, part):
    picked = jax.random.randint(key, (N_REQ, REQ_DEV), 0, GROUPS_DEV, dtype=jnp.int32)
    other = (picked[:, 0] + 1) % GROUPS_DEV
    picked = picked.at[:, REQ_DEV - 1].set(other)
    block_base = jnp.arange(N_REQ, dtype=jnp.int32)[:, None] * GROUPS_DEV
    return (block_base + picked).reshape(REQUESTS).astype(jnp.int32)


def place_ends(drawn, stream_key, low, largest):
    longest = drawn.shape.index(max(drawn.shape))
    spots = []
    for shift in (0, 1):
        where = [jax.random.randint(jax.random.fold_in(stream_key, axis), (), 0, length) for axis, length in enumerate(drawn.shape)]
        where[longest] = (where[longest] + shift) % drawn.shape[longest]
        spots.append(tuple(where))
    return drawn.at[spots[0]].set(low).at[spots[1]].set(largest)


def block_levels(own_key, shape, shards, least, largest):
    level = 1.0
    for dim, shards_of in shards:
        steps = jax.random.uniform(jax.random.fold_in(jax.random.fold_in(own_key, 6), dim), (shards_of,), jnp.float32, least / len(shards), largest / len(shards))
        level = level * jnp.repeat(jnp.exp(steps), shape[dim] // shards_of).reshape((-1,) + (1,) * (len(shape) - 1 - dim))
    return level


def bell_draw(key, dims, width, reach, shards=(), held_as=jnp.bfloat16):
    result = width * jax.random.normal(key, dims, jnp.float32)
    if shards:
        result = result * block_levels(key, dims, shards, -0.22, 0.18)
    return jnp.clip(result, -reach, reach).astype(held_as)


def setup_inputs(seed: int = 0) -> dict:
    seeds = jax.random.split(jax.random.key(seed), 21)
    return {
        "hidden_in": bell_draw(seeds[0], (REQUESTS, STEPS, D), 1.0, 6.0, ((0, 2),)),
        "attn_gain": jnp.clip(jax.random.uniform(seeds[1], (D,), jnp.float32, 0.5, 1.5), 0.5, 1.5),
        "q_gain": jnp.clip(jax.random.uniform(seeds[2], (HD,), jnp.float32, 0.5, 1.5), 0.5, 1.5),
        "k_gain": jnp.clip(jax.random.uniform(seeds[3], (HD,), jnp.float32, 0.5, 1.5), 0.5, 1.5),
        "post_attn_gain": jnp.clip(jax.random.uniform(seeds[4], (D,), jnp.float32, 0.5, 1.5), 0.5, 1.5),
        "ffn_gain": jnp.clip(jax.random.uniform(seeds[5], (D,), jnp.float32, 0.5, 1.5), 0.5, 1.5),
        "post_ffn_gain": jnp.clip(jax.random.uniform(seeds[6], (D,), jnp.float32, 0.5, 1.5), 0.5, 1.5),
        "w_qkv": bell_draw(seeds[7], (D, QKV), D ** -0.5, 0.125, ((0, 16), (1, 2))),
        "w_out": bell_draw(seeds[8], (H * HD, D), (H * HD) ** -0.5, 0.125, ((0, 16), (1, 2))),
        "w_gate": bell_draw(seeds[9], (D, FF), D ** -0.5, 0.125, ((0, 2), (1, 16))),
        "w_up": bell_draw(seeds[10], (D, FF), D ** -0.5, 0.125, ((0, 2), (1, 16))),
        "w_down": bell_draw(seeds[11], (FF, D), FF ** -0.5, 0.0625, ((0, 16), (1, 2))),
        "prompt_keys": draw_prompt_keys(jax.random.fold_in(seeds[20], 71), 0),
        "prompt_values": bell_draw(seeds[13], (GROUPS, PROMPT_MAX, KV * HD), 1.0, 6.0, ((0, 2), (1, 16))),
        "tail_keys": draw_tail_keys(jax.random.fold_in(seeds[20], 71), 0),
        "tail_values": bell_draw(seeds[15], (N_REQ, POOL, KV * HD), 1.0, 6.0, ((0, 2), (1, 16))),
        "group_of": draw_group_of(jax.random.fold_in(seeds[20], 71), 0),
        "prompt_lengths": place_ends(jax.random.randint(seeds[17], (GROUPS,), 1, PROMPT_MAX + 1), jax.random.fold_in(seeds[17], 1), 1, PROMPT_MAX).astype(jnp.int32),
        "tail_lengths": place_ends(jax.random.randint(seeds[18], (REQUESTS,), 1, TAIL_PAGES * PAGE + 1), jax.random.fold_in(seeds[18], 1), 1, TAIL_PAGES * PAGE).astype(jnp.int32),
        "page_table": jax.vmap(lambda own: jax.random.permutation(own, N_SEQ * SLOTS))(jax.random.split(seeds[19], N_REQ)).reshape((N_REQ, N_SEQ * SLOTS)).astype(jnp.int32),
    }


EPSILON = 1e-06
NEGATIVE = -1e+30

def normalize(values):
    return values * lax.rsqrt(lax.optimization_barrier(jnp.mean(values * values, axis=-1, keepdims=True)) + EPSILON)

def reference(hidden_in, attn_gain, q_gain, k_gain, post_attn_gain, ffn_gain, post_ffn_gain, w_qkv, w_out, w_gate, w_up, w_down, prompt_keys, prompt_values, tail_keys, tail_values, group_of, prompt_lengths, tail_lengths, page_table):
    group_size = H // KV
    hidden = hidden_in.astype(jnp.float32)
    normed = (normalize(hidden) * attn_gain).astype(jnp.bfloat16)
    projected = jnp.dot(normed.reshape(REQUESTS * STEPS, D), w_qkv, preferred_element_type=jnp.float32).reshape(REQUESTS, STEPS, QKV)
    queries = (normalize(projected[..., :H * HD].reshape(REQUESTS, STEPS, H, HD)) * q_gain).astype(jnp.bfloat16)
    keys_new = (normalize(projected[..., H * HD:(H + KV) * HD].reshape(REQUESTS, STEPS, KV, HD)) * k_gain).astype(jnp.bfloat16)
    values_new = normalize(projected[..., (H + KV) * HD:].reshape(REQUESTS, STEPS, KV, HD)).astype(jnp.bfloat16)
    query_groups = queries.reshape(N_REQ, REQ_DEV, STEPS, KV, group_size, HD).astype(jnp.float32)
    local_group = (group_of % GROUPS_DEV).reshape(N_REQ, REQ_DEV)
    member = local_group[:, :, None] == jnp.arange(GROUPS_DEV, dtype=jnp.int32)[None, None, :]
    prompt_len = prompt_lengths.reshape(N_REQ, GROUPS_DEV)
    tail_len = tail_lengths.reshape(N_REQ, REQ_DEV)
    page_count = N_SEQ * SLOTS
    inverse = jnp.zeros((N_REQ, page_count), jnp.int32).at[jnp.arange(N_REQ, dtype=jnp.int32)[:, None], page_table].set(jnp.arange(page_count, dtype=jnp.int32)[None, :])
    owners_rows = jnp.repeat(inverse // TAIL_PAGES, PAGE, axis=1)
    position_rows = jnp.repeat(inverse % TAIL_PAGES, PAGE, axis=1) * PAGE + jnp.tile(jnp.arange(PAGE, dtype=jnp.int32), page_count)[None, :]
    cache_keys = prompt_keys.reshape(N_REQ, GROUPS_DEV, N_SEQ, PROMPT_DEV, KV, HD)
    cache_values = prompt_values.reshape(N_REQ, GROUPS_DEV, N_SEQ, PROMPT_DEV, KV, HD)
    pool_keys = tail_keys.reshape(N_REQ, N_SEQ, SLOTS * PAGE, KV, HD)
    pool_values = tail_values.reshape(N_REQ, N_SEQ, SLOTS * PAGE, KV, HD)
    pool_block = SLOTS * PAGE

    def one_block(block_index):
        keys_here = lax.dynamic_index_in_dim(cache_keys, block_index, 2, keepdims=False).astype(jnp.float32)
        values_here = lax.dynamic_index_in_dim(cache_values, block_index, 2, keepdims=False).astype(jnp.float32)
        pool_keys_here = lax.dynamic_index_in_dim(pool_keys, block_index, 1, keepdims=False).astype(jnp.float32)
        pool_values_here = lax.dynamic_index_in_dim(pool_values, block_index, 1, keepdims=False).astype(jnp.float32)
        prompt_pos = block_index * PROMPT_DEV + jnp.arange(PROMPT_DEV, dtype=jnp.int32)
        prompt_live = prompt_pos[None, None, :] < prompt_len[:, :, None]
        prompt_mask = (member[:, :, :, None] & prompt_live[:, None, :, :])[:, :, None, None, None, :, :]
        prompt_scores = jnp.einsum('rnskgd,rcpkd->rnskgcp', query_groups, keys_here)
        prompt_scores = jnp.where(prompt_mask, prompt_scores, NEGATIVE)
        owners_here = lax.dynamic_slice_in_dim(owners_rows, block_index * pool_block, pool_block, 1)
        positions_here = lax.dynamic_slice_in_dim(position_rows, block_index * pool_block, pool_block, 1)
        tail_mask = (owners_here[:, None, :] == jnp.arange(REQ_DEV, dtype=jnp.int32)[None, :, None]) & (positions_here[:, None, :] < tail_len[:, :, None])
        tail_mask = tail_mask[:, :, None, None, None, :]
        tail_scores = jnp.einsum('rnskgd,rpkd->rnskgp', query_groups, pool_keys_here)
        tail_scores = jnp.where(tail_mask, tail_scores, NEGATIVE)
        block_top = jnp.maximum(lax.optimization_barrier(jnp.max(prompt_scores, axis=(5, 6))), lax.optimization_barrier(jnp.max(tail_scores, axis=5)))
        prompt_probs = jnp.where(prompt_mask, jnp.exp(prompt_scores - block_top[..., None, None]), 0.0)
        tail_probs = jnp.where(tail_mask, jnp.exp(tail_scores - block_top[..., None]), 0.0)
        block_total = lax.optimization_barrier(jnp.sum(prompt_probs, axis=(5, 6))) + lax.optimization_barrier(jnp.sum(tail_probs, axis=5))
        prompt_round = prompt_probs.astype(jnp.bfloat16).astype(jnp.float32)
        tail_round = tail_probs.astype(jnp.bfloat16).astype(jnp.float32)
        block_accum = jnp.einsum('rnskgcp,rcpkd->rnskgd', prompt_round, values_here) + jnp.einsum('rnskgp,rpkd->rnskgd', tail_round, pool_values_here)
        return (block_top, block_total, block_accum)
    tops, totals, accums = lax.map(one_block, jnp.arange(N_SEQ, dtype=jnp.int32))
    keys_fresh = keys_new.reshape(N_REQ, REQ_DEV, STEPS, KV, HD).astype(jnp.float32)
    values_fresh = values_new.reshape(N_REQ, REQ_DEV, STEPS, KV, HD).astype(jnp.float32)
    new_scores = jnp.einsum('rnskgd,rnukd->rnskgu', query_groups, keys_fresh)
    causal = (jnp.arange(STEPS)[:, None] >= jnp.arange(STEPS)[None, :])[None, None, :, None, None, :]
    new_scores = jnp.where(causal, new_scores, NEGATIVE)
    highest = jnp.maximum(lax.optimization_barrier(jnp.max(tops, axis=0)), lax.optimization_barrier(jnp.max(new_scores, axis=5)))
    weights_blocks = jnp.exp(tops - highest[None])
    new_probs = jnp.where(causal, jnp.exp(new_scores - highest[..., None]), 0.0)
    total_sum = lax.optimization_barrier(jnp.sum(totals * weights_blocks, axis=0)) + lax.optimization_barrier(jnp.sum(new_probs, axis=5))
    accumulated = lax.optimization_barrier(jnp.sum(accums * weights_blocks[..., None], axis=0)) + jnp.einsum('rnskgu,rnukd->rnskgd', new_probs, values_fresh)
    attention = (accumulated / total_sum[..., None]).astype(jnp.bfloat16).reshape(REQUESTS * STEPS, H * HD)
    attn_out = jnp.dot(attention, w_out, preferred_element_type=jnp.float32)
    residual = hidden.reshape(REQUESTS * STEPS, D) + normalize(attn_out) * post_attn_gain
    ffn_in = (normalize(residual) * ffn_gain).astype(jnp.bfloat16)
    gate_out = jnp.dot(ffn_in, w_gate, preferred_element_type=jnp.float32)
    up_out = jnp.dot(ffn_in, w_up, preferred_element_type=jnp.float32)
    activated = (jax.nn.gelu(gate_out, approximate=True) * up_out).astype(jnp.bfloat16)
    down_out = jnp.dot(activated, w_down, preferred_element_type=jnp.float32)
    layer_out = residual + normalize(down_out) * post_ffn_gain
    return layer_out.astype(jnp.bfloat16).reshape(REQUESTS, STEPS, D)
```

```python
import functools

import jax
import jax.numpy as jnp
from jax import lax
from jax.experimental import pallas as pl
from jax.experimental.pallas import tpu as pltpu
from jax.sharding import PartitionSpec as P

D = 2048
H = 8
KV = 2
HD = 256
PAGE = 16
QKV = 3072


EPSILON = 1e-06
NEGATIVE = -1e30
LINK_SCALE = 512.0


def normalize(values):
    return values * lax.rsqrt(jnp.mean(values * values, axis=-1, keepdims=True) + EPSILON)


def split_three(values):
    high = values.astype(jnp.bfloat16)
    rest = values - high.astype(jnp.float32)
    middle = rest.astype(jnp.bfloat16)
    low = (rest - middle.astype(jnp.float32)).astype(jnp.bfloat16)
    return jnp.stack([high, middle, low])


def exchange(blocks, axes, groups=None):
    return lax.all_to_all(
        blocks, axes, split_axis=0, concat_axis=0, tiled=True, axis_index_groups=groups
    )


def tie(*arrays):
    return lax.optimization_barrier(arrays)


def spread(block, copies):
    return jnp.broadcast_to(block[None], (copies,) + block.shape)


def gather_rows(rows, count):
    return exchange(spread(rows, count), "seq").reshape(count * rows.shape[0], rows.shape[1])


def call(kernel, name, out_shape, *operands, scratch=(), any_from=None, limit=24):
    in_specs = [pl.BlockSpec(memory_space=pltpu.SMEM)]
    for i in range(1, len(operands)):
        space = pl.ANY if any_from is not None and i >= any_from else pltpu.VMEM
        in_specs.append(pl.BlockSpec(memory_space=space))
    return pl.pallas_call(
        kernel,
        name=name,
        out_shape=out_shape,
        in_specs=in_specs,
        out_specs=jax.tree.map(lambda _: pl.BlockSpec(memory_space=pltpu.VMEM), out_shape),
        scratch_shapes=scratch,
        compiler_params=pltpu.CompilerParams(vmem_limit_bytes=limit * 1024 * 1024),
    )(*operands)


def norm_columns_kernel(where_ref, hidden_ref, gain_ref, out_ref):
    columns = out_ref.shape[1]
    hidden = hidden_ref[...].astype(jnp.float32)
    scale = lax.rsqrt(jnp.mean(hidden * hidden, axis=-1, keepdims=True) + EPSILON)
    cols = pl.ds(pl.multiple_of(where_ref[0] * columns, columns), columns)
    normed = hidden_ref[:, :, cols].astype(jnp.float32) * scale * gain_ref[:, cols]
    out_ref[...] = normed.reshape(out_ref.shape).astype(jnp.bfloat16)


def head_norm_kernel(where_ref, projected_ref, q_gain_ref, k_gain_ref, q_ref, k_ref, v_ref):
    width = projected_ref.shape[2]
    copies, rows, _ = q_ref.shape
    fill = jnp.zeros((k_ref.shape[0] - rows, HD), jnp.float32)
    for head in range(H + 2 * KV):
        half, first = divmod(head * HD, width)
        values = normalize(projected_ref[half, :, first : first + HD])
        if head < H:
            values = (values * q_gain_ref[...]).astype(jnp.bfloat16)
            for i in range(copies):
                q_ref[i, :, head * HD : (head + 1) * HD] = values
        else:
            if head < H + KV:
                values = values * k_gain_ref[...]
            values = values.astype(jnp.bfloat16).astype(jnp.float32)
            target, slot = (k_ref, head - H) if head < H + KV else (v_ref, head - H - KV)
            target[:, slot * HD : (slot + 1) * HD] = jnp.concatenate([values, fill])


def dot_last(a, b):
    return lax.dot_general(a, b, (((1,), (1,)), ((), ())), preferred_element_type=jnp.float32)


def block_kernel(
    step_count,
    where_ref,
    q_ref,
    live_ref,
    new_k_ref,
    new_v_ref,
    prompt_k_ref,
    prompt_v_ref,
    tail_k_ref,
    tail_v_ref,
    out_ref,
):
    copies, steps, _ = q_ref.shape
    tokens = copies * steps
    columns = out_ref.shape[2]
    group = H // KV
    queries = q_ref[...].reshape(tokens, H * HD)
    live = jnp.concatenate([live_ref[...]] * group) > 0.5
    first_token = where_ref[0] * step_count
    shape = (group * tokens, new_k_ref.shape[0])
    step = lax.broadcasted_iota(jnp.int32, shape, 0) % tokens - first_token
    new_index = lax.broadcasted_iota(jnp.int32, shape, 1)
    new_live = (step >= new_index) & (step < step_count)
    prompt_rows = prompt_k_ref.shape[0]
    for kv in range(KV):
        span = slice(kv * HD, (kv + 1) * HD)
        q = jnp.concatenate(
            [queries[:, (kv * group + g) * HD : (kv * group + g + 1) * HD] for g in range(group)]
        )
        scores = jnp.concatenate(
            [dot_last(q, prompt_k_ref[:, span]), dot_last(q, tail_k_ref[:, span])], axis=1
        )
        scores = jnp.where(live, scores, NEGATIVE)
        top = jnp.max(scores, axis=1, keepdims=True)
        probs = jnp.where(live, jnp.exp(scores - top), 0.0)
        total = jnp.sum(probs, axis=1, keepdims=True)
        rounded = probs.astype(jnp.bfloat16)
        accum = jnp.dot(
            rounded[:, :prompt_rows], prompt_v_ref[:, span], preferred_element_type=jnp.float32
        ) + jnp.dot(
            rounded[:, prompt_rows:], tail_v_ref[:, span], preferred_element_type=jnp.float32
        )
        new_scores = dot_last(q, new_k_ref[:, span].astype(jnp.bfloat16))
        new_scores = jnp.where(new_live, new_scores, NEGATIVE)
        both = jnp.maximum(top, jnp.max(new_scores, axis=1, keepdims=True))
        carried = jnp.exp(top - both)
        new_probs = jnp.where(new_live, jnp.exp(new_scores - both), 0.0)
        total = total * carried + jnp.sum(new_probs, axis=1, keepdims=True)
        accum = accum * carried
        for u in range(step_count):
            accum = accum + new_probs[:, u : u + 1] * new_v_ref[u : u + 1, span]
        sent = accum.astype(jnp.bfloat16)
        parts = []
        for value in (both, total):
            for _ in range(3):
                part = value.astype(jnp.bfloat16).astype(jnp.float32)
                parts.append(part)
                value = value - part
        lane = lax.broadcasted_iota(jnp.int32, (group * tokens, 128), 1)
        wide = jnp.zeros((group * tokens, 128), jnp.float32)
        for i, part in enumerate(parts):
            wide = jnp.where(lane == i, part, wide)
        turned = jnp.transpose(wide)[:16].astype(jnp.bfloat16)
        for g in range(group):
            pair = turned[:, g // 2 * 128 : (g // 2 + 1) * 128]
            for part in range(HD // columns):
                target = (kv * group + g) * (HD // columns) + part
                out_ref[target, :tokens, :] = sent[
                    g * tokens : (g + 1) * tokens, part * columns : (part + 1) * columns
                ]
                out_ref[target, tokens:, :] = pair


def out_kernel(req_count, where_ref, got_ref, *refs):
    w_refs = refs[:req_count]
    out_ref, turned_ref = refs[req_count:]
    blocks = got_ref.shape[0]
    copies, steps, _ = out_ref.shape
    tokens = copies * steps
    columns = got_ref.shape[2]
    head = where_ref[0] * columns // HD
    stats = got_ref[:, tokens:, :].astype(jnp.float32)
    tops = stats[:, 0, :] + stats[:, 1, :] + stats[:, 2, :]
    totals = stats[:, 3, :] + stats[:, 4, :] + stats[:, 5, :]
    rest = jnp.zeros((128 - 2 * blocks, 128), jnp.float32)
    turned_ref[...] = jnp.transpose(jnp.concatenate([tops, totals, rest]))
    mine = turned_ref[pl.ds(pl.multiple_of(head % 2 * tokens, tokens), tokens), :]
    tops = mine[:, :blocks]
    highest = jnp.max(tops, axis=1, keepdims=True)
    weights = jnp.exp(tops - highest)
    denominator = jnp.sum(mine[:, blocks : 2 * blocks] * weights, axis=1, keepdims=True)
    numerator = jnp.zeros((tokens, columns), jnp.float32)
    for b in range(blocks):
        numerator = numerator + got_ref[b, :tokens, :].astype(jnp.float32) * weights[:, b : b + 1]
    attention = (numerator / denominator).astype(jnp.bfloat16)
    for j, w_ref in enumerate(w_refs):
        width = w_ref.shape[1]
        part = jnp.dot(attention, w_ref[...], preferred_element_type=jnp.float32)
        part = part.astype(jnp.bfloat16)
        for i in range(copies):
            out_ref[i, :, j * width : (j + 1) * width] = part[i * steps : (i + 1) * steps]


def summed(req_count, where_ref, got_ref):
    width = got_ref.shape[2] // req_count
    blocks = []
    for i in range(req_count):
        j = lax.rem(where_ref[1] - i + req_count, req_count)
        cols = pl.ds(pl.multiple_of(j * width, width), width)
        blocks.append(jnp.sum(got_ref[:, :, cols].astype(jnp.float32), axis=0))
    return jnp.concatenate(blocks, axis=1)


def residual_kernel(
    req_count, where_ref, got_ref, hidden_ref, post_gain_ref, ffn_gain_ref, out_ref, residual_ref
):
    attn_out = summed(req_count, where_ref, got_ref)
    residual = hidden_ref[...].astype(jnp.float32) + normalize(attn_out) * post_gain_ref[...]
    residual_ref[...] = residual
    ffn_in = (normalize(residual) * ffn_gain_ref[...]).astype(jnp.bfloat16)
    for i in range(out_ref.shape[0]):
        out_ref[i] = ffn_in


def last_kernel(req_count, where_ref, got_ref, residual_ref, gain_ref, out_ref):
    down_out = summed(req_count, where_ref, got_ref)
    layer = (residual_ref[...] + normalize(down_out) * gain_ref[...]).astype(jnp.bfloat16)
    for i in range(out_ref.shape[0]):
        out_ref[i] = layer


def ffn_kernel(req_count, where_ref, x_ref, *refs):
    w_refs = refs[: 3 * req_count]
    out_ref = refs[3 * req_count]
    held_refs = refs[3 * req_count + 1 : 6 * req_count + 1]
    sem_ref = refs[6 * req_count + 1]
    copies = [
        pltpu.make_async_copy(w, held, sem_ref.at[i])
        for i, (w, held) in enumerate(zip(w_refs, held_refs))
    ]
    for copy in copies:
        copy.start()
    blocks, steps, _ = x_ref.shape
    tokens = blocks * steps
    gate_out = up_out = None
    for j in range(req_count):
        gate_ref, up_ref = held_refs[2 * j], held_refs[2 * j + 1]
        rows = gate_ref.shape[0]
        first = lax.rem(where_ref[1] - j + req_count, req_count) * rows
        part = x_ref[:, :, pl.ds(pl.multiple_of(first, rows), rows)].reshape(tokens, rows)
        copies[2 * j].wait()
        gate = jnp.dot(part, gate_ref[...], preferred_element_type=jnp.float32)
        copies[2 * j + 1].wait()
        up = jnp.dot(part, up_ref[...], preferred_element_type=jnp.float32)
        gate_out = gate if j == 0 else gate_out + gate
        up_out = up if j == 0 else up_out + up
    activated = (jax.nn.gelu(gate_out, approximate=True) * up_out).astype(jnp.bfloat16)
    for j in range(req_count):
        down_ref = held_refs[2 * req_count + j]
        width = down_ref.shape[1]
        copies[2 * req_count + j].wait()
        part = jnp.dot(activated, down_ref[...], preferred_element_type=jnp.float32)
        part = part.astype(jnp.bfloat16)
        for i in range(blocks):
            out_ref[i, :, j * width : (j + 1) * width] = part[i * steps : (i + 1) * steps]


def live_rows(
    seq_index, prompt_shape, pool_rows, group_of, prompt_lengths, tail_lengths, page_table
):
    group_count, prompt_span = prompt_shape
    rows_req = group_of.shape[0]
    member = (group_of % group_count)[:, None] == jnp.arange(group_count, dtype=jnp.int32)[None, :]
    prompt_pos = seq_index * prompt_span + jnp.arange(prompt_span, dtype=jnp.int32)
    prompt_live = prompt_pos[None, :] < prompt_lengths[:, None]
    prompt_mask = (member[:, :, None] & prompt_live[None, :, :]).reshape(
        rows_req, group_count * prompt_span
    )
    slot_count = pool_rows // PAGE
    table_row = page_table[0]
    table_len = table_row.shape[0]
    tail_pages = table_len // rows_req
    slot_ids = seq_index * slot_count + jnp.arange(slot_count, dtype=jnp.int32)
    matches = table_row[None, :] == slot_ids[:, None]
    entries = jnp.sum(
        jnp.where(matches, jnp.arange(table_len, dtype=jnp.int32)[None, :], 0), axis=1
    )
    owners = jnp.repeat(entries // tail_pages, PAGE)
    tail_pos = jnp.repeat(entries % tail_pages, PAGE) * PAGE + jnp.tile(
        jnp.arange(PAGE, dtype=jnp.int32), slot_count
    )
    tail_mask = (owners[None, :] == jnp.arange(rows_req, dtype=jnp.int32)[:, None]) & (
        tail_pos[None, :] < tail_lengths[:, None]
    )
    return jnp.concatenate([prompt_mask, tail_mask], axis=1)


def general_attention(
    seq_index,
    seq_count,
    rows_req,
    step_count,
    out_rows,
    projected,
    q_gain,
    k_gain,
    live,
    prompt_keys,
    prompt_values,
    tail_keys,
    tail_values,
):
    group_size = H // KV
    share = projected.shape[0]
    tokens = rows_req * step_count
    heads = normalize(projected.reshape(share, QKV // HD, HD))
    gains = jnp.concatenate(
        [
            jnp.broadcast_to(q_gain, (H, HD)),
            jnp.broadcast_to(k_gain, (KV, HD)),
            jnp.ones((KV, HD), jnp.float32),
        ]
    )
    mine = (heads * gains).astype(jnp.bfloat16).reshape(share, QKV)
    qkv = gather_rows(mine, seq_count)
    queries = qkv[:, : H * HD]
    keys_new = qkv[:, H * HD : (H + KV) * HD]
    values_new = qkv[:, (H + KV) * HD :]

    query_groups = queries.reshape(rows_req, step_count, KV, group_size, HD)
    mask = live[:, None, None, None, :]
    keys = jnp.concatenate([prompt_keys, tail_keys]).reshape(-1, KV, HD)
    values = jnp.concatenate([prompt_values, tail_values]).reshape(-1, KV, HD)
    scores = jnp.einsum("rskgd,pkd->rskgp", query_groups, keys, preferred_element_type=jnp.float32)
    scores = jnp.where(mask, scores, NEGATIVE)
    block_top = jnp.max(scores, axis=4)
    probs = jnp.where(mask, jnp.exp(scores - block_top[..., None]), 0.0)
    block_total = jnp.sum(probs, axis=4)
    block_accum = jnp.einsum(
        "rskgp,pkd->rskgd",
        probs.astype(jnp.bfloat16),
        values,
        preferred_element_type=jnp.float32,
    )

    stats = split_three(jnp.stack([block_top, block_total])).reshape(6, tokens, H)
    per_head = seq_count // H
    stats = jnp.repeat(stats.transpose(2, 0, 1).reshape(H, -1, out_rows), per_head, axis=0)
    accum_blocks = (
        block_accum.astype(jnp.bfloat16).reshape(tokens, seq_count, out_rows).transpose(1, 0, 2)
    )
    got = exchange(jnp.concatenate([accum_blocks, stats], axis=1), "seq")
    got_accum = got[:, :tokens].astype(jnp.float32)
    got_stats = got[:, tokens:].astype(jnp.float32).reshape(seq_count, 2 * 3, tokens)
    got_top = got_stats[:, 0] + got_stats[:, 2] + got_stats[:, 4]
    got_total = got_stats[:, 1] + got_stats[:, 3] + got_stats[:, 5]

    first_col = seq_index * out_rows
    head = first_col // HD
    kv_head = head // group_size
    head_queries = lax.dynamic_slice_in_dim(queries, head * HD, HD, 1)
    head_keys = lax.dynamic_slice_in_dim(keys_new, kv_head * HD, HD, 1)
    head_values = lax.dynamic_slice_in_dim(
        values_new, kv_head * HD + first_col % HD, out_rows, 1
    ).astype(jnp.float32)
    new_scores = jnp.dot(head_queries, head_keys.T, preferred_element_type=jnp.float32)
    token_ids = jnp.arange(tokens, dtype=jnp.int32)
    causal = (token_ids[:, None] // step_count == token_ids[None, :] // step_count) & (
        token_ids[:, None] >= token_ids[None, :]
    )
    new_scores = jnp.where(causal, new_scores, NEGATIVE)
    highest = jnp.maximum(jnp.max(got_top, axis=0), jnp.max(new_scores, axis=1))
    weights = jnp.exp(got_top - highest[None])
    new_probs = jnp.where(causal, jnp.exp(new_scores - highest[:, None]), 0.0)
    denominator = jnp.sum(got_total * weights, axis=0) + jnp.sum(new_probs, axis=1)
    numerator = jnp.sum(got_accum * weights[..., None], axis=0) + jnp.dot(
        new_probs, head_values, precision=lax.Precision.HIGHEST
    )
    return (numerator / denominator[:, None]).astype(jnp.bfloat16)


def on_device(
    req_count,
    seq_count,
    hidden_in,
    attn_gain,
    q_gain,
    k_gain,
    post_attn_gain,
    ffn_gain,
    post_ffn_gain,
    w_qkv,
    w_out,
    w_gate,
    w_up,
    w_down,
    prompt_keys,
    prompt_values,
    tail_keys,
    tail_values,
    group_of,
    prompt_lengths,
    tail_lengths,
    page_table,
):
    seq_index = lax.axis_index("seq")
    req_index = lax.axis_index("req")
    rows_req, step_count, _ = hidden_in.shape
    group_size = H // KV
    tokens = rows_req * step_count
    share = tokens // seq_count

    def shifted(values):
        return [values] + [
            lax.ppermute(values, "req", [(i, (i + j) % req_count) for i in range(req_count)])
            for j in range(1, req_count)
        ]

    where = jnp.stack([seq_index, req_index]).astype(jnp.int32)
    in_rows = w_qkv.shape[0]
    out_rows = w_out.shape[0]
    if in_rows % 128 == 0:
        normed_cols = call(
            norm_columns_kernel,
            "norm_columns",
            jax.ShapeDtypeStruct((tokens, in_rows), jnp.bfloat16),
            where,
            hidden_in,
            attn_gain.reshape(1, D),
        )
    else:
        normed = (normalize(hidden_in.astype(jnp.float32)) * attn_gain).astype(jnp.bfloat16)
        normed_cols = lax.dynamic_slice_in_dim(normed, seq_index * in_rows, in_rows, 2)
        normed_cols = normed_cols.reshape(tokens, in_rows)
    normed_all = lax.all_gather(normed_cols, "req", axis=0, tiled=True)
    out_blocks = shifted(w_out)
    gate_blocks = shifted(w_gate)
    up_blocks = shifted(w_up)
    down_blocks = shifted(w_down)

    qkv_part = jnp.dot(normed_all, w_qkv, preferred_element_type=jnp.float32)
    qkv_cols = w_qkv.shape[1]
    qkv_blocks = (
        (qkv_part * LINK_SCALE)
        .astype(jnp.float16)
        .reshape(req_count * seq_count, share, qkv_cols)
    )
    qkv_got = exchange(qkv_blocks, ("req", "seq"))
    qkv_got = qkv_got.reshape(req_count, seq_count, share, qkv_cols)
    projected = jnp.sum(qkv_got.astype(jnp.float32), axis=1) * (1.0 / LINK_SCALE)
    live = live_rows(
        seq_index, prompt_keys.shape[:2], tail_keys.shape[1], group_of, prompt_lengths,
        tail_lengths, page_table,
    )
    caches = [
        array.reshape(-1, KV * HD) for array in (prompt_keys, prompt_values, tail_keys, tail_values)
    ]
    direct = share == step_count and out_rows % 128 == 0 and tokens == 64 and qkv_cols % HD == 0
    if direct:
        q_blocks, new_keys, new_values = call(
            head_norm_kernel,
            "head_norm",
            (
                jax.ShapeDtypeStruct((seq_count, share, H * HD), jnp.bfloat16),
                jax.ShapeDtypeStruct((8, KV * HD), jnp.float32),
                jax.ShapeDtypeStruct((8, KV * HD), jnp.float32),
            ),
            where,
            projected,
            q_gain.reshape(1, HD),
            k_gain.reshape(1, HD),
        )
        live = jnp.repeat(live.astype(jnp.float32), step_count, axis=0)
        sent = call(
            functools.partial(block_kernel, step_count),
            "block_attention",
            jax.ShapeDtypeStruct((seq_count, tokens + 16, out_rows), jnp.bfloat16),
            where,
            exchange(q_blocks, "seq"),
            live,
            new_keys,
            new_values,
            *caches,
        )
        got = exchange(sent, "seq")
        got, out_blocks, gate_blocks = tie(got, out_blocks, gate_blocks)
        out_part = call(
            functools.partial(out_kernel, req_count),
            "combine_out",
            jax.ShapeDtypeStruct((seq_count, share, D), jnp.bfloat16),
            where,
            got,
            *out_blocks,
            scratch=[pltpu.VMEM((128, 128), jnp.float32)],
        )
    else:
        projected = projected.transpose(1, 0, 2).reshape(share, QKV)
        attention_cols = general_attention(
            seq_index, seq_count, rows_req, step_count, out_rows, projected, q_gain, k_gain,
            live, *caches,
        )
        out_part = jnp.concatenate(
            [jnp.dot(attention_cols, w, preferred_element_type=jnp.float32) for w in out_blocks],
            axis=1,
        )
        out_part = out_part.astype(jnp.bfloat16).reshape(seq_count, share, D)
    attn_got, up_blocks = tie(exchange(out_part, "seq"), up_blocks)
    hidden_mine = lax.dynamic_index_in_dim(
        hidden_in.reshape(seq_count, share, D), seq_index, 0, keepdims=False
    )
    ffn_blocks, residual = call(
        functools.partial(residual_kernel, req_count),
        "residual_norms",
        (
            jax.ShapeDtypeStruct((seq_count, share, D), jnp.bfloat16),
            jax.ShapeDtypeStruct((share, D), jnp.float32),
        ),
        where,
        attn_got,
        hidden_mine,
        post_attn_gain.reshape(1, D),
        ffn_gain.reshape(1, D),
    )
    ffn_in, down_blocks = tie(exchange(ffn_blocks, "seq"), down_blocks)
    weights = [w for pair in zip(gate_blocks, up_blocks) for w in pair] + list(down_blocks)
    down_part = call(
        functools.partial(ffn_kernel, req_count),
        "feed_forward",
        jax.ShapeDtypeStruct((seq_count, share, D), jnp.bfloat16),
        where,
        ffn_in,
        *weights,
        scratch=[pltpu.VMEM(w.shape, w.dtype) for w in weights]
        + [pltpu.SemaphoreType.DMA((len(weights),))],
        any_from=2,
    )
    layer_blocks = call(
        functools.partial(last_kernel, req_count),
        "last_norm",
        jax.ShapeDtypeStruct((seq_count, share, D), jnp.bfloat16),
        where,
        exchange(down_part, "seq"),
        residual,
        post_ffn_gain.reshape(1, D),
    )
    return exchange(layer_blocks, "seq").reshape(rows_req, step_count, D)


def solution(mesh):
    return jax.shard_map(
        functools.partial(on_device, mesh.shape["req"], mesh.shape["seq"]),
        mesh=mesh,
        in_specs=(
            P("req", None, None),
            P(),
            P(),
            P(),
            P(),
            P(),
            P(),
            P("seq", "req"),
            P("seq", "req"),
            P("req", "seq"),
            P("req", "seq"),
            P("seq", "req"),
            P("req", "seq", None),
            P("req", "seq", None),
            P("req", "seq", None),
            P("req", "seq", None),
            P("req"),
            P("req"),
            P("req"),
            P("req", None),
        ),
        out_specs=P("req", None, None),
        check_vma=False,
    )
```

```python
import functools

import jax
import jax.numpy as jnp
from jax import lax
from jax.experimental import pallas as pl
from jax.experimental.pallas import tpu as pltpu
from jax.sharding import PartitionSpec as P

D = 2048
H = 8
KV = 2
HD = 256
PAGE = 16
QKV = 3072


EPSILON = 1e-06
NEGATIVE = -1e30
LINK_SCALE = 512.0


def normalize(values):
    return values * lax.rsqrt(jnp.mean(values * values, axis=-1, keepdims=True) + EPSILON)


def split_three(values):
    high = values.astype(jnp.bfloat16)
    rest = values - high.astype(jnp.float32)
    middle = rest.astype(jnp.bfloat16)
    low = (rest - middle.astype(jnp.float32)).astype(jnp.bfloat16)
    return jnp.stack([high, middle, low])


def exchange(blocks, axes, groups=None):
    return lax.all_to_all(
        blocks, axes, split_axis=0, concat_axis=0, tiled=True, axis_index_groups=groups
    )


def tie(*arrays):
    return lax.optimization_barrier(arrays)


def gather_two(block, count):
    inner = 1
    while inner * inner < count:
        inner *= 2
    outer = count // inner
    near = [[o * inner + i for i in range(inner)] for o in range(outer)]
    far = [[o * inner + i for o in range(outer)] for i in range(inner)]
    held = lax.all_gather(block, "seq", axis_index_groups=near)
    held = lax.all_gather(held, "seq", axis_index_groups=far)
    return held.reshape((count,) + block.shape)


def spread(block, copies):
    return jnp.broadcast_to(block[None], (copies,) + block.shape)


def gather_rows(rows, count):
    return exchange(spread(rows, count), "seq").reshape(count * rows.shape[0], rows.shape[1])


def call(kernel, name, out_shape, *operands, scratch=(), any_from=None, limit=24):
    in_specs = [pl.BlockSpec(memory_space=pltpu.SMEM)]
    for i in range(1, len(operands)):
        space = pl.ANY if any_from is not None and i >= any_from else pltpu.VMEM
        in_specs.append(pl.BlockSpec(memory_space=space))
    return pl.pallas_call(
        kernel,
        name=name,
        out_shape=out_shape,
        in_specs=in_specs,
        out_specs=jax.tree.map(lambda _: pl.BlockSpec(memory_space=pltpu.VMEM), out_shape),
        scratch_shapes=scratch,
        compiler_params=pltpu.CompilerParams(vmem_limit_bytes=limit * 1024 * 1024),
    )(*operands)


def norm_columns_kernel(where_ref, hidden_ref, gain_ref, out_ref):
    columns = out_ref.shape[1]
    hidden = hidden_ref[...].astype(jnp.float32)
    scale = lax.rsqrt(jnp.mean(hidden * hidden, axis=-1, keepdims=True) + EPSILON)
    cols = pl.ds(pl.multiple_of(where_ref[0] * columns, columns), columns)
    normed = hidden_ref[:, :, cols].astype(jnp.float32) * scale * gain_ref[:, cols]
    out_ref[...] = normed.reshape(out_ref.shape).astype(jnp.bfloat16)


def head_norm_kernel(
    req_count, where_ref, projected_ref, q_gain_ref, k_gain_ref, q_ref, k_ref, v_ref
):
    rows, width = projected_ref.shape
    width = width // req_count
    fill = jnp.zeros((k_ref.shape[0] - rows, HD), jnp.float32)
    for head in range(H + 2 * KV):
        block, first = divmod(head * HD, width)
        first = lax.rem(where_ref[1] - block + req_count, req_count) * width + first
        cols = pl.ds(pl.multiple_of(first, HD), HD)
        values = normalize(projected_ref[:, cols])
        if head < H:
            q_ref[:, head * HD : (head + 1) * HD] = (values * q_gain_ref[...]).astype(jnp.bfloat16)
        else:
            if head < H + KV:
                values = values * k_gain_ref[...]
            values = values.astype(jnp.bfloat16).astype(jnp.float32)
            target, slot = (k_ref, head - H) if head < H + KV else (v_ref, head - H - KV)
            target[:, slot * HD : (slot + 1) * HD] = jnp.concatenate([values, fill])


def dot_last(a, b):
    return lax.dot_general(a, b, (((1,), (1,)), ((), ())), preferred_element_type=jnp.float32)


def block_kernel(
    step_count,
    where_ref,
    q_ref,
    live_ref,
    new_k_ref,
    new_v_ref,
    prompt_k_ref,
    prompt_v_ref,
    tail_k_ref,
    tail_v_ref,
    out_ref,
    *held,
):
    held, sem_ref = held[:4], held[4]
    sources = (prompt_k_ref, prompt_v_ref, tail_k_ref, tail_v_ref)
    loads = [pltpu.make_async_copy(a, b, sem_ref.at[i]) for i, (a, b) in enumerate(zip(sources, held))]
    for i in (0, 2, 1, 3):
        loads[i].start()
    prompt_k_ref, prompt_v_ref, tail_k_ref, tail_v_ref = held
    copies, steps, _ = q_ref.shape
    tokens = copies * steps
    columns = out_ref.shape[2]
    group = H // KV
    queries = q_ref[...].reshape(tokens, H * HD)
    live = jnp.concatenate([live_ref[...]] * group) > 0.5
    first_token = where_ref[0] * step_count
    shape = (group * tokens, new_k_ref.shape[0])
    step = lax.broadcasted_iota(jnp.int32, shape, 0) % tokens - first_token
    new_index = lax.broadcasted_iota(jnp.int32, shape, 1)
    new_live = (step >= new_index) & (step < step_count)
    prompt_rows = prompt_k_ref.shape[0]
    for kv in range(KV):
        span = slice(kv * HD, (kv + 1) * HD)
        q = jnp.concatenate(
            [queries[:, (kv * group + g) * HD : (kv * group + g + 1) * HD] for g in range(group)]
        )
        if kv == 0:
            loads[0].wait()
            loads[2].wait()
        scores = jnp.concatenate(
            [dot_last(q, prompt_k_ref[:, span]), dot_last(q, tail_k_ref[:, span])], axis=1
        )
        scores = jnp.where(live, scores, NEGATIVE)
        top = jnp.max(scores, axis=1, keepdims=True)
        probs = jnp.where(live, jnp.exp(scores - top), 0.0)
        total = jnp.sum(probs, axis=1, keepdims=True)
        rounded = probs.astype(jnp.bfloat16)
        if kv == 0:
            loads[1].wait()
            loads[3].wait()
        accum = jnp.dot(
            rounded[:, :prompt_rows], prompt_v_ref[:, span], preferred_element_type=jnp.float32
        ) + jnp.dot(
            rounded[:, prompt_rows:], tail_v_ref[:, span], preferred_element_type=jnp.float32
        )
        new_scores = dot_last(q, new_k_ref[:, span].astype(jnp.bfloat16))
        new_scores = jnp.where(new_live, new_scores, NEGATIVE)
        both = jnp.maximum(top, jnp.max(new_scores, axis=1, keepdims=True))
        carried = jnp.exp(top - both)
        new_probs = jnp.where(new_live, jnp.exp(new_scores - both), 0.0)
        total = total * carried + jnp.sum(new_probs, axis=1, keepdims=True)
        accum = accum * carried
        for u in range(step_count):
            accum = accum + new_probs[:, u : u + 1] * new_v_ref[u : u + 1, span]
        sent = accum.astype(jnp.bfloat16)
        parts = []
        for value in (both, total):
            for _ in range(3):
                part = value.astype(jnp.bfloat16).astype(jnp.float32)
                parts.append(part)
                value = value - part
        lane = lax.broadcasted_iota(jnp.int32, (group * tokens, 128), 1)
        wide = jnp.zeros((group * tokens, 128), jnp.float32)
        for i, part in enumerate(parts):
            wide = jnp.where(lane == i, part, wide)
        turned = jnp.transpose(wide)[:16].astype(jnp.bfloat16)
        for g in range(group):
            pair = turned[:, g // 2 * 128 : (g // 2 + 1) * 128]
            for part in range(HD // columns):
                target = (kv * group + g) * (HD // columns) + part
                out_ref[target, :tokens, :] = sent[
                    g * tokens : (g + 1) * tokens, part * columns : (part + 1) * columns
                ]
                out_ref[target, tokens:, :] = pair


def out_kernel(req_count, where_ref, got_ref, *refs):
    w_refs = refs[:req_count]
    out_ref, turned_ref = refs[req_count:]
    blocks = got_ref.shape[0]
    copies, steps, _ = out_ref.shape
    tokens = copies * steps
    columns = got_ref.shape[2]
    head = where_ref[0] * columns // HD
    stats = got_ref[:, tokens:, :].astype(jnp.float32)
    tops = stats[:, 0, :] + stats[:, 1, :] + stats[:, 2, :]
    totals = stats[:, 3, :] + stats[:, 4, :] + stats[:, 5, :]
    rest = jnp.zeros((128 - 2 * blocks, 128), jnp.float32)
    turned_ref[...] = jnp.transpose(jnp.concatenate([tops, totals, rest]))
    mine = turned_ref[pl.ds(pl.multiple_of(head % 2 * tokens, tokens), tokens), :]
    tops = mine[:, :blocks]
    highest = jnp.max(tops, axis=1, keepdims=True)
    weights = jnp.exp(tops - highest)
    denominator = jnp.sum(mine[:, blocks : 2 * blocks] * weights, axis=1, keepdims=True)
    numerator = jnp.zeros((tokens, columns), jnp.float32)
    for b in range(blocks):
        numerator = numerator + got_ref[b, :tokens, :].astype(jnp.float32) * weights[:, b : b + 1]
    attention = (numerator / denominator).astype(jnp.bfloat16)
    for j, w_ref in enumerate(w_refs):
        width = w_ref.shape[1]
        part = jnp.dot(attention, w_ref[...], preferred_element_type=jnp.float32)
        part = part.astype(jnp.bfloat16)
        for i in range(copies):
            out_ref[i, :, j * width : (j + 1) * width] = part[i * steps : (i + 1) * steps]


def summed(req_count, where_ref, got_ref):
    width = got_ref.shape[2] // req_count
    blocks = []
    for i in range(req_count):
        j = lax.rem(where_ref[1] - i + req_count, req_count)
        cols = pl.ds(pl.multiple_of(j * width, width), width)
        blocks.append(jnp.sum(got_ref[:, :, cols].astype(jnp.float32), axis=0))
    return jnp.concatenate(blocks, axis=1)


def residual_kernel(
    req_count, where_ref, got_ref, hidden_ref, post_gain_ref, ffn_gain_ref, out_ref, residual_ref
):
    attn_out = summed(req_count, where_ref, got_ref)
    residual = hidden_ref[...].astype(jnp.float32) + normalize(attn_out) * post_gain_ref[...]
    residual_ref[...] = residual
    ffn_in = (normalize(residual) * ffn_gain_ref[...]).astype(jnp.bfloat16)
    for i in range(out_ref.shape[0]):
        out_ref[i] = ffn_in


def last_kernel(req_count, where_ref, got_ref, residual_ref, gain_ref, out_ref):
    down_out = summed(req_count, where_ref, got_ref)
    out_ref[...] = (residual_ref[...] + normalize(down_out) * gain_ref[...]).astype(jnp.bfloat16)


def ffn_kernel(req_count, where_ref, x_ref, *refs):
    w_refs = refs[: 3 * req_count]
    out_ref = refs[3 * req_count]
    held_refs = refs[3 * req_count + 1 : 6 * req_count + 1]
    sem_ref = refs[6 * req_count + 1]
    copies = [
        pltpu.make_async_copy(w, held, sem_ref.at[i])
        for i, (w, held) in enumerate(zip(w_refs, held_refs))
    ]
    for copy in copies:
        copy.start()
    blocks, steps, _ = x_ref.shape
    tokens = blocks * steps
    gate_out = up_out = None
    for j in range(req_count):
        gate_ref, up_ref = held_refs[2 * j], held_refs[2 * j + 1]
        rows = gate_ref.shape[0]
        first = lax.rem(where_ref[1] - j + req_count, req_count) * rows
        part = x_ref[:, :, pl.ds(pl.multiple_of(first, rows), rows)].reshape(tokens, rows)
        copies[2 * j].wait()
        gate = jnp.dot(part, gate_ref[...], preferred_element_type=jnp.float32)
        copies[2 * j + 1].wait()
        up = jnp.dot(part, up_ref[...], preferred_element_type=jnp.float32)
        gate_out = gate if j == 0 else gate_out + gate
        up_out = up if j == 0 else up_out + up
    activated = (jax.nn.gelu(gate_out, approximate=True) * up_out).astype(jnp.bfloat16)
    for j in range(req_count):
        down_ref = held_refs[2 * req_count + j]
        width = down_ref.shape[1]
        copies[2 * req_count + j].wait()
        part = jnp.dot(activated, down_ref[...], preferred_element_type=jnp.float32)
        part = part.astype(jnp.bfloat16)
        for i in range(blocks):
            out_ref[i, :, j * width : (j + 1) * width] = part[i * steps : (i + 1) * steps]


def live_rows(
    seq_index, prompt_shape, pool_rows, group_of, prompt_lengths, tail_lengths, page_table
):
    group_count, prompt_span = prompt_shape
    rows_req = group_of.shape[0]
    member = (group_of % group_count)[:, None] == jnp.arange(group_count, dtype=jnp.int32)[None, :]
    prompt_pos = seq_index * prompt_span + jnp.arange(prompt_span, dtype=jnp.int32)
    prompt_live = prompt_pos[None, :] < prompt_lengths[:, None]
    prompt_mask = (member[:, :, None] & prompt_live[None, :, :]).reshape(
        rows_req, group_count * prompt_span
    )
    slot_count = pool_rows // PAGE
    table_row = page_table[0]
    table_len = table_row.shape[0]
    tail_pages = table_len // rows_req
    slot_ids = seq_index * slot_count + jnp.arange(slot_count, dtype=jnp.int32)
    matches = table_row[None, :] == slot_ids[:, None]
    entries = jnp.sum(
        jnp.where(matches, jnp.arange(table_len, dtype=jnp.int32)[None, :], 0), axis=1
    )
    owners = jnp.repeat(entries // tail_pages, PAGE)
    tail_pos = jnp.repeat(entries % tail_pages, PAGE) * PAGE + jnp.tile(
        jnp.arange(PAGE, dtype=jnp.int32), slot_count
    )
    tail_mask = (owners[None, :] == jnp.arange(rows_req, dtype=jnp.int32)[:, None]) & (
        tail_pos[None, :] < tail_lengths[:, None]
    )
    return jnp.concatenate([prompt_mask, tail_mask], axis=1)


def general_attention(
    seq_index,
    seq_count,
    rows_req,
    step_count,
    out_rows,
    projected,
    q_gain,
    k_gain,
    live,
    prompt_keys,
    prompt_values,
    tail_keys,
    tail_values,
):
    group_size = H // KV
    share = projected.shape[0]
    tokens = rows_req * step_count
    heads = normalize(projected.reshape(share, QKV // HD, HD))
    gains = jnp.concatenate(
        [
            jnp.broadcast_to(q_gain, (H, HD)),
            jnp.broadcast_to(k_gain, (KV, HD)),
            jnp.ones((KV, HD), jnp.float32),
        ]
    )
    mine = (heads * gains).astype(jnp.bfloat16).reshape(share, QKV)
    qkv = gather_rows(mine, seq_count)
    queries = qkv[:, : H * HD]
    keys_new = qkv[:, H * HD : (H + KV) * HD]
    values_new = qkv[:, (H + KV) * HD :]

    query_groups = queries.reshape(rows_req, step_count, KV, group_size, HD)
    mask = live[:, None, None, None, :]
    keys = jnp.concatenate([prompt_keys, tail_keys]).reshape(-1, KV, HD)
    values = jnp.concatenate([prompt_values, tail_values]).reshape(-1, KV, HD)
    scores = jnp.einsum("rskgd,pkd->rskgp", query_groups, keys, preferred_element_type=jnp.float32)
    scores = jnp.where(mask, scores, NEGATIVE)
    block_top = jnp.max(scores, axis=4)
    probs = jnp.where(mask, jnp.exp(scores - block_top[..., None]), 0.0)
    block_total = jnp.sum(probs, axis=4)
    block_accum = jnp.einsum(
        "rskgp,pkd->rskgd",
        probs.astype(jnp.bfloat16),
        values,
        preferred_element_type=jnp.float32,
    )

    stats = split_three(jnp.stack([block_top, block_total])).reshape(6, tokens, H)
    per_head = seq_count // H
    stats = jnp.repeat(stats.transpose(2, 0, 1).reshape(H, -1, out_rows), per_head, axis=0)
    accum_blocks = (
        block_accum.astype(jnp.bfloat16).reshape(tokens, seq_count, out_rows).transpose(1, 0, 2)
    )
    got = exchange(jnp.concatenate([accum_blocks, stats], axis=1), "seq")
    got_accum = got[:, :tokens].astype(jnp.float32)
    got_stats = got[:, tokens:].astype(jnp.float32).reshape(seq_count, 2 * 3, tokens)
    got_top = got_stats[:, 0] + got_stats[:, 2] + got_stats[:, 4]
    got_total = got_stats[:, 1] + got_stats[:, 3] + got_stats[:, 5]

    first_col = seq_index * out_rows
    head = first_col // HD
    kv_head = head // group_size
    head_queries = lax.dynamic_slice_in_dim(queries, head * HD, HD, 1)
    head_keys = lax.dynamic_slice_in_dim(keys_new, kv_head * HD, HD, 1)
    head_values = lax.dynamic_slice_in_dim(
        values_new, kv_head * HD + first_col % HD, out_rows, 1
    ).astype(jnp.float32)
    new_scores = jnp.dot(head_queries, head_keys.T, preferred_element_type=jnp.float32)
    token_ids = jnp.arange(tokens, dtype=jnp.int32)
    causal = (token_ids[:, None] // step_count == token_ids[None, :] // step_count) & (
        token_ids[:, None] >= token_ids[None, :]
    )
    new_scores = jnp.where(causal, new_scores, NEGATIVE)
    highest = jnp.maximum(jnp.max(got_top, axis=0), jnp.max(new_scores, axis=1))
    weights = jnp.exp(got_top - highest[None])
    new_probs = jnp.where(causal, jnp.exp(new_scores - highest[:, None]), 0.0)
    denominator = jnp.sum(got_total * weights, axis=0) + jnp.sum(new_probs, axis=1)
    numerator = jnp.sum(got_accum * weights[..., None], axis=0) + jnp.dot(
        new_probs, head_values, precision=lax.Precision.HIGHEST
    )
    return (numerator / denominator[:, None]).astype(jnp.bfloat16)


def on_device(
    req_count,
    seq_count,
    hidden_in,
    attn_gain,
    q_gain,
    k_gain,
    post_attn_gain,
    ffn_gain,
    post_ffn_gain,
    w_qkv,
    w_out,
    w_gate,
    w_up,
    w_down,
    prompt_keys,
    prompt_values,
    tail_keys,
    tail_values,
    group_of,
    prompt_lengths,
    tail_lengths,
    page_table,
):
    seq_index = lax.axis_index("seq")
    req_index = lax.axis_index("req")
    rows_req, step_count, _ = hidden_in.shape
    group_size = H // KV
    tokens = rows_req * step_count
    share = tokens // seq_count

    def shifted(values):
        return [values] + [
            lax.ppermute(values, "req", [(i, (i + j) % req_count) for i in range(req_count)])
            for j in range(1, req_count)
        ]

    def in_order(blocks):
        stacked = jnp.stack(blocks)
        return jnp.concatenate(
            [
                lax.dynamic_index_in_dim(stacked, (req_index - i) % req_count, 0, keepdims=False)
                for i in range(req_count)
            ],
            axis=-1,
        )

    where = jnp.stack([seq_index, req_index]).astype(jnp.int32)
    in_rows = w_qkv.shape[0]
    out_rows = w_out.shape[0]
    if in_rows % 128 == 0:
        normed_cols = call(
            norm_columns_kernel,
            "norm_columns",
            jax.ShapeDtypeStruct((tokens, in_rows), jnp.bfloat16),
            where,
            hidden_in,
            attn_gain.reshape(1, D),
        )
    else:
        normed = (normalize(hidden_in.astype(jnp.float32)) * attn_gain).astype(jnp.bfloat16)
        normed_cols = lax.dynamic_slice_in_dim(normed, seq_index * in_rows, in_rows, 2)
        normed_cols = normed_cols.reshape(tokens, in_rows)
    qkv_blocks, w_out, w_gate, w_up, w_down = tie(shifted(w_qkv), w_out, w_gate, w_up, w_down)
    out_blocks = shifted(w_out)
    gate_blocks = shifted(w_gate)

    qkv_cols = w_qkv.shape[1]
    qkv_part = jnp.concatenate(
        [jnp.dot(normed_cols, w, preferred_element_type=jnp.float32) for w in qkv_blocks], axis=1
    )
    qkv_part = (qkv_part * LINK_SCALE).astype(jnp.float16).reshape(seq_count, share, QKV)
    qkv_got = exchange(qkv_part, "seq")
    projected = jnp.sum(qkv_got.astype(jnp.float32), axis=0) * (1.0 / LINK_SCALE)
    live = live_rows(
        seq_index, prompt_keys.shape[:2], tail_keys.shape[1], group_of, prompt_lengths,
        tail_lengths, page_table,
    )
    caches = [
        array.reshape(-1, KV * HD) for array in (prompt_keys, prompt_values, tail_keys, tail_values)
    ]
    direct = share == step_count and out_rows % 128 == 0 and tokens == 64 and qkv_cols % HD == 0
    if direct:
        queries, new_keys, new_values = call(
            functools.partial(head_norm_kernel, req_count),
            "head_norm",
            (
                jax.ShapeDtypeStruct((share, H * HD), jnp.bfloat16),
                jax.ShapeDtypeStruct((8, KV * HD), jnp.float32),
                jax.ShapeDtypeStruct((8, KV * HD), jnp.float32),
            ),
            where,
            projected,
            q_gain.reshape(1, HD),
            k_gain.reshape(1, HD),
        )
        live = jnp.repeat(live.astype(jnp.float32), step_count, axis=0)
        where_block, out_blocks, gate_blocks, w_up, w_down = tie(
            where, out_blocks, gate_blocks, w_up, w_down
        )
        sent = call(
            functools.partial(block_kernel, step_count),
            "block_attention",
            jax.ShapeDtypeStruct((seq_count, tokens + 16, out_rows), jnp.bfloat16),
            where_block,
            gather_two(queries, seq_count),
            live,
            new_keys,
            new_values,
            *caches,
            scratch=[pltpu.VMEM(c.shape, c.dtype) for c in caches]
            + [pltpu.SemaphoreType.DMA((len(caches),))],
            any_from=5,
            limit=56,
        )
        got = exchange(sent, "seq")
        out_part = call(
            functools.partial(out_kernel, req_count),
            "combine_out",
            jax.ShapeDtypeStruct((seq_count, share, D), jnp.bfloat16),
            where,
            got,
            *out_blocks,
            scratch=[pltpu.VMEM((128, 128), jnp.float32)],
        )
    else:
        projected = in_order(jnp.split(projected, req_count, axis=1))
        attention_cols = general_attention(
            seq_index, seq_count, rows_req, step_count, out_rows, projected, q_gain, k_gain,
            live, *caches,
        )
        out_part = jnp.concatenate(
            [jnp.dot(attention_cols, w, preferred_element_type=jnp.float32) for w in out_blocks],
            axis=1,
        )
        out_part = out_part.astype(jnp.bfloat16).reshape(seq_count, share, D)
    up_blocks = shifted(w_up)
    down_blocks = shifted(w_down)
    hidden_mine = lax.dynamic_index_in_dim(
        hidden_in.reshape(seq_count, share, D), seq_index, 0, keepdims=False
    )
    ffn_blocks, residual = call(
        functools.partial(residual_kernel, req_count),
        "residual_norms",
        (
            jax.ShapeDtypeStruct((seq_count, share, D), jnp.bfloat16),
            jax.ShapeDtypeStruct((share, D), jnp.float32),
        ),
        where,
        exchange(out_part, "seq"),
        hidden_mine,
        post_attn_gain.reshape(1, D),
        ffn_gain.reshape(1, D),
    )
    weights = [w for pair in zip(gate_blocks, up_blocks) for w in pair] + list(down_blocks)
    down_part = call(
        functools.partial(ffn_kernel, req_count),
        "feed_forward",
        jax.ShapeDtypeStruct((seq_count, share, D), jnp.bfloat16),
        where,
        exchange(ffn_blocks, "seq"),
        *weights,
        scratch=[pltpu.VMEM(w.shape, w.dtype) for w in weights]
        + [pltpu.SemaphoreType.DMA((len(weights),))],
        any_from=2,
        limit=56,
    )
    layer_mine = call(
        functools.partial(last_kernel, req_count),
        "last_norm",
        jax.ShapeDtypeStruct((share, D), jnp.bfloat16),
        where,
        exchange(down_part, "seq"),
        residual,
        post_ffn_gain.reshape(1, D),
    )
    return gather_two(layer_mine, seq_count).reshape(rows_req, step_count, D)


def solution(mesh):
    return jax.shard_map(
        functools.partial(on_device, mesh.shape["req"], mesh.shape["seq"]),
        mesh=mesh,
        in_specs=(
            P("req", None, None),
            P(),
            P(),
            P(),
            P(),
            P(),
            P(),
            P("seq", "req"),
            P("seq", "req"),
            P("req", "seq"),
            P("req", "seq"),
            P("seq", "req"),
            P("req", "seq", None),
            P("req", "seq", None),
            P("req", "seq", None),
            P("req", "seq", None),
            P("req"),
            P("req"),
            P("req"),
            P("req", None),
        ),
        out_specs=P("req", None, None),
        check_vma=False,
    )
```

```python
import functools

import jax
import jax.numpy as jnp
from jax import lax
from jax.experimental import pallas as pl
from jax.experimental.pallas import tpu as pltpu
from jax.sharding import PartitionSpec as P

D = 2048
H = 8
KV = 2
HD = 256
PAGE = 16
QKV = 3072


EPSILON = 1e-06
NEGATIVE = -1e30
LINK_SCALE = 512.0


def normalize(values):
    return values * lax.rsqrt(jnp.mean(values * values, axis=-1, keepdims=True) + EPSILON)


def split_three(values):
    high = values.astype(jnp.bfloat16)
    rest = values - high.astype(jnp.float32)
    middle = rest.astype(jnp.bfloat16)
    low = (rest - middle.astype(jnp.float32)).astype(jnp.bfloat16)
    return jnp.stack([high, middle, low])


def exchange(blocks, axes, groups=None):
    return lax.all_to_all(
        blocks, axes, split_axis=0, concat_axis=0, tiled=True, axis_index_groups=groups
    )


def tie(*arrays):
    return lax.optimization_barrier(arrays)


def spread(block, copies):
    return jnp.broadcast_to(block[None], (copies,) + block.shape)


def gather_rows(rows, count):
    return exchange(spread(rows, count), "seq").reshape(count * rows.shape[0], rows.shape[1])


def call(kernel, name, out_shape, *operands, scratch=(), any_from=None, limit=24):
    in_specs = [pl.BlockSpec(memory_space=pltpu.SMEM)]
    for i in range(1, len(operands)):
        space = pl.ANY if any_from is not None and i >= any_from else pltpu.VMEM
        in_specs.append(pl.BlockSpec(memory_space=space))
    return pl.pallas_call(
        kernel,
        name=name,
        out_shape=out_shape,
        in_specs=in_specs,
        out_specs=jax.tree.map(lambda _: pl.BlockSpec(memory_space=pltpu.VMEM), out_shape),
        scratch_shapes=scratch,
        compiler_params=pltpu.CompilerParams(vmem_limit_bytes=limit * 1024 * 1024),
    )(*operands)


def norm_columns_kernel(
    where_ref, hidden_ref, gain_ref, q_gain_ref, k_gain_ref, out_ref, head_gains_ref
):
    head_gains_ref[0:1, :] = q_gain_ref[...]
    head_gains_ref[1:2, :] = k_gain_ref[...]
    columns = out_ref.shape[1]
    hidden = hidden_ref[...].astype(jnp.float32)
    scale = lax.rsqrt(jnp.mean(hidden * hidden, axis=-1, keepdims=True) + EPSILON)
    cols = pl.ds(pl.multiple_of(where_ref[0] * columns, columns), columns)
    normed = hidden_ref[:, :, cols].astype(jnp.float32) * scale * gain_ref[:, cols]
    out_ref[...] = normed.reshape(out_ref.shape).astype(jnp.bfloat16)


def head_norm_kernel(where_ref, projected_ref, gains_ref, q_ref, k_ref, v_ref):
    width = projected_ref.shape[2]
    copies, rows, _ = q_ref.shape
    fill = jnp.zeros((k_ref.shape[0] - rows, HD), jnp.float32)
    for head in range(H + 2 * KV):
        half, first = divmod(head * HD, width)
        values = normalize(projected_ref[half, :, first : first + HD])
        if head < H:
            values = (values * gains_ref[0:1, :]).astype(jnp.bfloat16)
            for i in range(copies):
                q_ref[i, :, head * HD : (head + 1) * HD] = values
        else:
            if head < H + KV:
                values = values * gains_ref[1:2, :]
            values = values.astype(jnp.bfloat16).astype(jnp.float32)
            target, slot = (k_ref, head - H) if head < H + KV else (v_ref, head - H - KV)
            target[:, slot * HD : (slot + 1) * HD] = jnp.concatenate([values, fill])


def stage_kernel(
    where_ref, after_ref, prompt_k_ref, prompt_v_ref, tail_k_ref, tail_v_ref, keys_ref, values_ref
):
    rows = prompt_k_ref.shape[0]
    keys_ref[:rows, :] = prompt_k_ref[...]
    keys_ref[rows:, :] = tail_k_ref[...]
    values_ref[:rows, :] = prompt_v_ref[...]
    values_ref[rows:, :] = tail_v_ref[...]


def dot_last(a, b):
    return lax.dot_general(a, b, (((1,), (1,)), ((), ())), preferred_element_type=jnp.float32)


def block_kernel(
    step_count,
    where_ref,
    q_ref,
    live_ref,
    new_k_ref,
    new_v_ref,
    keys_ref,
    values_ref,
    out_ref,
):
    copies, steps, _ = q_ref.shape
    tokens = copies * steps
    columns = out_ref.shape[2]
    group = H // KV
    queries = q_ref[...].reshape(tokens, H * HD)
    live = jnp.concatenate([live_ref[...]] * group) > 0.5
    first_token = where_ref[0] * step_count
    shape = (group * tokens, new_k_ref.shape[0])
    step = lax.broadcasted_iota(jnp.int32, shape, 0) % tokens - first_token
    new_index = lax.broadcasted_iota(jnp.int32, shape, 1)
    new_live = (step >= new_index) & (step < step_count)
    for kv in range(KV):
        span = slice(kv * HD, (kv + 1) * HD)
        q = jnp.concatenate(
            [queries[:, (kv * group + g) * HD : (kv * group + g + 1) * HD] for g in range(group)]
        )
        scores = jnp.where(live, dot_last(q, keys_ref[:, span]), NEGATIVE)
        top = jnp.max(scores, axis=1, keepdims=True)
        probs = jnp.where(live, jnp.exp(scores - top), 0.0)
        total = jnp.sum(probs, axis=1, keepdims=True)
        accum = jnp.dot(
            probs.astype(jnp.bfloat16), values_ref[:, span], preferred_element_type=jnp.float32
        )
        new_scores = dot_last(q, new_k_ref[:, span].astype(jnp.bfloat16))
        new_scores = jnp.where(new_live, new_scores, NEGATIVE)
        both = jnp.maximum(top, jnp.max(new_scores, axis=1, keepdims=True))
        carried = jnp.exp(top - both)
        new_probs = jnp.where(new_live, jnp.exp(new_scores - both), 0.0)
        total = total * carried + jnp.sum(new_probs, axis=1, keepdims=True)
        accum = accum * carried
        for u in range(step_count):
            accum = accum + new_probs[:, u : u + 1] * new_v_ref[u : u + 1, span]
        sent = accum.astype(jnp.bfloat16)
        parts = []
        for value in (both, total):
            for _ in range(3):
                part = value.astype(jnp.bfloat16).astype(jnp.float32)
                parts.append(part)
                value = value - part
        lane = lax.broadcasted_iota(jnp.int32, (group * tokens, 128), 1)
        wide = jnp.zeros((group * tokens, 128), jnp.float32)
        for i, part in enumerate(parts):
            wide = jnp.where(lane == i, part, wide)
        turned = jnp.transpose(wide)[:16].astype(jnp.bfloat16)
        for g in range(group):
            pair = turned[:, g // 2 * 128 : (g // 2 + 1) * 128]
            for part in range(HD // columns):
                target = (kv * group + g) * (HD // columns) + part
                out_ref[target, :tokens, :] = sent[
                    g * tokens : (g + 1) * tokens, part * columns : (part + 1) * columns
                ]
                out_ref[target, tokens:, :] = pair


def out_kernel(req_count, where_ref, got_ref, *refs):
    w_refs = refs[:req_count]
    out_ref, turned_ref = refs[req_count:]
    blocks = got_ref.shape[0]
    copies, steps, _ = out_ref.shape
    tokens = copies * steps
    columns = got_ref.shape[2]
    head = where_ref[0] * columns // HD
    stats = got_ref[:, tokens:, :].astype(jnp.float32)
    tops = stats[:, 0, :] + stats[:, 1, :] + stats[:, 2, :]
    totals = stats[:, 3, :] + stats[:, 4, :] + stats[:, 5, :]
    rest = jnp.zeros((128 - 2 * blocks, 128), jnp.float32)
    turned_ref[...] = jnp.transpose(jnp.concatenate([tops, totals, rest]))
    mine = turned_ref[pl.ds(pl.multiple_of(head % 2 * tokens, tokens), tokens), :]
    tops = mine[:, :blocks]
    highest = jnp.max(tops, axis=1, keepdims=True)
    weights = jnp.exp(tops - highest)
    denominator = jnp.sum(mine[:, blocks : 2 * blocks] * weights, axis=1, keepdims=True)
    numerator = jnp.zeros((tokens, columns), jnp.float32)
    for b in range(blocks):
        numerator = numerator + got_ref[b, :tokens, :].astype(jnp.float32) * weights[:, b : b + 1]
    attention = (numerator / denominator).astype(jnp.bfloat16)
    for j, w_ref in enumerate(w_refs):
        width = w_ref.shape[1]
        part = jnp.dot(attention, w_ref[...], preferred_element_type=jnp.float32)
        part = part.astype(jnp.bfloat16)
        for i in range(copies):
            out_ref[i, :, j * width : (j + 1) * width] = part[i * steps : (i + 1) * steps]


def summed(req_count, where_ref, got_ref):
    width = got_ref.shape[2] // req_count
    blocks = []
    for i in range(req_count):
        j = lax.rem(where_ref[1] - i + req_count, req_count)
        cols = pl.ds(pl.multiple_of(j * width, width), width)
        blocks.append(jnp.sum(got_ref[:, :, cols].astype(jnp.float32), axis=0))
    return jnp.concatenate(blocks, axis=1)


def residual_kernel(
    req_count, where_ref, got_ref, hidden_ref, post_gain_ref, ffn_gain_ref, out_ref, residual_ref
):
    attn_out = summed(req_count, where_ref, got_ref)
    residual = hidden_ref[...].astype(jnp.float32) + normalize(attn_out) * post_gain_ref[...]
    residual_ref[...] = residual
    ffn_in = (normalize(residual) * ffn_gain_ref[...]).astype(jnp.bfloat16)
    for i in range(out_ref.shape[0]):
        out_ref[i] = ffn_in


def last_kernel(req_count, where_ref, got_ref, residual_ref, gain_ref, out_ref):
    down_out = summed(req_count, where_ref, got_ref)
    layer = (residual_ref[...] + normalize(down_out) * gain_ref[...]).astype(jnp.bfloat16)
    for i in range(out_ref.shape[0]):
        out_ref[i] = layer


def ffn_kernel(req_count, where_ref, x_ref, *refs):
    count = req_count + 2
    w_refs, out_ref, held, sem_ref = refs[:count], refs[count], refs[count + 1 : -1], refs[-1]
    gate_rows, width = w_refs[0].shape
    down_rows, down_width = w_refs[2].shape
    copies = []

    def load(source, target):
        copies.append(pltpu.make_async_copy(source, target, sem_ref.at[len(copies)]))
        copies[-1].start()

    for i in range(3):
        load(w_refs[i], held[i])
    packed_rows = 2 * gate_rows + down_rows * (down_width // width)
    spans = [(0, gate_rows), (gate_rows, gate_rows), (2 * gate_rows, packed_rows - 2 * gate_rows)]
    for j in range(3, count):
        for first, rows in spans:
            load(w_refs[j].at[pl.ds(first, rows), :], held[j].at[pl.ds(first, rows), :])
    blocks, steps, _ = x_ref.shape
    tokens = blocks * steps
    gate_out = up_out = None
    for j in range(req_count):
        first = lax.rem(where_ref[1] - j + req_count, req_count) * gate_rows
        cols = pl.ds(pl.multiple_of(first, gate_rows), gate_rows)
        part = x_ref[:, :, cols].reshape(tokens, gate_rows)
        copies[3 * j].wait()
        gate_w = held[0][...] if j == 0 else held[j + 2][:gate_rows, :]
        gate = jnp.dot(part, gate_w, preferred_element_type=jnp.float32)
        copies[3 * j + 1].wait()
        up_w = held[1][...] if j == 0 else held[j + 2][gate_rows : 2 * gate_rows, :]
        up = jnp.dot(part, up_w, preferred_element_type=jnp.float32)
        gate_out = gate if j == 0 else gate_out + gate
        up_out = up if j == 0 else up_out + up
    activated = (jax.nn.gelu(gate_out, approximate=True) * up_out).astype(jnp.bfloat16)
    for j in range(req_count):
        copies[3 * j + 2].wait()
        for piece in range(down_width // width):
            if j == 0:
                down_w = held[2][:, piece * width : (piece + 1) * width]
            else:
                row = 2 * gate_rows + piece * down_rows
                down_w = held[j + 2][row : row + down_rows, :]
            part = jnp.dot(activated, down_w, preferred_element_type=jnp.float32)
            part = part.astype(jnp.bfloat16)
            first = j * down_width + piece * width
            for i in range(blocks):
                out_ref[i, :, first : first + width] = part[i * steps : (i + 1) * steps]


def live_rows(
    seq_index, prompt_shape, pool_rows, group_of, prompt_lengths, tail_lengths, page_table
):
    group_count, prompt_span = prompt_shape
    rows_req = group_of.shape[0]
    member = (group_of % group_count)[:, None] == jnp.arange(group_count, dtype=jnp.int32)[None, :]
    prompt_pos = seq_index * prompt_span + jnp.arange(prompt_span, dtype=jnp.int32)
    prompt_live = prompt_pos[None, :] < prompt_lengths[:, None]
    prompt_mask = (member[:, :, None] & prompt_live[None, :, :]).reshape(
        rows_req, group_count * prompt_span
    )
    slot_count = pool_rows // PAGE
    table_row = page_table[0]
    table_len = table_row.shape[0]
    tail_pages = table_len // rows_req
    slot_ids = seq_index * slot_count + jnp.arange(slot_count, dtype=jnp.int32)
    matches = table_row[None, :] == slot_ids[:, None]
    entries = jnp.sum(
        jnp.where(matches, jnp.arange(table_len, dtype=jnp.int32)[None, :], 0), axis=1
    )
    owners = jnp.repeat(entries // tail_pages, PAGE)
    tail_pos = jnp.repeat(entries % tail_pages, PAGE) * PAGE + jnp.tile(
        jnp.arange(PAGE, dtype=jnp.int32), slot_count
    )
    tail_mask = (owners[None, :] == jnp.arange(rows_req, dtype=jnp.int32)[:, None]) & (
        tail_pos[None, :] < tail_lengths[:, None]
    )
    return jnp.concatenate([prompt_mask, tail_mask], axis=1)


def general_attention(
    seq_index,
    seq_count,
    rows_req,
    step_count,
    out_rows,
    projected,
    q_gain,
    k_gain,
    live,
    prompt_keys,
    prompt_values,
    tail_keys,
    tail_values,
):
    group_size = H // KV
    share = projected.shape[0]
    tokens = rows_req * step_count
    heads = normalize(projected.reshape(share, QKV // HD, HD))
    gains = jnp.concatenate(
        [
            jnp.broadcast_to(q_gain, (H, HD)),
            jnp.broadcast_to(k_gain, (KV, HD)),
            jnp.ones((KV, HD), jnp.float32),
        ]
    )
    mine = (heads * gains).astype(jnp.bfloat16).reshape(share, QKV)
    qkv = gather_rows(mine, seq_count)
    queries = qkv[:, : H * HD]
    keys_new = qkv[:, H * HD : (H + KV) * HD]
    values_new = qkv[:, (H + KV) * HD :]

    query_groups = queries.reshape(rows_req, step_count, KV, group_size, HD)
    mask = live[:, None, None, None, :]
    keys = jnp.concatenate([prompt_keys, tail_keys]).reshape(-1, KV, HD)
    values = jnp.concatenate([prompt_values, tail_values]).reshape(-1, KV, HD)
    scores = jnp.einsum("rskgd,pkd->rskgp", query_groups, keys, preferred_element_type=jnp.float32)
    scores = jnp.where(mask, scores, NEGATIVE)
    block_top = jnp.max(scores, axis=4)
    probs = jnp.where(mask, jnp.exp(scores - block_top[..., None]), 0.0)
    block_total = jnp.sum(probs, axis=4)
    block_accum = jnp.einsum(
        "rskgp,pkd->rskgd",
        probs.astype(jnp.bfloat16),
        values,
        preferred_element_type=jnp.float32,
    )

    stats = split_three(jnp.stack([block_top, block_total])).reshape(6, tokens, H)
    per_head = seq_count // H
    stats = jnp.repeat(stats.transpose(2, 0, 1).reshape(H, -1, out_rows), per_head, axis=0)
    accum_blocks = (
        block_accum.astype(jnp.bfloat16).reshape(tokens, seq_count, out_rows).transpose(1, 0, 2)
    )
    got = exchange(jnp.concatenate([accum_blocks, stats], axis=1), "seq")
    got_accum = got[:, :tokens].astype(jnp.float32)
    got_stats = got[:, tokens:].astype(jnp.float32).reshape(seq_count, 2 * 3, tokens)
    got_top = got_stats[:, 0] + got_stats[:, 2] + got_stats[:, 4]
    got_total = got_stats[:, 1] + got_stats[:, 3] + got_stats[:, 5]

    first_col = seq_index * out_rows
    head = first_col // HD
    kv_head = head // group_size
    head_queries = lax.dynamic_slice_in_dim(queries, head * HD, HD, 1)
    head_keys = lax.dynamic_slice_in_dim(keys_new, kv_head * HD, HD, 1)
    head_values = lax.dynamic_slice_in_dim(
        values_new, kv_head * HD + first_col % HD, out_rows, 1
    ).astype(jnp.float32)
    new_scores = jnp.dot(head_queries, head_keys.T, preferred_element_type=jnp.float32)
    token_ids = jnp.arange(tokens, dtype=jnp.int32)
    causal = (token_ids[:, None] // step_count == token_ids[None, :] // step_count) & (
        token_ids[:, None] >= token_ids[None, :]
    )
    new_scores = jnp.where(causal, new_scores, NEGATIVE)
    highest = jnp.maximum(jnp.max(got_top, axis=0), jnp.max(new_scores, axis=1))
    weights = jnp.exp(got_top - highest[None])
    new_probs = jnp.where(causal, jnp.exp(new_scores - highest[:, None]), 0.0)
    denominator = jnp.sum(got_total * weights, axis=0) + jnp.sum(new_probs, axis=1)
    numerator = jnp.sum(got_accum * weights[..., None], axis=0) + jnp.dot(
        new_probs, head_values, precision=lax.Precision.HIGHEST
    )
    return (numerator / denominator[:, None]).astype(jnp.bfloat16)


def on_device(
    req_count,
    seq_count,
    hidden_in,
    attn_gain,
    q_gain,
    k_gain,
    post_attn_gain,
    ffn_gain,
    post_ffn_gain,
    w_qkv,
    w_out,
    w_gate,
    w_up,
    w_down,
    prompt_keys,
    prompt_values,
    tail_keys,
    tail_values,
    group_of,
    prompt_lengths,
    tail_lengths,
    page_table,
):
    seq_index = lax.axis_index("seq")
    req_index = lax.axis_index("req")
    rows_req, step_count, _ = hidden_in.shape
    group_size = H // KV
    tokens = rows_req * step_count
    share = tokens // seq_count

    def shifted(values):
        return [values] + [
            lax.ppermute(values, "req", [(i, (i + j) % req_count) for i in range(req_count)])
            for j in range(1, req_count)
        ]

    where = jnp.stack([seq_index, req_index]).astype(jnp.int32)
    in_rows = w_qkv.shape[0]
    out_rows = w_out.shape[0]
    if in_rows % 128 == 0:
        normed_cols, head_gains = call(
            norm_columns_kernel,
            "norm_columns",
            (
                jax.ShapeDtypeStruct((tokens, in_rows), jnp.bfloat16),
                jax.ShapeDtypeStruct((8, HD), jnp.float32),
            ),
            where,
            hidden_in,
            attn_gain.reshape(1, D),
            q_gain.reshape(1, HD),
            k_gain.reshape(1, HD),
            limit=56,
        )
    else:
        normed = (normalize(hidden_in.astype(jnp.float32)) * attn_gain).astype(jnp.bfloat16)
        normed_cols = lax.dynamic_slice_in_dim(normed, seq_index * in_rows, in_rows, 2)
        normed_cols = normed_cols.reshape(tokens, in_rows)
    normed_all = lax.all_gather(normed_cols, "req", axis=0, tiled=True)
    out_blocks = shifted(w_out)
    width = w_gate.shape[1]
    pieces = [w_down[:, c : c + width] for c in range(0, w_down.shape[1], width)]
    packed = shifted(jnp.concatenate([w_gate, w_up] + pieces))[1:]

    qkv_part = jnp.dot(normed_all, w_qkv, preferred_element_type=jnp.float32)
    qkv_cols = w_qkv.shape[1]
    qkv_blocks = (
        (qkv_part * LINK_SCALE)
        .astype(jnp.float16)
        .reshape(req_count * seq_count, share, qkv_cols)
    )
    qkv_got = exchange(qkv_blocks, ("req", "seq"))
    qkv_got = qkv_got.reshape(req_count, seq_count, share, qkv_cols)
    projected = jnp.sum(qkv_got.astype(jnp.float32), axis=1) * (1.0 / LINK_SCALE)
    live = live_rows(
        seq_index, prompt_keys.shape[:2], tail_keys.shape[1], group_of, prompt_lengths,
        tail_lengths, page_table,
    )
    caches = [
        array.reshape(-1, KV * HD) for array in (prompt_keys, prompt_values, tail_keys, tail_values)
    ]
    direct = share == step_count and out_rows % 128 == 0 and tokens == 64 and qkv_cols % HD == 0
    if direct:
        q_blocks, new_keys, new_values = call(
            head_norm_kernel,
            "head_norm",
            (
                jax.ShapeDtypeStruct((seq_count, share, H * HD), jnp.bfloat16),
                jax.ShapeDtypeStruct((8, KV * HD), jnp.float32),
                jax.ShapeDtypeStruct((8, KV * HD), jnp.float32),
            ),
            where,
            projected,
            head_gains,
        )
        cache_shape = jax.ShapeDtypeStruct(
            (caches[0].shape[0] + caches[2].shape[0], KV * HD), jnp.bfloat16
        )
        keys, values = call(
            stage_kernel, "stage_caches", (cache_shape, cache_shape), where, new_keys, *caches
        )
        where_block, out_blocks = tie(where, out_blocks)
        live = jnp.repeat(live.astype(jnp.float32), step_count, axis=0)
        sent = call(
            functools.partial(block_kernel, step_count),
            "block_attention",
            jax.ShapeDtypeStruct((seq_count, tokens + 16, out_rows), jnp.bfloat16),
            where_block,
            exchange(q_blocks, "seq"),
            live,
            new_keys,
            new_values,
            keys,
            values,
        )
        got = exchange(sent, "seq")
        out_part = call(
            functools.partial(out_kernel, req_count),
            "combine_out",
            jax.ShapeDtypeStruct((seq_count, share, D), jnp.bfloat16),
            where,
            got,
            *out_blocks,
            scratch=[pltpu.VMEM((128, 128), jnp.float32)],
        )
    else:
        projected = projected.transpose(1, 0, 2).reshape(share, QKV)
        attention_cols = general_attention(
            seq_index, seq_count, rows_req, step_count, out_rows, projected, q_gain, k_gain,
            live, *caches,
        )
        out_part = jnp.concatenate(
            [jnp.dot(attention_cols, w, preferred_element_type=jnp.float32) for w in out_blocks],
            axis=1,
        )
        out_part = out_part.astype(jnp.bfloat16).reshape(seq_count, share, D)
    hidden_mine = lax.dynamic_index_in_dim(
        hidden_in.reshape(seq_count, share, D), seq_index, 0, keepdims=False
    )
    ffn_blocks, residual = call(
        functools.partial(residual_kernel, req_count),
        "residual_norms",
        (
            jax.ShapeDtypeStruct((seq_count, share, D), jnp.bfloat16),
            jax.ShapeDtypeStruct((share, D), jnp.float32),
        ),
        where,
        exchange(out_part, "seq"),
        hidden_mine,
        post_attn_gain.reshape(1, D),
        ffn_gain.reshape(1, D),
    )
    held = [w_gate, w_up, w_down] + list(packed)
    down_part = call(
        functools.partial(ffn_kernel, req_count),
        "feed_forward",
        jax.ShapeDtypeStruct((seq_count, share, D), jnp.bfloat16),
        where,
        exchange(ffn_blocks, "seq"),
        *held,
        scratch=[pltpu.VMEM(w.shape, w.dtype) for w in held]
        + [pltpu.SemaphoreType.DMA((3 * req_count,))],
        any_from=2,
    )
    layer_blocks = call(
        functools.partial(last_kernel, req_count),
        "last_norm",
        jax.ShapeDtypeStruct((seq_count, share, D), jnp.bfloat16),
        where,
        exchange(down_part, "seq"),
        residual,
        post_ffn_gain.reshape(1, D),
    )
    layer_out, where = tie(exchange(layer_blocks, "seq"), where)
    return layer_out.reshape(rows_req, step_count, D)


def solution(mesh):
    return jax.shard_map(
        functools.partial(on_device, mesh.shape["req"], mesh.shape["seq"]),
        mesh=mesh,
        in_specs=(
            P("req", None, None),
            P(),
            P(),
            P(),
            P(),
            P(),
            P(),
            P("seq", "req"),
            P("seq", "req"),
            P("req", "seq"),
            P("req", "seq"),
            P("seq", "req"),
            P("req", "seq", None),
            P("req", "seq", None),
            P("req", "seq", None),
            P("req", "seq", None),
            P("req"),
            P("req"),
            P("req"),
            P("req", None),
        ),
        out_specs=P("req", None, None),
        check_vma=False,
    )
```

```python
import functools

import jax
import jax.numpy as jnp
from jax import lax
from jax.experimental import pallas as pl
from jax.experimental.pallas import tpu as pltpu
from jax.sharding import PartitionSpec as P

D = 2048
H = 8
KV = 2
HD = 256
PAGE = 16
QKV = 3072


EPSILON = 1e-06
NEGATIVE = -1e30
LINK_SCALE = 512.0


def normalize(values):
    return values * lax.rsqrt(jnp.mean(values * values, axis=-1, keepdims=True) + EPSILON)


def split_three(values):
    high = values.astype(jnp.bfloat16)
    rest = values - high.astype(jnp.float32)
    middle = rest.astype(jnp.bfloat16)
    low = (rest - middle.astype(jnp.float32)).astype(jnp.bfloat16)
    return jnp.stack([high, middle, low])


def exchange(blocks, axes, groups=None):
    return lax.all_to_all(
        blocks, axes, split_axis=0, concat_axis=0, tiled=True, axis_index_groups=groups
    )


def tie(*arrays):
    return lax.optimization_barrier(arrays)


def spread(block, copies):
    return jnp.broadcast_to(block[None], (copies,) + block.shape)


def gather_rows(rows, count):
    return exchange(spread(rows, count), "seq").reshape(count * rows.shape[0], rows.shape[1])


def call(kernel, name, out_shape, *operands, scratch=(), any_from=None, limit=14):
    in_specs = [pl.BlockSpec(memory_space=pltpu.SMEM)]
    for i in range(1, len(operands)):
        space = pl.ANY if any_from is not None and i >= any_from else pltpu.VMEM
        in_specs.append(pl.BlockSpec(memory_space=space))
    return pl.pallas_call(
        kernel,
        name=name,
        out_shape=out_shape,
        in_specs=in_specs,
        out_specs=jax.tree.map(lambda _: pl.BlockSpec(memory_space=pltpu.VMEM), out_shape),
        scratch_shapes=scratch,
        compiler_params=pltpu.CompilerParams(vmem_limit_bytes=limit * 1024 * 1024),
    )(*operands)


def norm_columns_kernel(
    where_ref, hidden_ref, gain_ref, q_gain_ref, k_gain_ref, out_ref, head_gains_ref
):
    head_gains_ref[0:1, :] = q_gain_ref[...]
    head_gains_ref[1:2, :] = k_gain_ref[...]
    columns = out_ref.shape[1]
    hidden = hidden_ref[...].astype(jnp.float32)
    scale = lax.rsqrt(jnp.mean(hidden * hidden, axis=-1, keepdims=True) + EPSILON)
    cols = pl.ds(pl.multiple_of(where_ref[0] * columns, columns), columns)
    normed = hidden_ref[:, :, cols].astype(jnp.float32) * scale * gain_ref[:, cols]
    out_ref[...] = normed.reshape(out_ref.shape).astype(jnp.bfloat16)


def head_norm_kernel(where_ref, projected_ref, gains_ref, q_ref, k_ref, v_ref):
    width = projected_ref.shape[2]
    copies, rows, _ = q_ref.shape
    fill = jnp.zeros((k_ref.shape[0] - rows, HD), jnp.float32)
    for head in range(H + 2 * KV):
        half, first = divmod(head * HD, width)
        values = normalize(projected_ref[half, :, first : first + HD])
        if head < H:
            values = (values * gains_ref[0:1, :]).astype(jnp.bfloat16)
            for i in range(copies):
                q_ref[i, :, head * HD : (head + 1) * HD] = values
        else:
            if head < H + KV:
                values = values * gains_ref[1:2, :]
            values = values.astype(jnp.bfloat16).astype(jnp.float32)
            target, slot = (k_ref, head - H) if head < H + KV else (v_ref, head - H - KV)
            target[:, slot * HD : (slot + 1) * HD] = jnp.concatenate([values, fill])


def stage_kernel(
    where_ref, after_ref, prompt_k_ref, prompt_v_ref, tail_k_ref, tail_v_ref, keys_ref, values_ref
):
    rows = prompt_k_ref.shape[0]
    keys_ref[:rows, :] = prompt_k_ref[...]
    keys_ref[rows:, :] = tail_k_ref[...]
    values_ref[:rows, :] = prompt_v_ref[...]
    values_ref[rows:, :] = tail_v_ref[...]


def dot_last(a, b):
    return lax.dot_general(a, b, (((1,), (1,)), ((), ())), preferred_element_type=jnp.float32)


def block_kernel(
    step_count,
    where_ref,
    q_ref,
    live_ref,
    new_k_ref,
    new_v_ref,
    keys_ref,
    values_ref,
    out_ref,
):
    copies, steps, _ = q_ref.shape
    tokens = copies * steps
    columns = out_ref.shape[2]
    group = H // KV
    queries = q_ref[...].reshape(tokens, H * HD)
    live = jnp.concatenate([live_ref[...]] * group) > 0.5
    first_token = where_ref[0] * step_count
    shape = (group * tokens, new_k_ref.shape[0])
    step = lax.broadcasted_iota(jnp.int32, shape, 0) % tokens - first_token
    new_index = lax.broadcasted_iota(jnp.int32, shape, 1)
    new_live = (step >= new_index) & (step < step_count)
    for kv in range(KV):
        span = slice(kv * HD, (kv + 1) * HD)
        q = jnp.concatenate(
            [queries[:, (kv * group + g) * HD : (kv * group + g + 1) * HD] for g in range(group)]
        )
        scores = jnp.where(live, dot_last(q, keys_ref[:, span]), NEGATIVE)
        top = jnp.max(scores, axis=1, keepdims=True)
        probs = jnp.where(live, jnp.exp(scores - top), 0.0)
        total = jnp.sum(probs, axis=1, keepdims=True)
        accum = jnp.dot(
            probs.astype(jnp.bfloat16), values_ref[:, span], preferred_element_type=jnp.float32
        )
        new_scores = dot_last(q, new_k_ref[:, span].astype(jnp.bfloat16))
        new_scores = jnp.where(new_live, new_scores, NEGATIVE)
        both = jnp.maximum(top, jnp.max(new_scores, axis=1, keepdims=True))
        carried = jnp.exp(top - both)
        new_probs = jnp.where(new_live, jnp.exp(new_scores - both), 0.0)
        total = total * carried + jnp.sum(new_probs, axis=1, keepdims=True)
        accum = accum * carried
        for u in range(step_count):
            accum = accum + new_probs[:, u : u + 1] * new_v_ref[u : u + 1, span]
        sent = accum.astype(jnp.bfloat16)
        parts = []
        for value in (both, total):
            for _ in range(3):
                part = value.astype(jnp.bfloat16).astype(jnp.float32)
                parts.append(part)
                value = value - part
        lane = lax.broadcasted_iota(jnp.int32, (group * tokens, 128), 1)
        wide = jnp.zeros((group * tokens, 128), jnp.float32)
        for i, part in enumerate(parts):
            wide = jnp.where(lane == i, part, wide)
        turned = jnp.transpose(wide)[:16].astype(jnp.bfloat16)
        for g in range(group):
            pair = turned[:, g // 2 * 128 : (g // 2 + 1) * 128]
            for part in range(HD // columns):
                target = (kv * group + g) * (HD // columns) + part
                out_ref[target, :tokens, :] = sent[
                    g * tokens : (g + 1) * tokens, part * columns : (part + 1) * columns
                ]
                out_ref[target, tokens:, :] = pair


def out_kernel(req_count, where_ref, got_ref, *refs):
    w_refs = refs[:req_count]
    out_ref, turned_ref = refs[req_count:]
    blocks = got_ref.shape[0]
    copies, steps, _ = out_ref.shape
    tokens = copies * steps
    columns = got_ref.shape[2]
    head = where_ref[0] * columns // HD
    stats = got_ref[:, tokens:, :].astype(jnp.float32)
    tops = stats[:, 0, :] + stats[:, 1, :] + stats[:, 2, :]
    totals = stats[:, 3, :] + stats[:, 4, :] + stats[:, 5, :]
    rest = jnp.zeros((128 - 2 * blocks, 128), jnp.float32)
    turned_ref[...] = jnp.transpose(jnp.concatenate([tops, totals, rest]))
    mine = turned_ref[pl.ds(pl.multiple_of(head % 2 * tokens, tokens), tokens), :]
    tops = mine[:, :blocks]
    highest = jnp.max(tops, axis=1, keepdims=True)
    weights = jnp.exp(tops - highest)
    denominator = jnp.sum(mine[:, blocks : 2 * blocks] * weights, axis=1, keepdims=True)
    numerator = jnp.zeros((tokens, columns), jnp.float32)
    for b in range(blocks):
        numerator = numerator + got_ref[b, :tokens, :].astype(jnp.float32) * weights[:, b : b + 1]
    attention = (numerator / denominator).astype(jnp.bfloat16)
    for j, w_ref in enumerate(w_refs):
        width = w_ref.shape[1]
        part = jnp.dot(attention, w_ref[...], preferred_element_type=jnp.float32)
        part = part.astype(jnp.bfloat16)
        for i in range(copies):
            out_ref[i, :, j * width : (j + 1) * width] = part[i * steps : (i + 1) * steps]


def summed(req_count, where_ref, got_ref):
    width = got_ref.shape[2] // req_count
    blocks = []
    for i in range(req_count):
        j = lax.rem(where_ref[1] - i + req_count, req_count)
        cols = pl.ds(pl.multiple_of(j * width, width), width)
        blocks.append(jnp.sum(got_ref[:, :, cols].astype(jnp.float32), axis=0))
    return jnp.concatenate(blocks, axis=1)


def residual_kernel(
    req_count, where_ref, got_ref, hidden_ref, post_gain_ref, ffn_gain_ref, out_ref, residual_ref
):
    attn_out = summed(req_count, where_ref, got_ref)
    residual = hidden_ref[...].astype(jnp.float32) + normalize(attn_out) * post_gain_ref[...]
    residual_ref[...] = residual
    ffn_in = (normalize(residual) * ffn_gain_ref[...]).astype(jnp.bfloat16)
    for i in range(out_ref.shape[0]):
        out_ref[i] = ffn_in


def last_kernel(req_count, where_ref, got_ref, residual_ref, gain_ref, out_ref):
    down_out = summed(req_count, where_ref, got_ref)
    layer = (residual_ref[...] + normalize(down_out) * gain_ref[...]).astype(jnp.bfloat16)
    for i in range(out_ref.shape[0]):
        out_ref[i] = layer


def ffn_kernel(req_count, where_ref, x_ref, *refs):
    count = req_count + 2
    w_refs, out_ref, held, sem_ref = refs[:count], refs[count], refs[count + 1 : -1], refs[-1]
    gate_rows, width = w_refs[0].shape
    down_rows, down_width = w_refs[2].shape
    copies = []

    def load(source, target):
        copies.append(pltpu.make_async_copy(source, target, sem_ref.at[len(copies)]))
        copies[-1].start()

    for i in range(3):
        load(w_refs[i], held[i])
    packed_rows = 2 * gate_rows + down_rows * (down_width // width)
    spans = [(0, gate_rows), (gate_rows, gate_rows), (2 * gate_rows, packed_rows - 2 * gate_rows)]
    for j in range(3, count):
        for first, rows in spans:
            load(w_refs[j].at[pl.ds(first, rows), :], held[j].at[pl.ds(first, rows), :])
    blocks, steps, _ = x_ref.shape
    tokens = blocks * steps
    gate_out = up_out = None
    for j in range(req_count):
        first = lax.rem(where_ref[1] - j + req_count, req_count) * gate_rows
        cols = pl.ds(pl.multiple_of(first, gate_rows), gate_rows)
        part = x_ref[:, :, cols].reshape(tokens, gate_rows)
        copies[3 * j].wait()
        gate_w = held[0][...] if j == 0 else held[j + 2][:gate_rows, :]
        gate = jnp.dot(part, gate_w, preferred_element_type=jnp.float32)
        copies[3 * j + 1].wait()
        up_w = held[1][...] if j == 0 else held[j + 2][gate_rows : 2 * gate_rows, :]
        up = jnp.dot(part, up_w, preferred_element_type=jnp.float32)
        gate_out = gate if j == 0 else gate_out + gate
        up_out = up if j == 0 else up_out + up
    activated = (jax.nn.gelu(gate_out, approximate=True) * up_out).astype(jnp.bfloat16)
    for j in range(req_count):
        copies[3 * j + 2].wait()
        for piece in range(down_width // width):
            if j == 0:
                down_w = held[2][:, piece * width : (piece + 1) * width]
            else:
                row = 2 * gate_rows + piece * down_rows
                down_w = held[j + 2][row : row + down_rows, :]
            part = jnp.dot(activated, down_w, preferred_element_type=jnp.float32)
            part = part.astype(jnp.bfloat16)
            first = j * down_width + piece * width
            for i in range(blocks):
                out_ref[i, :, first : first + width] = part[i * steps : (i + 1) * steps]


def live_rows(
    seq_index, prompt_shape, pool_rows, group_of, prompt_lengths, tail_lengths, page_table
):
    group_count, prompt_span = prompt_shape
    rows_req = group_of.shape[0]
    member = (group_of % group_count)[:, None] == jnp.arange(group_count, dtype=jnp.int32)[None, :]
    prompt_pos = seq_index * prompt_span + jnp.arange(prompt_span, dtype=jnp.int32)
    prompt_live = prompt_pos[None, :] < prompt_lengths[:, None]
    prompt_mask = (member[:, :, None] & prompt_live[None, :, :]).reshape(
        rows_req, group_count * prompt_span
    )
    slot_count = pool_rows // PAGE
    table_row = page_table[0]
    table_len = table_row.shape[0]
    tail_pages = table_len // rows_req
    slot_ids = seq_index * slot_count + jnp.arange(slot_count, dtype=jnp.int32)
    matches = table_row[None, :] == slot_ids[:, None]
    entries = jnp.sum(
        jnp.where(matches, jnp.arange(table_len, dtype=jnp.int32)[None, :], 0), axis=1
    )
    owners = jnp.repeat(entries // tail_pages, PAGE)
    tail_pos = jnp.repeat(entries % tail_pages, PAGE) * PAGE + jnp.tile(
        jnp.arange(PAGE, dtype=jnp.int32), slot_count
    )
    tail_mask = (owners[None, :] == jnp.arange(rows_req, dtype=jnp.int32)[:, None]) & (
        tail_pos[None, :] < tail_lengths[:, None]
    )
    return jnp.concatenate([prompt_mask, tail_mask], axis=1)


def general_attention(
    seq_index,
    seq_count,
    rows_req,
    step_count,
    out_rows,
    projected,
    q_gain,
    k_gain,
    live,
    prompt_keys,
    prompt_values,
    tail_keys,
    tail_values,
):
    group_size = H // KV
    share = projected.shape[0]
    tokens = rows_req * step_count
    heads = normalize(projected.reshape(share, QKV // HD, HD))
    gains = jnp.concatenate(
        [
            jnp.broadcast_to(q_gain, (H, HD)),
            jnp.broadcast_to(k_gain, (KV, HD)),
            jnp.ones((KV, HD), jnp.float32),
        ]
    )
    mine = (heads * gains).astype(jnp.bfloat16).reshape(share, QKV)
    qkv = gather_rows(mine, seq_count)
    queries = qkv[:, : H * HD]
    keys_new = qkv[:, H * HD : (H + KV) * HD]
    values_new = qkv[:, (H + KV) * HD :]

    query_groups = queries.reshape(rows_req, step_count, KV, group_size, HD)
    mask = live[:, None, None, None, :]
    keys = jnp.concatenate([prompt_keys, tail_keys]).reshape(-1, KV, HD)
    values = jnp.concatenate([prompt_values, tail_values]).reshape(-1, KV, HD)
    scores = jnp.einsum("rskgd,pkd->rskgp", query_groups, keys, preferred_element_type=jnp.float32)
    scores = jnp.where(mask, scores, NEGATIVE)
    block_top = jnp.max(scores, axis=4)
    probs = jnp.where(mask, jnp.exp(scores - block_top[..., None]), 0.0)
    block_total = jnp.sum(probs, axis=4)
    block_accum = jnp.einsum(
        "rskgp,pkd->rskgd",
        probs.astype(jnp.bfloat16),
        values,
        preferred_element_type=jnp.float32,
    )

    stats = split_three(jnp.stack([block_top, block_total])).reshape(6, tokens, H)
    per_head = seq_count // H
    stats = jnp.repeat(stats.transpose(2, 0, 1).reshape(H, -1, out_rows), per_head, axis=0)
    accum_blocks = (
        block_accum.astype(jnp.bfloat16).reshape(tokens, seq_count, out_rows).transpose(1, 0, 2)
    )
    got = exchange(jnp.concatenate([accum_blocks, stats], axis=1), "seq")
    got_accum = got[:, :tokens].astype(jnp.float32)
    got_stats = got[:, tokens:].astype(jnp.float32).reshape(seq_count, 2 * 3, tokens)
    got_top = got_stats[:, 0] + got_stats[:, 2] + got_stats[:, 4]
    got_total = got_stats[:, 1] + got_stats[:, 3] + got_stats[:, 5]

    first_col = seq_index * out_rows
    head = first_col // HD
    kv_head = head // group_size
    head_queries = lax.dynamic_slice_in_dim(queries, head * HD, HD, 1)
    head_keys = lax.dynamic_slice_in_dim(keys_new, kv_head * HD, HD, 1)
    head_values = lax.dynamic_slice_in_dim(
        values_new, kv_head * HD + first_col % HD, out_rows, 1
    ).astype(jnp.float32)
    new_scores = jnp.dot(head_queries, head_keys.T, preferred_element_type=jnp.float32)
    token_ids = jnp.arange(tokens, dtype=jnp.int32)
    causal = (token_ids[:, None] // step_count == token_ids[None, :] // step_count) & (
        token_ids[:, None] >= token_ids[None, :]
    )
    new_scores = jnp.where(causal, new_scores, NEGATIVE)
    highest = jnp.maximum(jnp.max(got_top, axis=0), jnp.max(new_scores, axis=1))
    weights = jnp.exp(got_top - highest[None])
    new_probs = jnp.where(causal, jnp.exp(new_scores - highest[:, None]), 0.0)
    denominator = jnp.sum(got_total * weights, axis=0) + jnp.sum(new_probs, axis=1)
    numerator = jnp.sum(got_accum * weights[..., None], axis=0) + jnp.dot(
        new_probs, head_values, precision=lax.Precision.HIGHEST
    )
    return (numerator / denominator[:, None]).astype(jnp.bfloat16)


def on_device(
    req_count,
    seq_count,
    hidden_in,
    attn_gain,
    q_gain,
    k_gain,
    post_attn_gain,
    ffn_gain,
    post_ffn_gain,
    w_qkv,
    w_out,
    w_gate,
    w_up,
    w_down,
    prompt_keys,
    prompt_values,
    tail_keys,
    tail_values,
    group_of,
    prompt_lengths,
    tail_lengths,
    page_table,
):
    seq_index = lax.axis_index("seq")
    req_index = lax.axis_index("req")
    rows_req, step_count, _ = hidden_in.shape
    group_size = H // KV
    tokens = rows_req * step_count
    share = tokens // seq_count

    def shifted(values):
        return [values] + [
            lax.ppermute(values, "req", [(i, (i + j) % req_count) for i in range(req_count)])
            for j in range(1, req_count)
        ]

    where = jnp.stack([seq_index, req_index]).astype(jnp.int32)
    in_rows = w_qkv.shape[0]
    out_rows = w_out.shape[0]
    if in_rows % 128 == 0:
        normed_cols, head_gains = call(
            norm_columns_kernel,
            "norm_columns",
            (
                jax.ShapeDtypeStruct((tokens, in_rows), jnp.bfloat16),
                jax.ShapeDtypeStruct((8, HD), jnp.float32),
            ),
            where,
            hidden_in,
            attn_gain.reshape(1, D),
            q_gain.reshape(1, HD),
            k_gain.reshape(1, HD),
        )
    else:
        normed = (normalize(hidden_in.astype(jnp.float32)) * attn_gain).astype(jnp.bfloat16)
        normed_cols = lax.dynamic_slice_in_dim(normed, seq_index * in_rows, in_rows, 2)
        normed_cols = normed_cols.reshape(tokens, in_rows)
    normed_all = lax.all_gather(normed_cols, "req", axis=0, tiled=True)
    out_blocks = shifted(w_out)
    width = w_gate.shape[1]
    pieces = [w_down[:, c : c + width] for c in range(0, w_down.shape[1], width)]
    packed = shifted(jnp.concatenate([w_gate, w_up] + pieces))[1:]

    qkv_part = jnp.dot(normed_all, w_qkv, preferred_element_type=jnp.float32)
    qkv_cols = w_qkv.shape[1]
    qkv_blocks = (
        (qkv_part * LINK_SCALE)
        .astype(jnp.float16)
        .reshape(req_count * seq_count, share, qkv_cols)
    )
    qkv_got = exchange(qkv_blocks, ("req", "seq"))
    qkv_got = qkv_got.reshape(req_count, seq_count, share, qkv_cols)
    projected = jnp.sum(qkv_got.astype(jnp.float32), axis=1) * (1.0 / LINK_SCALE)
    live = live_rows(
        seq_index, prompt_keys.shape[:2], tail_keys.shape[1], group_of, prompt_lengths,
        tail_lengths, page_table,
    )
    caches = [
        array.reshape(-1, KV * HD) for array in (prompt_keys, prompt_values, tail_keys, tail_values)
    ]
    direct = share == step_count and out_rows % 128 == 0 and tokens == 64 and qkv_cols % HD == 0
    if direct:
        q_blocks, new_keys, new_values = call(
            head_norm_kernel,
            "head_norm",
            (
                jax.ShapeDtypeStruct((seq_count, share, H * HD), jnp.bfloat16),
                jax.ShapeDtypeStruct((8, KV * HD), jnp.float32),
                jax.ShapeDtypeStruct((8, KV * HD), jnp.float32),
            ),
            where,
            projected,
            head_gains,
        )
        cache_shape = jax.ShapeDtypeStruct(
            (caches[0].shape[0] + caches[2].shape[0], KV * HD), jnp.bfloat16
        )
        keys, values = call(
            stage_kernel, "stage_caches", (cache_shape, cache_shape), where, new_keys, *caches
        )
        where_block, out_blocks = tie(where, out_blocks)
        live = jnp.repeat(live.astype(jnp.float32), step_count, axis=0)
        sent = call(
            functools.partial(block_kernel, step_count),
            "block_attention",
            jax.ShapeDtypeStruct((seq_count, tokens + 16, out_rows), jnp.bfloat16),
            where_block,
            exchange(q_blocks, "seq"),
            live,
            new_keys,
            new_values,
            keys,
            values,
        )
        got = exchange(sent, "seq")
        out_part = call(
            functools.partial(out_kernel, req_count),
            "combine_out",
            jax.ShapeDtypeStruct((seq_count, share, D), jnp.bfloat16),
            where,
            got,
            *out_blocks,
            scratch=[pltpu.VMEM((128, 128), jnp.float32)],
        )
    else:
        projected = projected.transpose(1, 0, 2).reshape(share, QKV)
        attention_cols = general_attention(
            seq_index, seq_count, rows_req, step_count, out_rows, projected, q_gain, k_gain,
            live, *caches,
        )
        out_part = jnp.concatenate(
            [jnp.dot(attention_cols, w, preferred_element_type=jnp.float32) for w in out_blocks],
            axis=1,
        )
        out_part = out_part.astype(jnp.bfloat16).reshape(seq_count, share, D)
    hidden_mine = lax.dynamic_index_in_dim(
        hidden_in.reshape(seq_count, share, D), seq_index, 0, keepdims=False
    )
    ffn_blocks, residual = call(
        functools.partial(residual_kernel, req_count),
        "residual_norms",
        (
            jax.ShapeDtypeStruct((seq_count, share, D), jnp.bfloat16),
            jax.ShapeDtypeStruct((share, D), jnp.float32),
        ),
        where,
        exchange(out_part, "seq"),
        hidden_mine,
        post_attn_gain.reshape(1, D),
        ffn_gain.reshape(1, D),
    )
    held = [w_gate, w_up, w_down] + list(packed)
    down_part = call(
        functools.partial(ffn_kernel, req_count),
        "feed_forward",
        jax.ShapeDtypeStruct((seq_count, share, D), jnp.bfloat16),
        where,
        exchange(ffn_blocks, "seq"),
        *held,
        scratch=[pltpu.VMEM(w.shape, w.dtype) for w in held]
        + [pltpu.SemaphoreType.DMA((3 * req_count,))],
        any_from=2,
    )
    layer_blocks = call(
        functools.partial(last_kernel, req_count),
        "last_norm",
        jax.ShapeDtypeStruct((seq_count, share, D), jnp.bfloat16),
        where,
        exchange(down_part, "seq"),
        residual,
        post_ffn_gain.reshape(1, D),
    )
    layer_out, where = tie(exchange(layer_blocks, "seq"), where)
    return layer_out.reshape(rows_req, step_count, D)


def solution(mesh):
    return jax.shard_map(
        functools.partial(on_device, mesh.shape["req"], mesh.shape["seq"]),
        mesh=mesh,
        in_specs=(
            P("req", None, None),
            P(),
            P(),
            P(),
            P(),
            P(),
            P(),
            P("seq", "req"),
            P("seq", "req"),
            P("req", "seq"),
            P("req", "seq"),
            P("seq", "req"),
            P("req", "seq", None),
            P("req", "seq", None),
            P("req", "seq", None),
            P("req", "seq", None),
            P("req"),
            P("req"),
            P("req"),
            P("req", None),
        ),
        out_specs=P("req", None, None),
        check_vma=False,
    )
```

```python
import functools

import jax
import jax.numpy as jnp
from jax import lax
from jax.experimental import pallas as pl
from jax.experimental.pallas import tpu as pltpu
from jax.sharding import PartitionSpec as P

D = 2048
H = 8
KV = 2
HD = 256
PAGE = 16
QKV = 3072


EPSILON = 1e-06
NEGATIVE = -1e30
LINK_SCALE = 512.0


def normalize(values):
    return values * lax.rsqrt(jnp.mean(values * values, axis=-1, keepdims=True) + EPSILON)


def split_three(values):
    high = values.astype(jnp.bfloat16)
    rest = values - high.astype(jnp.float32)
    middle = rest.astype(jnp.bfloat16)
    low = (rest - middle.astype(jnp.float32)).astype(jnp.bfloat16)
    return jnp.stack([high, middle, low])


def exchange(blocks, axes, groups=None):
    return lax.all_to_all(
        blocks, axes, split_axis=0, concat_axis=0, tiled=True, axis_index_groups=groups
    )


def tie(*arrays):
    return lax.optimization_barrier(arrays)


def spread(block, copies):
    return jnp.broadcast_to(block[None], (copies,) + block.shape)


def gather_rows(rows, count):
    return exchange(spread(rows, count), "seq").reshape(count * rows.shape[0], rows.shape[1])


def call(kernel, name, out_shape, *operands, scratch=(), any_from=None, limit=16):
    in_specs = [pl.BlockSpec(memory_space=pltpu.SMEM)]
    for i in range(1, len(operands)):
        space = pl.ANY if any_from is not None and i >= any_from else pltpu.VMEM
        in_specs.append(pl.BlockSpec(memory_space=space))
    return pl.pallas_call(
        kernel,
        name=name,
        out_shape=out_shape,
        in_specs=in_specs,
        out_specs=jax.tree.map(lambda _: pl.BlockSpec(memory_space=pltpu.VMEM), out_shape),
        scratch_shapes=scratch,
        compiler_params=pltpu.CompilerParams(vmem_limit_bytes=limit * 1024 * 1024),
    )(*operands)


def norm_columns_kernel(where_ref, hidden_ref, gain_ref, out_ref):
    columns = out_ref.shape[1]
    hidden = hidden_ref[...].astype(jnp.float32)
    scale = lax.rsqrt(jnp.mean(hidden * hidden, axis=-1, keepdims=True) + EPSILON)
    cols = pl.ds(pl.multiple_of(where_ref[0] * columns, columns), columns)
    normed = hidden_ref[:, :, cols].astype(jnp.float32) * scale * gain_ref[:, cols]
    out_ref[...] = normed.reshape(out_ref.shape).astype(jnp.bfloat16)


def head_norm_kernel(where_ref, projected_ref, gains_ref, q_ref, k_ref, v_ref):
    width = projected_ref.shape[2]
    copies, rows, _ = q_ref.shape
    fill = jnp.zeros((k_ref.shape[0] - rows, HD), jnp.float32)
    for head in range(H + 2 * KV):
        half, first = divmod(head * HD, width)
        values = normalize(projected_ref[half, :, first : first + HD])
        if head < H:
            values = (values * gains_ref[0:1, :]).astype(jnp.bfloat16)
            for i in range(copies):
                q_ref[i, :, head * HD : (head + 1) * HD] = values
        else:
            if head < H + KV:
                values = values * gains_ref[1:2, :]
            values = values.astype(jnp.bfloat16).astype(jnp.float32)
            target, slot = (k_ref, head - H) if head < H + KV else (v_ref, head - H - KV)
            target[:, slot * HD : (slot + 1) * HD] = jnp.concatenate([values, fill])


def dot_last(a, b):
    return lax.dot_general(a, b, (((1,), (1,)), ((), ())), preferred_element_type=jnp.float32)


def block_kernel(
    step_count,
    where_ref,
    q_ref,
    live_ref,
    new_k_ref,
    new_v_ref,
    prompt_k_ref,
    prompt_v_ref,
    tail_k_ref,
    tail_v_ref,
    out_ref,
):
    copies, steps, _ = q_ref.shape
    tokens = copies * steps
    columns = out_ref.shape[2]
    group = H // KV
    queries = q_ref[...].reshape(tokens, H * HD)
    live = jnp.concatenate([live_ref[...]] * group) > 0.5
    first_token = where_ref[0] * step_count
    shape = (group * tokens, new_k_ref.shape[0])
    step = lax.broadcasted_iota(jnp.int32, shape, 0) % tokens - first_token
    new_index = lax.broadcasted_iota(jnp.int32, shape, 1)
    new_live = (step >= new_index) & (step < step_count)
    prompt_rows = prompt_k_ref.shape[0]
    for kv in range(KV):
        span = slice(kv * HD, (kv + 1) * HD)
        q = jnp.concatenate(
            [queries[:, (kv * group + g) * HD : (kv * group + g + 1) * HD] for g in range(group)]
        )
        scores = jnp.concatenate(
            [dot_last(q, prompt_k_ref[:, span]), dot_last(q, tail_k_ref[:, span])], axis=1
        )
        scores = jnp.where(live, scores, NEGATIVE)
        top = jnp.max(scores, axis=1, keepdims=True)
        probs = jnp.where(live, jnp.exp(scores - top), 0.0)
        total = jnp.sum(probs, axis=1, keepdims=True)
        rounded = probs.astype(jnp.bfloat16)
        accum = jnp.dot(
            rounded[:, :prompt_rows], prompt_v_ref[:, span], preferred_element_type=jnp.float32
        ) + jnp.dot(
            rounded[:, prompt_rows:], tail_v_ref[:, span], preferred_element_type=jnp.float32
        )
        new_scores = dot_last(q, new_k_ref[:, span].astype(jnp.bfloat16))
        new_scores = jnp.where(new_live, new_scores, NEGATIVE)
        both = jnp.maximum(top, jnp.max(new_scores, axis=1, keepdims=True))
        carried = jnp.exp(top - both)
        new_probs = jnp.where(new_live, jnp.exp(new_scores - both), 0.0)
        total = total * carried + jnp.sum(new_probs, axis=1, keepdims=True)
        accum = accum * carried
        for u in range(step_count):
            accum = accum + new_probs[:, u : u + 1] * new_v_ref[u : u + 1, span]
        sent = accum.astype(jnp.bfloat16)
        parts = []
        for value in (both, total):
            for _ in range(3):
                part = value.astype(jnp.bfloat16).astype(jnp.float32)
                parts.append(part)
                value = value - part
        lane = lax.broadcasted_iota(jnp.int32, (group * tokens, 128), 1)
        wide = jnp.zeros((group * tokens, 128), jnp.float32)
        for i, part in enumerate(parts):
            wide = jnp.where(lane == i, part, wide)
        turned = jnp.transpose(wide)[:16].astype(jnp.bfloat16)
        for g in range(group):
            pair = turned[:, g // 2 * 128 : (g // 2 + 1) * 128]
            for part in range(HD // columns):
                target = (kv * group + g) * (HD // columns) + part
                out_ref[target, :tokens, :] = sent[
                    g * tokens : (g + 1) * tokens, part * columns : (part + 1) * columns
                ]
                out_ref[target, tokens:, :] = pair


def out_kernel(req_count, where_ref, got_ref, *refs):
    w_refs = refs[:req_count]
    out_ref, turned_ref = refs[req_count:]
    blocks = got_ref.shape[0]
    copies, steps, _ = out_ref.shape
    tokens = copies * steps
    columns = got_ref.shape[2]
    head = where_ref[0] * columns // HD
    stats = got_ref[:, tokens:, :].astype(jnp.float32)
    tops = stats[:, 0, :] + stats[:, 1, :] + stats[:, 2, :]
    totals = stats[:, 3, :] + stats[:, 4, :] + stats[:, 5, :]
    rest = jnp.zeros((128 - 2 * blocks, 128), jnp.float32)
    turned_ref[...] = jnp.transpose(jnp.concatenate([tops, totals, rest]))
    mine = turned_ref[pl.ds(pl.multiple_of(head % 2 * tokens, tokens), tokens), :]
    tops = mine[:, :blocks]
    highest = jnp.max(tops, axis=1, keepdims=True)
    weights = jnp.exp(tops - highest)
    denominator = jnp.sum(mine[:, blocks : 2 * blocks] * weights, axis=1, keepdims=True)
    numerator = jnp.zeros((tokens, columns), jnp.float32)
    for b in range(blocks):
        numerator = numerator + got_ref[b, :tokens, :].astype(jnp.float32) * weights[:, b : b + 1]
    attention = (numerator / denominator).astype(jnp.bfloat16)
    for j, w_ref in enumerate(w_refs):
        width = w_ref.shape[1]
        part = jnp.dot(attention, w_ref[...], preferred_element_type=jnp.float32)
        part = part.astype(jnp.bfloat16)
        for i in range(copies):
            out_ref[i, :, j * width : (j + 1) * width] = part[i * steps : (i + 1) * steps]


def summed(req_count, where_ref, got_ref):
    width = got_ref.shape[2] // req_count
    blocks = []
    for i in range(req_count):
        j = lax.rem(where_ref[1] - i + req_count, req_count)
        cols = pl.ds(pl.multiple_of(j * width, width), width)
        blocks.append(jnp.sum(got_ref[:, :, cols].astype(jnp.float32), axis=0))
    return jnp.concatenate(blocks, axis=1)


def residual_kernel(
    req_count, where_ref, got_ref, hidden_ref, post_gain_ref, ffn_gain_ref, out_ref, residual_ref
):
    attn_out = summed(req_count, where_ref, got_ref)
    residual = hidden_ref[...].astype(jnp.float32) + normalize(attn_out) * post_gain_ref[...]
    residual_ref[...] = residual
    ffn_in = (normalize(residual) * ffn_gain_ref[...]).astype(jnp.bfloat16)
    for i in range(out_ref.shape[0]):
        out_ref[i] = ffn_in


def last_kernel(req_count, where_ref, got_ref, residual_ref, gain_ref, out_ref):
    down_out = summed(req_count, where_ref, got_ref)
    layer = (residual_ref[...] + normalize(down_out) * gain_ref[...]).astype(jnp.bfloat16)
    for i in range(out_ref.shape[0]):
        out_ref[i] = layer


def ffn_kernel(gate_rows, down_shape, where_ref, x_ref, *refs):
    req_count = len(refs) // 2 - 1
    w_refs, out_ref, held, sem_ref = refs[:req_count], refs[req_count], refs[req_count + 1 : -1], refs[-1]
    down_rows, down_width = down_shape
    packed_rows, width = w_refs[0].shape
    spans = [(0, gate_rows), (gate_rows, gate_rows), (2 * gate_rows, packed_rows - 2 * gate_rows)]
    copies = []
    for j in range(req_count):
        for first, rows in spans:
            part = pl.ds(first, rows)
            copies.append(
                pltpu.make_async_copy(
                    w_refs[j].at[part, :], held[j].at[part, :], sem_ref.at[len(copies)]
                )
            )
            copies[-1].start()
    blocks, steps, _ = x_ref.shape
    tokens = blocks * steps
    gate_out = up_out = None
    for j in range(req_count):
        first = lax.rem(where_ref[1] - j + req_count, req_count) * gate_rows
        cols = pl.ds(pl.multiple_of(first, gate_rows), gate_rows)
        part = x_ref[:, :, cols].reshape(tokens, gate_rows)
        copies[3 * j].wait()
        gate_w = held[j][:gate_rows, :]
        gate = jnp.dot(part, gate_w, preferred_element_type=jnp.float32)
        copies[3 * j + 1].wait()
        up_w = held[j][gate_rows : 2 * gate_rows, :]
        up = jnp.dot(part, up_w, preferred_element_type=jnp.float32)
        gate_out = gate if j == 0 else gate_out + gate
        up_out = up if j == 0 else up_out + up
    activated = (jax.nn.gelu(gate_out, approximate=True) * up_out).astype(jnp.bfloat16)
    for j in range(req_count):
        copies[3 * j + 2].wait()
        for piece in range(down_width // width):
            row = 2 * gate_rows + piece * down_rows
            down_w = held[j][row : row + down_rows, :]
            part = jnp.dot(activated, down_w, preferred_element_type=jnp.float32)
            part = part.astype(jnp.bfloat16)
            first = j * down_width + piece * width
            for i in range(blocks):
                out_ref[i, :, first : first + width] = part[i * steps : (i + 1) * steps]


def live_rows(
    seq_index, prompt_shape, pool_rows, group_of, prompt_lengths, tail_lengths, page_table
):
    group_count, prompt_span = prompt_shape
    rows_req = group_of.shape[0]
    member = (group_of % group_count)[:, None] == jnp.arange(group_count, dtype=jnp.int32)[None, :]
    prompt_pos = seq_index * prompt_span + jnp.arange(prompt_span, dtype=jnp.int32)
    prompt_live = prompt_pos[None, :] < prompt_lengths[:, None]
    prompt_mask = (member[:, :, None] & prompt_live[None, :, :]).reshape(
        rows_req, group_count * prompt_span
    )
    slot_count = pool_rows // PAGE
    table_row = page_table[0]
    table_len = table_row.shape[0]
    tail_pages = table_len // rows_req
    slot_ids = seq_index * slot_count + jnp.arange(slot_count, dtype=jnp.int32)
    matches = table_row[None, :] == slot_ids[:, None]
    entries = jnp.sum(
        jnp.where(matches, jnp.arange(table_len, dtype=jnp.int32)[None, :], 0), axis=1
    )
    owners = jnp.repeat(entries // tail_pages, PAGE)
    tail_pos = jnp.repeat(entries % tail_pages, PAGE) * PAGE + jnp.tile(
        jnp.arange(PAGE, dtype=jnp.int32), slot_count
    )
    tail_mask = (owners[None, :] == jnp.arange(rows_req, dtype=jnp.int32)[:, None]) & (
        tail_pos[None, :] < tail_lengths[:, None]
    )
    return jnp.concatenate([prompt_mask, tail_mask], axis=1)


def general_attention(
    seq_index,
    seq_count,
    rows_req,
    step_count,
    out_rows,
    projected,
    q_gain,
    k_gain,
    live,
    prompt_keys,
    prompt_values,
    tail_keys,
    tail_values,
):
    group_size = H // KV
    share = projected.shape[0]
    tokens = rows_req * step_count
    heads = normalize(projected.reshape(share, QKV // HD, HD))
    gains = jnp.concatenate(
        [
            jnp.broadcast_to(q_gain, (H, HD)),
            jnp.broadcast_to(k_gain, (KV, HD)),
            jnp.ones((KV, HD), jnp.float32),
        ]
    )
    mine = (heads * gains).astype(jnp.bfloat16).reshape(share, QKV)
    qkv = gather_rows(mine, seq_count)
    queries = qkv[:, : H * HD]
    keys_new = qkv[:, H * HD : (H + KV) * HD]
    values_new = qkv[:, (H + KV) * HD :]

    query_groups = queries.reshape(rows_req, step_count, KV, group_size, HD)
    mask = live[:, None, None, None, :]
    keys = jnp.concatenate([prompt_keys, tail_keys]).reshape(-1, KV, HD)
    values = jnp.concatenate([prompt_values, tail_values]).reshape(-1, KV, HD)
    scores = jnp.einsum("rskgd,pkd->rskgp", query_groups, keys, preferred_element_type=jnp.float32)
    scores = jnp.where(mask, scores, NEGATIVE)
    block_top = jnp.max(scores, axis=4)
    probs = jnp.where(mask, jnp.exp(scores - block_top[..., None]), 0.0)
    block_total = jnp.sum(probs, axis=4)
    block_accum = jnp.einsum(
        "rskgp,pkd->rskgd",
        probs.astype(jnp.bfloat16),
        values,
        preferred_element_type=jnp.float32,
    )

    stats = split_three(jnp.stack([block_top, block_total])).reshape(6, tokens, H)
    per_head = seq_count // H
    stats = jnp.repeat(stats.transpose(2, 0, 1).reshape(H, -1, out_rows), per_head, axis=0)
    accum_blocks = (
        block_accum.astype(jnp.bfloat16).reshape(tokens, seq_count, out_rows).transpose(1, 0, 2)
    )
    got = exchange(jnp.concatenate([accum_blocks, stats], axis=1), "seq")
    got_accum = got[:, :tokens].astype(jnp.float32)
    got_stats = got[:, tokens:].astype(jnp.float32).reshape(seq_count, 2 * 3, tokens)
    got_top = got_stats[:, 0] + got_stats[:, 2] + got_stats[:, 4]
    got_total = got_stats[:, 1] + got_stats[:, 3] + got_stats[:, 5]

    first_col = seq_index * out_rows
    head = first_col // HD
    kv_head = head // group_size
    head_queries = lax.dynamic_slice_in_dim(queries, head * HD, HD, 1)
    head_keys = lax.dynamic_slice_in_dim(keys_new, kv_head * HD, HD, 1)
    head_values = lax.dynamic_slice_in_dim(
        values_new, kv_head * HD + first_col % HD, out_rows, 1
    ).astype(jnp.float32)
    new_scores = jnp.dot(head_queries, head_keys.T, preferred_element_type=jnp.float32)
    token_ids = jnp.arange(tokens, dtype=jnp.int32)
    causal = (token_ids[:, None] // step_count == token_ids[None, :] // step_count) & (
        token_ids[:, None] >= token_ids[None, :]
    )
    new_scores = jnp.where(causal, new_scores, NEGATIVE)
    highest = jnp.maximum(jnp.max(got_top, axis=0), jnp.max(new_scores, axis=1))
    weights = jnp.exp(got_top - highest[None])
    new_probs = jnp.where(causal, jnp.exp(new_scores - highest[:, None]), 0.0)
    denominator = jnp.sum(got_total * weights, axis=0) + jnp.sum(new_probs, axis=1)
    numerator = jnp.sum(got_accum * weights[..., None], axis=0) + jnp.dot(
        new_probs, head_values, precision=lax.Precision.HIGHEST
    )
    return (numerator / denominator[:, None]).astype(jnp.bfloat16)


def on_device(
    req_count,
    seq_count,
    hidden_in,
    attn_gain,
    q_gain,
    k_gain,
    post_attn_gain,
    ffn_gain,
    post_ffn_gain,
    w_qkv,
    w_out,
    w_gate,
    w_up,
    w_down,
    prompt_keys,
    prompt_values,
    tail_keys,
    tail_values,
    group_of,
    prompt_lengths,
    tail_lengths,
    page_table,
):
    seq_index = lax.axis_index("seq")
    req_index = lax.axis_index("req")
    rows_req, step_count, _ = hidden_in.shape
    group_size = H // KV
    tokens = rows_req * step_count
    share = tokens // seq_count

    def shifted(values):
        return [values] + [
            lax.ppermute(values, "req", [(i, (i + j) % req_count) for i in range(req_count)])
            for j in range(1, req_count)
        ]

    where = jnp.stack([seq_index, req_index]).astype(jnp.int32)
    in_rows = w_qkv.shape[0]
    out_rows = w_out.shape[0]
    if in_rows % 128 == 0:
        normed_cols = call(
            norm_columns_kernel,
            "norm_columns",
            jax.ShapeDtypeStruct((tokens, in_rows), jnp.bfloat16),
            where,
            hidden_in,
            attn_gain.reshape(1, D),
        )
    else:
        normed = (normalize(hidden_in.astype(jnp.float32)) * attn_gain).astype(jnp.bfloat16)
        normed_cols = lax.dynamic_slice_in_dim(normed, seq_index * in_rows, in_rows, 2)
        normed_cols = normed_cols.reshape(tokens, in_rows)
    normed_all = lax.all_gather(normed_cols, "req", axis=0, tiled=True)
    out_blocks = shifted(w_out)
    width = w_gate.shape[1]
    pieces = [w_down[:, c : c + width] for c in range(0, w_down.shape[1], width)]
    packed = shifted(jnp.concatenate([w_gate, w_up] + pieces))

    qkv_part = jnp.dot(normed_all, w_qkv, preferred_element_type=jnp.float32)
    qkv_cols = w_qkv.shape[1]
    qkv_blocks = (
        (qkv_part * LINK_SCALE)
        .astype(jnp.float16)
        .reshape(req_count * seq_count, share, qkv_cols)
    )
    qkv_got = exchange(qkv_blocks, ("req", "seq"))
    qkv_got = qkv_got.reshape(req_count, seq_count, share, qkv_cols)
    projected = jnp.sum(qkv_got.astype(jnp.float32), axis=1) * (1.0 / LINK_SCALE)
    live = live_rows(
        seq_index, prompt_keys.shape[:2], tail_keys.shape[1], group_of, prompt_lengths,
        tail_lengths, page_table,
    )
    caches = [
        array.reshape(-1, KV * HD) for array in (prompt_keys, prompt_values, tail_keys, tail_values)
    ]
    direct = share == step_count and out_rows % 128 == 0 and tokens == 64 and qkv_cols % HD == 0
    if direct:
        q_blocks, new_keys, new_values = call(
            head_norm_kernel,
            "head_norm",
            (
                jax.ShapeDtypeStruct((seq_count, share, H * HD), jnp.bfloat16),
                jax.ShapeDtypeStruct((8, KV * HD), jnp.float32),
                jax.ShapeDtypeStruct((8, KV * HD), jnp.float32),
            ),
            where,
            projected,
            jnp.stack([q_gain, k_gain]),
        )
        live = jnp.repeat(live.astype(jnp.float32), step_count, axis=0)
        sent = call(
            functools.partial(block_kernel, step_count),
            "block_attention",
            jax.ShapeDtypeStruct((seq_count, tokens + 16, out_rows), jnp.bfloat16),
            where,
            exchange(q_blocks, "seq"),
            live,
            new_keys,
            new_values,
            *caches,
        )
        got, out_blocks = tie(exchange(sent, "seq"), out_blocks)
        out_part = call(
            functools.partial(out_kernel, req_count),
            "combine_out",
            jax.ShapeDtypeStruct((seq_count, share, D), jnp.bfloat16),
            where,
            got,
            *out_blocks,
            scratch=[pltpu.VMEM((128, 128), jnp.float32)],
        )
    else:
        projected = projected.transpose(1, 0, 2).reshape(share, QKV)
        attention_cols = general_attention(
            seq_index, seq_count, rows_req, step_count, out_rows, projected, q_gain, k_gain,
            live, *caches,
        )
        out_part = jnp.concatenate(
            [jnp.dot(attention_cols, w, preferred_element_type=jnp.float32) for w in out_blocks],
            axis=1,
        )
        out_part = out_part.astype(jnp.bfloat16).reshape(seq_count, share, D)
    hidden_mine = lax.dynamic_index_in_dim(
        hidden_in.reshape(seq_count, share, D), seq_index, 0, keepdims=False
    )
    ffn_blocks, residual = call(
        functools.partial(residual_kernel, req_count),
        "residual_norms",
        (
            jax.ShapeDtypeStruct((seq_count, share, D), jnp.bfloat16),
            jax.ShapeDtypeStruct((share, D), jnp.float32),
        ),
        where,
        exchange(out_part, "seq"),
        hidden_mine,
        post_attn_gain.reshape(1, D),
        ffn_gain.reshape(1, D),
    )
    down_part = call(
        functools.partial(ffn_kernel, w_gate.shape[0], w_down.shape),
        "feed_forward",
        jax.ShapeDtypeStruct((seq_count, share, D), jnp.bfloat16),
        where,
        exchange(ffn_blocks, "seq"),
        *packed,
        scratch=[pltpu.VMEM(w.shape, w.dtype) for w in packed]
        + [pltpu.SemaphoreType.DMA((3 * req_count,))],
        any_from=2,
    )
    layer_blocks = call(
        functools.partial(last_kernel, req_count),
        "last_norm",
        jax.ShapeDtypeStruct((seq_count, share, D), jnp.bfloat16),
        where,
        exchange(down_part, "seq"),
        residual,
        post_ffn_gain.reshape(1, D),
    )
    layer_out, where = tie(exchange(layer_blocks, "seq"), where)
    return layer_out.reshape(rows_req, step_count, D)


def solution(mesh):
    return jax.shard_map(
        functools.partial(on_device, mesh.shape["req"], mesh.shape["seq"]),
        mesh=mesh,
        in_specs=(
            P("req", None, None),
            P(),
            P(),
            P(),
            P(),
            P(),
            P(),
            P("seq", "req"),
            P("seq", "req"),
            P("req", "seq"),
            P("req", "seq"),
            P("seq", "req"),
            P("req", "seq", None),
            P("req", "seq", None),
            P("req", "seq", None),
            P("req", "seq", None),
            P("req"),
            P("req"),
            P("req"),
            P("req", None),
        ),
        out_specs=P("req", None, None),
        check_vma=False,
    )
```

```python
import functools

import jax
import jax.numpy as jnp
from jax import lax
from jax.experimental import pallas as pl
from jax.experimental.pallas import tpu as pltpu
from jax.sharding import PartitionSpec as P

D = 2048
H = 8
KV = 2
HD = 256
PAGE = 16
QKV = 3072


EPSILON = 1e-06
NEGATIVE = -1e30
LINK_SCALE = 512.0


def normalize(values):
    return values * lax.rsqrt(jnp.mean(values * values, axis=-1, keepdims=True) + EPSILON)


def split_three(values):
    high = values.astype(jnp.bfloat16)
    rest = values - high.astype(jnp.float32)
    middle = rest.astype(jnp.bfloat16)
    low = (rest - middle.astype(jnp.float32)).astype(jnp.bfloat16)
    return jnp.stack([high, middle, low])


def exchange(blocks, axes, groups=None):
    return lax.all_to_all(
        blocks, axes, split_axis=0, concat_axis=0, tiled=True, axis_index_groups=groups
    )


def tie(*arrays):
    return lax.optimization_barrier(arrays)


def spread(block, copies):
    return jnp.broadcast_to(block[None], (copies,) + block.shape)


def gather_rows(rows, count):
    return exchange(spread(rows, count), "seq").reshape(count * rows.shape[0], rows.shape[1])


def call(kernel, name, out_shape, *operands, scratch=(), any_from=None, limit=24):
    in_specs = [pl.BlockSpec(memory_space=pltpu.SMEM)]
    for i in range(1, len(operands)):
        space = pl.ANY if any_from is not None and i >= any_from else pltpu.VMEM
        in_specs.append(pl.BlockSpec(memory_space=space))
    return pl.pallas_call(
        kernel,
        name=name,
        out_shape=out_shape,
        in_specs=in_specs,
        out_specs=jax.tree.map(lambda _: pl.BlockSpec(memory_space=pltpu.VMEM), out_shape),
        scratch_shapes=scratch,
        compiler_params=pltpu.CompilerParams(vmem_limit_bytes=limit * 1024 * 1024),
    )(*operands)


def norm_columns_kernel(where_ref, hidden_ref, gain_ref, out_ref):
    columns = out_ref.shape[1]
    hidden = hidden_ref[...].astype(jnp.float32)
    scale = lax.rsqrt(jnp.mean(hidden * hidden, axis=-1, keepdims=True) + EPSILON)
    cols = pl.ds(pl.multiple_of(where_ref[0] * columns, columns), columns)
    normed = hidden_ref[:, :, cols].astype(jnp.float32) * scale * gain_ref[:, cols]
    out_ref[...] = normed.reshape(out_ref.shape).astype(jnp.bfloat16)


def head_norm_kernel(where_ref, projected_ref, gains_ref, q_ref, k_ref, v_ref):
    width = projected_ref.shape[2]
    copies, rows, _ = q_ref.shape
    fill = jnp.zeros((k_ref.shape[0] - rows, HD), jnp.float32)
    for head in range(H + 2 * KV):
        half, first = divmod(head * HD, width)
        values = normalize(projected_ref[half, :, first : first + HD])
        if head < H:
            values = (values * gains_ref[0:1, :]).astype(jnp.bfloat16)
            for i in range(copies):
                q_ref[i, :, head * HD : (head + 1) * HD] = values
        else:
            if head < H + KV:
                values = values * gains_ref[1:2, :]
            values = values.astype(jnp.bfloat16).astype(jnp.float32)
            target, slot = (k_ref, head - H) if head < H + KV else (v_ref, head - H - KV)
            target[:, slot * HD : (slot + 1) * HD] = jnp.concatenate([values, fill])


def dot_last(a, b):
    return lax.dot_general(a, b, (((1,), (1,)), ((), ())), preferred_element_type=jnp.float32)


def block_kernel(
    step_count,
    where_ref,
    q_ref,
    live_ref,
    new_k_ref,
    new_v_ref,
    keys_ref,
    values_ref,
    out_ref,
):
    copies, steps, _ = q_ref.shape
    tokens = copies * steps
    columns = out_ref.shape[2]
    group = H // KV
    queries = q_ref[...].reshape(tokens, H * HD)
    live = jnp.concatenate([live_ref[...]] * group) > 0.5
    first_token = where_ref[0] * step_count
    shape = (group * tokens, new_k_ref.shape[0])
    step = lax.broadcasted_iota(jnp.int32, shape, 0) % tokens - first_token
    new_index = lax.broadcasted_iota(jnp.int32, shape, 1)
    new_live = (step >= new_index) & (step < step_count)
    for kv in range(KV):
        span = slice(kv * HD, (kv + 1) * HD)
        q = jnp.concatenate(
            [queries[:, (kv * group + g) * HD : (kv * group + g + 1) * HD] for g in range(group)]
        )
        scores = jnp.where(live, dot_last(q, keys_ref[:, span]), NEGATIVE)
        top = jnp.max(scores, axis=1, keepdims=True)
        probs = jnp.where(live, jnp.exp(scores - top), 0.0)
        total = jnp.sum(probs, axis=1, keepdims=True)
        accum = jnp.dot(
            probs.astype(jnp.bfloat16), values_ref[:, span], preferred_element_type=jnp.float32
        )
        new_scores = dot_last(q, new_k_ref[:, span].astype(jnp.bfloat16))
        new_scores = jnp.where(new_live, new_scores, NEGATIVE)
        both = jnp.maximum(top, jnp.max(new_scores, axis=1, keepdims=True))
        carried = jnp.exp(top - both)
        new_probs = jnp.where(new_live, jnp.exp(new_scores - both), 0.0)
        total = total * carried + jnp.sum(new_probs, axis=1, keepdims=True)
        accum = accum * carried
        for u in range(step_count):
            accum = accum + new_probs[:, u : u + 1] * new_v_ref[u : u + 1, span]
        sent = accum.astype(jnp.bfloat16)
        parts = []
        for value in (both, total):
            for _ in range(3):
                part = value.astype(jnp.bfloat16).astype(jnp.float32)
                parts.append(part)
                value = value - part
        lane = lax.broadcasted_iota(jnp.int32, (group * tokens, 128), 1)
        wide = jnp.zeros((group * tokens, 128), jnp.float32)
        for i, part in enumerate(parts):
            wide = jnp.where(lane == i, part, wide)
        turned = jnp.transpose(wide)[:16].astype(jnp.bfloat16)
        for g in range(group):
            pair = turned[:, g // 2 * 128 : (g // 2 + 1) * 128]
            for part in range(HD // columns):
                target = (kv * group + g) * (HD // columns) + part
                out_ref[target, :tokens, :] = sent[
                    g * tokens : (g + 1) * tokens, part * columns : (part + 1) * columns
                ]
                out_ref[target, tokens:, :] = pair


def out_kernel(req_count, where_ref, got_ref, *refs):
    w_refs = refs[:req_count]
    out_ref, turned_ref = refs[req_count:]
    blocks = got_ref.shape[0]
    copies, steps, _ = out_ref.shape
    tokens = copies * steps
    columns = got_ref.shape[2]
    head = where_ref[0] * columns // HD
    stats = got_ref[:, tokens:, :].astype(jnp.float32)
    tops = stats[:, 0, :] + stats[:, 1, :] + stats[:, 2, :]
    totals = stats[:, 3, :] + stats[:, 4, :] + stats[:, 5, :]
    rest = jnp.zeros((128 - 2 * blocks, 128), jnp.float32)
    turned_ref[...] = jnp.transpose(jnp.concatenate([tops, totals, rest]))
    mine = turned_ref[pl.ds(pl.multiple_of(head % 2 * tokens, tokens), tokens), :]
    tops = mine[:, :blocks]
    highest = jnp.max(tops, axis=1, keepdims=True)
    weights = jnp.exp(tops - highest)
    denominator = jnp.sum(mine[:, blocks : 2 * blocks] * weights, axis=1, keepdims=True)
    numerator = jnp.zeros((tokens, columns), jnp.float32)
    for b in range(blocks):
        numerator = numerator + got_ref[b, :tokens, :].astype(jnp.float32) * weights[:, b : b + 1]
    attention = (numerator / denominator).astype(jnp.bfloat16)
    for j, w_ref in enumerate(w_refs):
        width = w_ref.shape[1]
        part = jnp.dot(attention, w_ref[...], preferred_element_type=jnp.float32)
        part = part.astype(jnp.bfloat16)
        for i in range(copies):
            out_ref[i, :, j * width : (j + 1) * width] = part[i * steps : (i + 1) * steps]


def summed(req_count, where_ref, got_ref):
    width = got_ref.shape[2] // req_count
    blocks = []
    for i in range(req_count):
        j = lax.rem(where_ref[1] - i + req_count, req_count)
        cols = pl.ds(pl.multiple_of(j * width, width), width)
        blocks.append(jnp.sum(got_ref[:, :, cols].astype(jnp.float32), axis=0))
    return jnp.concatenate(blocks, axis=1)


def residual_kernel(
    req_count, where_ref, got_ref, hidden_ref, post_gain_ref, ffn_gain_ref, out_ref, residual_ref
):
    attn_out = summed(req_count, where_ref, got_ref)
    residual = hidden_ref[...].astype(jnp.float32) + normalize(attn_out) * post_gain_ref[...]
    residual_ref[...] = residual
    ffn_in = (normalize(residual) * ffn_gain_ref[...]).astype(jnp.bfloat16)
    for i in range(out_ref.shape[0]):
        out_ref[i] = ffn_in


def last_kernel(req_count, where_ref, got_ref, residual_ref, gain_ref, out_ref):
    down_out = summed(req_count, where_ref, got_ref)
    layer = (residual_ref[...] + normalize(down_out) * gain_ref[...]).astype(jnp.bfloat16)
    for i in range(out_ref.shape[0]):
        out_ref[i] = layer


def ffn_kernel(req_count, where_ref, x_ref, *refs):
    w_refs = refs[: 3 * req_count]
    out_ref = refs[3 * req_count]
    held_refs = refs[3 * req_count + 1 : 6 * req_count + 1]
    sem_ref = refs[6 * req_count + 1]
    copies = [
        pltpu.make_async_copy(w, held, sem_ref.at[i])
        for i, (w, held) in enumerate(zip(w_refs, held_refs))
    ]
    for copy in copies:
        copy.start()
    blocks, steps, _ = x_ref.shape
    tokens = blocks * steps
    gate_out = up_out = None
    for j in range(req_count):
        gate_ref, up_ref = held_refs[2 * j], held_refs[2 * j + 1]
        rows = gate_ref.shape[0]
        first = lax.rem(where_ref[1] - j + req_count, req_count) * rows
        part = x_ref[:, :, pl.ds(pl.multiple_of(first, rows), rows)].reshape(tokens, rows)
        copies[2 * j].wait()
        gate = jnp.dot(part, gate_ref[...], preferred_element_type=jnp.float32)
        copies[2 * j + 1].wait()
        up = jnp.dot(part, up_ref[...], preferred_element_type=jnp.float32)
        gate_out = gate if j == 0 else gate_out + gate
        up_out = up if j == 0 else up_out + up
    activated = (jax.nn.gelu(gate_out, approximate=True) * up_out).astype(jnp.bfloat16)
    for j in range(req_count):
        down_ref = held_refs[2 * req_count + j]
        width = down_ref.shape[1]
        copies[2 * req_count + j].wait()
        part = jnp.dot(activated, down_ref[...], preferred_element_type=jnp.float32)
        part = part.astype(jnp.bfloat16)
        for i in range(blocks):
            out_ref[i, :, j * width : (j + 1) * width] = part[i * steps : (i + 1) * steps]


def live_rows(
    seq_index, prompt_shape, pool_rows, group_of, prompt_lengths, tail_lengths, page_table
):
    group_count, prompt_span = prompt_shape
    rows_req = group_of.shape[0]
    member = (group_of % group_count)[:, None] == jnp.arange(group_count, dtype=jnp.int32)[None, :]
    prompt_pos = seq_index * prompt_span + jnp.arange(prompt_span, dtype=jnp.int32)
    prompt_live = prompt_pos[None, :] < prompt_lengths[:, None]
    prompt_mask = (member[:, :, None] & prompt_live[None, :, :]).reshape(
        rows_req, group_count * prompt_span
    )
    slot_count = pool_rows // PAGE
    table_row = page_table[0]
    table_len = table_row.shape[0]
    tail_pages = table_len // rows_req
    slot_ids = seq_index * slot_count + jnp.arange(slot_count, dtype=jnp.int32)
    matches = table_row[None, :] == slot_ids[:, None]
    entries = jnp.sum(
        jnp.where(matches, jnp.arange(table_len, dtype=jnp.int32)[None, :], 0), axis=1
    )
    owners = jnp.repeat(entries // tail_pages, PAGE)
    tail_pos = jnp.repeat(entries % tail_pages, PAGE) * PAGE + jnp.tile(
        jnp.arange(PAGE, dtype=jnp.int32), slot_count
    )
    tail_mask = (owners[None, :] == jnp.arange(rows_req, dtype=jnp.int32)[:, None]) & (
        tail_pos[None, :] < tail_lengths[:, None]
    )
    return jnp.concatenate([prompt_mask, tail_mask], axis=1)


def general_attention(
    seq_index,
    seq_count,
    rows_req,
    step_count,
    out_rows,
    projected,
    q_gain,
    k_gain,
    live,
    prompt_keys,
    prompt_values,
    tail_keys,
    tail_values,
):
    group_size = H // KV
    share = projected.shape[0]
    tokens = rows_req * step_count
    heads = normalize(projected.reshape(share, QKV // HD, HD))
    gains = jnp.concatenate(
        [
            jnp.broadcast_to(q_gain, (H, HD)),
            jnp.broadcast_to(k_gain, (KV, HD)),
            jnp.ones((KV, HD), jnp.float32),
        ]
    )
    mine = (heads * gains).astype(jnp.bfloat16).reshape(share, QKV)
    qkv = gather_rows(mine, seq_count)
    queries = qkv[:, : H * HD]
    keys_new = qkv[:, H * HD : (H + KV) * HD]
    values_new = qkv[:, (H + KV) * HD :]

    query_groups = queries.reshape(rows_req, step_count, KV, group_size, HD)
    mask = live[:, None, None, None, :]
    keys = jnp.concatenate([prompt_keys, tail_keys]).reshape(-1, KV, HD)
    values = jnp.concatenate([prompt_values, tail_values]).reshape(-1, KV, HD)
    scores = jnp.einsum("rskgd,pkd->rskgp", query_groups, keys, preferred_element_type=jnp.float32)
    scores = jnp.where(mask, scores, NEGATIVE)
    block_top = jnp.max(scores, axis=4)
    probs = jnp.where(mask, jnp.exp(scores - block_top[..., None]), 0.0)
    block_total = jnp.sum(probs, axis=4)
    block_accum = jnp.einsum(
        "rskgp,pkd->rskgd",
        probs.astype(jnp.bfloat16),
        values,
        preferred_element_type=jnp.float32,
    )

    stats = split_three(jnp.stack([block_top, block_total])).reshape(6, tokens, H)
    per_head = seq_count // H
    stats = jnp.repeat(stats.transpose(2, 0, 1).reshape(H, -1, out_rows), per_head, axis=0)
    accum_blocks = (
        block_accum.astype(jnp.bfloat16).reshape(tokens, seq_count, out_rows).transpose(1, 0, 2)
    )
    got = exchange(jnp.concatenate([accum_blocks, stats], axis=1), "seq")
    got_accum = got[:, :tokens].astype(jnp.float32)
    got_stats = got[:, tokens:].astype(jnp.float32).reshape(seq_count, 2 * 3, tokens)
    got_top = got_stats[:, 0] + got_stats[:, 2] + got_stats[:, 4]
    got_total = got_stats[:, 1] + got_stats[:, 3] + got_stats[:, 5]

    first_col = seq_index * out_rows
    head = first_col // HD
    kv_head = head // group_size
    head_queries = lax.dynamic_slice_in_dim(queries, head * HD, HD, 1)
    head_keys = lax.dynamic_slice_in_dim(keys_new, kv_head * HD, HD, 1)
    head_values = lax.dynamic_slice_in_dim(
        values_new, kv_head * HD + first_col % HD, out_rows, 1
    ).astype(jnp.float32)
    new_scores = jnp.dot(head_queries, head_keys.T, preferred_element_type=jnp.float32)
    token_ids = jnp.arange(tokens, dtype=jnp.int32)
    causal = (token_ids[:, None] // step_count == token_ids[None, :] // step_count) & (
        token_ids[:, None] >= token_ids[None, :]
    )
    new_scores = jnp.where(causal, new_scores, NEGATIVE)
    highest = jnp.maximum(jnp.max(got_top, axis=0), jnp.max(new_scores, axis=1))
    weights = jnp.exp(got_top - highest[None])
    new_probs = jnp.where(causal, jnp.exp(new_scores - highest[:, None]), 0.0)
    denominator = jnp.sum(got_total * weights, axis=0) + jnp.sum(new_probs, axis=1)
    numerator = jnp.sum(got_accum * weights[..., None], axis=0) + jnp.dot(
        new_probs, head_values, precision=lax.Precision.HIGHEST
    )
    return (numerator / denominator[:, None]).astype(jnp.bfloat16)


def on_device(
    req_count,
    seq_count,
    hidden_in,
    attn_gain,
    q_gain,
    k_gain,
    post_attn_gain,
    ffn_gain,
    post_ffn_gain,
    w_qkv,
    w_out,
    w_gate,
    w_up,
    w_down,
    prompt_keys,
    prompt_values,
    tail_keys,
    tail_values,
    group_of,
    prompt_lengths,
    tail_lengths,
    page_table,
):
    seq_index = lax.axis_index("seq")
    req_index = lax.axis_index("req")
    rows_req, step_count, _ = hidden_in.shape
    group_size = H // KV
    tokens = rows_req * step_count
    share = tokens // seq_count

    def shifted(values):
        return [values] + [
            lax.ppermute(values, "req", [(i, (i + j) % req_count) for i in range(req_count)])
            for j in range(1, req_count)
        ]

    where = jnp.stack([seq_index, req_index]).astype(jnp.int32)
    in_rows = w_qkv.shape[0]
    out_rows = w_out.shape[0]
    if in_rows % 128 == 0:
        normed_cols = call(
            norm_columns_kernel,
            "norm_columns",
            jax.ShapeDtypeStruct((tokens, in_rows), jnp.bfloat16),
            where,
            hidden_in,
            attn_gain.reshape(1, D),
        )
    else:
        normed = (normalize(hidden_in.astype(jnp.float32)) * attn_gain).astype(jnp.bfloat16)
        normed_cols = lax.dynamic_slice_in_dim(normed, seq_index * in_rows, in_rows, 2)
        normed_cols = normed_cols.reshape(tokens, in_rows)
    normed_all = lax.all_gather(normed_cols, "req", axis=0, tiled=True)
    out_blocks = shifted(w_out)
    gate_blocks = shifted(w_gate)
    down_blocks = shifted(w_down)

    qkv_part = jnp.dot(normed_all, w_qkv, preferred_element_type=jnp.float32)
    qkv_cols = w_qkv.shape[1]
    qkv_blocks = (
        (qkv_part * LINK_SCALE)
        .astype(jnp.float16)
        .reshape(req_count * seq_count, share, qkv_cols)
    )
    qkv_got = exchange(qkv_blocks, ("req", "seq"))
    qkv_got = qkv_got.reshape(req_count, seq_count, share, qkv_cols)
    projected = jnp.sum(qkv_got.astype(jnp.float32), axis=1) * (1.0 / LINK_SCALE)
    projected, w_up = tie(projected, w_up)
    up_blocks = shifted(w_up)
    live = live_rows(
        seq_index, prompt_keys.shape[:2], tail_keys.shape[1], group_of, prompt_lengths,
        tail_lengths, page_table,
    )
    caches = [
        array.reshape(-1, KV * HD) for array in (prompt_keys, prompt_values, tail_keys, tail_values)
    ]
    direct = share == step_count and out_rows % 128 == 0 and tokens == 64 and qkv_cols % HD == 0
    if direct:
        q_blocks, new_keys, new_values = call(
            head_norm_kernel,
            "head_norm",
            (
                jax.ShapeDtypeStruct((seq_count, share, H * HD), jnp.bfloat16),
                jax.ShapeDtypeStruct((8, KV * HD), jnp.float32),
                jax.ShapeDtypeStruct((8, KV * HD), jnp.float32),
            ),
            where,
            projected,
            jnp.stack([q_gain, k_gain]),
        )
        q_got, out_blocks = tie(exchange(q_blocks, "seq"), out_blocks)
        live = jnp.repeat(live.astype(jnp.float32), step_count, axis=0)
        sent = call(
            functools.partial(block_kernel, step_count),
            "block_attention",
            jax.ShapeDtypeStruct((seq_count, tokens + 16, out_rows), jnp.bfloat16),
            where,
            q_got,
            live,
            new_keys,
            new_values,
            jnp.concatenate([caches[0], caches[2]]),
            jnp.concatenate([caches[1], caches[3]]),
        )
        got, gate_blocks, up_blocks = tie(exchange(sent, "seq"), gate_blocks, up_blocks)
        out_part = call(
            functools.partial(out_kernel, req_count),
            "combine_out",
            jax.ShapeDtypeStruct((seq_count, share, D), jnp.bfloat16),
            where,
            got,
            *out_blocks,
            scratch=[pltpu.VMEM((128, 128), jnp.float32)],
        )
    else:
        projected = projected.transpose(1, 0, 2).reshape(share, QKV)
        attention_cols = general_attention(
            seq_index, seq_count, rows_req, step_count, out_rows, projected, q_gain, k_gain,
            live, *caches,
        )
        out_part = jnp.concatenate(
            [jnp.dot(attention_cols, w, preferred_element_type=jnp.float32) for w in out_blocks],
            axis=1,
        )
        out_part = out_part.astype(jnp.bfloat16).reshape(seq_count, share, D)
    hidden_mine = lax.dynamic_index_in_dim(
        hidden_in.reshape(seq_count, share, D), seq_index, 0, keepdims=False
    )
    ffn_blocks, residual = call(
        functools.partial(residual_kernel, req_count),
        "residual_norms",
        (
            jax.ShapeDtypeStruct((seq_count, share, D), jnp.bfloat16),
            jax.ShapeDtypeStruct((share, D), jnp.float32),
        ),
        where,
        exchange(out_part, "seq"),
        hidden_mine,
        post_attn_gain.reshape(1, D),
        ffn_gain.reshape(1, D),
    )
    weights = [w for pair in zip(gate_blocks, up_blocks) for w in pair] + list(down_blocks)
    down_part = call(
        functools.partial(ffn_kernel, req_count),
        "feed_forward",
        jax.ShapeDtypeStruct((seq_count, share, D), jnp.bfloat16),
        where,
        exchange(ffn_blocks, "seq"),
        *weights,
        scratch=[pltpu.VMEM(w.shape, w.dtype) for w in weights]
        + [pltpu.SemaphoreType.DMA((len(weights),))],
        any_from=2,
    )
    layer_blocks = call(
        functools.partial(last_kernel, req_count),
        "last_norm",
        jax.ShapeDtypeStruct((seq_count, share, D), jnp.bfloat16),
        where,
        exchange(down_part, "seq"),
        residual,
        post_ffn_gain.reshape(1, D),
    )
    return exchange(layer_blocks, "seq").reshape(rows_req, step_count, D)


def solution(mesh):
    return jax.shard_map(
        functools.partial(on_device, mesh.shape["req"], mesh.shape["seq"]),
        mesh=mesh,
        in_specs=(
            P("req", None, None),
            P(),
            P(),
            P(),
            P(),
            P(),
            P(),
            P("seq", "req"),
            P("seq", "req"),
            P("req", "seq"),
            P("req", "seq"),
            P("seq", "req"),
            P("req", "seq", None),
            P("req", "seq", None),
            P("req", "seq", None),
            P("req", "seq", None),
            P("req"),
            P("req"),
            P("req"),
            P("req", None),
        ),
        out_specs=P("req", None, None),
        check_vma=False,
    )
```

```python
import functools

import jax
import jax.numpy as jnp
from jax import lax
from jax.experimental import pallas as pl
from jax.experimental.pallas import tpu as pltpu
from jax.sharding import PartitionSpec as P

D = 2048
H = 8
KV = 2
HD = 256
PAGE = 16
QKV = 3072


EPSILON = 1e-06
NEGATIVE = -1e30
LINK_SCALE = 512.0


def normalize(values):
    return values * lax.rsqrt(jnp.mean(values * values, axis=-1, keepdims=True) + EPSILON)


def split_three(values):
    high = values.astype(jnp.bfloat16)
    rest = values - high.astype(jnp.float32)
    middle = rest.astype(jnp.bfloat16)
    low = (rest - middle.astype(jnp.float32)).astype(jnp.bfloat16)
    return jnp.stack([high, middle, low])


def exchange(blocks, axes, groups=None):
    return lax.all_to_all(
        blocks, axes, split_axis=0, concat_axis=0, tiled=True, axis_index_groups=groups
    )


def tie(*arrays):
    return lax.optimization_barrier(arrays)


def spread(block, copies):
    return jnp.broadcast_to(block[None], (copies,) + block.shape)


def gather_rows(rows, count):
    return exchange(spread(rows, count), "seq").reshape(count * rows.shape[0], rows.shape[1])


def call(kernel, name, out_shape, *operands, scratch=(), any_from=None, limit=24):
    in_specs = [pl.BlockSpec(memory_space=pltpu.SMEM)]
    for i in range(1, len(operands)):
        space = pl.ANY if any_from is not None and i >= any_from else pltpu.VMEM
        in_specs.append(pl.BlockSpec(memory_space=space))
    return pl.pallas_call(
        kernel,
        name=name,
        out_shape=out_shape,
        in_specs=in_specs,
        out_specs=jax.tree.map(lambda _: pl.BlockSpec(memory_space=pltpu.VMEM), out_shape),
        scratch_shapes=scratch,
        compiler_params=pltpu.CompilerParams(vmem_limit_bytes=limit * 1024 * 1024),
    )(*operands)


def norm_columns_kernel(where_ref, hidden_ref, gain_ref, out_ref):
    columns = out_ref.shape[1]
    hidden = hidden_ref[...].astype(jnp.float32)
    scale = lax.rsqrt(jnp.mean(hidden * hidden, axis=-1, keepdims=True) + EPSILON)
    cols = pl.ds(pl.multiple_of(where_ref[0] * columns, columns), columns)
    normed = hidden_ref[:, :, cols].astype(jnp.float32) * scale * gain_ref[:, cols]
    out_ref[...] = normed.reshape(out_ref.shape).astype(jnp.bfloat16)


def head_norm_kernel(where_ref, projected_ref, gains_ref, q_ref, k_ref, v_ref):
    width = projected_ref.shape[2]
    copies, rows, _ = q_ref.shape
    fill = jnp.zeros((k_ref.shape[0] - rows, HD), jnp.float32)
    for head in range(H + 2 * KV):
        half, first = divmod(head * HD, width)
        values = normalize(projected_ref[half, :, first : first + HD])
        if head < H:
            values = (values * gains_ref[0:1, :]).astype(jnp.bfloat16)
            for i in range(copies):
                q_ref[i, :, head * HD : (head + 1) * HD] = values
        else:
            if head < H + KV:
                values = values * gains_ref[1:2, :]
            values = values.astype(jnp.bfloat16).astype(jnp.float32)
            target, slot = (k_ref, head - H) if head < H + KV else (v_ref, head - H - KV)
            target[:, slot * HD : (slot + 1) * HD] = jnp.concatenate([values, fill])


def dot_last(a, b):
    return lax.dot_general(a, b, (((1,), (1,)), ((), ())), preferred_element_type=jnp.float32)


def block_kernel(
    step_count,
    where_ref,
    q_ref,
    live_ref,
    new_k_ref,
    new_v_ref,
    keys_ref,
    values_ref,
    out_ref,
):
    copies, steps, _ = q_ref.shape
    tokens = copies * steps
    columns = out_ref.shape[2]
    group = H // KV
    queries = q_ref[...].reshape(tokens, H * HD)
    live = jnp.concatenate([live_ref[...]] * group) > 0.5
    first_token = where_ref[0] * step_count
    shape = (group * tokens, new_k_ref.shape[0])
    step = lax.broadcasted_iota(jnp.int32, shape, 0) % tokens - first_token
    new_index = lax.broadcasted_iota(jnp.int32, shape, 1)
    new_live = (step >= new_index) & (step < step_count)
    for kv in range(KV):
        span = slice(kv * HD, (kv + 1) * HD)
        q = jnp.concatenate(
            [queries[:, (kv * group + g) * HD : (kv * group + g + 1) * HD] for g in range(group)]
        )
        scores = jnp.where(live, dot_last(q, keys_ref[:, span]), NEGATIVE)
        top = jnp.max(scores, axis=1, keepdims=True)
        probs = jnp.where(live, jnp.exp(scores - top), 0.0)
        total = jnp.sum(probs, axis=1, keepdims=True)
        accum = jnp.dot(
            probs.astype(jnp.bfloat16), values_ref[:, span], preferred_element_type=jnp.float32
        )
        new_scores = dot_last(q, new_k_ref[:, span].astype(jnp.bfloat16))
        new_scores = jnp.where(new_live, new_scores, NEGATIVE)
        both = jnp.maximum(top, jnp.max(new_scores, axis=1, keepdims=True))
        carried = jnp.exp(top - both)
        new_probs = jnp.where(new_live, jnp.exp(new_scores - both), 0.0)
        total = total * carried + jnp.sum(new_probs, axis=1, keepdims=True)
        accum = accum * carried
        for u in range(step_count):
            accum = accum + new_probs[:, u : u + 1] * new_v_ref[u : u + 1, span]
        sent = accum.astype(jnp.bfloat16)
        parts = []
        for value in (both, total):
            for _ in range(3):
                part = value.astype(jnp.bfloat16).astype(jnp.float32)
                parts.append(part)
                value = value - part
        lane = lax.broadcasted_iota(jnp.int32, (group * tokens, 128), 1)
        wide = jnp.zeros((group * tokens, 128), jnp.float32)
        for i, part in enumerate(parts):
            wide = jnp.where(lane == i, part, wide)
        turned = jnp.transpose(wide)[:16].astype(jnp.bfloat16)
        for g in range(group):
            pair = turned[:, g // 2 * 128 : (g // 2 + 1) * 128]
            for part in range(HD // columns):
                target = (kv * group + g) * (HD // columns) + part
                out_ref[target, :tokens, :] = sent[
                    g * tokens : (g + 1) * tokens, part * columns : (part + 1) * columns
                ]
                out_ref[target, tokens:, :] = pair


def out_kernel(req_count, where_ref, got_ref, *refs):
    w_refs = refs[:req_count]
    out_ref, turned_ref = refs[req_count:]
    blocks = got_ref.shape[0]
    copies, steps, _ = out_ref.shape
    tokens = copies * steps
    columns = got_ref.shape[2]
    head = where_ref[0] * columns // HD
    stats = got_ref[:, tokens:, :].astype(jnp.float32)
    tops = stats[:, 0, :] + stats[:, 1, :] + stats[:, 2, :]
    totals = stats[:, 3, :] + stats[:, 4, :] + stats[:, 5, :]
    rest = jnp.zeros((128 - 2 * blocks, 128), jnp.float32)
    turned_ref[...] = jnp.transpose(jnp.concatenate([tops, totals, rest]))
    mine = turned_ref[pl.ds(pl.multiple_of(head % 2 * tokens, tokens), tokens), :]
    tops = mine[:, :blocks]
    highest = jnp.max(tops, axis=1, keepdims=True)
    weights = jnp.exp(tops - highest)
    denominator = jnp.sum(mine[:, blocks : 2 * blocks] * weights, axis=1, keepdims=True)
    numerator = jnp.zeros((tokens, columns), jnp.float32)
    for b in range(blocks):
        numerator = numerator + got_ref[b, :tokens, :].astype(jnp.float32) * weights[:, b : b + 1]
    attention = (numerator / denominator).astype(jnp.bfloat16)
    for j, w_ref in enumerate(w_refs):
        width = w_ref.shape[1]
        part = jnp.dot(attention, w_ref[...], preferred_element_type=jnp.float32)
        part = part.astype(jnp.bfloat16)
        for i in range(copies):
            out_ref[i, :, j * width : (j + 1) * width] = part[i * steps : (i + 1) * steps]


def summed(req_count, where_ref, got_ref):
    width = got_ref.shape[2] // req_count
    blocks = []
    for i in range(req_count):
        j = lax.rem(where_ref[1] - i + req_count, req_count)
        cols = pl.ds(pl.multiple_of(j * width, width), width)
        blocks.append(jnp.sum(got_ref[:, :, cols].astype(jnp.float32), axis=0))
    return jnp.concatenate(blocks, axis=1)


def residual_kernel(
    req_count, where_ref, got_ref, hidden_ref, post_gain_ref, ffn_gain_ref, out_ref, residual_ref
):
    attn_out = summed(req_count, where_ref, got_ref)
    hidden = hidden_ref[where_ref[0]].astype(jnp.float32)
    residual = hidden + normalize(attn_out) * post_gain_ref[...]
    residual_ref[...] = residual
    ffn_in = (normalize(residual) * ffn_gain_ref[...]).astype(jnp.bfloat16)
    for i in range(out_ref.shape[0]):
        out_ref[i] = ffn_in


def last_kernel(req_count, where_ref, got_ref, residual_ref, gain_ref, out_ref):
    down_out = summed(req_count, where_ref, got_ref)
    layer = (residual_ref[...] + normalize(down_out) * gain_ref[...]).astype(jnp.bfloat16)
    for i in range(out_ref.shape[0]):
        out_ref[i] = layer


def ffn_kernel(req_count, where_ref, x_ref, *refs):
    w_refs, out_ref, gates, ups, downs, sem_ref = refs[:-5], *refs[-5:]
    half = ups.shape[1] // 2
    targets = [gates.at[0], ups.at[0], downs.at[0]]
    for j in range(1, req_count):
        targets += [gates.at[j], ups.at[j, pl.ds(0, half)], ups.at[j, pl.ds(half, half)], downs.at[j]]
    copies = [
        pltpu.make_async_copy(w, target, sem_ref.at[i])
        for i, (w, target) in enumerate(zip(w_refs, targets))
    ]
    for copy in copies:
        copy.start()
    blocks, steps, _ = x_ref.shape
    tokens = blocks * steps
    gate_out = up_out = None
    for j in range(req_count):
        first = 0 if j == 0 else 4 * j - 1
        rows = gates.shape[1]
        start = lax.rem(where_ref[1] - j + req_count, req_count) * rows
        part = x_ref[:, :, pl.ds(pl.multiple_of(start, rows), rows)].reshape(tokens, rows)
        copies[first].wait()
        gate = jnp.dot(part, gates[j], preferred_element_type=jnp.float32)
        copies[first + 1].wait()
        if j > 0:
            copies[first + 2].wait()
        up = jnp.dot(part, ups[j], preferred_element_type=jnp.float32)
        gate_out = gate if j == 0 else gate_out + gate
        up_out = up if j == 0 else up_out + up
    activated = (jax.nn.gelu(gate_out, approximate=True) * up_out).astype(jnp.bfloat16)
    for j in range(req_count):
        width = downs.shape[2]
        copies[2 if j == 0 else 4 * j + 2].wait()
        part = jnp.dot(activated, downs[j], preferred_element_type=jnp.float32)
        part = part.astype(jnp.bfloat16)
        for i in range(blocks):
            out_ref[i, :, j * width : (j + 1) * width] = part[i * steps : (i + 1) * steps]


def live_rows(
    seq_index, prompt_shape, pool_rows, group_of, prompt_lengths, tail_lengths, page_table
):
    group_count, prompt_span = prompt_shape
    rows_req = group_of.shape[0]
    member = (group_of % group_count)[:, None] == jnp.arange(group_count, dtype=jnp.int32)[None, :]
    prompt_pos = seq_index * prompt_span + jnp.arange(prompt_span, dtype=jnp.int32)
    prompt_live = prompt_pos[None, :] < prompt_lengths[:, None]
    prompt_mask = (member[:, :, None] & prompt_live[None, :, :]).reshape(
        rows_req, group_count * prompt_span
    )
    slot_count = pool_rows // PAGE
    table_row = page_table[0]
    table_len = table_row.shape[0]
    tail_pages = table_len // rows_req
    slot_ids = seq_index * slot_count + jnp.arange(slot_count, dtype=jnp.int32)
    matches = table_row[None, :] == slot_ids[:, None]
    entries = jnp.sum(
        jnp.where(matches, jnp.arange(table_len, dtype=jnp.int32)[None, :], 0), axis=1
    )
    owners = jnp.repeat(entries // tail_pages, PAGE)
    tail_pos = jnp.repeat(entries % tail_pages, PAGE) * PAGE + jnp.tile(
        jnp.arange(PAGE, dtype=jnp.int32), slot_count
    )
    tail_mask = (owners[None, :] == jnp.arange(rows_req, dtype=jnp.int32)[:, None]) & (
        tail_pos[None, :] < tail_lengths[:, None]
    )
    return jnp.concatenate([prompt_mask, tail_mask], axis=1)


def general_attention(
    seq_index,
    seq_count,
    rows_req,
    step_count,
    out_rows,
    projected,
    q_gain,
    k_gain,
    live,
    prompt_keys,
    prompt_values,
    tail_keys,
    tail_values,
):
    group_size = H // KV
    share = projected.shape[0]
    tokens = rows_req * step_count
    heads = normalize(projected.reshape(share, QKV // HD, HD))
    gains = jnp.concatenate(
        [
            jnp.broadcast_to(q_gain, (H, HD)),
            jnp.broadcast_to(k_gain, (KV, HD)),
            jnp.ones((KV, HD), jnp.float32),
        ]
    )
    mine = (heads * gains).astype(jnp.bfloat16).reshape(share, QKV)
    qkv = gather_rows(mine, seq_count)
    queries = qkv[:, : H * HD]
    keys_new = qkv[:, H * HD : (H + KV) * HD]
    values_new = qkv[:, (H + KV) * HD :]

    query_groups = queries.reshape(rows_req, step_count, KV, group_size, HD)
    mask = live[:, None, None, None, :]
    keys = jnp.concatenate([prompt_keys, tail_keys]).reshape(-1, KV, HD)
    values = jnp.concatenate([prompt_values, tail_values]).reshape(-1, KV, HD)
    scores = jnp.einsum("rskgd,pkd->rskgp", query_groups, keys, preferred_element_type=jnp.float32)
    scores = jnp.where(mask, scores, NEGATIVE)
    block_top = jnp.max(scores, axis=4)
    probs = jnp.where(mask, jnp.exp(scores - block_top[..., None]), 0.0)
    block_total = jnp.sum(probs, axis=4)
    block_accum = jnp.einsum(
        "rskgp,pkd->rskgd",
        probs.astype(jnp.bfloat16),
        values,
        preferred_element_type=jnp.float32,
    )

    stats = split_three(jnp.stack([block_top, block_total])).reshape(6, tokens, H)
    per_head = seq_count // H
    stats = jnp.repeat(stats.transpose(2, 0, 1).reshape(H, -1, out_rows), per_head, axis=0)
    accum_blocks = (
        block_accum.astype(jnp.bfloat16).reshape(tokens, seq_count, out_rows).transpose(1, 0, 2)
    )
    got = exchange(jnp.concatenate([accum_blocks, stats], axis=1), "seq")
    got_accum = got[:, :tokens].astype(jnp.float32)
    got_stats = got[:, tokens:].astype(jnp.float32).reshape(seq_count, 2 * 3, tokens)
    got_top = got_stats[:, 0] + got_stats[:, 2] + got_stats[:, 4]
    got_total = got_stats[:, 1] + got_stats[:, 3] + got_stats[:, 5]

    first_col = seq_index * out_rows
    head = first_col // HD
    kv_head = head // group_size
    head_queries = lax.dynamic_slice_in_dim(queries, head * HD, HD, 1)
    head_keys = lax.dynamic_slice_in_dim(keys_new, kv_head * HD, HD, 1)
    head_values = lax.dynamic_slice_in_dim(
        values_new, kv_head * HD + first_col % HD, out_rows, 1
    ).astype(jnp.float32)
    new_scores = jnp.dot(head_queries, head_keys.T, preferred_element_type=jnp.float32)
    token_ids = jnp.arange(tokens, dtype=jnp.int32)
    causal = (token_ids[:, None] // step_count == token_ids[None, :] // step_count) & (
        token_ids[:, None] >= token_ids[None, :]
    )
    new_scores = jnp.where(causal, new_scores, NEGATIVE)
    highest = jnp.maximum(jnp.max(got_top, axis=0), jnp.max(new_scores, axis=1))
    weights = jnp.exp(got_top - highest[None])
    new_probs = jnp.where(causal, jnp.exp(new_scores - highest[:, None]), 0.0)
    denominator = jnp.sum(got_total * weights, axis=0) + jnp.sum(new_probs, axis=1)
    numerator = jnp.sum(got_accum * weights[..., None], axis=0) + jnp.dot(
        new_probs, head_values, precision=lax.Precision.HIGHEST
    )
    return (numerator / denominator[:, None]).astype(jnp.bfloat16)


def on_device(
    req_count,
    seq_count,
    hidden_in,
    attn_gain,
    q_gain,
    k_gain,
    post_attn_gain,
    ffn_gain,
    post_ffn_gain,
    w_qkv,
    w_out,
    w_gate,
    w_up,
    w_down,
    prompt_keys,
    prompt_values,
    tail_keys,
    tail_values,
    group_of,
    prompt_lengths,
    tail_lengths,
    page_table,
):
    seq_index = lax.axis_index("seq")
    req_index = lax.axis_index("req")
    rows_req, step_count, _ = hidden_in.shape
    group_size = H // KV
    tokens = rows_req * step_count
    share = tokens // seq_count

    def shifted(values):
        return [values] + [
            lax.ppermute(values, "req", [(i, (i + j) % req_count) for i in range(req_count)])
            for j in range(1, req_count)
        ]

    where = jnp.stack([seq_index, req_index]).astype(jnp.int32)
    in_rows = w_qkv.shape[0]
    out_rows = w_out.shape[0]
    if in_rows % 128 == 0:
        normed_cols = call(
            norm_columns_kernel,
            "norm_columns",
            jax.ShapeDtypeStruct((tokens, in_rows), jnp.bfloat16),
            where,
            hidden_in,
            attn_gain.reshape(1, D),
        )
    else:
        normed = (normalize(hidden_in.astype(jnp.float32)) * attn_gain).astype(jnp.bfloat16)
        normed_cols = lax.dynamic_slice_in_dim(normed, seq_index * in_rows, in_rows, 2)
        normed_cols = normed_cols.reshape(tokens, in_rows)
    normed_all = lax.all_gather(normed_cols, "req", axis=0, tiled=True)
    out_blocks = shifted(w_out)
    gate_blocks = shifted(w_gate)
    down_blocks = shifted(w_down)

    qkv_part = jnp.dot(normed_all, w_qkv, preferred_element_type=jnp.float32)
    qkv_cols = w_qkv.shape[1]
    qkv_blocks = (
        (qkv_part * LINK_SCALE)
        .astype(jnp.float16)
        .reshape(req_count * seq_count, share, qkv_cols)
    )
    qkv_got = exchange(qkv_blocks, ("req", "seq"))
    qkv_got = qkv_got.reshape(req_count, seq_count, share, qkv_cols)
    projected = jnp.sum(qkv_got.astype(jnp.float32), axis=1) * (1.0 / LINK_SCALE)
    projected, w_up_late = tie(projected, w_up)
    up_half = w_up.shape[0] // 2
    up_low = shifted(w_up_late[:up_half])[1:]
    up_high = shifted(w_up_late[up_half:])[1:]
    live = live_rows(
        seq_index, prompt_keys.shape[:2], tail_keys.shape[1], group_of, prompt_lengths,
        tail_lengths, page_table,
    )
    caches = [
        array.reshape(-1, KV * HD) for array in (prompt_keys, prompt_values, tail_keys, tail_values)
    ]
    direct = share == step_count and out_rows % 128 == 0 and tokens == 64 and qkv_cols % HD == 0
    if direct:
        q_blocks, new_keys, new_values = call(
            head_norm_kernel,
            "head_norm",
            (
                jax.ShapeDtypeStruct((seq_count, share, H * HD), jnp.bfloat16),
                jax.ShapeDtypeStruct((8, KV * HD), jnp.float32),
                jax.ShapeDtypeStruct((8, KV * HD), jnp.float32),
            ),
            where,
            projected,
            jnp.stack([q_gain, k_gain]),
        )
        q_got, out_blocks = tie(exchange(q_blocks, "seq"), out_blocks)
        live = jnp.repeat(live.astype(jnp.float32), step_count, axis=0)
        sent = call(
            functools.partial(block_kernel, step_count),
            "block_attention",
            jax.ShapeDtypeStruct((seq_count, tokens + 16, out_rows), jnp.bfloat16),
            where,
            q_got,
            live,
            new_keys,
            new_values,
            jnp.concatenate([caches[0], caches[2]]),
            jnp.concatenate([caches[1], caches[3]]),
        )
        got, gate_blocks, up_low = tie(exchange(sent, "seq"), gate_blocks, up_low)
        out_part = call(
            functools.partial(out_kernel, req_count),
            "combine_out",
            jax.ShapeDtypeStruct((seq_count, share, D), jnp.bfloat16),
            where,
            got,
            *out_blocks,
            scratch=[pltpu.VMEM((128, 128), jnp.float32)],
        )
    else:
        projected = projected.transpose(1, 0, 2).reshape(share, QKV)
        attention_cols = general_attention(
            seq_index, seq_count, rows_req, step_count, out_rows, projected, q_gain, k_gain,
            live, *caches,
        )
        out_part = jnp.concatenate(
            [jnp.dot(attention_cols, w, preferred_element_type=jnp.float32) for w in out_blocks],
            axis=1,
        )
        out_part = out_part.astype(jnp.bfloat16).reshape(seq_count, share, D)
    attn_got, up_high = tie(exchange(out_part, "seq"), up_high)
    ffn_blocks, residual = call(
        functools.partial(residual_kernel, req_count),
        "residual_norms",
        (
            jax.ShapeDtypeStruct((seq_count, share, D), jnp.bfloat16),
            jax.ShapeDtypeStruct((share, D), jnp.float32),
        ),
        where,
        attn_got,
        hidden_in.reshape(seq_count, share, D),
        post_attn_gain.reshape(1, D),
        ffn_gain.reshape(1, D),
    )
    weights = [w_gate, w_up, w_down]
    for j in range(1, req_count):
        weights += [gate_blocks[j], up_low[j - 1], up_high[j - 1], down_blocks[j]]
    down_part = call(
        functools.partial(ffn_kernel, req_count),
        "feed_forward",
        jax.ShapeDtypeStruct((seq_count, share, D), jnp.bfloat16),
        where,
        exchange(ffn_blocks, "seq"),
        *weights,
        scratch=[pltpu.VMEM((req_count,) + w.shape, w.dtype) for w in weights[:3]]
        + [pltpu.SemaphoreType.DMA((len(weights),))],
        any_from=2,
    )
    layer_blocks = call(
        functools.partial(last_kernel, req_count),
        "last_norm",
        jax.ShapeDtypeStruct((seq_count, share, D), jnp.bfloat16),
        where,
        exchange(down_part, "seq"),
        residual,
        post_ffn_gain.reshape(1, D),
    )
    return exchange(layer_blocks, "seq").reshape(rows_req, step_count, D)


def solution(mesh):
    return jax.shard_map(
        functools.partial(on_device, mesh.shape["req"], mesh.shape["seq"]),
        mesh=mesh,
        in_specs=(
            P("req", None, None),
            P(),
            P(),
            P(),
            P(),
            P(),
            P(),
            P("seq", "req"),
            P("seq", "req"),
            P("req", "seq"),
            P("req", "seq"),
            P("seq", "req"),
            P("req", "seq", None),
            P("req", "seq", None),
            P("req", "seq", None),
            P("req", "seq", None),
            P("req"),
            P("req"),
            P("req"),
            P("req", None),
        ),
        out_specs=P("req", None, None),
        check_vma=False,
    )
```

```python
import functools

import jax
import jax.numpy as jnp
from jax import lax
from jax.experimental import pallas as pl
from jax.experimental.pallas import tpu as pltpu
from jax.sharding import PartitionSpec as P

D = 2048
H = 8
KV = 2
HD = 256
PAGE = 16
QKV = 3072


EPSILON = 1e-06
NEGATIVE = -1e30
LINK_SCALE = 512.0


def normalize(values):
    return values * lax.rsqrt(jnp.mean(values * values, axis=-1, keepdims=True) + EPSILON)


def split_three(values):
    high = values.astype(jnp.bfloat16)
    rest = values - high.astype(jnp.float32)
    middle = rest.astype(jnp.bfloat16)
    low = (rest - middle.astype(jnp.float32)).astype(jnp.bfloat16)
    return jnp.stack([high, middle, low])


def exchange(blocks, axes, groups=None):
    return lax.all_to_all(
        blocks, axes, split_axis=0, concat_axis=0, tiled=True, axis_index_groups=groups
    )


def tie(*arrays):
    return lax.optimization_barrier(arrays)


def spread(block, copies):
    return jnp.broadcast_to(block[None], (copies,) + block.shape)


def gather_rows(rows, count):
    return exchange(spread(rows, count), "seq").reshape(count * rows.shape[0], rows.shape[1])


def call(kernel, name, out_shape, *operands, scratch=(), any_from=None, limit=24):
    in_specs = [pl.BlockSpec(memory_space=pltpu.SMEM)]
    for i in range(1, len(operands)):
        space = pl.ANY if any_from is not None and i >= any_from else pltpu.VMEM
        in_specs.append(pl.BlockSpec(memory_space=space))
    return pl.pallas_call(
        kernel,
        name=name,
        out_shape=out_shape,
        in_specs=in_specs,
        out_specs=jax.tree.map(lambda _: pl.BlockSpec(memory_space=pltpu.VMEM), out_shape),
        scratch_shapes=scratch,
        compiler_params=pltpu.CompilerParams(vmem_limit_bytes=limit * 1024 * 1024),
    )(*operands)


def norm_columns_kernel(where_ref, hidden_ref, gain_ref, out_ref):
    columns = out_ref.shape[1]
    hidden = hidden_ref[...].astype(jnp.float32)
    scale = lax.rsqrt(jnp.mean(hidden * hidden, axis=-1, keepdims=True) + EPSILON)
    cols = pl.ds(pl.multiple_of(where_ref[0] * columns, columns), columns)
    normed = hidden_ref[:, :, cols].astype(jnp.float32) * scale * gain_ref[:, cols]
    out_ref[...] = normed.reshape(out_ref.shape).astype(jnp.bfloat16)


def head_norm_kernel(where_ref, projected_ref, gains_ref, q_ref, k_ref, v_ref):
    width = projected_ref.shape[2]
    copies, rows, _ = q_ref.shape
    fill = jnp.zeros((k_ref.shape[0] - rows, HD), jnp.float32)
    for head in range(H + 2 * KV):
        half, first = divmod(head * HD, width)
        values = normalize(projected_ref[half, :, first : first + HD])
        if head < H:
            values = (values * gains_ref[0:1, :]).astype(jnp.bfloat16)
            for i in range(copies):
                q_ref[i, :, head * HD : (head + 1) * HD] = values
        else:
            if head < H + KV:
                values = values * gains_ref[1:2, :]
            values = values.astype(jnp.bfloat16).astype(jnp.float32)
            target, slot = (k_ref, head - H) if head < H + KV else (v_ref, head - H - KV)
            target[:, slot * HD : (slot + 1) * HD] = jnp.concatenate([values, fill])


def dot_last(a, b):
    return lax.dot_general(a, b, (((1,), (1,)), ((), ())), preferred_element_type=jnp.float32)


def block_kernel(
    step_count,
    where_ref,
    q_ref,
    live_ref,
    new_k_ref,
    new_v_ref,
    keys_ref,
    values_ref,
    out_ref,
):
    copies, steps, _ = q_ref.shape
    tokens = copies * steps
    columns = out_ref.shape[2]
    group = H // KV
    queries = q_ref[...].reshape(tokens, H * HD)
    live = jnp.concatenate([live_ref[...]] * group) > 0.5
    first_token = where_ref[0] * step_count
    shape = (group * tokens, new_k_ref.shape[0])
    step = lax.broadcasted_iota(jnp.int32, shape, 0) % tokens - first_token
    new_index = lax.broadcasted_iota(jnp.int32, shape, 1)
    new_live = (step >= new_index) & (step < step_count)
    for kv in range(KV):
        span = slice(kv * HD, (kv + 1) * HD)
        q = jnp.concatenate(
            [queries[:, (kv * group + g) * HD : (kv * group + g + 1) * HD] for g in range(group)]
        )
        scores = jnp.where(live, dot_last(q, keys_ref[:, span]), NEGATIVE)
        top = jnp.max(scores, axis=1, keepdims=True)
        probs = jnp.where(live, jnp.exp(scores - top), 0.0)
        total = jnp.sum(probs, axis=1, keepdims=True)
        accum = jnp.dot(
            probs.astype(jnp.bfloat16), values_ref[:, span], preferred_element_type=jnp.float32
        )
        new_scores = dot_last(q, new_k_ref[:, span].astype(jnp.bfloat16))
        new_scores = jnp.where(new_live, new_scores, NEGATIVE)
        both = jnp.maximum(top, jnp.max(new_scores, axis=1, keepdims=True))
        carried = jnp.exp(top - both)
        new_probs = jnp.where(new_live, jnp.exp(new_scores - both), 0.0)
        total = total * carried + jnp.sum(new_probs, axis=1, keepdims=True)
        accum = accum * carried
        for u in range(step_count):
            accum = accum + new_probs[:, u : u + 1] * new_v_ref[u : u + 1, span]
        sent = accum.astype(jnp.bfloat16)
        parts = []
        for value in (both, total):
            for _ in range(3):
                part = value.astype(jnp.bfloat16).astype(jnp.float32)
                parts.append(part)
                value = value - part
        lane = lax.broadcasted_iota(jnp.int32, (group * tokens, 128), 1)
        wide = jnp.zeros((group * tokens, 128), jnp.float32)
        for i, part in enumerate(parts):
            wide = jnp.where(lane == i, part, wide)
        turned = jnp.transpose(wide)[:16].astype(jnp.bfloat16)
        for g in range(group):
            pair = turned[:, g // 2 * 128 : (g // 2 + 1) * 128]
            for part in range(HD // columns):
                target = (kv * group + g) * (HD // columns) + part
                out_ref[target, :tokens, :] = sent[
                    g * tokens : (g + 1) * tokens, part * columns : (part + 1) * columns
                ]
                out_ref[target, tokens:, :] = pair


def out_kernel(req_count, where_ref, got_ref, *refs):
    w_refs = refs[:req_count]
    out_ref, turned_ref = refs[req_count:]
    blocks = got_ref.shape[0]
    copies, steps, _ = out_ref.shape
    tokens = copies * steps
    columns = got_ref.shape[2]
    head = where_ref[0] * columns // HD
    stats = got_ref[:, tokens:, :].astype(jnp.float32)
    tops = stats[:, 0, :] + stats[:, 1, :] + stats[:, 2, :]
    totals = stats[:, 3, :] + stats[:, 4, :] + stats[:, 5, :]
    rest = jnp.zeros((128 - 2 * blocks, 128), jnp.float32)
    turned_ref[...] = jnp.transpose(jnp.concatenate([tops, totals, rest]))
    mine = turned_ref[pl.ds(pl.multiple_of(head % 2 * tokens, tokens), tokens), :]
    tops = mine[:, :blocks]
    highest = jnp.max(tops, axis=1, keepdims=True)
    weights = jnp.exp(tops - highest)
    denominator = jnp.sum(mine[:, blocks : 2 * blocks] * weights, axis=1, keepdims=True)
    numerator = jnp.zeros((tokens, columns), jnp.float32)
    for b in range(blocks):
        numerator = numerator + got_ref[b, :tokens, :].astype(jnp.float32) * weights[:, b : b + 1]
    attention = (numerator / denominator).astype(jnp.bfloat16)
    for j, w_ref in enumerate(w_refs):
        width = w_ref.shape[1]
        part = jnp.dot(attention, w_ref[...], preferred_element_type=jnp.float32)
        part = part.astype(jnp.bfloat16)
        for i in range(copies):
            out_ref[i, :, j * width : (j + 1) * width] = part[i * steps : (i + 1) * steps]


def summed(req_count, where_ref, got_ref):
    width = got_ref.shape[2] // req_count
    blocks = []
    for i in range(req_count):
        j = lax.rem(where_ref[1] - i + req_count, req_count)
        cols = pl.ds(pl.multiple_of(j * width, width), width)
        blocks.append(jnp.sum(got_ref[:, :, cols].astype(jnp.float32), axis=0))
    return jnp.concatenate(blocks, axis=1)


def residual_kernel(
    req_count, where_ref, got_ref, hidden_ref, post_gain_ref, ffn_gain_ref, out_ref, residual_ref
):
    attn_out = summed(req_count, where_ref, got_ref)
    residual = hidden_ref[...].astype(jnp.float32) + normalize(attn_out) * post_gain_ref[...]
    residual_ref[...] = residual
    ffn_in = (normalize(residual) * ffn_gain_ref[...]).astype(jnp.bfloat16)
    for i in range(out_ref.shape[0]):
        out_ref[i] = ffn_in


def last_kernel(req_count, where_ref, got_ref, residual_ref, gain_ref, out_ref):
    down_out = summed(req_count, where_ref, got_ref)
    layer = (residual_ref[...] + normalize(down_out) * gain_ref[...]).astype(jnp.bfloat16)
    for i in range(out_ref.shape[0]):
        out_ref[i] = layer


def ffn_kernel(req_count, where_ref, x_ref, *refs):
    count = 2 * req_count + 1
    w_refs, out_ref, held, sem_ref = refs[:count], refs[count], refs[count + 1 : -1], refs[-1]
    gate_rows, width = w_refs[0].shape
    half = w_refs[1].shape[0] // 2
    down_rows, down_width = w_refs[2].shape
    copies = []

    def load(i, first, rows):
        part = pl.ds(first, rows)
        copies.append(
            pltpu.make_async_copy(
                w_refs[i].at[part, :], held[i].at[part, :], sem_ref.at[len(copies)]
            )
        )
        copies[-1].start()

    for i in range(3):
        load(i, 0, w_refs[i].shape[0])
    for i in range(3, count, 2):
        load(i, 0, gate_rows)
        load(i, gate_rows, half)
        load(i + 1, 0, half)
        load(i + 1, half, w_refs[i + 1].shape[0] - half)
    blocks, steps, _ = x_ref.shape
    tokens = blocks * steps
    gate_out = up_out = None
    for j in range(req_count):
        start = lax.rem(where_ref[1] - j + req_count, req_count) * gate_rows
        part = x_ref[:, :, pl.ds(pl.multiple_of(start, gate_rows), gate_rows)]
        part = part.reshape(tokens, gate_rows)
        first = 0 if j == 0 else 4 * j - 1
        copies[first].wait()
        copies[first + 1].wait()
        if j == 0:
            gate_w, up_w = held[0][...], held[1][...]
            up = jnp.dot(part, up_w, preferred_element_type=jnp.float32)
        else:
            copies[first + 2].wait()
            gate_w = held[2 * j + 1][:gate_rows, :]
            low, high = held[2 * j + 1][gate_rows:, :], held[2 * j + 2][:half, :]
            up = jnp.dot(part[:, :half], low, preferred_element_type=jnp.float32)
            up = up + jnp.dot(part[:, half:], high, preferred_element_type=jnp.float32)
        gate = jnp.dot(part, gate_w, preferred_element_type=jnp.float32)
        gate_out = gate if j == 0 else gate_out + gate
        up_out = up if j == 0 else up_out + up
    activated = (jax.nn.gelu(gate_out, approximate=True) * up_out).astype(jnp.bfloat16)
    for j in range(req_count):
        copies[2 if j == 0 else 4 * j + 2].wait()
        for piece in range(down_width // width):
            if j == 0:
                down_w = held[2][:, piece * width : (piece + 1) * width]
            else:
                row = half + piece * down_rows
                down_w = held[2 * j + 2][row : row + down_rows, :]
            part = jnp.dot(activated, down_w, preferred_element_type=jnp.float32)
            part = part.astype(jnp.bfloat16)
            first = j * down_width + piece * width
            for i in range(blocks):
                out_ref[i, :, first : first + width] = part[i * steps : (i + 1) * steps]


def live_rows(
    seq_index, prompt_shape, pool_rows, group_of, prompt_lengths, tail_lengths, page_table
):
    group_count, prompt_span = prompt_shape
    rows_req = group_of.shape[0]
    member = (group_of % group_count)[:, None] == jnp.arange(group_count, dtype=jnp.int32)[None, :]
    prompt_pos = seq_index * prompt_span + jnp.arange(prompt_span, dtype=jnp.int32)
    prompt_live = prompt_pos[None, :] < prompt_lengths[:, None]
    prompt_mask = (member[:, :, None] & prompt_live[None, :, :]).reshape(
        rows_req, group_count * prompt_span
    )
    slot_count = pool_rows // PAGE
    table_row = page_table[0]
    table_len = table_row.shape[0]
    tail_pages = table_len // rows_req
    slot_ids = seq_index * slot_count + jnp.arange(slot_count, dtype=jnp.int32)
    matches = table_row[None, :] == slot_ids[:, None]
    entries = jnp.sum(
        jnp.where(matches, jnp.arange(table_len, dtype=jnp.int32)[None, :], 0), axis=1
    )
    owners = jnp.repeat(entries // tail_pages, PAGE)
    tail_pos = jnp.repeat(entries % tail_pages, PAGE) * PAGE + jnp.tile(
        jnp.arange(PAGE, dtype=jnp.int32), slot_count
    )
    tail_mask = (owners[None, :] == jnp.arange(rows_req, dtype=jnp.int32)[:, None]) & (
        tail_pos[None, :] < tail_lengths[:, None]
    )
    return jnp.concatenate([prompt_mask, tail_mask], axis=1)


def general_attention(
    seq_index,
    seq_count,
    rows_req,
    step_count,
    out_rows,
    projected,
    q_gain,
    k_gain,
    live,
    prompt_keys,
    prompt_values,
    tail_keys,
    tail_values,
):
    group_size = H // KV
    share = projected.shape[0]
    tokens = rows_req * step_count
    heads = normalize(projected.reshape(share, QKV // HD, HD))
    gains = jnp.concatenate(
        [
            jnp.broadcast_to(q_gain, (H, HD)),
            jnp.broadcast_to(k_gain, (KV, HD)),
            jnp.ones((KV, HD), jnp.float32),
        ]
    )
    mine = (heads * gains).astype(jnp.bfloat16).reshape(share, QKV)
    qkv = gather_rows(mine, seq_count)
    queries = qkv[:, : H * HD]
    keys_new = qkv[:, H * HD : (H + KV) * HD]
    values_new = qkv[:, (H + KV) * HD :]

    query_groups = queries.reshape(rows_req, step_count, KV, group_size, HD)
    mask = live[:, None, None, None, :]
    keys = jnp.concatenate([prompt_keys, tail_keys]).reshape(-1, KV, HD)
    values = jnp.concatenate([prompt_values, tail_values]).reshape(-1, KV, HD)
    scores = jnp.einsum("rskgd,pkd->rskgp", query_groups, keys, preferred_element_type=jnp.float32)
    scores = jnp.where(mask, scores, NEGATIVE)
    block_top = jnp.max(scores, axis=4)
    probs = jnp.where(mask, jnp.exp(scores - block_top[..., None]), 0.0)
    block_total = jnp.sum(probs, axis=4)
    block_accum = jnp.einsum(
        "rskgp,pkd->rskgd",
        probs.astype(jnp.bfloat16),
        values,
        preferred_element_type=jnp.float32,
    )

    stats = split_three(jnp.stack([block_top, block_total])).reshape(6, tokens, H)
    per_head = seq_count // H
    stats = jnp.repeat(stats.transpose(2, 0, 1).reshape(H, -1, out_rows), per_head, axis=0)
    accum_blocks = (
        block_accum.astype(jnp.bfloat16).reshape(tokens, seq_count, out_rows).transpose(1, 0, 2)
    )
    got = exchange(jnp.concatenate([accum_blocks, stats], axis=1), "seq")
    got_accum = got[:, :tokens].astype(jnp.float32)
    got_stats = got[:, tokens:].astype(jnp.float32).reshape(seq_count, 2 * 3, tokens)
    got_top = got_stats[:, 0] + got_stats[:, 2] + got_stats[:, 4]
    got_total = got_stats[:, 1] + got_stats[:, 3] + got_stats[:, 5]

    first_col = seq_index * out_rows
    head = first_col // HD
    kv_head = head // group_size
    head_queries = lax.dynamic_slice_in_dim(queries, head * HD, HD, 1)
    head_keys = lax.dynamic_slice_in_dim(keys_new, kv_head * HD, HD, 1)
    head_values = lax.dynamic_slice_in_dim(
        values_new, kv_head * HD + first_col % HD, out_rows, 1
    ).astype(jnp.float32)
    new_scores = jnp.dot(head_queries, head_keys.T, preferred_element_type=jnp.float32)
    token_ids = jnp.arange(tokens, dtype=jnp.int32)
    causal = (token_ids[:, None] // step_count == token_ids[None, :] // step_count) & (
        token_ids[:, None] >= token_ids[None, :]
    )
    new_scores = jnp.where(causal, new_scores, NEGATIVE)
    highest = jnp.maximum(jnp.max(got_top, axis=0), jnp.max(new_scores, axis=1))
    weights = jnp.exp(got_top - highest[None])
    new_probs = jnp.where(causal, jnp.exp(new_scores - highest[:, None]), 0.0)
    denominator = jnp.sum(got_total * weights, axis=0) + jnp.sum(new_probs, axis=1)
    numerator = jnp.sum(got_accum * weights[..., None], axis=0) + jnp.dot(
        new_probs, head_values, precision=lax.Precision.HIGHEST
    )
    return (numerator / denominator[:, None]).astype(jnp.bfloat16)


def on_device(
    req_count,
    seq_count,
    hidden_in,
    attn_gain,
    q_gain,
    k_gain,
    post_attn_gain,
    ffn_gain,
    post_ffn_gain,
    w_qkv,
    w_out,
    w_gate,
    w_up,
    w_down,
    prompt_keys,
    prompt_values,
    tail_keys,
    tail_values,
    group_of,
    prompt_lengths,
    tail_lengths,
    page_table,
):
    seq_index = lax.axis_index("seq")
    req_index = lax.axis_index("req")
    rows_req, step_count, _ = hidden_in.shape
    group_size = H // KV
    tokens = rows_req * step_count
    share = tokens // seq_count

    def shifted(values):
        return [values] + [
            lax.ppermute(values, "req", [(i, (i + j) % req_count) for i in range(req_count)])
            for j in range(1, req_count)
        ]

    where = jnp.stack([seq_index, req_index]).astype(jnp.int32)
    in_rows = w_qkv.shape[0]
    out_rows = w_out.shape[0]
    if in_rows % 128 == 0:
        normed_cols = call(
            norm_columns_kernel,
            "norm_columns",
            jax.ShapeDtypeStruct((tokens, in_rows), jnp.bfloat16),
            where,
            hidden_in,
            attn_gain.reshape(1, D),
        )
    else:
        normed = (normalize(hidden_in.astype(jnp.float32)) * attn_gain).astype(jnp.bfloat16)
        normed_cols = lax.dynamic_slice_in_dim(normed, seq_index * in_rows, in_rows, 2)
        normed_cols = normed_cols.reshape(tokens, in_rows)
    normed_all = lax.all_gather(normed_cols, "req", axis=0, tiled=True)
    out_blocks = shifted(w_out)
    width = w_gate.shape[1]
    up_half = w_up.shape[0] // 2
    down_pieces = [w_down[:, c : c + width] for c in range(0, w_down.shape[1], width)]
    early = shifted(jnp.concatenate([w_gate, w_up[:up_half]]))[1:]
    late = shifted(jnp.concatenate([w_up[up_half:]] + down_pieces))[1:]

    qkv_part = jnp.dot(normed_all, w_qkv, preferred_element_type=jnp.float32)
    qkv_cols = w_qkv.shape[1]
    qkv_blocks = (
        (qkv_part * LINK_SCALE)
        .astype(jnp.float16)
        .reshape(req_count * seq_count, share, qkv_cols)
    )
    qkv_got = exchange(qkv_blocks, ("req", "seq"))
    qkv_got = qkv_got.reshape(req_count, seq_count, share, qkv_cols)
    projected = jnp.sum(qkv_got.astype(jnp.float32), axis=1) * (1.0 / LINK_SCALE)
    live = live_rows(
        seq_index, prompt_keys.shape[:2], tail_keys.shape[1], group_of, prompt_lengths,
        tail_lengths, page_table,
    )
    caches = [
        array.reshape(-1, KV * HD) for array in (prompt_keys, prompt_values, tail_keys, tail_values)
    ]
    direct = share == step_count and out_rows % 128 == 0 and tokens == 64 and qkv_cols % HD == 0
    if direct:
        q_blocks, new_keys, new_values = call(
            head_norm_kernel,
            "head_norm",
            (
                jax.ShapeDtypeStruct((seq_count, share, H * HD), jnp.bfloat16),
                jax.ShapeDtypeStruct((8, KV * HD), jnp.float32),
                jax.ShapeDtypeStruct((8, KV * HD), jnp.float32),
            ),
            where,
            projected,
            jnp.stack([q_gain, k_gain]),
        )
        q_got, out_blocks = tie(exchange(q_blocks, "seq"), out_blocks)
        live = jnp.repeat(live.astype(jnp.float32), step_count, axis=0)
        sent = call(
            functools.partial(block_kernel, step_count),
            "block_attention",
            jax.ShapeDtypeStruct((seq_count, tokens + 16, out_rows), jnp.bfloat16),
            where,
            q_got,
            live,
            new_keys,
            new_values,
            jnp.concatenate([caches[0], caches[2]]),
            jnp.concatenate([caches[1], caches[3]]),
        )
        got, early = tie(exchange(sent, "seq"), early)
        out_part = call(
            functools.partial(out_kernel, req_count),
            "combine_out",
            jax.ShapeDtypeStruct((seq_count, share, D), jnp.bfloat16),
            where,
            got,
            *out_blocks,
            scratch=[pltpu.VMEM((128, 128), jnp.float32)],
        )
    else:
        projected = projected.transpose(1, 0, 2).reshape(share, QKV)
        attention_cols = general_attention(
            seq_index, seq_count, rows_req, step_count, out_rows, projected, q_gain, k_gain,
            live, *caches,
        )
        out_part = jnp.concatenate(
            [jnp.dot(attention_cols, w, preferred_element_type=jnp.float32) for w in out_blocks],
            axis=1,
        )
        out_part = out_part.astype(jnp.bfloat16).reshape(seq_count, share, D)
    attn_got, w_gate, w_up, w_down = tie(exchange(out_part, "seq"), w_gate, w_up, w_down)
    hidden_mine = lax.dynamic_index_in_dim(
        hidden_in.reshape(seq_count, share, D), seq_index, 0, keepdims=False
    )
    ffn_blocks, residual = call(
        functools.partial(residual_kernel, req_count),
        "residual_norms",
        (
            jax.ShapeDtypeStruct((seq_count, share, D), jnp.bfloat16),
            jax.ShapeDtypeStruct((share, D), jnp.float32),
        ),
        where,
        attn_got,
        hidden_mine,
        post_attn_gain.reshape(1, D),
        ffn_gain.reshape(1, D),
    )
    weights = [w_gate, w_up, w_down] + [w for pair in zip(early, late) for w in pair]
    down_part = call(
        functools.partial(ffn_kernel, req_count),
        "feed_forward",
        jax.ShapeDtypeStruct((seq_count, share, D), jnp.bfloat16),
        where,
        exchange(ffn_blocks, "seq"),
        *weights,
        scratch=[pltpu.VMEM(w.shape, w.dtype) for w in weights]
        + [pltpu.SemaphoreType.DMA((3 + 4 * (req_count - 1),))],
        any_from=2,
    )
    layer_blocks = call(
        functools.partial(last_kernel, req_count),
        "last_norm",
        jax.ShapeDtypeStruct((seq_count, share, D), jnp.bfloat16),
        where,
        exchange(down_part, "seq"),
        residual,
        post_ffn_gain.reshape(1, D),
    )
    return exchange(layer_blocks, "seq").reshape(rows_req, step_count, D)


def solution(mesh):
    return jax.shard_map(
        functools.partial(on_device, mesh.shape["req"], mesh.shape["seq"]),
        mesh=mesh,
        in_specs=(
            P("req", None, None),
            P(),
            P(),
            P(),
            P(),
            P(),
            P(),
            P("seq", "req"),
            P("seq", "req"),
            P("req", "seq"),
            P("req", "seq"),
            P("seq", "req"),
            P("req", "seq", None),
            P("req", "seq", None),
            P("req", "seq", None),
            P("req", "seq", None),
            P("req"),
            P("req"),
            P("req"),
            P("req", None),
        ),
        out_specs=P("req", None, None),
        check_vma=False,
    )
```

```python
import functools

import jax
import jax.numpy as jnp
from jax import lax
from jax.experimental import pallas as pl
from jax.experimental.pallas import tpu as pltpu
from jax.sharding import PartitionSpec as P

D = 2048
H = 8
KV = 2
HD = 256
PAGE = 16
QKV = 3072


EPSILON = 1e-06
NEGATIVE = -1e30
LINK_SCALE = 512.0


def normalize(values):
    return values * lax.rsqrt(jnp.mean(values * values, axis=-1, keepdims=True) + EPSILON)


def split_three(values):
    high = values.astype(jnp.bfloat16)
    rest = values - high.astype(jnp.float32)
    middle = rest.astype(jnp.bfloat16)
    low = (rest - middle.astype(jnp.float32)).astype(jnp.bfloat16)
    return jnp.stack([high, middle, low])


def exchange(blocks, axes, groups=None):
    return lax.all_to_all(
        blocks, axes, split_axis=0, concat_axis=0, tiled=True, axis_index_groups=groups
    )


def tie(*arrays):
    return lax.optimization_barrier(arrays)


def spread(block, copies):
    return jnp.broadcast_to(block[None], (copies,) + block.shape)


def gather_rows(rows, count):
    return exchange(spread(rows, count), "seq").reshape(count * rows.shape[0], rows.shape[1])


def call(kernel, name, out_shape, *operands, scratch=(), hbm_from=None, limit=16):
    in_specs = [pl.BlockSpec(memory_space=pltpu.SMEM)]
    for i in range(1, len(operands)):
        space = pltpu.HBM if hbm_from is not None and i >= hbm_from else pltpu.VMEM
        in_specs.append(pl.BlockSpec(memory_space=space))
    return pl.pallas_call(
        kernel,
        name=name,
        out_shape=out_shape,
        in_specs=in_specs,
        out_specs=jax.tree.map(lambda _: pl.BlockSpec(memory_space=pltpu.VMEM), out_shape),
        scratch_shapes=scratch,
        compiler_params=pltpu.CompilerParams(vmem_limit_bytes=limit * 1024 * 1024),
    )(*operands)


def norm_columns_kernel(where_ref, hidden_ref, gain_ref, out_ref):
    columns = out_ref.shape[1]
    hidden = hidden_ref[...].astype(jnp.float32)
    scale = lax.rsqrt(jnp.mean(hidden * hidden, axis=-1, keepdims=True) + EPSILON)
    cols = pl.ds(pl.multiple_of(where_ref[0] * columns, columns), columns)
    normed = hidden_ref[:, :, cols].astype(jnp.float32) * scale * gain_ref[:, cols]
    out_ref[...] = normed.reshape(out_ref.shape).astype(jnp.bfloat16)


def head_norm_kernel(where_ref, projected_ref, gains_ref, q_ref, k_ref, v_ref):
    width = projected_ref.shape[2]
    copies, rows, _ = q_ref.shape
    fill = jnp.zeros((k_ref.shape[0] - rows, HD), jnp.float32)
    for head in range(H + 2 * KV):
        half, first = divmod(head * HD, width)
        values = normalize(projected_ref[half, :, first : first + HD])
        if head < H:
            values = (values * gains_ref[0:1, :]).astype(jnp.bfloat16)
            for i in range(copies):
                q_ref[i, :, head * HD : (head + 1) * HD] = values
        else:
            if head < H + KV:
                values = values * gains_ref[1:2, :]
            values = values.astype(jnp.bfloat16).astype(jnp.float32)
            target, slot = (k_ref, head - H) if head < H + KV else (v_ref, head - H - KV)
            target[:, slot * HD : (slot + 1) * HD] = jnp.concatenate([values, fill])


def dot_last(a, b):
    return lax.dot_general(a, b, (((1,), (1,)), ((), ())), preferred_element_type=jnp.float32)


def block_kernel(
    step_count,
    where_ref,
    q_ref,
    live_ref,
    new_k_ref,
    new_v_ref,
    keys_ref,
    values_ref,
    out_ref,
):
    copies, steps, _ = q_ref.shape
    tokens = copies * steps
    columns = out_ref.shape[2]
    group = H // KV
    queries = q_ref[...].reshape(tokens, H * HD)
    live = jnp.concatenate([live_ref[...]] * group) > 0.5
    first_token = where_ref[0] * step_count
    shape = (group * tokens, new_k_ref.shape[0])
    step = lax.broadcasted_iota(jnp.int32, shape, 0) % tokens - first_token
    new_index = lax.broadcasted_iota(jnp.int32, shape, 1)
    new_live = (step >= new_index) & (step < step_count)
    for kv in range(KV):
        span = slice(kv * HD, (kv + 1) * HD)
        q = jnp.concatenate(
            [queries[:, (kv * group + g) * HD : (kv * group + g + 1) * HD] for g in range(group)]
        )
        scores = jnp.where(live, dot_last(q, keys_ref[:, span]), NEGATIVE)
        top = jnp.max(scores, axis=1, keepdims=True)
        probs = jnp.where(live, jnp.exp(scores - top), 0.0)
        total = jnp.sum(probs, axis=1, keepdims=True)
        accum = jnp.dot(
            probs.astype(jnp.bfloat16), values_ref[:, span], preferred_element_type=jnp.float32
        )
        new_scores = dot_last(q, new_k_ref[:, span].astype(jnp.bfloat16))
        new_scores = jnp.where(new_live, new_scores, NEGATIVE)
        both = jnp.maximum(top, jnp.max(new_scores, axis=1, keepdims=True))
        carried = jnp.exp(top - both)
        new_probs = jnp.where(new_live, jnp.exp(new_scores - both), 0.0)
        total = total * carried + jnp.sum(new_probs, axis=1, keepdims=True)
        accum = accum * carried
        for u in range(step_count):
            accum = accum + new_probs[:, u : u + 1] * new_v_ref[u : u + 1, span]
        sent = accum.astype(jnp.bfloat16)
        parts = []
        for value in (both, total):
            for _ in range(3):
                part = value.astype(jnp.bfloat16).astype(jnp.float32)
                parts.append(part)
                value = value - part
        lane = lax.broadcasted_iota(jnp.int32, (group * tokens, 128), 1)
        wide = jnp.zeros((group * tokens, 128), jnp.float32)
        for i, part in enumerate(parts):
            wide = jnp.where(lane == i, part, wide)
        turned = jnp.transpose(wide)[:16].astype(jnp.bfloat16)
        for g in range(group):
            pair = turned[:, g // 2 * 128 : (g // 2 + 1) * 128]
            for part in range(HD // columns):
                target = (kv * group + g) * (HD // columns) + part
                out_ref[target, :tokens, :] = sent[
                    g * tokens : (g + 1) * tokens, part * columns : (part + 1) * columns
                ]
                out_ref[target, tokens:, :] = pair


def out_kernel(req_count, where_ref, got_ref, *refs):
    w_refs = refs[:req_count]
    out_ref, turned_ref = refs[req_count:]
    blocks = got_ref.shape[0]
    copies, steps, _ = out_ref.shape
    tokens = copies * steps
    columns = got_ref.shape[2]
    head = where_ref[0] * columns // HD
    stats = got_ref[:, tokens:, :].astype(jnp.float32)
    tops = stats[:, 0, :] + stats[:, 1, :] + stats[:, 2, :]
    totals = stats[:, 3, :] + stats[:, 4, :] + stats[:, 5, :]
    rest = jnp.zeros((128 - 2 * blocks, 128), jnp.float32)
    turned_ref[...] = jnp.transpose(jnp.concatenate([tops, totals, rest]))
    mine = turned_ref[pl.ds(pl.multiple_of(head % 2 * tokens, tokens), tokens), :]
    tops = mine[:, :blocks]
    highest = jnp.max(tops, axis=1, keepdims=True)
    weights = jnp.exp(tops - highest)
    denominator = jnp.sum(mine[:, blocks : 2 * blocks] * weights, axis=1, keepdims=True)
    numerator = jnp.zeros((tokens, columns), jnp.float32)
    for b in range(blocks):
        numerator = numerator + got_ref[b, :tokens, :].astype(jnp.float32) * weights[:, b : b + 1]
    attention = (numerator / denominator).astype(jnp.bfloat16)
    for j, w_ref in enumerate(w_refs):
        width = w_ref.shape[1]
        part = jnp.dot(attention, w_ref[...], preferred_element_type=jnp.float32)
        part = part.astype(jnp.bfloat16)
        for i in range(copies):
            out_ref[i, :, j * width : (j + 1) * width] = part[i * steps : (i + 1) * steps]


def summed(req_count, where_ref, got_ref):
    width = got_ref.shape[2] // req_count
    blocks = []
    for i in range(req_count):
        j = lax.rem(where_ref[1] - i + req_count, req_count)
        cols = pl.ds(pl.multiple_of(j * width, width), width)
        blocks.append(jnp.sum(got_ref[:, :, cols].astype(jnp.float32), axis=0))
    return jnp.concatenate(blocks, axis=1)


def residual_kernel(
    req_count, where_ref, got_ref, hidden_ref, post_gain_ref, ffn_gain_ref, out_ref, residual_ref
):
    attn_out = summed(req_count, where_ref, got_ref)
    residual = hidden_ref[...].astype(jnp.float32) + normalize(attn_out) * post_gain_ref[...]
    residual_ref[...] = residual
    ffn_in = (normalize(residual) * ffn_gain_ref[...]).astype(jnp.bfloat16)
    for i in range(out_ref.shape[0]):
        out_ref[i] = ffn_in


def last_kernel(req_count, where_ref, got_ref, residual_ref, gain_ref, out_ref):
    down_out = summed(req_count, where_ref, got_ref)
    layer = (residual_ref[...] + normalize(down_out) * gain_ref[...]).astype(jnp.bfloat16)
    for i in range(out_ref.shape[0]):
        out_ref[i] = layer


def ffn_kernel(gate_rows, down_shape, where_ref, x_ref, *refs):
    req_count = len(refs) // 2 - 1
    w_refs, out_ref, held, sem_ref = refs[:req_count], refs[req_count], refs[req_count + 1 : -1], refs[-1]
    down_rows, down_width = down_shape
    packed_rows, width = w_refs[0].shape
    spans = [(0, gate_rows), (gate_rows, gate_rows), (2 * gate_rows, packed_rows - 2 * gate_rows)]
    copies = []
    for j in range(req_count):
        for first, rows in spans:
            part = pl.ds(first, rows)
            copies.append(
                pltpu.make_async_copy(
                    w_refs[j].at[part, :], held[j].at[part, :], sem_ref.at[len(copies)]
                )
            )
            copies[-1].start()
    blocks, steps, _ = x_ref.shape
    tokens = blocks * steps
    gate_out = up_out = None
    for j in range(req_count):
        first = lax.rem(where_ref[1] - j + req_count, req_count) * gate_rows
        cols = pl.ds(pl.multiple_of(first, gate_rows), gate_rows)
        part = x_ref[:, :, cols].reshape(tokens, gate_rows)
        copies[3 * j].wait()
        gate_w = held[j][:gate_rows, :]
        gate = jnp.dot(part, gate_w, preferred_element_type=jnp.float32)
        copies[3 * j + 1].wait()
        up_w = held[j][gate_rows : 2 * gate_rows, :]
        up = jnp.dot(part, up_w, preferred_element_type=jnp.float32)
        gate_out = gate if j == 0 else gate_out + gate
        up_out = up if j == 0 else up_out + up
    activated = (jax.nn.gelu(gate_out, approximate=True) * up_out).astype(jnp.bfloat16)
    for j in range(req_count):
        copies[3 * j + 2].wait()
        for piece in range(down_width // width):
            row = 2 * gate_rows + piece * down_rows
            down_w = held[j][row : row + down_rows, :]
            part = jnp.dot(activated, down_w, preferred_element_type=jnp.float32)
            part = part.astype(jnp.bfloat16)
            first = j * down_width + piece * width
            for i in range(blocks):
                out_ref[i, :, first : first + width] = part[i * steps : (i + 1) * steps]


def live_rows(
    seq_index, prompt_shape, pool_rows, group_of, prompt_lengths, tail_lengths, page_table
):
    group_count, prompt_span = prompt_shape
    rows_req = group_of.shape[0]
    member = (group_of % group_count)[:, None] == jnp.arange(group_count, dtype=jnp.int32)[None, :]
    prompt_pos = seq_index * prompt_span + jnp.arange(prompt_span, dtype=jnp.int32)
    prompt_live = prompt_pos[None, :] < prompt_lengths[:, None]
    prompt_mask = (member[:, :, None] & prompt_live[None, :, :]).reshape(
        rows_req, group_count * prompt_span
    )
    slot_count = pool_rows // PAGE
    table_row = page_table[0]
    table_len = table_row.shape[0]
    tail_pages = table_len // rows_req
    slot_ids = seq_index * slot_count + jnp.arange(slot_count, dtype=jnp.int32)
    matches = table_row[None, :] == slot_ids[:, None]
    entries = jnp.sum(
        jnp.where(matches, jnp.arange(table_len, dtype=jnp.int32)[None, :], 0), axis=1
    )
    owners = jnp.repeat(entries // tail_pages, PAGE)
    tail_pos = jnp.repeat(entries % tail_pages, PAGE) * PAGE + jnp.tile(
        jnp.arange(PAGE, dtype=jnp.int32), slot_count
    )
    tail_mask = (owners[None, :] == jnp.arange(rows_req, dtype=jnp.int32)[:, None]) & (
        tail_pos[None, :] < tail_lengths[:, None]
    )
    return jnp.concatenate([prompt_mask, tail_mask], axis=1)


def general_attention(
    seq_index,
    seq_count,
    rows_req,
    step_count,
    out_rows,
    projected,
    q_gain,
    k_gain,
    live,
    prompt_keys,
    prompt_values,
    tail_keys,
    tail_values,
):
    group_size = H // KV
    share = projected.shape[0]
    tokens = rows_req * step_count
    heads = normalize(projected.reshape(share, QKV // HD, HD))
    gains = jnp.concatenate(
        [
            jnp.broadcast_to(q_gain, (H, HD)),
            jnp.broadcast_to(k_gain, (KV, HD)),
            jnp.ones((KV, HD), jnp.float32),
        ]
    )
    mine = (heads * gains).astype(jnp.bfloat16).reshape(share, QKV)
    qkv = gather_rows(mine, seq_count)
    queries = qkv[:, : H * HD]
    keys_new = qkv[:, H * HD : (H + KV) * HD]
    values_new = qkv[:, (H + KV) * HD :]

    query_groups = queries.reshape(rows_req, step_count, KV, group_size, HD)
    mask = live[:, None, None, None, :]
    keys = jnp.concatenate([prompt_keys, tail_keys]).reshape(-1, KV, HD)
    values = jnp.concatenate([prompt_values, tail_values]).reshape(-1, KV, HD)
    scores = jnp.einsum("rskgd,pkd->rskgp", query_groups, keys, preferred_element_type=jnp.float32)
    scores = jnp.where(mask, scores, NEGATIVE)
    block_top = jnp.max(scores, axis=4)
    probs = jnp.where(mask, jnp.exp(scores - block_top[..., None]), 0.0)
    block_total = jnp.sum(probs, axis=4)
    block_accum = jnp.einsum(
        "rskgp,pkd->rskgd",
        probs.astype(jnp.bfloat16),
        values,
        preferred_element_type=jnp.float32,
    )

    stats = split_three(jnp.stack([block_top, block_total])).reshape(6, tokens, H)
    per_head = seq_count // H
    stats = jnp.repeat(stats.transpose(2, 0, 1).reshape(H, -1, out_rows), per_head, axis=0)
    accum_blocks = (
        block_accum.astype(jnp.bfloat16).reshape(tokens, seq_count, out_rows).transpose(1, 0, 2)
    )
    got = exchange(jnp.concatenate([accum_blocks, stats], axis=1), "seq")
    got_accum = got[:, :tokens].astype(jnp.float32)
    got_stats = got[:, tokens:].astype(jnp.float32).reshape(seq_count, 2 * 3, tokens)
    got_top = got_stats[:, 0] + got_stats[:, 2] + got_stats[:, 4]
    got_total = got_stats[:, 1] + got_stats[:, 3] + got_stats[:, 5]

    first_col = seq_index * out_rows
    head = first_col // HD
    kv_head = head // group_size
    head_queries = lax.dynamic_slice_in_dim(queries, head * HD, HD, 1)
    head_keys = lax.dynamic_slice_in_dim(keys_new, kv_head * HD, HD, 1)
    head_values = lax.dynamic_slice_in_dim(
        values_new, kv_head * HD + first_col % HD, out_rows, 1
    ).astype(jnp.float32)
    new_scores = jnp.dot(head_queries, head_keys.T, preferred_element_type=jnp.float32)
    token_ids = jnp.arange(tokens, dtype=jnp.int32)
    causal = (token_ids[:, None] // step_count == token_ids[None, :] // step_count) & (
        token_ids[:, None] >= token_ids[None, :]
    )
    new_scores = jnp.where(causal, new_scores, NEGATIVE)
    highest = jnp.maximum(jnp.max(got_top, axis=0), jnp.max(new_scores, axis=1))
    weights = jnp.exp(got_top - highest[None])
    new_probs = jnp.where(causal, jnp.exp(new_scores - highest[:, None]), 0.0)
    denominator = jnp.sum(got_total * weights, axis=0) + jnp.sum(new_probs, axis=1)
    numerator = jnp.sum(got_accum * weights[..., None], axis=0) + jnp.dot(
        new_probs, head_values, precision=lax.Precision.HIGHEST
    )
    return (numerator / denominator[:, None]).astype(jnp.bfloat16)


def on_device(
    req_count,
    seq_count,
    hidden_in,
    attn_gain,
    q_gain,
    k_gain,
    post_attn_gain,
    ffn_gain,
    post_ffn_gain,
    w_qkv,
    w_out,
    w_gate,
    w_up,
    w_down,
    prompt_keys,
    prompt_values,
    tail_keys,
    tail_values,
    group_of,
    prompt_lengths,
    tail_lengths,
    page_table,
):
    seq_index = lax.axis_index("seq")
    req_index = lax.axis_index("req")
    rows_req, step_count, _ = hidden_in.shape
    group_size = H // KV
    tokens = rows_req * step_count
    share = tokens // seq_count

    def shifted(values):
        return [values] + [
            lax.ppermute(values, "req", [(i, (i + j) % req_count) for i in range(req_count)])
            for j in range(1, req_count)
        ]

    where = jnp.stack([seq_index, req_index]).astype(jnp.int32)
    in_rows = w_qkv.shape[0]
    out_rows = w_out.shape[0]
    if in_rows % 128 == 0:
        normed_cols = call(
            norm_columns_kernel,
            "norm_columns",
            jax.ShapeDtypeStruct((tokens, in_rows), jnp.bfloat16),
            where,
            hidden_in,
            attn_gain.reshape(1, D),
        )
    else:
        normed = (normalize(hidden_in.astype(jnp.float32)) * attn_gain).astype(jnp.bfloat16)
        normed_cols = lax.dynamic_slice_in_dim(normed, seq_index * in_rows, in_rows, 2)
        normed_cols = normed_cols.reshape(tokens, in_rows)
    normed_all = lax.all_gather(normed_cols, "req", axis=0, tiled=True)
    out_blocks = shifted(w_out)
    width = w_gate.shape[1]
    pieces = [w_down[:, c : c + width] for c in range(0, w_down.shape[1], width)]
    packed = shifted(jnp.concatenate([w_gate, w_up] + pieces))

    qkv_part = jnp.dot(normed_all, w_qkv, preferred_element_type=jnp.float32)
    qkv_cols = w_qkv.shape[1]
    qkv_blocks = (
        (qkv_part * LINK_SCALE)
        .astype(jnp.float16)
        .reshape(req_count * seq_count, share, qkv_cols)
    )
    qkv_got = exchange(qkv_blocks, ("req", "seq"))
    qkv_got = qkv_got.reshape(req_count, seq_count, share, qkv_cols)
    projected = jnp.sum(qkv_got.astype(jnp.float32), axis=1) * (1.0 / LINK_SCALE)
    live = live_rows(
        seq_index, prompt_keys.shape[:2], tail_keys.shape[1], group_of, prompt_lengths,
        tail_lengths, page_table,
    )
    caches = [
        array.reshape(-1, KV * HD) for array in (prompt_keys, prompt_values, tail_keys, tail_values)
    ]
    direct = share == step_count and out_rows % 128 == 0 and tokens == 64 and qkv_cols % HD == 0
    if direct:
        q_blocks, new_keys, new_values = call(
            head_norm_kernel,
            "head_norm",
            (
                jax.ShapeDtypeStruct((seq_count, share, H * HD), jnp.bfloat16),
                jax.ShapeDtypeStruct((8, KV * HD), jnp.float32),
                jax.ShapeDtypeStruct((8, KV * HD), jnp.float32),
            ),
            where,
            projected,
            jnp.stack([q_gain, k_gain]),
        )
        q_got, out_blocks = tie(exchange(q_blocks, "seq"), out_blocks)
        live = jnp.repeat(live.astype(jnp.float32), step_count, axis=0)
        sent = call(
            functools.partial(block_kernel, step_count),
            "block_attention",
            jax.ShapeDtypeStruct((seq_count, tokens + 16, out_rows), jnp.bfloat16),
            where,
            q_got,
            live,
            new_keys,
            new_values,
            jnp.concatenate([caches[0], caches[2]]),
            jnp.concatenate([caches[1], caches[3]]),
        )
        got = exchange(sent, "seq")
        out_part = call(
            functools.partial(out_kernel, req_count),
            "combine_out",
            jax.ShapeDtypeStruct((seq_count, share, D), jnp.bfloat16),
            where,
            got,
            *out_blocks,
            scratch=[pltpu.VMEM((128, 128), jnp.float32)],
        )
    else:
        projected = projected.transpose(1, 0, 2).reshape(share, QKV)
        attention_cols = general_attention(
            seq_index, seq_count, rows_req, step_count, out_rows, projected, q_gain, k_gain,
            live, *caches,
        )
        out_part = jnp.concatenate(
            [jnp.dot(attention_cols, w, preferred_element_type=jnp.float32) for w in out_blocks],
            axis=1,
        )
        out_part = out_part.astype(jnp.bfloat16).reshape(seq_count, share, D)
    hidden_mine = lax.dynamic_index_in_dim(
        hidden_in.reshape(seq_count, share, D), seq_index, 0, keepdims=False
    )
    ffn_blocks, residual = call(
        functools.partial(residual_kernel, req_count),
        "residual_norms",
        (
            jax.ShapeDtypeStruct((seq_count, share, D), jnp.bfloat16),
            jax.ShapeDtypeStruct((share, D), jnp.float32),
        ),
        where,
        exchange(out_part, "seq"),
        hidden_mine,
        post_attn_gain.reshape(1, D),
        ffn_gain.reshape(1, D),
    )
    down_part = call(
        functools.partial(ffn_kernel, w_gate.shape[0], w_down.shape),
        "feed_forward",
        jax.ShapeDtypeStruct((seq_count, share, D), jnp.bfloat16),
        where,
        exchange(ffn_blocks, "seq"),
        *packed,
        scratch=[pltpu.VMEM(w.shape, w.dtype) for w in packed]
        + [pltpu.SemaphoreType.DMA((3 * req_count,))],
        hbm_from=2,
    )
    layer_blocks = call(
        functools.partial(last_kernel, req_count),
        "last_norm",
        jax.ShapeDtypeStruct((seq_count, share, D), jnp.bfloat16),
        where,
        exchange(down_part, "seq"),
        residual,
        post_ffn_gain.reshape(1, D),
    )
    return exchange(layer_blocks, "seq").reshape(rows_req, step_count, D)


def solution(mesh):
    return jax.shard_map(
        functools.partial(on_device, mesh.shape["req"], mesh.shape["seq"]),
        mesh=mesh,
        in_specs=(
            P("req", None, None),
            P(),
            P(),
            P(),
            P(),
            P(),
            P(),
            P("seq", "req"),
            P("seq", "req"),
            P("req", "seq"),
            P("req", "seq"),
            P("seq", "req"),
            P("req", "seq", None),
            P("req", "seq", None),
            P("req", "seq", None),
            P("req", "seq", None),
            P("req"),
            P("req"),
            P("req"),
            P("req", None),
        ),
        out_specs=P("req", None, None),
        check_vma=False,
    )
```

```python
import functools

import jax
import jax.numpy as jnp
from jax import lax
from jax.experimental import pallas as pl
from jax.experimental.pallas import tpu as pltpu
from jax.sharding import PartitionSpec as P

D = 2048
H = 8
KV = 2
HD = 256
PAGE = 16
QKV = 3072


EPSILON = 1e-06
NEGATIVE = -1e30
LINK_SCALE = 512.0


def normalize(values):
    return values * lax.rsqrt(jnp.mean(values * values, axis=-1, keepdims=True) + EPSILON)


def split_three(values):
    high = values.astype(jnp.bfloat16)
    rest = values - high.astype(jnp.float32)
    middle = rest.astype(jnp.bfloat16)
    low = (rest - middle.astype(jnp.float32)).astype(jnp.bfloat16)
    return jnp.stack([high, middle, low])


def exchange(blocks, axes, groups=None):
    return lax.all_to_all(
        blocks, axes, split_axis=0, concat_axis=0, tiled=True, axis_index_groups=groups
    )


def tie(*arrays):
    return lax.optimization_barrier(arrays)


def spread(block, copies):
    return jnp.broadcast_to(block[None], (copies,) + block.shape)


def gather_rows(rows, count):
    return exchange(spread(rows, count), "seq").reshape(count * rows.shape[0], rows.shape[1])


def call(kernel, name, out_shape, *operands, scratch=(), hbm_from=None, limit=16):
    in_specs = [pl.BlockSpec(memory_space=pltpu.SMEM)]
    for i in range(1, len(operands)):
        space = pltpu.HBM if hbm_from is not None and i >= hbm_from else pltpu.VMEM
        in_specs.append(pl.BlockSpec(memory_space=space))
    return pl.pallas_call(
        kernel,
        name=name,
        out_shape=out_shape,
        in_specs=in_specs,
        out_specs=jax.tree.map(lambda _: pl.BlockSpec(memory_space=pltpu.VMEM), out_shape),
        scratch_shapes=scratch,
        compiler_params=pltpu.CompilerParams(vmem_limit_bytes=limit * 1024 * 1024),
    )(*operands)


def norm_columns_kernel(where_ref, hidden_ref, gain_ref, out_ref):
    columns = out_ref.shape[1]
    hidden = hidden_ref[...].astype(jnp.float32)
    scale = lax.rsqrt(jnp.mean(hidden * hidden, axis=-1, keepdims=True) + EPSILON)
    cols = pl.ds(pl.multiple_of(where_ref[0] * columns, columns), columns)
    normed = hidden_ref[:, :, cols].astype(jnp.float32) * scale * gain_ref[:, cols]
    out_ref[...] = normed.reshape(out_ref.shape).astype(jnp.bfloat16)


def head_norm_kernel(where_ref, projected_ref, gains_ref, q_ref, k_ref, v_ref):
    width = projected_ref.shape[2]
    copies, rows, _ = q_ref.shape
    fill = jnp.zeros((k_ref.shape[0] - rows, HD), jnp.float32)
    for head in range(H + 2 * KV):
        half, first = divmod(head * HD, width)
        values = normalize(projected_ref[half, :, first : first + HD])
        if head < H:
            values = (values * gains_ref[0:1, :]).astype(jnp.bfloat16)
            for i in range(copies):
                q_ref[i, :, head * HD : (head + 1) * HD] = values
        else:
            if head < H + KV:
                values = values * gains_ref[1:2, :]
            values = values.astype(jnp.bfloat16).astype(jnp.float32)
            target, slot = (k_ref, head - H) if head < H + KV else (v_ref, head - H - KV)
            target[:, slot * HD : (slot + 1) * HD] = jnp.concatenate([values, fill])


def dot_last(a, b):
    return lax.dot_general(a, b, (((1,), (1,)), ((), ())), preferred_element_type=jnp.float32)


def block_kernel(
    step_count,
    where_ref,
    q_ref,
    live_ref,
    new_k_ref,
    new_v_ref,
    keys_ref,
    values_ref,
    out_ref,
):
    copies, steps, _ = q_ref.shape
    tokens = copies * steps
    columns = out_ref.shape[2]
    group = H // KV
    queries = q_ref[...].reshape(tokens, H * HD)
    live = jnp.concatenate([live_ref[...]] * group) > 0.5
    first_token = where_ref[0] * step_count
    shape = (group * tokens, new_k_ref.shape[0])
    step = lax.broadcasted_iota(jnp.int32, shape, 0) % tokens - first_token
    new_index = lax.broadcasted_iota(jnp.int32, shape, 1)
    new_live = (step >= new_index) & (step < step_count)
    for kv in range(KV):
        span = slice(kv * HD, (kv + 1) * HD)
        q = jnp.concatenate(
            [queries[:, (kv * group + g) * HD : (kv * group + g + 1) * HD] for g in range(group)]
        )
        scores = jnp.where(live, dot_last(q, keys_ref[:, span]), NEGATIVE)
        top = jnp.max(scores, axis=1, keepdims=True)
        probs = jnp.where(live, jnp.exp(scores - top), 0.0)
        total = jnp.sum(probs, axis=1, keepdims=True)
        accum = jnp.dot(
            probs.astype(jnp.bfloat16), values_ref[:, span], preferred_element_type=jnp.float32
        )
        new_scores = dot_last(q, new_k_ref[:, span].astype(jnp.bfloat16))
        new_scores = jnp.where(new_live, new_scores, NEGATIVE)
        both = jnp.maximum(top, jnp.max(new_scores, axis=1, keepdims=True))
        carried = jnp.exp(top - both)
        new_probs = jnp.where(new_live, jnp.exp(new_scores - both), 0.0)
        total = total * carried + jnp.sum(new_probs, axis=1, keepdims=True)
        accum = accum * carried
        for u in range(step_count):
            accum = accum + new_probs[:, u : u + 1] * new_v_ref[u : u + 1, span]
        sent = accum.astype(jnp.bfloat16)
        parts = []
        for value in (both, total):
            for _ in range(3):
                part = value.astype(jnp.bfloat16).astype(jnp.float32)
                parts.append(part)
                value = value - part
        lane = lax.broadcasted_iota(jnp.int32, (group * tokens, 128), 1)
        wide = jnp.zeros((group * tokens, 128), jnp.float32)
        for i, part in enumerate(parts):
            wide = jnp.where(lane == i, part, wide)
        turned = jnp.transpose(wide)[:16].astype(jnp.bfloat16)
        for g in range(group):
            pair = turned[:, g // 2 * 128 : (g // 2 + 1) * 128]
            for part in range(HD // columns):
                target = (kv * group + g) * (HD // columns) + part
                out_ref[target, :tokens, :] = sent[
                    g * tokens : (g + 1) * tokens, part * columns : (part + 1) * columns
                ]
                out_ref[target, tokens:, :] = pair


def out_kernel(req_count, where_ref, got_ref, *refs):
    w_refs = refs[:req_count]
    out_ref, turned_ref = refs[req_count:]
    blocks = got_ref.shape[0]
    copies, steps, _ = out_ref.shape
    tokens = copies * steps
    columns = got_ref.shape[2]
    head = where_ref[0] * columns // HD
    stats = got_ref[:, tokens:, :].astype(jnp.float32)
    tops = stats[:, 0, :] + stats[:, 1, :] + stats[:, 2, :]
    totals = stats[:, 3, :] + stats[:, 4, :] + stats[:, 5, :]
    rest = jnp.zeros((128 - 2 * blocks, 128), jnp.float32)
    turned_ref[...] = jnp.transpose(jnp.concatenate([tops, totals, rest]))
    mine = turned_ref[pl.ds(pl.multiple_of(head % 2 * tokens, tokens), tokens), :]
    tops = mine[:, :blocks]
    highest = jnp.max(tops, axis=1, keepdims=True)
    weights = jnp.exp(tops - highest)
    denominator = jnp.sum(mine[:, blocks : 2 * blocks] * weights, axis=1, keepdims=True)
    numerator = jnp.zeros((tokens, columns), jnp.float32)
    for b in range(blocks):
        numerator = numerator + got_ref[b, :tokens, :].astype(jnp.float32) * weights[:, b : b + 1]
    attention = (numerator / denominator).astype(jnp.bfloat16)
    for j, w_ref in enumerate(w_refs):
        width = w_ref.shape[1]
        part = jnp.dot(attention, w_ref[...], preferred_element_type=jnp.float32)
        part = part.astype(jnp.bfloat16)
        for i in range(copies):
            out_ref[i, :, j * width : (j + 1) * width] = part[i * steps : (i + 1) * steps]


def summed(req_count, where_ref, got_ref):
    width = got_ref.shape[2] // req_count
    blocks = []
    for i in range(req_count):
        j = lax.rem(where_ref[1] - i + req_count, req_count)
        cols = pl.ds(pl.multiple_of(j * width, width), width)
        blocks.append(jnp.sum(got_ref[:, :, cols].astype(jnp.float32), axis=0))
    return jnp.concatenate(blocks, axis=1)


def residual_kernel(
    req_count, where_ref, got_ref, hidden_ref, post_gain_ref, ffn_gain_ref, out_ref, residual_ref
):
    attn_out = summed(req_count, where_ref, got_ref)
    residual = hidden_ref[...].astype(jnp.float32) + normalize(attn_out) * post_gain_ref[...]
    residual_ref[...] = residual
    ffn_in = (normalize(residual) * ffn_gain_ref[...]).astype(jnp.bfloat16)
    for i in range(out_ref.shape[0]):
        out_ref[i] = ffn_in


def last_kernel(req_count, where_ref, got_ref, residual_ref, gain_ref, out_ref):
    down_out = summed(req_count, where_ref, got_ref)
    layer = (residual_ref[...] + normalize(down_out) * gain_ref[...]).astype(jnp.bfloat16)
    for i in range(out_ref.shape[0]):
        out_ref[i] = layer


def ffn_kernel(req_count, where_ref, x_ref, *refs):
    count = req_count + 2
    w_refs, out_ref, held, sem_ref = refs[:count], refs[count], refs[count + 1 : -1], refs[-1]
    gate_rows, width = w_refs[0].shape
    down_rows, down_width = w_refs[2].shape
    copies = []

    def load(source, target):
        copies.append(pltpu.make_async_copy(source, target, sem_ref.at[len(copies)]))
        copies[-1].start()

    for i in range(3):
        load(w_refs[i], held[i])
    packed_rows = 2 * gate_rows + down_rows * (down_width // width)
    spans = [(0, gate_rows), (gate_rows, gate_rows), (2 * gate_rows, packed_rows - 2 * gate_rows)]
    for j in range(3, count):
        for first, rows in spans:
            load(w_refs[j].at[pl.ds(first, rows), :], held[j].at[pl.ds(first, rows), :])
    blocks, steps, _ = x_ref.shape
    tokens = blocks * steps
    gate_out = up_out = None
    for j in range(req_count):
        first = lax.rem(where_ref[1] - j + req_count, req_count) * gate_rows
        cols = pl.ds(pl.multiple_of(first, gate_rows), gate_rows)
        part = x_ref[:, :, cols].reshape(tokens, gate_rows)
        copies[3 * j].wait()
        gate_w = held[0][...] if j == 0 else held[j + 2][:gate_rows, :]
        gate = jnp.dot(part, gate_w, preferred_element_type=jnp.float32)
        copies[3 * j + 1].wait()
        up_w = held[1][...] if j == 0 else held[j + 2][gate_rows : 2 * gate_rows, :]
        up = jnp.dot(part, up_w, preferred_element_type=jnp.float32)
        gate_out = gate if j == 0 else gate_out + gate
        up_out = up if j == 0 else up_out + up
    activated = (jax.nn.gelu(gate_out, approximate=True) * up_out).astype(jnp.bfloat16)
    for j in range(req_count):
        copies[3 * j + 2].wait()
        for piece in range(down_width // width):
            if j == 0:
                down_w = held[2][:, piece * width : (piece + 1) * width]
            else:
                row = 2 * gate_rows + piece * down_rows
                down_w = held[j + 2][row : row + down_rows, :]
            part = jnp.dot(activated, down_w, preferred_element_type=jnp.float32)
            part = part.astype(jnp.bfloat16)
            first = j * down_width + piece * width
            for i in range(blocks):
                out_ref[i, :, first : first + width] = part[i * steps : (i + 1) * steps]


def live_rows(
    seq_index, prompt_shape, pool_rows, group_of, prompt_lengths, tail_lengths, page_table
):
    group_count, prompt_span = prompt_shape
    rows_req = group_of.shape[0]
    member = (group_of % group_count)[:, None] == jnp.arange(group_count, dtype=jnp.int32)[None, :]
    prompt_pos = seq_index * prompt_span + jnp.arange(prompt_span, dtype=jnp.int32)
    prompt_live = prompt_pos[None, :] < prompt_lengths[:, None]
    prompt_mask = (member[:, :, None] & prompt_live[None, :, :]).reshape(
        rows_req, group_count * prompt_span
    )
    slot_count = pool_rows // PAGE
    table_row = page_table[0]
    table_len = table_row.shape[0]
    tail_pages = table_len // rows_req
    slot_ids = seq_index * slot_count + jnp.arange(slot_count, dtype=jnp.int32)
    matches = table_row[None, :] == slot_ids[:, None]
    entries = jnp.sum(
        jnp.where(matches, jnp.arange(table_len, dtype=jnp.int32)[None, :], 0), axis=1
    )
    owners = jnp.repeat(entries // tail_pages, PAGE)
    tail_pos = jnp.repeat(entries % tail_pages, PAGE) * PAGE + jnp.tile(
        jnp.arange(PAGE, dtype=jnp.int32), slot_count
    )
    tail_mask = (owners[None, :] == jnp.arange(rows_req, dtype=jnp.int32)[:, None]) & (
        tail_pos[None, :] < tail_lengths[:, None]
    )
    return jnp.concatenate([prompt_mask, tail_mask], axis=1)


def general_attention(
    seq_index,
    seq_count,
    rows_req,
    step_count,
    out_rows,
    projected,
    q_gain,
    k_gain,
    live,
    prompt_keys,
    prompt_values,
    tail_keys,
    tail_values,
):
    group_size = H // KV
    share = projected.shape[0]
    tokens = rows_req * step_count
    heads = normalize(projected.reshape(share, QKV // HD, HD))
    gains = jnp.concatenate(
        [
            jnp.broadcast_to(q_gain, (H, HD)),
            jnp.broadcast_to(k_gain, (KV, HD)),
            jnp.ones((KV, HD), jnp.float32),
        ]
    )
    mine = (heads * gains).astype(jnp.bfloat16).reshape(share, QKV)
    qkv = gather_rows(mine, seq_count)
    queries = qkv[:, : H * HD]
    keys_new = qkv[:, H * HD : (H + KV) * HD]
    values_new = qkv[:, (H + KV) * HD :]

    query_groups = queries.reshape(rows_req, step_count, KV, group_size, HD)
    mask = live[:, None, None, None, :]
    keys = jnp.concatenate([prompt_keys, tail_keys]).reshape(-1, KV, HD)
    values = jnp.concatenate([prompt_values, tail_values]).reshape(-1, KV, HD)
    scores = jnp.einsum("rskgd,pkd->rskgp", query_groups, keys, preferred_element_type=jnp.float32)
    scores = jnp.where(mask, scores, NEGATIVE)
    block_top = jnp.max(scores, axis=4)
    probs = jnp.where(mask, jnp.exp(scores - block_top[..., None]), 0.0)
    block_total = jnp.sum(probs, axis=4)
    block_accum = jnp.einsum(
        "rskgp,pkd->rskgd",
        probs.astype(jnp.bfloat16),
        values,
        preferred_element_type=jnp.float32,
    )

    stats = split_three(jnp.stack([block_top, block_total])).reshape(6, tokens, H)
    per_head = seq_count // H
    stats = jnp.repeat(stats.transpose(2, 0, 1).reshape(H, -1, out_rows), per_head, axis=0)
    accum_blocks = (
        block_accum.astype(jnp.bfloat16).reshape(tokens, seq_count, out_rows).transpose(1, 0, 2)
    )
    got = exchange(jnp.concatenate([accum_blocks, stats], axis=1), "seq")
    got_accum = got[:, :tokens].astype(jnp.float32)
    got_stats = got[:, tokens:].astype(jnp.float32).reshape(seq_count, 2 * 3, tokens)
    got_top = got_stats[:, 0] + got_stats[:, 2] + got_stats[:, 4]
    got_total = got_stats[:, 1] + got_stats[:, 3] + got_stats[:, 5]

    first_col = seq_index * out_rows
    head = first_col // HD
    kv_head = head // group_size
    head_queries = lax.dynamic_slice_in_dim(queries, head * HD, HD, 1)
    head_keys = lax.dynamic_slice_in_dim(keys_new, kv_head * HD, HD, 1)
    head_values = lax.dynamic_slice_in_dim(
        values_new, kv_head * HD + first_col % HD, out_rows, 1
    ).astype(jnp.float32)
    new_scores = jnp.dot(head_queries, head_keys.T, preferred_element_type=jnp.float32)
    token_ids = jnp.arange(tokens, dtype=jnp.int32)
    causal = (token_ids[:, None] // step_count == token_ids[None, :] // step_count) & (
        token_ids[:, None] >= token_ids[None, :]
    )
    new_scores = jnp.where(causal, new_scores, NEGATIVE)
    highest = jnp.maximum(jnp.max(got_top, axis=0), jnp.max(new_scores, axis=1))
    weights = jnp.exp(got_top - highest[None])
    new_probs = jnp.where(causal, jnp.exp(new_scores - highest[:, None]), 0.0)
    denominator = jnp.sum(got_total * weights, axis=0) + jnp.sum(new_probs, axis=1)
    numerator = jnp.sum(got_accum * weights[..., None], axis=0) + jnp.dot(
        new_probs, head_values, precision=lax.Precision.HIGHEST
    )
    return (numerator / denominator[:, None]).astype(jnp.bfloat16)


def on_device(
    req_count,
    seq_count,
    hidden_in,
    attn_gain,
    q_gain,
    k_gain,
    post_attn_gain,
    ffn_gain,
    post_ffn_gain,
    w_qkv,
    w_out,
    w_gate,
    w_up,
    w_down,
    prompt_keys,
    prompt_values,
    tail_keys,
    tail_values,
    group_of,
    prompt_lengths,
    tail_lengths,
    page_table,
):
    seq_index = lax.axis_index("seq")
    req_index = lax.axis_index("req")
    rows_req, step_count, _ = hidden_in.shape
    group_size = H // KV
    tokens = rows_req * step_count
    share = tokens // seq_count

    def shifted(values):
        return [values] + [
            lax.ppermute(values, "req", [(i, (i + j) % req_count) for i in range(req_count)])
            for j in range(1, req_count)
        ]

    where = jnp.stack([seq_index, req_index]).astype(jnp.int32)
    in_rows = w_qkv.shape[0]
    out_rows = w_out.shape[0]
    if in_rows % 128 == 0:
        normed_cols = call(
            norm_columns_kernel,
            "norm_columns",
            jax.ShapeDtypeStruct((tokens, in_rows), jnp.bfloat16),
            where,
            hidden_in,
            attn_gain.reshape(1, D),
        )
    else:
        normed = (normalize(hidden_in.astype(jnp.float32)) * attn_gain).astype(jnp.bfloat16)
        normed_cols = lax.dynamic_slice_in_dim(normed, seq_index * in_rows, in_rows, 2)
        normed_cols = normed_cols.reshape(tokens, in_rows)
    normed_all = lax.all_gather(normed_cols, "req", axis=0, tiled=True)
    out_blocks = shifted(w_out)
    width = w_gate.shape[1]
    pieces = [w_down[:, c : c + width] for c in range(0, w_down.shape[1], width)]
    packed = shifted(jnp.concatenate([w_gate, w_up] + pieces))[1:]

    qkv_part = jnp.dot(normed_all, w_qkv, preferred_element_type=jnp.float32)
    qkv_cols = w_qkv.shape[1]
    qkv_blocks = (
        (qkv_part * LINK_SCALE)
        .astype(jnp.float16)
        .reshape(req_count * seq_count, share, qkv_cols)
    )
    qkv_got = exchange(qkv_blocks, ("req", "seq"))
    qkv_got = qkv_got.reshape(req_count, seq_count, share, qkv_cols)
    projected = jnp.sum(qkv_got.astype(jnp.float32), axis=1) * (1.0 / LINK_SCALE)
    live = live_rows(
        seq_index, prompt_keys.shape[:2], tail_keys.shape[1], group_of, prompt_lengths,
        tail_lengths, page_table,
    )
    caches = [
        array.reshape(-1, KV * HD) for array in (prompt_keys, prompt_values, tail_keys, tail_values)
    ]
    direct = share == step_count and out_rows % 128 == 0 and tokens == 64 and qkv_cols % HD == 0
    if direct:
        q_blocks, new_keys, new_values = call(
            head_norm_kernel,
            "head_norm",
            (
                jax.ShapeDtypeStruct((seq_count, share, H * HD), jnp.bfloat16),
                jax.ShapeDtypeStruct((8, KV * HD), jnp.float32),
                jax.ShapeDtypeStruct((8, KV * HD), jnp.float32),
            ),
            where,
            projected,
            jnp.stack([q_gain, k_gain]),
        )
        q_got, out_blocks = tie(exchange(q_blocks, "seq"), out_blocks)
        live = jnp.repeat(live.astype(jnp.float32), step_count, axis=0)
        sent = call(
            functools.partial(block_kernel, step_count),
            "block_attention",
            jax.ShapeDtypeStruct((seq_count, tokens + 16, out_rows), jnp.bfloat16),
            where,
            q_got,
            live,
            new_keys,
            new_values,
            jnp.concatenate([caches[0], caches[2]]),
            jnp.concatenate([caches[1], caches[3]]),
        )
        got = exchange(sent, "seq")
        out_part = call(
            functools.partial(out_kernel, req_count),
            "combine_out",
            jax.ShapeDtypeStruct((seq_count, share, D), jnp.bfloat16),
            where,
            got,
            *out_blocks,
            scratch=[pltpu.VMEM((128, 128), jnp.float32)],
        )
    else:
        projected = projected.transpose(1, 0, 2).reshape(share, QKV)
        attention_cols = general_attention(
            seq_index, seq_count, rows_req, step_count, out_rows, projected, q_gain, k_gain,
            live, *caches,
        )
        out_part = jnp.concatenate(
            [jnp.dot(attention_cols, w, preferred_element_type=jnp.float32) for w in out_blocks],
            axis=1,
        )
        out_part = out_part.astype(jnp.bfloat16).reshape(seq_count, share, D)
    hidden_mine = lax.dynamic_index_in_dim(
        hidden_in.reshape(seq_count, share, D), seq_index, 0, keepdims=False
    )
    ffn_blocks, residual = call(
        functools.partial(residual_kernel, req_count),
        "residual_norms",
        (
            jax.ShapeDtypeStruct((seq_count, share, D), jnp.bfloat16),
            jax.ShapeDtypeStruct((share, D), jnp.float32),
        ),
        where,
        exchange(out_part, "seq"),
        hidden_mine,
        post_attn_gain.reshape(1, D),
        ffn_gain.reshape(1, D),
    )
    held = [w_gate, w_up, w_down] + list(packed)
    down_part = call(
        functools.partial(ffn_kernel, req_count),
        "feed_forward",
        jax.ShapeDtypeStruct((seq_count, share, D), jnp.bfloat16),
        where,
        exchange(ffn_blocks, "seq"),
        *held,
        scratch=[pltpu.VMEM(w.shape, w.dtype) for w in held]
        + [pltpu.SemaphoreType.DMA((3 * req_count,))],
        hbm_from=2,
        limit=56,
    )
    layer_blocks = call(
        functools.partial(last_kernel, req_count),
        "last_norm",
        jax.ShapeDtypeStruct((seq_count, share, D), jnp.bfloat16),
        where,
        exchange(down_part, "seq"),
        residual,
        post_ffn_gain.reshape(1, D),
    )
    return exchange(layer_blocks, "seq").reshape(rows_req, step_count, D)


def solution(mesh):
    return jax.shard_map(
        functools.partial(on_device, mesh.shape["req"], mesh.shape["seq"]),
        mesh=mesh,
        in_specs=(
            P("req", None, None),
            P(),
            P(),
            P(),
            P(),
            P(),
            P(),
            P("seq", "req"),
            P("seq", "req"),
            P("req", "seq"),
            P("req", "seq"),
            P("seq", "req"),
            P("req", "seq", None),
            P("req", "seq", None),
            P("req", "seq", None),
            P("req", "seq", None),
            P("req"),
            P("req"),
            P("req"),
            P("req", None),
        ),
        out_specs=P("req", None, None),
        check_vma=False,
    )
```

```python
import functools

import jax
import jax.numpy as jnp
from jax import lax
from jax.experimental import pallas as pl
from jax.experimental.pallas import tpu as pltpu
from jax.sharding import PartitionSpec as P

D = 2048
H = 8
KV = 2
HD = 256
PAGE = 16
QKV = 3072


EPSILON = 1e-06
NEGATIVE = -1e30
LINK_SCALE = 512.0


def normalize(values):
    return values * lax.rsqrt(jnp.mean(values * values, axis=-1, keepdims=True) + EPSILON)


def split_three(values):
    high = values.astype(jnp.bfloat16)
    rest = values - high.astype(jnp.float32)
    middle = rest.astype(jnp.bfloat16)
    low = (rest - middle.astype(jnp.float32)).astype(jnp.bfloat16)
    return jnp.stack([high, middle, low])


def exchange(blocks, axes, groups=None):
    return lax.all_to_all(
        blocks, axes, split_axis=0, concat_axis=0, tiled=True, axis_index_groups=groups
    )


def tie(*arrays):
    return lax.optimization_barrier(arrays)


def spread(block, copies):
    return jnp.broadcast_to(block[None], (copies,) + block.shape)


def gather_rows(rows, count):
    return exchange(spread(rows, count), "seq").reshape(count * rows.shape[0], rows.shape[1])


def call(kernel, name, out_shape, *operands, scratch=(), hbm_from=None, limit=16):
    in_specs = [pl.BlockSpec(memory_space=pltpu.SMEM)]
    for i in range(1, len(operands)):
        space = pltpu.HBM if hbm_from is not None and i >= hbm_from else pltpu.VMEM
        in_specs.append(pl.BlockSpec(memory_space=space))
    return pl.pallas_call(
        kernel,
        name=name,
        out_shape=out_shape,
        in_specs=in_specs,
        out_specs=jax.tree.map(lambda _: pl.BlockSpec(memory_space=pltpu.VMEM), out_shape),
        scratch_shapes=scratch,
        compiler_params=pltpu.CompilerParams(vmem_limit_bytes=limit * 1024 * 1024),
    )(*operands)


def norm_columns_kernel(where_ref, hidden_ref, gain_ref, out_ref):
    columns = out_ref.shape[1]
    hidden = hidden_ref[...].astype(jnp.float32)
    scale = lax.rsqrt(jnp.mean(hidden * hidden, axis=-1, keepdims=True) + EPSILON)
    cols = pl.ds(pl.multiple_of(where_ref[0] * columns, columns), columns)
    normed = hidden_ref[:, :, cols].astype(jnp.float32) * scale * gain_ref[:, cols]
    out_ref[...] = normed.reshape(out_ref.shape).astype(jnp.bfloat16)


def head_norm_kernel(where_ref, projected_ref, gains_ref, q_ref, k_ref, v_ref):
    width = projected_ref.shape[2]
    copies, rows, _ = q_ref.shape
    fill = jnp.zeros((k_ref.shape[0] - rows, HD), jnp.float32)
    for head in range(H + 2 * KV):
        half, first = divmod(head * HD, width)
        values = normalize(projected_ref[half, :, first : first + HD])
        if head < H:
            values = (values * gains_ref[0:1, :]).astype(jnp.bfloat16)
            for i in range(copies):
                q_ref[i, :, head * HD : (head + 1) * HD] = values
        else:
            if head < H + KV:
                values = values * gains_ref[1:2, :]
            values = values.astype(jnp.bfloat16).astype(jnp.float32)
            target, slot = (k_ref, head - H) if head < H + KV else (v_ref, head - H - KV)
            target[:, slot * HD : (slot + 1) * HD] = jnp.concatenate([values, fill])


def dot_last(a, b):
    return lax.dot_general(a, b, (((1,), (1,)), ((), ())), preferred_element_type=jnp.float32)


def block_kernel(
    step_count,
    where_ref,
    q_ref,
    live_ref,
    new_k_ref,
    new_v_ref,
    keys_ref,
    values_ref,
    out_ref,
):
    copies, steps, _ = q_ref.shape
    tokens = copies * steps
    columns = out_ref.shape[2]
    group = H // KV
    queries = q_ref[...].reshape(tokens, H * HD)
    live = jnp.concatenate([live_ref[...]] * group) > 0.5
    first_token = where_ref[0] * step_count
    shape = (group * tokens, new_k_ref.shape[0])
    step = lax.broadcasted_iota(jnp.int32, shape, 0) % tokens - first_token
    new_index = lax.broadcasted_iota(jnp.int32, shape, 1)
    new_live = (step >= new_index) & (step < step_count)
    for kv in range(KV):
        span = slice(kv * HD, (kv + 1) * HD)
        q = jnp.concatenate(
            [queries[:, (kv * group + g) * HD : (kv * group + g + 1) * HD] for g in range(group)]
        )
        scores = jnp.where(live, dot_last(q, keys_ref[:, span]), NEGATIVE)
        top = jnp.max(scores, axis=1, keepdims=True)
        probs = jnp.where(live, jnp.exp(scores - top), 0.0)
        total = jnp.sum(probs, axis=1, keepdims=True)
        accum = jnp.dot(
            probs.astype(jnp.bfloat16), values_ref[:, span], preferred_element_type=jnp.float32
        )
        new_scores = dot_last(q, new_k_ref[:, span].astype(jnp.bfloat16))
        new_scores = jnp.where(new_live, new_scores, NEGATIVE)
        both = jnp.maximum(top, jnp.max(new_scores, axis=1, keepdims=True))
        carried = jnp.exp(top - both)
        new_probs = jnp.where(new_live, jnp.exp(new_scores - both), 0.0)
        total = total * carried + jnp.sum(new_probs, axis=1, keepdims=True)
        accum = accum * carried
        for u in range(step_count):
            accum = accum + new_probs[:, u : u + 1] * new_v_ref[u : u + 1, span]
        sent = accum.astype(jnp.bfloat16)
        parts = []
        for value in (both, total):
            for _ in range(3):
                part = value.astype(jnp.bfloat16).astype(jnp.float32)
                parts.append(part)
                value = value - part
        lane = lax.broadcasted_iota(jnp.int32, (group * tokens, 128), 1)
        wide = jnp.zeros((group * tokens, 128), jnp.float32)
        for i, part in enumerate(parts):
            wide = jnp.where(lane == i, part, wide)
        turned = jnp.transpose(wide)[:16].astype(jnp.bfloat16)
        for g in range(group):
            pair = turned[:, g // 2 * 128 : (g // 2 + 1) * 128]
            for part in range(HD // columns):
                target = (kv * group + g) * (HD // columns) + part
                out_ref[target, :tokens, :] = sent[
                    g * tokens : (g + 1) * tokens, part * columns : (part + 1) * columns
                ]
                out_ref[target, tokens:, :] = pair


def out_kernel(req_count, where_ref, got_ref, *refs):
    w_refs = refs[:req_count]
    out_ref, turned_ref = refs[req_count:]
    blocks = got_ref.shape[0]
    copies, steps, _ = out_ref.shape
    tokens = copies * steps
    columns = got_ref.shape[2]
    head = where_ref[0] * columns // HD
    stats = got_ref[:, tokens:, :].astype(jnp.float32)
    tops = stats[:, 0, :] + stats[:, 1, :] + stats[:, 2, :]
    totals = stats[:, 3, :] + stats[:, 4, :] + stats[:, 5, :]
    rest = jnp.zeros((128 - 2 * blocks, 128), jnp.float32)
    turned_ref[...] = jnp.transpose(jnp.concatenate([tops, totals, rest]))
    mine = turned_ref[pl.ds(pl.multiple_of(head % 2 * tokens, tokens), tokens), :]
    tops = mine[:, :blocks]
    highest = jnp.max(tops, axis=1, keepdims=True)
    weights = jnp.exp(tops - highest)
    denominator = jnp.sum(mine[:, blocks : 2 * blocks] * weights, axis=1, keepdims=True)
    numerator = jnp.zeros((tokens, columns), jnp.float32)
    for b in range(blocks):
        numerator = numerator + got_ref[b, :tokens, :].astype(jnp.float32) * weights[:, b : b + 1]
    attention = (numerator / denominator).astype(jnp.bfloat16)
    for j, w_ref in enumerate(w_refs):
        width = w_ref.shape[1]
        part = jnp.dot(attention, w_ref[...], preferred_element_type=jnp.float32)
        part = part.astype(jnp.bfloat16)
        for i in range(copies):
            out_ref[i, :, j * width : (j + 1) * width] = part[i * steps : (i + 1) * steps]


def summed(req_count, where_ref, got_ref):
    width = got_ref.shape[2] // req_count
    blocks = []
    for i in range(req_count):
        j = lax.rem(where_ref[1] - i + req_count, req_count)
        cols = pl.ds(pl.multiple_of(j * width, width), width)
        blocks.append(jnp.sum(got_ref[:, :, cols].astype(jnp.float32), axis=0))
    return jnp.concatenate(blocks, axis=1)


def residual_kernel(
    req_count, where_ref, got_ref, hidden_ref, post_gain_ref, ffn_gain_ref, out_ref, residual_ref
):
    attn_out = summed(req_count, where_ref, got_ref)
    residual = hidden_ref[...].astype(jnp.float32) + normalize(attn_out) * post_gain_ref[...]
    residual_ref[...] = residual
    ffn_in = (normalize(residual) * ffn_gain_ref[...]).astype(jnp.bfloat16)
    for i in range(out_ref.shape[0]):
        out_ref[i] = ffn_in


def last_kernel(req_count, where_ref, got_ref, residual_ref, gain_ref, out_ref):
    down_out = summed(req_count, where_ref, got_ref)
    layer = (residual_ref[...] + normalize(down_out) * gain_ref[...]).astype(jnp.bfloat16)
    for i in range(out_ref.shape[0]):
        out_ref[i] = layer


def ffn_kernel(req_count, where_ref, x_ref, *refs):
    gate_ref, up_ref, down_ref = refs[:3]
    pair_refs, other_refs = refs[3 : req_count + 2], refs[req_count + 2 : 2 * req_count + 1]
    out_ref, pairs, downs, sem_ref = refs[2 * req_count + 1 :]
    rows = gate_ref.shape[0]
    moves = [(gate_ref, pairs.at[0, 0]), (up_ref, pairs.at[0, 1])]
    for j, pair_ref in enumerate(pair_refs):
        for i in range(2):
            moves.append((pair_ref.at[pl.ds(i * rows, rows), :], pairs.at[j + 1, i]))
    moves.append((down_ref, downs.at[0]))
    moves += [(other_ref, downs.at[j + 1]) for j, other_ref in enumerate(other_refs)]
    copies = [
        pltpu.make_async_copy(source, target, sem_ref.at[i])
        for i, (source, target) in enumerate(moves)
    ]
    ahead = 3
    for copy in copies[:ahead]:
        copy.start()

    def arrive(i):
        copies[i].wait()
        if i + ahead < len(copies):
            copies[i + ahead].start()

    blocks, steps, _ = x_ref.shape
    tokens = blocks * steps
    gate_out = up_out = None
    for j in range(req_count):
        start = lax.rem(where_ref[1] - j + req_count, req_count) * rows
        part = x_ref[:, :, pl.ds(pl.multiple_of(start, rows), rows)].reshape(tokens, rows)
        arrive(2 * j)
        gate = jnp.dot(part, pairs[j, 0], preferred_element_type=jnp.float32)
        arrive(2 * j + 1)
        up = jnp.dot(part, pairs[j, 1], preferred_element_type=jnp.float32)
        gate_out = gate if j == 0 else gate_out + gate
        up_out = up if j == 0 else up_out + up
    activated = (jax.nn.gelu(gate_out, approximate=True) * up_out).astype(jnp.bfloat16)
    for j in range(req_count):
        width = downs.shape[2]
        arrive(2 * req_count + j)
        part = jnp.dot(activated, downs[j], preferred_element_type=jnp.float32)
        part = part.astype(jnp.bfloat16)
        for i in range(blocks):
            out_ref[i, :, j * width : (j + 1) * width] = part[i * steps : (i + 1) * steps]


def live_rows(
    seq_index, prompt_shape, pool_rows, group_of, prompt_lengths, tail_lengths, page_table
):
    group_count, prompt_span = prompt_shape
    rows_req = group_of.shape[0]
    member = (group_of % group_count)[:, None] == jnp.arange(group_count, dtype=jnp.int32)[None, :]
    prompt_pos = seq_index * prompt_span + jnp.arange(prompt_span, dtype=jnp.int32)
    prompt_live = prompt_pos[None, :] < prompt_lengths[:, None]
    prompt_mask = (member[:, :, None] & prompt_live[None, :, :]).reshape(
        rows_req, group_count * prompt_span
    )
    slot_count = pool_rows // PAGE
    table_row = page_table[0]
    table_len = table_row.shape[0]
    tail_pages = table_len // rows_req
    slot_ids = seq_index * slot_count + jnp.arange(slot_count, dtype=jnp.int32)
    matches = table_row[None, :] == slot_ids[:, None]
    entries = jnp.sum(
        jnp.where(matches, jnp.arange(table_len, dtype=jnp.int32)[None, :], 0), axis=1
    )
    owners = jnp.repeat(entries // tail_pages, PAGE)
    tail_pos = jnp.repeat(entries % tail_pages, PAGE) * PAGE + jnp.tile(
        jnp.arange(PAGE, dtype=jnp.int32), slot_count
    )
    tail_mask = (owners[None, :] == jnp.arange(rows_req, dtype=jnp.int32)[:, None]) & (
        tail_pos[None, :] < tail_lengths[:, None]
    )
    return jnp.concatenate([prompt_mask, tail_mask], axis=1)


def general_attention(
    seq_index,
    seq_count,
    rows_req,
    step_count,
    out_rows,
    projected,
    q_gain,
    k_gain,
    live,
    prompt_keys,
    prompt_values,
    tail_keys,
    tail_values,
):
    group_size = H // KV
    share = projected.shape[0]
    tokens = rows_req * step_count
    heads = normalize(projected.reshape(share, QKV // HD, HD))
    gains = jnp.concatenate(
        [
            jnp.broadcast_to(q_gain, (H, HD)),
            jnp.broadcast_to(k_gain, (KV, HD)),
            jnp.ones((KV, HD), jnp.float32),
        ]
    )
    mine = (heads * gains).astype(jnp.bfloat16).reshape(share, QKV)
    qkv = gather_rows(mine, seq_count)
    queries = qkv[:, : H * HD]
    keys_new = qkv[:, H * HD : (H + KV) * HD]
    values_new = qkv[:, (H + KV) * HD :]

    query_groups = queries.reshape(rows_req, step_count, KV, group_size, HD)
    mask = live[:, None, None, None, :]
    keys = jnp.concatenate([prompt_keys, tail_keys]).reshape(-1, KV, HD)
    values = jnp.concatenate([prompt_values, tail_values]).reshape(-1, KV, HD)
    scores = jnp.einsum("rskgd,pkd->rskgp", query_groups, keys, preferred_element_type=jnp.float32)
    scores = jnp.where(mask, scores, NEGATIVE)
    block_top = jnp.max(scores, axis=4)
    probs = jnp.where(mask, jnp.exp(scores - block_top[..., None]), 0.0)
    block_total = jnp.sum(probs, axis=4)
    block_accum = jnp.einsum(
        "rskgp,pkd->rskgd",
        probs.astype(jnp.bfloat16),
        values,
        preferred_element_type=jnp.float32,
    )

    stats = split_three(jnp.stack([block_top, block_total])).reshape(6, tokens, H)
    per_head = seq_count // H
    stats = jnp.repeat(stats.transpose(2, 0, 1).reshape(H, -1, out_rows), per_head, axis=0)
    accum_blocks = (
        block_accum.astype(jnp.bfloat16).reshape(tokens, seq_count, out_rows).transpose(1, 0, 2)
    )
    got = exchange(jnp.concatenate([accum_blocks, stats], axis=1), "seq")
    got_accum = got[:, :tokens].astype(jnp.float32)
    got_stats = got[:, tokens:].astype(jnp.float32).reshape(seq_count, 2 * 3, tokens)
    got_top = got_stats[:, 0] + got_stats[:, 2] + got_stats[:, 4]
    got_total = got_stats[:, 1] + got_stats[:, 3] + got_stats[:, 5]

    first_col = seq_index * out_rows
    head = first_col // HD
    kv_head = head // group_size
    head_queries = lax.dynamic_slice_in_dim(queries, head * HD, HD, 1)
    head_keys = lax.dynamic_slice_in_dim(keys_new, kv_head * HD, HD, 1)
    head_values = lax.dynamic_slice_in_dim(
        values_new, kv_head * HD + first_col % HD, out_rows, 1
    ).astype(jnp.float32)
    new_scores = jnp.dot(head_queries, head_keys.T, preferred_element_type=jnp.float32)
    token_ids = jnp.arange(tokens, dtype=jnp.int32)
    causal = (token_ids[:, None] // step_count == token_ids[None, :] // step_count) & (
        token_ids[:, None] >= token_ids[None, :]
    )
    new_scores = jnp.where(causal, new_scores, NEGATIVE)
    highest = jnp.maximum(jnp.max(got_top, axis=0), jnp.max(new_scores, axis=1))
    weights = jnp.exp(got_top - highest[None])
    new_probs = jnp.where(causal, jnp.exp(new_scores - highest[:, None]), 0.0)
    denominator = jnp.sum(got_total * weights, axis=0) + jnp.sum(new_probs, axis=1)
    numerator = jnp.sum(got_accum * weights[..., None], axis=0) + jnp.dot(
        new_probs, head_values, precision=lax.Precision.HIGHEST
    )
    return (numerator / denominator[:, None]).astype(jnp.bfloat16)


def on_device(
    req_count,
    seq_count,
    hidden_in,
    attn_gain,
    q_gain,
    k_gain,
    post_attn_gain,
    ffn_gain,
    post_ffn_gain,
    w_qkv,
    w_out,
    w_gate,
    w_up,
    w_down,
    prompt_keys,
    prompt_values,
    tail_keys,
    tail_values,
    group_of,
    prompt_lengths,
    tail_lengths,
    page_table,
):
    seq_index = lax.axis_index("seq")
    req_index = lax.axis_index("req")
    rows_req, step_count, _ = hidden_in.shape
    group_size = H // KV
    tokens = rows_req * step_count
    share = tokens // seq_count

    def shifted(values):
        return [values] + [
            lax.ppermute(values, "req", [(i, (i + j) % req_count) for i in range(req_count)])
            for j in range(1, req_count)
        ]

    where = jnp.stack([seq_index, req_index]).astype(jnp.int32)
    in_rows = w_qkv.shape[0]
    out_rows = w_out.shape[0]
    if in_rows % 128 == 0:
        normed_cols = call(
            norm_columns_kernel,
            "norm_columns",
            jax.ShapeDtypeStruct((tokens, in_rows), jnp.bfloat16),
            where,
            hidden_in,
            attn_gain.reshape(1, D),
        )
    else:
        normed = (normalize(hidden_in.astype(jnp.float32)) * attn_gain).astype(jnp.bfloat16)
        normed_cols = lax.dynamic_slice_in_dim(normed, seq_index * in_rows, in_rows, 2)
        normed_cols = normed_cols.reshape(tokens, in_rows)
    normed_all = lax.all_gather(normed_cols, "req", axis=0, tiled=True)
    out_blocks = shifted(w_out)
    pairs = shifted(jnp.concatenate([w_gate, w_up]))[1:]
    downs = shifted(w_down)[1:]

    qkv_part = jnp.dot(normed_all, w_qkv, preferred_element_type=jnp.float32)
    qkv_cols = w_qkv.shape[1]
    qkv_blocks = (
        (qkv_part * LINK_SCALE)
        .astype(jnp.float16)
        .reshape(req_count * seq_count, share, qkv_cols)
    )
    qkv_got = exchange(qkv_blocks, ("req", "seq"))
    qkv_got = qkv_got.reshape(req_count, seq_count, share, qkv_cols)
    projected = jnp.sum(qkv_got.astype(jnp.float32), axis=1) * (1.0 / LINK_SCALE)
    live = live_rows(
        seq_index, prompt_keys.shape[:2], tail_keys.shape[1], group_of, prompt_lengths,
        tail_lengths, page_table,
    )
    caches = [
        array.reshape(-1, KV * HD) for array in (prompt_keys, prompt_values, tail_keys, tail_values)
    ]
    direct = share == step_count and out_rows % 128 == 0 and tokens == 64 and qkv_cols % HD == 0
    if direct:
        q_blocks, new_keys, new_values = call(
            head_norm_kernel,
            "head_norm",
            (
                jax.ShapeDtypeStruct((seq_count, share, H * HD), jnp.bfloat16),
                jax.ShapeDtypeStruct((8, KV * HD), jnp.float32),
                jax.ShapeDtypeStruct((8, KV * HD), jnp.float32),
            ),
            where,
            projected,
            jnp.stack([q_gain, k_gain]),
        )
        q_got, out_blocks = tie(exchange(q_blocks, "seq"), out_blocks)
        live = jnp.repeat(live.astype(jnp.float32), step_count, axis=0)
        sent = call(
            functools.partial(block_kernel, step_count),
            "block_attention",
            jax.ShapeDtypeStruct((seq_count, tokens + 16, out_rows), jnp.bfloat16),
            where,
            q_got,
            live,
            new_keys,
            new_values,
            jnp.concatenate([caches[0], caches[2]]),
            jnp.concatenate([caches[1], caches[3]]),
        )
        got = exchange(sent, "seq")
        out_part = call(
            functools.partial(out_kernel, req_count),
            "combine_out",
            jax.ShapeDtypeStruct((seq_count, share, D), jnp.bfloat16),
            where,
            got,
            *out_blocks,
            scratch=[pltpu.VMEM((128, 128), jnp.float32)],
        )
    else:
        projected = projected.transpose(1, 0, 2).reshape(share, QKV)
        attention_cols = general_attention(
            seq_index, seq_count, rows_req, step_count, out_rows, projected, q_gain, k_gain,
            live, *caches,
        )
        out_part = jnp.concatenate(
            [jnp.dot(attention_cols, w, preferred_element_type=jnp.float32) for w in out_blocks],
            axis=1,
        )
        out_part = out_part.astype(jnp.bfloat16).reshape(seq_count, share, D)
    attn_got, pairs = tie(exchange(out_part, "seq"), pairs)
    hidden_mine = lax.dynamic_index_in_dim(
        hidden_in.reshape(seq_count, share, D), seq_index, 0, keepdims=False
    )
    ffn_blocks, residual = call(
        functools.partial(residual_kernel, req_count),
        "residual_norms",
        (
            jax.ShapeDtypeStruct((seq_count, share, D), jnp.bfloat16),
            jax.ShapeDtypeStruct((share, D), jnp.float32),
        ),
        where,
        attn_got,
        hidden_mine,
        post_attn_gain.reshape(1, D),
        ffn_gain.reshape(1, D),
    )
    held = [w_gate, w_up, w_down] + list(pairs) + list(downs)
    down_part = call(
        functools.partial(ffn_kernel, req_count),
        "feed_forward",
        jax.ShapeDtypeStruct((seq_count, share, D), jnp.bfloat16),
        where,
        exchange(ffn_blocks, "seq"),
        *held,
        scratch=[
            pltpu.VMEM((req_count, 2) + w_gate.shape, jnp.bfloat16),
            pltpu.VMEM((req_count,) + w_down.shape, jnp.bfloat16),
            pltpu.SemaphoreType.DMA((3 * req_count,)),
        ],
        hbm_from=2,
        limit=56,
    )
    layer_blocks = call(
        functools.partial(last_kernel, req_count),
        "last_norm",
        jax.ShapeDtypeStruct((seq_count, share, D), jnp.bfloat16),
        where,
        exchange(down_part, "seq"),
        residual,
        post_ffn_gain.reshape(1, D),
    )
    return exchange(layer_blocks, "seq").reshape(rows_req, step_count, D)


def solution(mesh):
    return jax.shard_map(
        functools.partial(on_device, mesh.shape["req"], mesh.shape["seq"]),
        mesh=mesh,
        in_specs=(
            P("req", None, None),
            P(),
            P(),
            P(),
            P(),
            P(),
            P(),
            P("seq", "req"),
            P("seq", "req"),
            P("req", "seq"),
            P("req", "seq"),
            P("seq", "req"),
            P("req", "seq", None),
            P("req", "seq", None),
            P("req", "seq", None),
            P("req", "seq", None),
            P("req"),
            P("req"),
            P("req"),
            P("req", None),
        ),
        out_specs=P("req", None, None),
        check_vma=False,
    )
```

```python
import functools

import jax
import jax.numpy as jnp
from jax import lax
from jax.experimental import pallas as pl
from jax.experimental.pallas import tpu as pltpu
from jax.sharding import PartitionSpec as P

D = 2048
H = 8
KV = 2
HD = 256
PAGE = 16
QKV = 3072


EPSILON = 1e-06
NEGATIVE = -1e30
LINK_SCALE = 512.0


def normalize(values):
    return values * lax.rsqrt(jnp.mean(values * values, axis=-1, keepdims=True) + EPSILON)


def split_three(values):
    high = values.astype(jnp.bfloat16)
    rest = values - high.astype(jnp.float32)
    middle = rest.astype(jnp.bfloat16)
    low = (rest - middle.astype(jnp.float32)).astype(jnp.bfloat16)
    return jnp.stack([high, middle, low])


def exchange(blocks, axes, groups=None):
    return lax.all_to_all(
        blocks, axes, split_axis=0, concat_axis=0, tiled=True, axis_index_groups=groups
    )


def tie(*arrays):
    return lax.optimization_barrier(arrays)


def spread(block, copies):
    return jnp.broadcast_to(block[None], (copies,) + block.shape)


def gather_rows(rows, count):
    return exchange(spread(rows, count), "seq").reshape(count * rows.shape[0], rows.shape[1])


def call(kernel, name, out_shape, *operands, scratch=(), hbm_from=None, limit=16):
    in_specs = [pl.BlockSpec(memory_space=pltpu.SMEM)]
    for i in range(1, len(operands)):
        space = pltpu.HBM if hbm_from is not None and i >= hbm_from else pltpu.VMEM
        in_specs.append(pl.BlockSpec(memory_space=space))
    return pl.pallas_call(
        kernel,
        name=name,
        out_shape=out_shape,
        in_specs=in_specs,
        out_specs=jax.tree.map(lambda _: pl.BlockSpec(memory_space=pltpu.VMEM), out_shape),
        scratch_shapes=scratch,
        compiler_params=pltpu.CompilerParams(vmem_limit_bytes=limit * 1024 * 1024),
    )(*operands)


def norm_columns_kernel(where_ref, hidden_ref, gain_ref, out_ref):
    columns = out_ref.shape[1]
    hidden = hidden_ref[...].astype(jnp.float32)
    scale = lax.rsqrt(jnp.mean(hidden * hidden, axis=-1, keepdims=True) + EPSILON)
    cols = pl.ds(pl.multiple_of(where_ref[0] * columns, columns), columns)
    normed = hidden_ref[:, :, cols].astype(jnp.float32) * scale * gain_ref[:, cols]
    out_ref[...] = normed.reshape(out_ref.shape).astype(jnp.bfloat16)


def head_norm_kernel(where_ref, projected_ref, gains_ref, q_ref, k_ref, v_ref):
    width = projected_ref.shape[2]
    copies, rows, _ = q_ref.shape
    fill = jnp.zeros((k_ref.shape[0] - rows, HD), jnp.float32)
    for head in range(H + 2 * KV):
        half, first = divmod(head * HD, width)
        values = normalize(projected_ref[half, :, first : first + HD])
        if head < H:
            values = (values * gains_ref[0:1, :]).astype(jnp.bfloat16)
            for i in range(copies):
                q_ref[i, :, head * HD : (head + 1) * HD] = values
        else:
            if head < H + KV:
                values = values * gains_ref[1:2, :]
            values = values.astype(jnp.bfloat16).astype(jnp.float32)
            target, slot = (k_ref, head - H) if head < H + KV else (v_ref, head - H - KV)
            target[:, slot * HD : (slot + 1) * HD] = jnp.concatenate([values, fill])


def dot_last(a, b):
    return lax.dot_general(a, b, (((1,), (1,)), ((), ())), preferred_element_type=jnp.float32)


def block_kernel(
    step_count,
    where_ref,
    q_ref,
    live_ref,
    new_k_ref,
    new_v_ref,
    keys_ref,
    values_ref,
    out_ref,
):
    copies, steps, _ = q_ref.shape
    tokens = copies * steps
    columns = out_ref.shape[2]
    group = H // KV
    queries = q_ref[...].reshape(tokens, H * HD)
    live = jnp.concatenate([live_ref[...]] * group) > 0.5
    first_token = where_ref[0] * step_count
    shape = (group * tokens, new_k_ref.shape[0])
    step = lax.broadcasted_iota(jnp.int32, shape, 0) % tokens - first_token
    new_index = lax.broadcasted_iota(jnp.int32, shape, 1)
    new_live = (step >= new_index) & (step < step_count)
    for kv in range(KV):
        span = slice(kv * HD, (kv + 1) * HD)
        q = jnp.concatenate(
            [queries[:, (kv * group + g) * HD : (kv * group + g + 1) * HD] for g in range(group)]
        )
        scores = jnp.where(live, dot_last(q, keys_ref[:, span]), NEGATIVE)
        top = jnp.max(scores, axis=1, keepdims=True)
        probs = jnp.where(live, jnp.exp(scores - top), 0.0)
        total = jnp.sum(probs, axis=1, keepdims=True)
        accum = jnp.dot(
            probs.astype(jnp.bfloat16), values_ref[:, span], preferred_element_type=jnp.float32
        )
        new_scores = dot_last(q, new_k_ref[:, span].astype(jnp.bfloat16))
        new_scores = jnp.where(new_live, new_scores, NEGATIVE)
        both = jnp.maximum(top, jnp.max(new_scores, axis=1, keepdims=True))
        carried = jnp.exp(top - both)
        new_probs = jnp.where(new_live, jnp.exp(new_scores - both), 0.0)
        total = total * carried + jnp.sum(new_probs, axis=1, keepdims=True)
        accum = accum * carried
        for u in range(step_count):
            accum = accum + new_probs[:, u : u + 1] * new_v_ref[u : u + 1, span]
        sent = accum.astype(jnp.bfloat16)
        parts = []
        for value in (both, total):
            for _ in range(3):
                part = value.astype(jnp.bfloat16).astype(jnp.float32)
                parts.append(part)
                value = value - part
        lane = lax.broadcasted_iota(jnp.int32, (group * tokens, 128), 1)
        wide = jnp.zeros((group * tokens, 128), jnp.float32)
        for i, part in enumerate(parts):
            wide = jnp.where(lane == i, part, wide)
        turned = jnp.transpose(wide)[:16].astype(jnp.bfloat16)
        for g in range(group):
            pair = turned[:, g // 2 * 128 : (g // 2 + 1) * 128]
            for part in range(HD // columns):
                target = (kv * group + g) * (HD // columns) + part
                out_ref[target, :tokens, :] = sent[
                    g * tokens : (g + 1) * tokens, part * columns : (part + 1) * columns
                ]
                out_ref[target, tokens:, :] = pair


def out_kernel(req_count, where_ref, got_ref, *refs):
    w_refs = refs[:req_count]
    out_ref, turned_ref = refs[req_count:]
    blocks = got_ref.shape[0]
    copies, steps, _ = out_ref.shape
    tokens = copies * steps
    columns = got_ref.shape[2]
    head = where_ref[0] * columns // HD
    stats = got_ref[:, tokens:, :].astype(jnp.float32)
    tops = stats[:, 0, :] + stats[:, 1, :] + stats[:, 2, :]
    totals = stats[:, 3, :] + stats[:, 4, :] + stats[:, 5, :]
    rest = jnp.zeros((128 - 2 * blocks, 128), jnp.float32)
    turned_ref[...] = jnp.transpose(jnp.concatenate([tops, totals, rest]))
    mine = turned_ref[pl.ds(pl.multiple_of(head % 2 * tokens, tokens), tokens), :]
    tops = mine[:, :blocks]
    highest = jnp.max(tops, axis=1, keepdims=True)
    weights = jnp.exp(tops - highest)
    denominator = jnp.sum(mine[:, blocks : 2 * blocks] * weights, axis=1, keepdims=True)
    numerator = jnp.zeros((tokens, columns), jnp.float32)
    for b in range(blocks):
        numerator = numerator + got_ref[b, :tokens, :].astype(jnp.float32) * weights[:, b : b + 1]
    attention = (numerator / denominator).astype(jnp.bfloat16)
    for j, w_ref in enumerate(w_refs):
        width = w_ref.shape[1]
        part = jnp.dot(attention, w_ref[...], preferred_element_type=jnp.float32)
        part = part.astype(jnp.bfloat16)
        for i in range(copies):
            out_ref[i, :, j * width : (j + 1) * width] = part[i * steps : (i + 1) * steps]


def summed(req_count, where_ref, got_ref):
    width = got_ref.shape[2] // req_count
    blocks = []
    for i in range(req_count):
        j = lax.rem(where_ref[1] - i + req_count, req_count)
        cols = pl.ds(pl.multiple_of(j * width, width), width)
        blocks.append(jnp.sum(got_ref[:, :, cols].astype(jnp.float32), axis=0))
    return jnp.concatenate(blocks, axis=1)


def residual_kernel(
    req_count, where_ref, got_ref, hidden_ref, post_gain_ref, ffn_gain_ref, out_ref, residual_ref
):
    attn_out = summed(req_count, where_ref, got_ref)
    residual = hidden_ref[...].astype(jnp.float32) + normalize(attn_out) * post_gain_ref[...]
    residual_ref[...] = residual
    ffn_in = (normalize(residual) * ffn_gain_ref[...]).astype(jnp.bfloat16)
    for i in range(out_ref.shape[0]):
        out_ref[i] = ffn_in


def last_kernel(req_count, where_ref, got_ref, residual_ref, gain_ref, out_ref):
    down_out = summed(req_count, where_ref, got_ref)
    layer = (residual_ref[...] + normalize(down_out) * gain_ref[...]).astype(jnp.bfloat16)
    for i in range(out_ref.shape[0]):
        out_ref[i] = layer


def start_copies(moves, sem_ref):
    copies = [
        pltpu.make_async_copy(source, target, sem_ref.at[i])
        for i, (source, target) in enumerate(moves)
    ]
    for copy in copies:
        copy.start()
    return copies


def gate_kernel(req_count, where_ref, x_ref, gate_ref, up_ref, *refs):
    pair_refs, (out_ref, held, sem_ref) = refs[: req_count - 1], refs[req_count - 1 :]
    rows = gate_ref.shape[0]
    moves = [(gate_ref, held.at[0, 0]), (up_ref, held.at[0, 1])]
    for j, pair_ref in enumerate(pair_refs):
        for i in range(2):
            moves.append((pair_ref.at[pl.ds(i * rows, rows), :], held.at[j + 1, i]))
    copies = start_copies(moves, sem_ref)
    blocks, steps, _ = x_ref.shape
    gate_out = up_out = None
    for j in range(req_count):
        start = lax.rem(where_ref[1] - j + req_count, req_count) * rows
        part = x_ref[:, :, pl.ds(pl.multiple_of(start, rows), rows)].reshape(blocks * steps, rows)
        copies[2 * j].wait()
        gate = jnp.dot(part, held[j, 0], preferred_element_type=jnp.float32)
        copies[2 * j + 1].wait()
        up = jnp.dot(part, held[j, 1], preferred_element_type=jnp.float32)
        gate_out = gate if j == 0 else gate_out + gate
        up_out = up if j == 0 else up_out + up
    out_ref[...] = (jax.nn.gelu(gate_out, approximate=True) * up_out).astype(jnp.bfloat16)


def down_kernel(where_ref, x_ref, *refs):
    w_refs, (out_ref, held, sem_ref) = refs[:-3], refs[-3:]
    copies = start_copies([(w, held.at[j]) for j, w in enumerate(w_refs)], sem_ref)
    blocks, steps, _ = out_ref.shape
    width = held.shape[2]
    activated = x_ref[...]
    for j, copy in enumerate(copies):
        copy.wait()
        part = jnp.dot(activated, held[j], preferred_element_type=jnp.float32)
        part = part.astype(jnp.bfloat16)
        for i in range(blocks):
            out_ref[i, :, j * width : (j + 1) * width] = part[i * steps : (i + 1) * steps]


def live_rows(
    seq_index, prompt_shape, pool_rows, group_of, prompt_lengths, tail_lengths, page_table
):
    group_count, prompt_span = prompt_shape
    rows_req = group_of.shape[0]
    member = (group_of % group_count)[:, None] == jnp.arange(group_count, dtype=jnp.int32)[None, :]
    prompt_pos = seq_index * prompt_span + jnp.arange(prompt_span, dtype=jnp.int32)
    prompt_live = prompt_pos[None, :] < prompt_lengths[:, None]
    prompt_mask = (member[:, :, None] & prompt_live[None, :, :]).reshape(
        rows_req, group_count * prompt_span
    )
    slot_count = pool_rows // PAGE
    table_row = page_table[0]
    table_len = table_row.shape[0]
    tail_pages = table_len // rows_req
    slot_ids = seq_index * slot_count + jnp.arange(slot_count, dtype=jnp.int32)
    matches = table_row[None, :] == slot_ids[:, None]
    entries = jnp.sum(
        jnp.where(matches, jnp.arange(table_len, dtype=jnp.int32)[None, :], 0), axis=1
    )
    owners = jnp.repeat(entries // tail_pages, PAGE)
    tail_pos = jnp.repeat(entries % tail_pages, PAGE) * PAGE + jnp.tile(
        jnp.arange(PAGE, dtype=jnp.int32), slot_count
    )
    tail_mask = (owners[None, :] == jnp.arange(rows_req, dtype=jnp.int32)[:, None]) & (
        tail_pos[None, :] < tail_lengths[:, None]
    )
    return jnp.concatenate([prompt_mask, tail_mask], axis=1)


def general_attention(
    seq_index,
    seq_count,
    rows_req,
    step_count,
    out_rows,
    projected,
    q_gain,
    k_gain,
    live,
    prompt_keys,
    prompt_values,
    tail_keys,
    tail_values,
):
    group_size = H // KV
    share = projected.shape[0]
    tokens = rows_req * step_count
    heads = normalize(projected.reshape(share, QKV // HD, HD))
    gains = jnp.concatenate(
        [
            jnp.broadcast_to(q_gain, (H, HD)),
            jnp.broadcast_to(k_gain, (KV, HD)),
            jnp.ones((KV, HD), jnp.float32),
        ]
    )
    mine = (heads * gains).astype(jnp.bfloat16).reshape(share, QKV)
    qkv = gather_rows(mine, seq_count)
    queries = qkv[:, : H * HD]
    keys_new = qkv[:, H * HD : (H + KV) * HD]
    values_new = qkv[:, (H + KV) * HD :]

    query_groups = queries.reshape(rows_req, step_count, KV, group_size, HD)
    mask = live[:, None, None, None, :]
    keys = jnp.concatenate([prompt_keys, tail_keys]).reshape(-1, KV, HD)
    values = jnp.concatenate([prompt_values, tail_values]).reshape(-1, KV, HD)
    scores = jnp.einsum("rskgd,pkd->rskgp", query_groups, keys, preferred_element_type=jnp.float32)
    scores = jnp.where(mask, scores, NEGATIVE)
    block_top = jnp.max(scores, axis=4)
    probs = jnp.where(mask, jnp.exp(scores - block_top[..., None]), 0.0)
    block_total = jnp.sum(probs, axis=4)
    block_accum = jnp.einsum(
        "rskgp,pkd->rskgd",
        probs.astype(jnp.bfloat16),
        values,
        preferred_element_type=jnp.float32,
    )

    stats = split_three(jnp.stack([block_top, block_total])).reshape(6, tokens, H)
    per_head = seq_count // H
    stats = jnp.repeat(stats.transpose(2, 0, 1).reshape(H, -1, out_rows), per_head, axis=0)
    accum_blocks = (
        block_accum.astype(jnp.bfloat16).reshape(tokens, seq_count, out_rows).transpose(1, 0, 2)
    )
    got = exchange(jnp.concatenate([accum_blocks, stats], axis=1), "seq")
    got_accum = got[:, :tokens].astype(jnp.float32)
    got_stats = got[:, tokens:].astype(jnp.float32).reshape(seq_count, 2 * 3, tokens)
    got_top = got_stats[:, 0] + got_stats[:, 2] + got_stats[:, 4]
    got_total = got_stats[:, 1] + got_stats[:, 3] + got_stats[:, 5]

    first_col = seq_index * out_rows
    head = first_col // HD
    kv_head = head // group_size
    head_queries = lax.dynamic_slice_in_dim(queries, head * HD, HD, 1)
    head_keys = lax.dynamic_slice_in_dim(keys_new, kv_head * HD, HD, 1)
    head_values = lax.dynamic_slice_in_dim(
        values_new, kv_head * HD + first_col % HD, out_rows, 1
    ).astype(jnp.float32)
    new_scores = jnp.dot(head_queries, head_keys.T, preferred_element_type=jnp.float32)
    token_ids = jnp.arange(tokens, dtype=jnp.int32)
    causal = (token_ids[:, None] // step_count == token_ids[None, :] // step_count) & (
        token_ids[:, None] >= token_ids[None, :]
    )
    new_scores = jnp.where(causal, new_scores, NEGATIVE)
    highest = jnp.maximum(jnp.max(got_top, axis=0), jnp.max(new_scores, axis=1))
    weights = jnp.exp(got_top - highest[None])
    new_probs = jnp.where(causal, jnp.exp(new_scores - highest[:, None]), 0.0)
    denominator = jnp.sum(got_total * weights, axis=0) + jnp.sum(new_probs, axis=1)
    numerator = jnp.sum(got_accum * weights[..., None], axis=0) + jnp.dot(
        new_probs, head_values, precision=lax.Precision.HIGHEST
    )
    return (numerator / denominator[:, None]).astype(jnp.bfloat16)


def on_device(
    req_count,
    seq_count,
    hidden_in,
    attn_gain,
    q_gain,
    k_gain,
    post_attn_gain,
    ffn_gain,
    post_ffn_gain,
    w_qkv,
    w_out,
    w_gate,
    w_up,
    w_down,
    prompt_keys,
    prompt_values,
    tail_keys,
    tail_values,
    group_of,
    prompt_lengths,
    tail_lengths,
    page_table,
):
    seq_index = lax.axis_index("seq")
    req_index = lax.axis_index("req")
    rows_req, step_count, _ = hidden_in.shape
    group_size = H // KV
    tokens = rows_req * step_count
    share = tokens // seq_count

    def shifted(values):
        return [values] + [
            lax.ppermute(values, "req", [(i, (i + j) % req_count) for i in range(req_count)])
            for j in range(1, req_count)
        ]

    where = jnp.stack([seq_index, req_index]).astype(jnp.int32)
    in_rows = w_qkv.shape[0]
    out_rows = w_out.shape[0]
    if in_rows % 128 == 0:
        normed_cols = call(
            norm_columns_kernel,
            "norm_columns",
            jax.ShapeDtypeStruct((tokens, in_rows), jnp.bfloat16),
            where,
            hidden_in,
            attn_gain.reshape(1, D),
        )
    else:
        normed = (normalize(hidden_in.astype(jnp.float32)) * attn_gain).astype(jnp.bfloat16)
        normed_cols = lax.dynamic_slice_in_dim(normed, seq_index * in_rows, in_rows, 2)
        normed_cols = normed_cols.reshape(tokens, in_rows)
    normed_all = lax.all_gather(normed_cols, "req", axis=0, tiled=True)
    out_blocks = shifted(w_out)
    pairs = shifted(jnp.concatenate([w_gate, w_up]))[1:]
    downs = shifted(w_down)[1:]

    qkv_part = jnp.dot(normed_all, w_qkv, preferred_element_type=jnp.float32)
    qkv_cols = w_qkv.shape[1]
    qkv_blocks = (
        (qkv_part * LINK_SCALE)
        .astype(jnp.float16)
        .reshape(req_count * seq_count, share, qkv_cols)
    )
    qkv_got = exchange(qkv_blocks, ("req", "seq"))
    qkv_got = qkv_got.reshape(req_count, seq_count, share, qkv_cols)
    projected = jnp.sum(qkv_got.astype(jnp.float32), axis=1) * (1.0 / LINK_SCALE)
    projected, out_blocks = tie(projected, out_blocks)
    live = live_rows(
        seq_index, prompt_keys.shape[:2], tail_keys.shape[1], group_of, prompt_lengths,
        tail_lengths, page_table,
    )
    caches = [
        array.reshape(-1, KV * HD) for array in (prompt_keys, prompt_values, tail_keys, tail_values)
    ]
    direct = share == step_count and out_rows % 128 == 0 and tokens == 64 and qkv_cols % HD == 0
    if direct:
        q_blocks, new_keys, new_values = call(
            head_norm_kernel,
            "head_norm",
            (
                jax.ShapeDtypeStruct((seq_count, share, H * HD), jnp.bfloat16),
                jax.ShapeDtypeStruct((8, KV * HD), jnp.float32),
                jax.ShapeDtypeStruct((8, KV * HD), jnp.float32),
            ),
            where,
            projected,
            jnp.stack([q_gain, k_gain]),
        )
        live = jnp.repeat(live.astype(jnp.float32), step_count, axis=0)
        sent = call(
            functools.partial(block_kernel, step_count),
            "block_attention",
            jax.ShapeDtypeStruct((seq_count, tokens + 16, out_rows), jnp.bfloat16),
            where,
            exchange(q_blocks, "seq"),
            live,
            new_keys,
            new_values,
            jnp.concatenate([caches[0], caches[2]]),
            jnp.concatenate([caches[1], caches[3]]),
        )
        got = exchange(sent, "seq")
        out_part = call(
            functools.partial(out_kernel, req_count),
            "combine_out",
            jax.ShapeDtypeStruct((seq_count, share, D), jnp.bfloat16),
            where,
            got,
            *out_blocks,
            scratch=[pltpu.VMEM((128, 128), jnp.float32)],
        )
    else:
        projected = projected.transpose(1, 0, 2).reshape(share, QKV)
        attention_cols = general_attention(
            seq_index, seq_count, rows_req, step_count, out_rows, projected, q_gain, k_gain,
            live, *caches,
        )
        out_part = jnp.concatenate(
            [jnp.dot(attention_cols, w, preferred_element_type=jnp.float32) for w in out_blocks],
            axis=1,
        )
        out_part = out_part.astype(jnp.bfloat16).reshape(seq_count, share, D)
    attn_got, pairs = tie(exchange(out_part, "seq"), pairs)
    hidden_mine = lax.dynamic_index_in_dim(
        hidden_in.reshape(seq_count, share, D), seq_index, 0, keepdims=False
    )
    ffn_blocks, residual = call(
        functools.partial(residual_kernel, req_count),
        "residual_norms",
        (
            jax.ShapeDtypeStruct((seq_count, share, D), jnp.bfloat16),
            jax.ShapeDtypeStruct((share, D), jnp.float32),
        ),
        where,
        attn_got,
        hidden_mine,
        post_attn_gain.reshape(1, D),
        ffn_gain.reshape(1, D),
    )
    activated = call(
        functools.partial(gate_kernel, req_count),
        "gate_up",
        jax.ShapeDtypeStruct((tokens, w_gate.shape[1]), jnp.bfloat16),
        where,
        exchange(ffn_blocks, "seq"),
        w_gate,
        w_up,
        *pairs,
        scratch=[
            pltpu.VMEM((req_count, 2) + w_gate.shape, jnp.bfloat16),
            pltpu.SemaphoreType.DMA((2 * req_count,)),
        ],
        hbm_from=2,
        limit=55,
    )
    down_part = call(
        down_kernel,
        "down",
        jax.ShapeDtypeStruct((seq_count, share, D), jnp.bfloat16),
        where,
        activated,
        w_down,
        *downs,
        scratch=[
            pltpu.VMEM((req_count,) + w_down.shape, jnp.bfloat16),
            pltpu.SemaphoreType.DMA((req_count,)),
        ],
        hbm_from=2,
        limit=55,
    )
    layer_blocks = call(
        functools.partial(last_kernel, req_count),
        "last_norm",
        jax.ShapeDtypeStruct((seq_count, share, D), jnp.bfloat16),
        where,
        exchange(down_part, "seq"),
        residual,
        post_ffn_gain.reshape(1, D),
    )
    return exchange(layer_blocks, "seq").reshape(rows_req, step_count, D)


def solution(mesh):
    return jax.shard_map(
        functools.partial(on_device, mesh.shape["req"], mesh.shape["seq"]),
        mesh=mesh,
        in_specs=(
            P("req", None, None),
            P(),
            P(),
            P(),
            P(),
            P(),
            P(),
            P("seq", "req"),
            P("seq", "req"),
            P("req", "seq"),
            P("req", "seq"),
            P("seq", "req"),
            P("req", "seq", None),
            P("req", "seq", None),
            P("req", "seq", None),
            P("req", "seq", None),
            P("req"),
            P("req"),
            P("req"),
            P("req", None),
        ),
        out_specs=P("req", None, None),
        check_vma=False,
    )
```

```python
import functools

import jax
import jax.numpy as jnp
from jax import lax
from jax.experimental import pallas as pl
from jax.experimental.pallas import tpu as pltpu
from jax.sharding import PartitionSpec as P

D = 2048
H = 8
KV = 2
HD = 256
PAGE = 16
QKV = 3072


EPSILON = 1e-06
NEGATIVE = -1e30
LINK_SCALE = 512.0


def normalize(values):
    return values * lax.rsqrt(jnp.mean(values * values, axis=-1, keepdims=True) + EPSILON)


def split_three(values):
    high = values.astype(jnp.bfloat16)
    rest = values - high.astype(jnp.float32)
    middle = rest.astype(jnp.bfloat16)
    low = (rest - middle.astype(jnp.float32)).astype(jnp.bfloat16)
    return jnp.stack([high, middle, low])


def exchange(blocks, axes, groups=None):
    return lax.all_to_all(
        blocks, axes, split_axis=0, concat_axis=0, tiled=True, axis_index_groups=groups
    )


def tie(*arrays):
    return lax.optimization_barrier(arrays)


def spread(block, copies):
    return jnp.broadcast_to(block[None], (copies,) + block.shape)


def gather_rows(rows, count):
    return exchange(spread(rows, count), "seq").reshape(count * rows.shape[0], rows.shape[1])


def call(kernel, name, out_shape, *operands, scratch=(), hbm_from=None, limit=16):
    in_specs = [pl.BlockSpec(memory_space=pltpu.SMEM)]
    for i in range(1, len(operands)):
        space = pltpu.HBM if hbm_from is not None and i >= hbm_from else pltpu.VMEM
        in_specs.append(pl.BlockSpec(memory_space=space))
    return pl.pallas_call(
        kernel,
        name=name,
        out_shape=out_shape,
        in_specs=in_specs,
        out_specs=jax.tree.map(lambda _: pl.BlockSpec(memory_space=pltpu.VMEM), out_shape),
        scratch_shapes=scratch,
        compiler_params=pltpu.CompilerParams(vmem_limit_bytes=limit * 1024 * 1024),
    )(*operands)


def norm_columns_kernel(where_ref, hidden_ref, gain_ref, out_ref):
    columns = out_ref.shape[1]
    hidden = hidden_ref[...].astype(jnp.float32)
    scale = lax.rsqrt(jnp.mean(hidden * hidden, axis=-1, keepdims=True) + EPSILON)
    cols = pl.ds(pl.multiple_of(where_ref[0] * columns, columns), columns)
    normed = hidden_ref[:, :, cols].astype(jnp.float32) * scale * gain_ref[:, cols]
    out_ref[...] = normed.reshape(out_ref.shape).astype(jnp.bfloat16)


def head_norm_kernel(where_ref, projected_ref, gains_ref, q_ref, k_ref, v_ref):
    width = projected_ref.shape[2]
    copies, rows, _ = q_ref.shape
    fill = jnp.zeros((k_ref.shape[0] - rows, HD), jnp.float32)
    for head in range(H + 2 * KV):
        half, first = divmod(head * HD, width)
        values = normalize(projected_ref[half, :, first : first + HD])
        if head < H:
            values = (values * gains_ref[0:1, :]).astype(jnp.bfloat16)
            for i in range(copies):
                q_ref[i, :, head * HD : (head + 1) * HD] = values
        else:
            if head < H + KV:
                values = values * gains_ref[1:2, :]
            values = values.astype(jnp.bfloat16).astype(jnp.float32)
            target, slot = (k_ref, head - H) if head < H + KV else (v_ref, head - H - KV)
            target[:, slot * HD : (slot + 1) * HD] = jnp.concatenate([values, fill])


def dot_last(a, b):
    return lax.dot_general(a, b, (((1,), (1,)), ((), ())), preferred_element_type=jnp.float32)


def block_kernel(
    step_count,
    where_ref,
    q_ref,
    live_ref,
    new_k_ref,
    new_v_ref,
    keys_ref,
    values_ref,
    out_ref,
):
    copies, steps, _ = q_ref.shape
    tokens = copies * steps
    columns = out_ref.shape[2]
    group = H // KV
    queries = q_ref[...].reshape(tokens, H * HD)
    live = jnp.concatenate([live_ref[...]] * group) > 0.5
    first_token = where_ref[0] * step_count
    shape = (group * tokens, new_k_ref.shape[0])
    step = lax.broadcasted_iota(jnp.int32, shape, 0) % tokens - first_token
    new_index = lax.broadcasted_iota(jnp.int32, shape, 1)
    new_live = (step >= new_index) & (step < step_count)
    for kv in range(KV):
        span = slice(kv * HD, (kv + 1) * HD)
        q = jnp.concatenate(
            [queries[:, (kv * group + g) * HD : (kv * group + g + 1) * HD] for g in range(group)]
        )
        scores = jnp.where(live, dot_last(q, keys_ref[:, span]), NEGATIVE)
        top = jnp.max(scores, axis=1, keepdims=True)
        probs = jnp.where(live, jnp.exp(scores - top), 0.0)
        total = jnp.sum(probs, axis=1, keepdims=True)
        accum = jnp.dot(
            probs.astype(jnp.bfloat16), values_ref[:, span], preferred_element_type=jnp.float32
        )
        new_scores = dot_last(q, new_k_ref[:, span].astype(jnp.bfloat16))
        new_scores = jnp.where(new_live, new_scores, NEGATIVE)
        both = jnp.maximum(top, jnp.max(new_scores, axis=1, keepdims=True))
        carried = jnp.exp(top - both)
        new_probs = jnp.where(new_live, jnp.exp(new_scores - both), 0.0)
        total = total * carried + jnp.sum(new_probs, axis=1, keepdims=True)
        accum = accum * carried
        for u in range(step_count):
            accum = accum + new_probs[:, u : u + 1] * new_v_ref[u : u + 1, span]
        sent = accum.astype(jnp.bfloat16)
        parts = []
        for value in (both, total):
            for _ in range(3):
                part = value.astype(jnp.bfloat16).astype(jnp.float32)
                parts.append(part)
                value = value - part
        lane = lax.broadcasted_iota(jnp.int32, (group * tokens, 128), 1)
        wide = jnp.zeros((group * tokens, 128), jnp.float32)
        for i, part in enumerate(parts):
            wide = jnp.where(lane == i, part, wide)
        turned = jnp.transpose(wide)[:16].astype(jnp.bfloat16)
        for g in range(group):
            pair = turned[:, g // 2 * 128 : (g // 2 + 1) * 128]
            for part in range(HD // columns):
                target = (kv * group + g) * (HD // columns) + part
                out_ref[target, :tokens, :] = sent[
                    g * tokens : (g + 1) * tokens, part * columns : (part + 1) * columns
                ]
                out_ref[target, tokens:, :] = pair


def out_kernel(req_count, where_ref, got_ref, *refs):
    w_refs = refs[:req_count]
    out_ref, turned_ref = refs[req_count:]
    blocks = got_ref.shape[0]
    copies, steps, _ = out_ref.shape
    tokens = copies * steps
    columns = got_ref.shape[2]
    head = where_ref[0] * columns // HD
    stats = got_ref[:, tokens:, :].astype(jnp.float32)
    tops = stats[:, 0, :] + stats[:, 1, :] + stats[:, 2, :]
    totals = stats[:, 3, :] + stats[:, 4, :] + stats[:, 5, :]
    rest = jnp.zeros((128 - 2 * blocks, 128), jnp.float32)
    turned_ref[...] = jnp.transpose(jnp.concatenate([tops, totals, rest]))
    mine = turned_ref[pl.ds(pl.multiple_of(head % 2 * tokens, tokens), tokens), :]
    tops = mine[:, :blocks]
    highest = jnp.max(tops, axis=1, keepdims=True)
    weights = jnp.exp(tops - highest)
    denominator = jnp.sum(mine[:, blocks : 2 * blocks] * weights, axis=1, keepdims=True)
    numerator = jnp.zeros((tokens, columns), jnp.float32)
    for b in range(blocks):
        numerator = numerator + got_ref[b, :tokens, :].astype(jnp.float32) * weights[:, b : b + 1]
    attention = (numerator / denominator).astype(jnp.bfloat16)
    own = w_refs[0].shape[1]
    weights = [(0, w_refs[0][...])]
    for j, w_ref in enumerate(w_refs[1:]):
        width = w_ref.shape[1]
        for piece in range(own // width):
            rows = slice(piece * columns, (piece + 1) * columns)
            weights.append(((j + 1) * own + piece * width, w_ref[rows, :]))
    for first, values in weights:
        part = jnp.dot(attention, values, preferred_element_type=jnp.float32)
        part = part.astype(jnp.bfloat16)
        for i in range(copies):
            out_ref[i, :, first : first + values.shape[1]] = part[i * steps : (i + 1) * steps]


def summed(req_count, where_ref, got_ref):
    width = got_ref.shape[2] // req_count
    blocks = []
    for i in range(req_count):
        j = lax.rem(where_ref[1] - i + req_count, req_count)
        cols = pl.ds(pl.multiple_of(j * width, width), width)
        blocks.append(jnp.sum(got_ref[:, :, cols].astype(jnp.float32), axis=0))
    return jnp.concatenate(blocks, axis=1)


def residual_kernel(
    req_count, where_ref, got_ref, hidden_ref, post_gain_ref, ffn_gain_ref, out_ref, residual_ref
):
    attn_out = summed(req_count, where_ref, got_ref)
    residual = hidden_ref[...].astype(jnp.float32) + normalize(attn_out) * post_gain_ref[...]
    residual_ref[...] = residual
    ffn_in = (normalize(residual) * ffn_gain_ref[...]).astype(jnp.bfloat16)
    for i in range(out_ref.shape[0]):
        out_ref[i] = ffn_in


def last_kernel(req_count, where_ref, got_ref, residual_ref, gain_ref, out_ref):
    down_out = summed(req_count, where_ref, got_ref)
    layer = (residual_ref[...] + normalize(down_out) * gain_ref[...]).astype(jnp.bfloat16)
    for i in range(out_ref.shape[0]):
        out_ref[i] = layer


def ffn_kernel(req_count, where_ref, x_ref, gate_ref, up_ref, down_ref, *refs):
    others = req_count - 1
    early_refs, packed_refs = refs[:others], refs[others : 2 * others]
    out_ref, pairs, downs, sem_ref = refs[2 * others :]
    rows, width = gate_ref.shape
    down_rows = down_ref.shape[0]
    piece_count = downs.shape[1]
    some = rows // 4
    copies = []

    def load(source, target):
        copies.append(pltpu.make_async_copy(source, target, sem_ref.at[len(copies)]))
        copies[-1].start()

    load(gate_ref, pairs.at[0, 0])
    load(up_ref, pairs.at[0, 1])
    for j in range(others):
        early_ref, packed_ref = early_refs[j], packed_refs[j]
        gate, up = pairs.at[j + 1, 0], pairs.at[j + 1, 1]
        load(early_ref.at[pl.ds(early_ref.shape[0] - some, some), :], gate.at[pl.ds(0, some), :])
        load(packed_ref.at[pl.ds(0, rows - some), :], gate.at[pl.ds(some, rows - some), :])
        load(packed_ref.at[pl.ds(rows - some, rows), :], up)
    for piece in range(piece_count):
        load(down_ref.at[:, pl.ds(piece * width, width)], downs.at[0, piece])
    for j in range(others):
        for piece in range(piece_count):
            first = 2 * rows - some + piece * down_rows
            load(packed_refs[j].at[pl.ds(first, down_rows), :], downs.at[j + 1, piece])
    waits = iter(copies)
    blocks, steps, _ = x_ref.shape
    tokens = blocks * steps
    gate_out = up_out = None
    for j in range(req_count):
        start = lax.rem(where_ref[1] - j + req_count, req_count) * rows
        part = x_ref[:, :, pl.ds(pl.multiple_of(start, rows), rows)].reshape(tokens, rows)
        next(waits).wait()
        if j > 0:
            next(waits).wait()
        gate = jnp.dot(part, pairs[j, 0], preferred_element_type=jnp.float32)
        next(waits).wait()
        up = jnp.dot(part, pairs[j, 1], preferred_element_type=jnp.float32)
        gate_out = gate if j == 0 else gate_out + gate
        up_out = up if j == 0 else up_out + up
    activated = (jax.nn.gelu(gate_out, approximate=True) * up_out).astype(jnp.bfloat16)
    for j in range(req_count):
        for piece in range(piece_count):
            next(waits).wait()
            part = jnp.dot(activated, downs[j, piece], preferred_element_type=jnp.float32)
            part = part.astype(jnp.bfloat16)
            first = (j * piece_count + piece) * width
            for i in range(blocks):
                out_ref[i, :, first : first + width] = part[i * steps : (i + 1) * steps]


def live_rows(
    seq_index, prompt_shape, pool_rows, group_of, prompt_lengths, tail_lengths, page_table
):
    group_count, prompt_span = prompt_shape
    rows_req = group_of.shape[0]
    member = (group_of % group_count)[:, None] == jnp.arange(group_count, dtype=jnp.int32)[None, :]
    prompt_pos = seq_index * prompt_span + jnp.arange(prompt_span, dtype=jnp.int32)
    prompt_live = prompt_pos[None, :] < prompt_lengths[:, None]
    prompt_mask = (member[:, :, None] & prompt_live[None, :, :]).reshape(
        rows_req, group_count * prompt_span
    )
    slot_count = pool_rows // PAGE
    table_row = page_table[0]
    table_len = table_row.shape[0]
    tail_pages = table_len // rows_req
    slot_ids = seq_index * slot_count + jnp.arange(slot_count, dtype=jnp.int32)
    matches = table_row[None, :] == slot_ids[:, None]
    entries = jnp.sum(
        jnp.where(matches, jnp.arange(table_len, dtype=jnp.int32)[None, :], 0), axis=1
    )
    owners = jnp.repeat(entries // tail_pages, PAGE)
    tail_pos = jnp.repeat(entries % tail_pages, PAGE) * PAGE + jnp.tile(
        jnp.arange(PAGE, dtype=jnp.int32), slot_count
    )
    tail_mask = (owners[None, :] == jnp.arange(rows_req, dtype=jnp.int32)[:, None]) & (
        tail_pos[None, :] < tail_lengths[:, None]
    )
    return jnp.concatenate([prompt_mask, tail_mask], axis=1)


def general_attention(
    seq_index,
    seq_count,
    rows_req,
    step_count,
    out_rows,
    projected,
    q_gain,
    k_gain,
    live,
    prompt_keys,
    prompt_values,
    tail_keys,
    tail_values,
):
    group_size = H // KV
    share = projected.shape[0]
    tokens = rows_req * step_count
    heads = normalize(projected.reshape(share, QKV // HD, HD))
    gains = jnp.concatenate(
        [
            jnp.broadcast_to(q_gain, (H, HD)),
            jnp.broadcast_to(k_gain, (KV, HD)),
            jnp.ones((KV, HD), jnp.float32),
        ]
    )
    mine = (heads * gains).astype(jnp.bfloat16).reshape(share, QKV)
    qkv = gather_rows(mine, seq_count)
    queries = qkv[:, : H * HD]
    keys_new = qkv[:, H * HD : (H + KV) * HD]
    values_new = qkv[:, (H + KV) * HD :]

    query_groups = queries.reshape(rows_req, step_count, KV, group_size, HD)
    mask = live[:, None, None, None, :]
    keys = jnp.concatenate([prompt_keys, tail_keys]).reshape(-1, KV, HD)
    values = jnp.concatenate([prompt_values, tail_values]).reshape(-1, KV, HD)
    scores = jnp.einsum("rskgd,pkd->rskgp", query_groups, keys, preferred_element_type=jnp.float32)
    scores = jnp.where(mask, scores, NEGATIVE)
    block_top = jnp.max(scores, axis=4)
    probs = jnp.where(mask, jnp.exp(scores - block_top[..., None]), 0.0)
    block_total = jnp.sum(probs, axis=4)
    block_accum = jnp.einsum(
        "rskgp,pkd->rskgd",
        probs.astype(jnp.bfloat16),
        values,
        preferred_element_type=jnp.float32,
    )

    stats = split_three(jnp.stack([block_top, block_total])).reshape(6, tokens, H)
    per_head = seq_count // H
    stats = jnp.repeat(stats.transpose(2, 0, 1).reshape(H, -1, out_rows), per_head, axis=0)
    accum_blocks = (
        block_accum.astype(jnp.bfloat16).reshape(tokens, seq_count, out_rows).transpose(1, 0, 2)
    )
    got = exchange(jnp.concatenate([accum_blocks, stats], axis=1), "seq")
    got_accum = got[:, :tokens].astype(jnp.float32)
    got_stats = got[:, tokens:].astype(jnp.float32).reshape(seq_count, 2 * 3, tokens)
    got_top = got_stats[:, 0] + got_stats[:, 2] + got_stats[:, 4]
    got_total = got_stats[:, 1] + got_stats[:, 3] + got_stats[:, 5]

    first_col = seq_index * out_rows
    head = first_col // HD
    kv_head = head // group_size
    head_queries = lax.dynamic_slice_in_dim(queries, head * HD, HD, 1)
    head_keys = lax.dynamic_slice_in_dim(keys_new, kv_head * HD, HD, 1)
    head_values = lax.dynamic_slice_in_dim(
        values_new, kv_head * HD + first_col % HD, out_rows, 1
    ).astype(jnp.float32)
    new_scores = jnp.dot(head_queries, head_keys.T, preferred_element_type=jnp.float32)
    token_ids = jnp.arange(tokens, dtype=jnp.int32)
    causal = (token_ids[:, None] // step_count == token_ids[None, :] // step_count) & (
        token_ids[:, None] >= token_ids[None, :]
    )
    new_scores = jnp.where(causal, new_scores, NEGATIVE)
    highest = jnp.maximum(jnp.max(got_top, axis=0), jnp.max(new_scores, axis=1))
    weights = jnp.exp(got_top - highest[None])
    new_probs = jnp.where(causal, jnp.exp(new_scores - highest[:, None]), 0.0)
    denominator = jnp.sum(got_total * weights, axis=0) + jnp.sum(new_probs, axis=1)
    numerator = jnp.sum(got_accum * weights[..., None], axis=0) + jnp.dot(
        new_probs, head_values, precision=lax.Precision.HIGHEST
    )
    return (numerator / denominator[:, None]).astype(jnp.bfloat16)


def on_device(
    req_count,
    seq_count,
    hidden_in,
    attn_gain,
    q_gain,
    k_gain,
    post_attn_gain,
    ffn_gain,
    post_ffn_gain,
    w_qkv,
    w_out,
    w_gate,
    w_up,
    w_down,
    prompt_keys,
    prompt_values,
    tail_keys,
    tail_values,
    group_of,
    prompt_lengths,
    tail_lengths,
    page_table,
):
    seq_index = lax.axis_index("seq")
    req_index = lax.axis_index("req")
    rows_req, step_count, _ = hidden_in.shape
    group_size = H // KV
    tokens = rows_req * step_count
    share = tokens // seq_count

    def shifted(values):
        return [values] + [
            lax.ppermute(values, "req", [(i, (i + j) % req_count) for i in range(req_count)])
            for j in range(1, req_count)
        ]

    where = jnp.stack([seq_index, req_index]).astype(jnp.int32)
    in_rows = w_qkv.shape[0]
    out_rows = w_out.shape[0]
    if in_rows % 128 == 0:
        normed_cols = call(
            norm_columns_kernel,
            "norm_columns",
            jax.ShapeDtypeStruct((tokens, in_rows), jnp.bfloat16),
            where,
            hidden_in,
            attn_gain.reshape(1, D),
        )
    else:
        normed = (normalize(hidden_in.astype(jnp.float32)) * attn_gain).astype(jnp.bfloat16)
        normed_cols = lax.dynamic_slice_in_dim(normed, seq_index * in_rows, in_rows, 2)
        normed_cols = normed_cols.reshape(tokens, in_rows)
    normed_all = lax.all_gather(normed_cols, "req", axis=0, tiled=True)
    width = w_gate.shape[1]
    first_rows = w_gate.shape[0] // 4

    def pieces(weights):
        return [weights[:, c : c + width] for c in range(0, weights.shape[1], width)]

    normed_all, w_out_late = tie(normed_all, w_out)
    early = shifted(jnp.concatenate(pieces(w_out_late) + [w_gate[:first_rows]]))[1:]
    packed = shifted(jnp.concatenate([w_gate[first_rows:], w_up] + pieces(w_down)))[1:]

    qkv_part = jnp.dot(normed_all, w_qkv, preferred_element_type=jnp.float32)
    qkv_cols = w_qkv.shape[1]
    qkv_blocks = (
        (qkv_part * LINK_SCALE)
        .astype(jnp.float16)
        .reshape(req_count * seq_count, share, qkv_cols)
    )
    qkv_got = exchange(qkv_blocks, ("req", "seq"))
    qkv_got = qkv_got.reshape(req_count, seq_count, share, qkv_cols)
    projected = jnp.sum(qkv_got.astype(jnp.float32), axis=1) * (1.0 / LINK_SCALE)
    live = live_rows(
        seq_index, prompt_keys.shape[:2], tail_keys.shape[1], group_of, prompt_lengths,
        tail_lengths, page_table,
    )
    caches = [
        array.reshape(-1, KV * HD) for array in (prompt_keys, prompt_values, tail_keys, tail_values)
    ]
    direct = share == step_count and out_rows % 128 == 0 and tokens == 64 and qkv_cols % HD == 0
    if direct:
        q_blocks, new_keys, new_values = call(
            head_norm_kernel,
            "head_norm",
            (
                jax.ShapeDtypeStruct((seq_count, share, H * HD), jnp.bfloat16),
                jax.ShapeDtypeStruct((8, KV * HD), jnp.float32),
                jax.ShapeDtypeStruct((8, KV * HD), jnp.float32),
            ),
            where,
            projected,
            jnp.stack([q_gain, k_gain]),
        )
        q_got, early = tie(exchange(q_blocks, "seq"), early)
        live = jnp.repeat(live.astype(jnp.float32), step_count, axis=0)
        sent = call(
            functools.partial(block_kernel, step_count),
            "block_attention",
            jax.ShapeDtypeStruct((seq_count, tokens + 16, out_rows), jnp.bfloat16),
            where,
            q_got,
            live,
            new_keys,
            new_values,
            jnp.concatenate([caches[0], caches[2]]),
            jnp.concatenate([caches[1], caches[3]]),
        )
        got = exchange(sent, "seq")
        out_part = call(
            functools.partial(out_kernel, req_count),
            "combine_out",
            jax.ShapeDtypeStruct((seq_count, share, D), jnp.bfloat16),
            where,
            got,
            w_out,
            *early,
            scratch=[pltpu.VMEM((128, 128), jnp.float32)],
        )
    else:
        projected = projected.transpose(1, 0, 2).reshape(share, QKV)
        attention_cols = general_attention(
            seq_index, seq_count, rows_req, step_count, out_rows, projected, q_gain, k_gain,
            live, *caches,
        )
        out_part = jnp.concatenate(
            [
                jnp.dot(attention_cols, w, preferred_element_type=jnp.float32)
                for w in pieces(w_out)
                + [block[i : i + out_rows] for block in early for i in range(0, out_rows * (w_out.shape[1] // width), out_rows)]
            ],
            axis=1,
        )
        out_part = out_part.astype(jnp.bfloat16).reshape(seq_count, share, D)
    hidden_mine = lax.dynamic_index_in_dim(
        hidden_in.reshape(seq_count, share, D), seq_index, 0, keepdims=False
    )
    ffn_blocks, residual = call(
        functools.partial(residual_kernel, req_count),
        "residual_norms",
        (
            jax.ShapeDtypeStruct((seq_count, share, D), jnp.bfloat16),
            jax.ShapeDtypeStruct((share, D), jnp.float32),
        ),
        where,
        exchange(out_part, "seq"),
        hidden_mine,
        post_attn_gain.reshape(1, D),
        ffn_gain.reshape(1, D),
    )
    down_part = call(
        functools.partial(ffn_kernel, req_count),
        "feed_forward",
        jax.ShapeDtypeStruct((seq_count, share, D), jnp.bfloat16),
        where,
        exchange(ffn_blocks, "seq"),
        w_gate,
        w_up,
        w_down,
        *early,
        *packed,
        scratch=[
            pltpu.VMEM((req_count, 2) + w_gate.shape, jnp.bfloat16),
            pltpu.VMEM((req_count, w_down.shape[1] // width, w_down.shape[0], width), jnp.bfloat16),
            pltpu.SemaphoreType.DMA((5 * req_count * (w_down.shape[1] // width),)),
        ],
        hbm_from=2,
        limit=56,
    )
    layer_blocks = call(
        functools.partial(last_kernel, req_count),
        "last_norm",
        jax.ShapeDtypeStruct((seq_count, share, D), jnp.bfloat16),
        where,
        exchange(down_part, "seq"),
        residual,
        post_ffn_gain.reshape(1, D),
    )
    return exchange(layer_blocks, "seq").reshape(rows_req, step_count, D)


def solution(mesh):
    return jax.shard_map(
        functools.partial(on_device, mesh.shape["req"], mesh.shape["seq"]),
        mesh=mesh,
        in_specs=(
            P("req", None, None),
            P(),
            P(),
            P(),
            P(),
            P(),
            P(),
            P("seq", "req"),
            P("seq", "req"),
            P("req", "seq"),
            P("req", "seq"),
            P("seq", "req"),
            P("req", "seq", None),
            P("req", "seq", None),
            P("req", "seq", None),
            P("req", "seq", None),
            P("req"),
            P("req"),
            P("req"),
            P("req", None),
        ),
        out_specs=P("req", None, None),
        check_vma=False,
    )
```

```python
import functools

import jax
import jax.numpy as jnp
from jax import lax
from jax.experimental import pallas as pl
from jax.experimental.pallas import tpu as pltpu
from jax.sharding import PartitionSpec as P

D = 2048
H = 8
KV = 2
HD = 256
PAGE = 16
QKV = 3072


EPSILON = 1e-06
NEGATIVE = -1e30
LINK_SCALE = 512.0


def normalize(values):
    return values * lax.rsqrt(jnp.mean(values * values, axis=-1, keepdims=True) + EPSILON)


def split_three(values):
    high = values.astype(jnp.bfloat16)
    rest = values - high.astype(jnp.float32)
    middle = rest.astype(jnp.bfloat16)
    low = (rest - middle.astype(jnp.float32)).astype(jnp.bfloat16)
    return jnp.stack([high, middle, low])


def exchange(blocks, axes, groups=None):
    return lax.all_to_all(
        blocks, axes, split_axis=0, concat_axis=0, tiled=True, axis_index_groups=groups
    )


def tie(*arrays):
    return lax.optimization_barrier(arrays)


def spread(block, copies):
    return jnp.broadcast_to(block[None], (copies,) + block.shape)


def gather_rows(rows, count):
    return exchange(spread(rows, count), "seq").reshape(count * rows.shape[0], rows.shape[1])


def call(
    kernel, name, out_shape, *operands, scratch=(), hbm_from=None, out_space=pltpu.VMEM, limit=16
):
    in_specs = [pl.BlockSpec(memory_space=pltpu.SMEM)]
    for i in range(1, len(operands)):
        space = pltpu.HBM if hbm_from is not None and i >= hbm_from else pltpu.VMEM
        in_specs.append(pl.BlockSpec(memory_space=space))
    return pl.pallas_call(
        kernel,
        name=name,
        out_shape=out_shape,
        in_specs=in_specs,
        out_specs=jax.tree.map(lambda _: pl.BlockSpec(memory_space=out_space), out_shape),
        scratch_shapes=scratch,
        compiler_params=pltpu.CompilerParams(vmem_limit_bytes=limit * 1024 * 1024),
    )(*operands)


def norm_columns_kernel(where_ref, hidden_ref, gain_ref, out_ref):
    columns = out_ref.shape[1]
    hidden = hidden_ref[...].astype(jnp.float32)
    scale = lax.rsqrt(jnp.mean(hidden * hidden, axis=-1, keepdims=True) + EPSILON)
    cols = pl.ds(pl.multiple_of(where_ref[0] * columns, columns), columns)
    normed = hidden_ref[:, :, cols].astype(jnp.float32) * scale * gain_ref[:, cols]
    out_ref[...] = normed.reshape(out_ref.shape).astype(jnp.bfloat16)


def head_norm_kernel(where_ref, projected_ref, gains_ref, q_ref, k_ref, v_ref):
    width = projected_ref.shape[2]
    copies, rows, _ = q_ref.shape
    fill = jnp.zeros((k_ref.shape[0] - rows, HD), jnp.float32)
    for head in range(H + 2 * KV):
        half, first = divmod(head * HD, width)
        values = normalize(projected_ref[half, :, first : first + HD])
        if head < H:
            values = (values * gains_ref[0:1, :]).astype(jnp.bfloat16)
            for i in range(copies):
                q_ref[i, :, head * HD : (head + 1) * HD] = values
        else:
            if head < H + KV:
                values = values * gains_ref[1:2, :]
            values = values.astype(jnp.bfloat16).astype(jnp.float32)
            target, slot = (k_ref, head - H) if head < H + KV else (v_ref, head - H - KV)
            target[:, slot * HD : (slot + 1) * HD] = jnp.concatenate([values, fill])


def dot_last(a, b):
    return lax.dot_general(a, b, (((1,), (1,)), ((), ())), preferred_element_type=jnp.float32)


def block_kernel(
    step_count,
    where_ref,
    q_ref,
    live_ref,
    new_k_ref,
    new_v_ref,
    keys_ref,
    values_ref,
    out_ref,
):
    copies, steps, _ = q_ref.shape
    tokens = copies * steps
    columns = out_ref.shape[2]
    group = H // KV
    queries = q_ref[...].reshape(tokens, H * HD)
    live = jnp.concatenate([live_ref[...]] * group) > 0.5
    first_token = where_ref[0] * step_count
    shape = (group * tokens, new_k_ref.shape[0])
    step = lax.broadcasted_iota(jnp.int32, shape, 0) % tokens - first_token
    new_index = lax.broadcasted_iota(jnp.int32, shape, 1)
    new_live = (step >= new_index) & (step < step_count)
    for kv in range(KV):
        span = slice(kv * HD, (kv + 1) * HD)
        q = jnp.concatenate(
            [queries[:, (kv * group + g) * HD : (kv * group + g + 1) * HD] for g in range(group)]
        )
        scores = jnp.where(live, dot_last(q, keys_ref[:, span]), NEGATIVE)
        top = jnp.max(scores, axis=1, keepdims=True)
        probs = jnp.where(live, jnp.exp(scores - top), 0.0)
        total = jnp.sum(probs, axis=1, keepdims=True)
        accum = jnp.dot(
            probs.astype(jnp.bfloat16), values_ref[:, span], preferred_element_type=jnp.float32
        )
        new_scores = dot_last(q, new_k_ref[:, span].astype(jnp.bfloat16))
        new_scores = jnp.where(new_live, new_scores, NEGATIVE)
        both = jnp.maximum(top, jnp.max(new_scores, axis=1, keepdims=True))
        carried = jnp.exp(top - both)
        new_probs = jnp.where(new_live, jnp.exp(new_scores - both), 0.0)
        total = total * carried + jnp.sum(new_probs, axis=1, keepdims=True)
        accum = accum * carried
        for u in range(step_count):
            accum = accum + new_probs[:, u : u + 1] * new_v_ref[u : u + 1, span]
        sent = accum.astype(jnp.bfloat16)
        parts = []
        for value in (both, total):
            for _ in range(3):
                part = value.astype(jnp.bfloat16).astype(jnp.float32)
                parts.append(part)
                value = value - part
        lane = lax.broadcasted_iota(jnp.int32, (group * tokens, 128), 1)
        wide = jnp.zeros((group * tokens, 128), jnp.float32)
        for i, part in enumerate(parts):
            wide = jnp.where(lane == i, part, wide)
        turned = jnp.transpose(wide)[:16].astype(jnp.bfloat16)
        for g in range(group):
            pair = turned[:, g // 2 * 128 : (g // 2 + 1) * 128]
            for part in range(HD // columns):
                target = (kv * group + g) * (HD // columns) + part
                out_ref[target, :tokens, :] = sent[
                    g * tokens : (g + 1) * tokens, part * columns : (part + 1) * columns
                ]
                out_ref[target, tokens:, :] = pair


def out_kernel(req_count, where_ref, got_ref, *refs):
    w_refs = refs[:req_count]
    out_ref, turned_ref = refs[req_count:]
    blocks = got_ref.shape[0]
    copies, steps, _ = out_ref.shape
    tokens = copies * steps
    columns = got_ref.shape[2]
    head = where_ref[0] * columns // HD
    stats = got_ref[:, tokens:, :].astype(jnp.float32)
    tops = stats[:, 0, :] + stats[:, 1, :] + stats[:, 2, :]
    totals = stats[:, 3, :] + stats[:, 4, :] + stats[:, 5, :]
    rest = jnp.zeros((128 - 2 * blocks, 128), jnp.float32)
    turned_ref[...] = jnp.transpose(jnp.concatenate([tops, totals, rest]))
    mine = turned_ref[pl.ds(pl.multiple_of(head % 2 * tokens, tokens), tokens), :]
    tops = mine[:, :blocks]
    highest = jnp.max(tops, axis=1, keepdims=True)
    weights = jnp.exp(tops - highest)
    denominator = jnp.sum(mine[:, blocks : 2 * blocks] * weights, axis=1, keepdims=True)
    numerator = jnp.zeros((tokens, columns), jnp.float32)
    for b in range(blocks):
        numerator = numerator + got_ref[b, :tokens, :].astype(jnp.float32) * weights[:, b : b + 1]
    attention = (numerator / denominator).astype(jnp.bfloat16)
    for j, w_ref in enumerate(w_refs):
        width = w_ref.shape[1]
        part = jnp.dot(attention, w_ref[...], preferred_element_type=jnp.float32)
        part = part.astype(jnp.bfloat16)
        for i in range(copies):
            out_ref[i, :, j * width : (j + 1) * width] = part[i * steps : (i + 1) * steps]


def summed(req_count, where_ref, got_ref):
    width = got_ref.shape[2] // req_count
    blocks = []
    for i in range(req_count):
        j = lax.rem(where_ref[1] - i + req_count, req_count)
        cols = pl.ds(pl.multiple_of(j * width, width), width)
        blocks.append(jnp.sum(got_ref[:, :, cols].astype(jnp.float32), axis=0))
    return jnp.concatenate(blocks, axis=1)


def residual_kernel(
    req_count, where_ref, got_ref, hidden_ref, post_gain_ref, ffn_gain_ref, out_ref, residual_ref
):
    attn_out = summed(req_count, where_ref, got_ref)
    residual = hidden_ref[...].astype(jnp.float32) + normalize(attn_out) * post_gain_ref[...]
    residual_ref[...] = residual
    ffn_in = (normalize(residual) * ffn_gain_ref[...]).astype(jnp.bfloat16)
    for i in range(out_ref.shape[0]):
        out_ref[i] = ffn_in


def last_kernel(req_count, where_ref, got_ref, residual_ref, gain_ref, out_ref):
    down_out = summed(req_count, where_ref, got_ref)
    layer = (residual_ref[...] + normalize(down_out) * gain_ref[...]).astype(jnp.bfloat16)
    for i in range(out_ref.shape[0]):
        out_ref[i] = layer


def ffn_kernel(req_count, where_ref, x_ref, *refs):
    count = req_count + 2
    w_refs, out_ref, x_held, parts_ref = refs[:count], *refs[count : count + 3]
    held, sem_ref = refs[count + 3 : -1], refs[-1]
    gate_rows, width = w_refs[0].shape
    down_rows, down_width = w_refs[2].shape
    load_x = pltpu.make_async_copy(x_ref, x_held, sem_ref.at[3 * req_count])
    load_x.start()
    x_ref = x_held
    copies = []

    def load(source, target):
        copies.append(pltpu.make_async_copy(source, target, sem_ref.at[len(copies)]))
        copies[-1].start()

    for i in range(3):
        load(w_refs[i], held[i])
    packed_rows = 2 * gate_rows + down_rows * (down_width // width)
    spans = [(0, gate_rows), (gate_rows, gate_rows), (2 * gate_rows, packed_rows - 2 * gate_rows)]
    for j in range(3, count):
        for first, rows in spans:
            load(w_refs[j].at[pl.ds(first, rows), :], held[j].at[pl.ds(first, rows), :])
    blocks, steps, _ = x_ref.shape
    tokens = blocks * steps
    load_x.wait()
    gate_out = up_out = None
    for j in range(req_count):
        first = lax.rem(where_ref[1] - j + req_count, req_count) * gate_rows
        cols = pl.ds(pl.multiple_of(first, gate_rows), gate_rows)
        part = x_ref[:, :, cols].reshape(tokens, gate_rows)
        copies[3 * j].wait()
        gate_w = held[0][...] if j == 0 else held[j + 2][:gate_rows, :]
        gate = jnp.dot(part, gate_w, preferred_element_type=jnp.float32)
        copies[3 * j + 1].wait()
        up_w = held[1][...] if j == 0 else held[j + 2][gate_rows : 2 * gate_rows, :]
        up = jnp.dot(part, up_w, preferred_element_type=jnp.float32)
        gate_out = gate if j == 0 else gate_out + gate
        up_out = up if j == 0 else up_out + up
    activated = (jax.nn.gelu(gate_out, approximate=True) * up_out).astype(jnp.bfloat16)
    sends = []
    for j in range(req_count):
        copies[3 * j + 2].wait()
        for piece in range(down_width // width):
            if j == 0:
                down_w = held[2][:, piece * width : (piece + 1) * width]
            else:
                row = 2 * gate_rows + piece * down_rows
                down_w = held[j + 2][row : row + down_rows, :]
            part = jnp.dot(activated, down_w, preferred_element_type=jnp.float32)
            part = part.astype(jnp.bfloat16)
            index = j * (down_width // width) + piece
            for i in range(blocks):
                parts_ref[index, i] = part[i * steps : (i + 1) * steps]
            sends.append(
                pltpu.make_async_copy(
                    parts_ref.at[index],
                    out_ref.at[:, :, pl.ds(index * width, width)],
                    sem_ref.at[3 * req_count + 1 + index],
                )
            )
            sends[-1].start()
    for send in sends:
        send.wait()


def live_rows(
    seq_index, prompt_shape, pool_rows, group_of, prompt_lengths, tail_lengths, page_table
):
    group_count, prompt_span = prompt_shape
    rows_req = group_of.shape[0]
    member = (group_of % group_count)[:, None] == jnp.arange(group_count, dtype=jnp.int32)[None, :]
    prompt_pos = seq_index * prompt_span + jnp.arange(prompt_span, dtype=jnp.int32)
    prompt_live = prompt_pos[None, :] < prompt_lengths[:, None]
    prompt_mask = (member[:, :, None] & prompt_live[None, :, :]).reshape(
        rows_req, group_count * prompt_span
    )
    slot_count = pool_rows // PAGE
    table_row = page_table[0]
    table_len = table_row.shape[0]
    tail_pages = table_len // rows_req
    slot_ids = seq_index * slot_count + jnp.arange(slot_count, dtype=jnp.int32)
    matches = table_row[None, :] == slot_ids[:, None]
    entries = jnp.sum(
        jnp.where(matches, jnp.arange(table_len, dtype=jnp.int32)[None, :], 0), axis=1
    )
    owners = jnp.repeat(entries // tail_pages, PAGE)
    tail_pos = jnp.repeat(entries % tail_pages, PAGE) * PAGE + jnp.tile(
        jnp.arange(PAGE, dtype=jnp.int32), slot_count
    )
    tail_mask = (owners[None, :] == jnp.arange(rows_req, dtype=jnp.int32)[:, None]) & (
        tail_pos[None, :] < tail_lengths[:, None]
    )
    return jnp.concatenate([prompt_mask, tail_mask], axis=1)


def general_attention(
    seq_index,
    seq_count,
    rows_req,
    step_count,
    out_rows,
    projected,
    q_gain,
    k_gain,
    live,
    prompt_keys,
    prompt_values,
    tail_keys,
    tail_values,
):
    group_size = H // KV
    share = projected.shape[0]
    tokens = rows_req * step_count
    heads = normalize(projected.reshape(share, QKV // HD, HD))
    gains = jnp.concatenate(
        [
            jnp.broadcast_to(q_gain, (H, HD)),
            jnp.broadcast_to(k_gain, (KV, HD)),
            jnp.ones((KV, HD), jnp.float32),
        ]
    )
    mine = (heads * gains).astype(jnp.bfloat16).reshape(share, QKV)
    qkv = gather_rows(mine, seq_count)
    queries = qkv[:, : H * HD]
    keys_new = qkv[:, H * HD : (H + KV) * HD]
    values_new = qkv[:, (H + KV) * HD :]

    query_groups = queries.reshape(rows_req, step_count, KV, group_size, HD)
    mask = live[:, None, None, None, :]
    keys = jnp.concatenate([prompt_keys, tail_keys]).reshape(-1, KV, HD)
    values = jnp.concatenate([prompt_values, tail_values]).reshape(-1, KV, HD)
    scores = jnp.einsum("rskgd,pkd->rskgp", query_groups, keys, preferred_element_type=jnp.float32)
    scores = jnp.where(mask, scores, NEGATIVE)
    block_top = jnp.max(scores, axis=4)
    probs = jnp.where(mask, jnp.exp(scores - block_top[..., None]), 0.0)
    block_total = jnp.sum(probs, axis=4)
    block_accum = jnp.einsum(
        "rskgp,pkd->rskgd",
        probs.astype(jnp.bfloat16),
        values,
        preferred_element_type=jnp.float32,
    )

    stats = split_three(jnp.stack([block_top, block_total])).reshape(6, tokens, H)
    per_head = seq_count // H
    stats = jnp.repeat(stats.transpose(2, 0, 1).reshape(H, -1, out_rows), per_head, axis=0)
    accum_blocks = (
        block_accum.astype(jnp.bfloat16).reshape(tokens, seq_count, out_rows).transpose(1, 0, 2)
    )
    got = exchange(jnp.concatenate([accum_blocks, stats], axis=1), "seq")
    got_accum = got[:, :tokens].astype(jnp.float32)
    got_stats = got[:, tokens:].astype(jnp.float32).reshape(seq_count, 2 * 3, tokens)
    got_top = got_stats[:, 0] + got_stats[:, 2] + got_stats[:, 4]
    got_total = got_stats[:, 1] + got_stats[:, 3] + got_stats[:, 5]

    first_col = seq_index * out_rows
    head = first_col // HD
    kv_head = head // group_size
    head_queries = lax.dynamic_slice_in_dim(queries, head * HD, HD, 1)
    head_keys = lax.dynamic_slice_in_dim(keys_new, kv_head * HD, HD, 1)
    head_values = lax.dynamic_slice_in_dim(
        values_new, kv_head * HD + first_col % HD, out_rows, 1
    ).astype(jnp.float32)
    new_scores = jnp.dot(head_queries, head_keys.T, preferred_element_type=jnp.float32)
    token_ids = jnp.arange(tokens, dtype=jnp.int32)
    causal = (token_ids[:, None] // step_count == token_ids[None, :] // step_count) & (
        token_ids[:, None] >= token_ids[None, :]
    )
    new_scores = jnp.where(causal, new_scores, NEGATIVE)
    highest = jnp.maximum(jnp.max(got_top, axis=0), jnp.max(new_scores, axis=1))
    weights = jnp.exp(got_top - highest[None])
    new_probs = jnp.where(causal, jnp.exp(new_scores - highest[:, None]), 0.0)
    denominator = jnp.sum(got_total * weights, axis=0) + jnp.sum(new_probs, axis=1)
    numerator = jnp.sum(got_accum * weights[..., None], axis=0) + jnp.dot(
        new_probs, head_values, precision=lax.Precision.HIGHEST
    )
    return (numerator / denominator[:, None]).astype(jnp.bfloat16)


def on_device(
    req_count,
    seq_count,
    hidden_in,
    attn_gain,
    q_gain,
    k_gain,
    post_attn_gain,
    ffn_gain,
    post_ffn_gain,
    w_qkv,
    w_out,
    w_gate,
    w_up,
    w_down,
    prompt_keys,
    prompt_values,
    tail_keys,
    tail_values,
    group_of,
    prompt_lengths,
    tail_lengths,
    page_table,
):
    seq_index = lax.axis_index("seq")
    req_index = lax.axis_index("req")
    rows_req, step_count, _ = hidden_in.shape
    group_size = H // KV
    tokens = rows_req * step_count
    share = tokens // seq_count

    def shifted(values):
        return [values] + [
            lax.ppermute(values, "req", [(i, (i + j) % req_count) for i in range(req_count)])
            for j in range(1, req_count)
        ]

    where = jnp.stack([seq_index, req_index]).astype(jnp.int32)
    in_rows = w_qkv.shape[0]
    out_rows = w_out.shape[0]
    if in_rows % 128 == 0:
        normed_cols = call(
            norm_columns_kernel,
            "norm_columns",
            jax.ShapeDtypeStruct((tokens, in_rows), jnp.bfloat16),
            seq_index.astype(jnp.int32).reshape(1),
            hidden_in,
            attn_gain.reshape(1, D),
            limit=56,
        )
    else:
        normed = (normalize(hidden_in.astype(jnp.float32)) * attn_gain).astype(jnp.bfloat16)
        normed_cols = lax.dynamic_slice_in_dim(normed, seq_index * in_rows, in_rows, 2)
        normed_cols = normed_cols.reshape(tokens, in_rows)
    normed_all = lax.all_gather(normed_cols, "req", axis=0, tiled=True)
    out_blocks = shifted(w_out)
    width = w_gate.shape[1]
    pieces = [w_down[:, c : c + width] for c in range(0, w_down.shape[1], width)]
    packed = shifted(jnp.concatenate([w_gate, w_up] + pieces))[1:]

    qkv_part = jnp.dot(normed_all, w_qkv, preferred_element_type=jnp.float32)
    qkv_cols = w_qkv.shape[1]
    qkv_blocks = (
        (qkv_part * LINK_SCALE)
        .astype(jnp.float16)
        .reshape(req_count * seq_count, share, qkv_cols)
    )
    qkv_got = exchange(qkv_blocks, ("req", "seq"))
    qkv_got = qkv_got.reshape(req_count, seq_count, share, qkv_cols)
    projected = jnp.sum(qkv_got.astype(jnp.float32), axis=1) * (1.0 / LINK_SCALE)
    live = live_rows(
        seq_index, prompt_keys.shape[:2], tail_keys.shape[1], group_of, prompt_lengths,
        tail_lengths, page_table,
    )
    caches = [
        array.reshape(-1, KV * HD) for array in (prompt_keys, prompt_values, tail_keys, tail_values)
    ]
    direct = share == step_count and out_rows % 128 == 0 and tokens == 64 and qkv_cols % HD == 0
    if direct:
        q_blocks, new_keys, new_values = call(
            head_norm_kernel,
            "head_norm",
            (
                jax.ShapeDtypeStruct((seq_count, share, H * HD), jnp.bfloat16),
                jax.ShapeDtypeStruct((8, KV * HD), jnp.float32),
                jax.ShapeDtypeStruct((8, KV * HD), jnp.float32),
            ),
            where,
            projected,
            jnp.stack([q_gain, k_gain]),
        )
        q_got, out_blocks = tie(exchange(q_blocks, "seq"), out_blocks)
        live = jnp.repeat(live.astype(jnp.float32), step_count, axis=0)
        sent = call(
            functools.partial(block_kernel, step_count),
            "block_attention",
            jax.ShapeDtypeStruct((seq_count, tokens + 16, out_rows), jnp.bfloat16),
            where,
            q_got,
            live,
            new_keys,
            new_values,
            jnp.concatenate([caches[0], caches[2]]),
            jnp.concatenate([caches[1], caches[3]]),
        )
        got = exchange(sent, "seq")
        out_part = call(
            functools.partial(out_kernel, req_count),
            "combine_out",
            jax.ShapeDtypeStruct((seq_count, share, D), jnp.bfloat16),
            where,
            got,
            *out_blocks,
            scratch=[pltpu.VMEM((128, 128), jnp.float32)],
        )
    else:
        projected = projected.transpose(1, 0, 2).reshape(share, QKV)
        attention_cols = general_attention(
            seq_index, seq_count, rows_req, step_count, out_rows, projected, q_gain, k_gain,
            live, *caches,
        )
        out_part = jnp.concatenate(
            [jnp.dot(attention_cols, w, preferred_element_type=jnp.float32) for w in out_blocks],
            axis=1,
        )
        out_part = out_part.astype(jnp.bfloat16).reshape(seq_count, share, D)
    hidden_mine = lax.dynamic_index_in_dim(
        hidden_in.reshape(seq_count, share, D), seq_index, 0, keepdims=False
    )
    ffn_blocks, residual = call(
        functools.partial(residual_kernel, req_count),
        "residual_norms",
        (
            jax.ShapeDtypeStruct((seq_count, share, D), jnp.bfloat16),
            jax.ShapeDtypeStruct((share, D), jnp.float32),
        ),
        where,
        exchange(out_part, "seq"),
        hidden_mine,
        post_attn_gain.reshape(1, D),
        ffn_gain.reshape(1, D),
    )
    held = [w_gate, w_up, w_down] + list(packed)
    down_part = call(
        functools.partial(ffn_kernel, req_count),
        "feed_forward",
        jax.ShapeDtypeStruct((seq_count, share, D), jnp.bfloat16),
        where,
        exchange(ffn_blocks, "seq"),
        *held,
        scratch=[
            pltpu.VMEM((seq_count, share, D), jnp.bfloat16),
            pltpu.VMEM((D // width, seq_count, share, width), jnp.bfloat16),
        ]
        + [pltpu.VMEM(w.shape, w.dtype) for w in held]
        + [pltpu.SemaphoreType.DMA((3 * req_count + 1 + D // width,))],
        hbm_from=1,
        out_space=pltpu.HBM,
        limit=56,
    )
    layer_blocks = call(
        functools.partial(last_kernel, req_count),
        "last_norm",
        jax.ShapeDtypeStruct((seq_count, share, D), jnp.bfloat16),
        where,
        exchange(down_part, "seq"),
        residual,
        post_ffn_gain.reshape(1, D),
    )
    return exchange(layer_blocks, "seq").reshape(rows_req, step_count, D)


def solution(mesh):
    return jax.shard_map(
        functools.partial(on_device, mesh.shape["req"], mesh.shape["seq"]),
        mesh=mesh,
        in_specs=(
            P("req", None, None),
            P(),
            P(),
            P(),
            P(),
            P(),
            P(),
            P("seq", "req"),
            P("seq", "req"),
            P("req", "seq"),
            P("req", "seq"),
            P("seq", "req"),
            P("req", "seq", None),
            P("req", "seq", None),
            P("req", "seq", None),
            P("req", "seq", None),
            P("req"),
            P("req"),
            P("req"),
            P("req", None),
        ),
        out_specs=P("req", None, None),
        check_vma=False,
    )
```

```python
import functools

import jax
import jax.numpy as jnp
from jax import lax
from jax.experimental import pallas as pl
from jax.experimental.pallas import tpu as pltpu
from jax.sharding import PartitionSpec as P

D = 2048
H = 8
KV = 2
HD = 256
PAGE = 16
QKV = 3072


EPSILON = 1e-06
NEGATIVE = -1e30
LINK_SCALE = 512.0


def normalize(values):
    return values * lax.rsqrt(jnp.mean(values * values, axis=-1, keepdims=True) + EPSILON)


def split_three(values):
    high = values.astype(jnp.bfloat16)
    rest = values - high.astype(jnp.float32)
    middle = rest.astype(jnp.bfloat16)
    low = (rest - middle.astype(jnp.float32)).astype(jnp.bfloat16)
    return jnp.stack([high, middle, low])


def exchange(blocks, axes, groups=None):
    return lax.all_to_all(
        blocks, axes, split_axis=0, concat_axis=0, tiled=True, axis_index_groups=groups
    )


def tie(*arrays):
    return lax.optimization_barrier(arrays)


def spread(block, copies):
    return jnp.broadcast_to(block[None], (copies,) + block.shape)


def gather_rows(rows, count):
    return exchange(spread(rows, count), "seq").reshape(count * rows.shape[0], rows.shape[1])


def call(kernel, name, out_shape, *operands, scratch=(), hbm_from=None, limit=16):
    in_specs = [pl.BlockSpec(memory_space=pltpu.SMEM)]
    for i in range(1, len(operands)):
        space = pltpu.HBM if hbm_from is not None and i >= hbm_from else pltpu.VMEM
        in_specs.append(pl.BlockSpec(memory_space=space))
    return pl.pallas_call(
        kernel,
        name=name,
        out_shape=out_shape,
        in_specs=in_specs,
        out_specs=jax.tree.map(lambda _: pl.BlockSpec(memory_space=pltpu.VMEM), out_shape),
        scratch_shapes=scratch,
        compiler_params=pltpu.CompilerParams(vmem_limit_bytes=limit * 1024 * 1024),
    )(*operands)


def norm_columns_kernel(where_ref, hidden_ref, gain_ref, out_ref):
    columns = out_ref.shape[1]
    hidden = hidden_ref[...].astype(jnp.float32)
    scale = lax.rsqrt(jnp.mean(hidden * hidden, axis=-1, keepdims=True) + EPSILON)
    cols = pl.ds(pl.multiple_of(where_ref[0] * columns, columns), columns)
    normed = hidden_ref[:, :, cols].astype(jnp.float32) * scale * gain_ref[:, cols]
    out_ref[...] = normed.reshape(out_ref.shape).astype(jnp.bfloat16)


def head_norm_kernel(where_ref, projected_ref, gains_ref, q_ref, k_ref, v_ref):
    width = projected_ref.shape[2]
    copies, rows, _ = q_ref.shape
    fill = jnp.zeros((k_ref.shape[0] - rows, HD), jnp.float32)
    for head in range(H + 2 * KV):
        half, first = divmod(head * HD, width)
        values = normalize(projected_ref[half, :, first : first + HD])
        if head < H:
            values = (values * gains_ref[0:1, :]).astype(jnp.bfloat16)
            for i in range(copies):
                q_ref[i, :, head * HD : (head + 1) * HD] = values
        else:
            if head < H + KV:
                values = values * gains_ref[1:2, :]
            values = values.astype(jnp.bfloat16).astype(jnp.float32)
            target, slot = (k_ref, head - H) if head < H + KV else (v_ref, head - H - KV)
            target[:, slot * HD : (slot + 1) * HD] = jnp.concatenate([values, fill])


def dot_last(a, b):
    return lax.dot_general(a, b, (((1,), (1,)), ((), ())), preferred_element_type=jnp.float32)


def block_kernel(
    step_count,
    where_ref,
    q_ref,
    live_ref,
    new_k_ref,
    new_v_ref,
    keys_ref,
    values_ref,
    out_ref,
):
    copies, steps, _ = q_ref.shape
    tokens = copies * steps
    columns = out_ref.shape[2]
    group = H // KV
    queries = q_ref[...].reshape(tokens, H * HD)
    live = jnp.concatenate([live_ref[...]] * group) > 0.5
    first_token = where_ref[0] * step_count
    shape = (group * tokens, new_k_ref.shape[0])
    step = lax.broadcasted_iota(jnp.int32, shape, 0) % tokens - first_token
    new_index = lax.broadcasted_iota(jnp.int32, shape, 1)
    new_live = (step >= new_index) & (step < step_count)
    for kv in range(KV):
        span = slice(kv * HD, (kv + 1) * HD)
        q = jnp.concatenate(
            [queries[:, (kv * group + g) * HD : (kv * group + g + 1) * HD] for g in range(group)]
        )
        scores = jnp.where(live, dot_last(q, keys_ref[:, span]), NEGATIVE)
        top = jnp.max(scores, axis=1, keepdims=True)
        probs = jnp.where(live, jnp.exp(scores - top), 0.0)
        total = jnp.sum(probs, axis=1, keepdims=True)
        accum = jnp.dot(
            probs.astype(jnp.bfloat16), values_ref[:, span], preferred_element_type=jnp.float32
        )
        new_scores = dot_last(q, new_k_ref[:, span].astype(jnp.bfloat16))
        new_scores = jnp.where(new_live, new_scores, NEGATIVE)
        both = jnp.maximum(top, jnp.max(new_scores, axis=1, keepdims=True))
        carried = jnp.exp(top - both)
        new_probs = jnp.where(new_live, jnp.exp(new_scores - both), 0.0)
        total = total * carried + jnp.sum(new_probs, axis=1, keepdims=True)
        accum = accum * carried
        for u in range(step_count):
            accum = accum + new_probs[:, u : u + 1] * new_v_ref[u : u + 1, span]
        sent = accum.astype(jnp.bfloat16)
        parts = []
        for value in (both, total):
            for _ in range(3):
                part = value.astype(jnp.bfloat16).astype(jnp.float32)
                parts.append(part)
                value = value - part
        lane = lax.broadcasted_iota(jnp.int32, (group * tokens, 128), 1)
        wide = jnp.zeros((group * tokens, 128), jnp.float32)
        for i, part in enumerate(parts):
            wide = jnp.where(lane == i, part, wide)
        turned = jnp.transpose(wide)[:16].astype(jnp.bfloat16)
        for g in range(group):
            pair = turned[:, g // 2 * 128 : (g // 2 + 1) * 128]
            for part in range(HD // columns):
                target = (kv * group + g) * (HD // columns) + part
                out_ref[target, :tokens, :] = sent[
                    g * tokens : (g + 1) * tokens, part * columns : (part + 1) * columns
                ]
                out_ref[target, tokens:, :] = pair


def out_kernel(req_count, where_ref, got_ref, *refs):
    w_refs = refs[:req_count]
    out_ref, turned_ref = refs[req_count:]
    blocks = got_ref.shape[0]
    copies, steps, _ = out_ref.shape
    tokens = copies * steps
    columns = got_ref.shape[2]
    head = where_ref[0] * columns // HD
    stats = got_ref[:, tokens:, :].astype(jnp.float32)
    tops = stats[:, 0, :] + stats[:, 1, :] + stats[:, 2, :]
    totals = stats[:, 3, :] + stats[:, 4, :] + stats[:, 5, :]
    rest = jnp.zeros((128 - 2 * blocks, 128), jnp.float32)
    turned_ref[...] = jnp.transpose(jnp.concatenate([tops, totals, rest]))
    mine = turned_ref[pl.ds(pl.multiple_of(head % 2 * tokens, tokens), tokens), :]
    tops = mine[:, :blocks]
    highest = jnp.max(tops, axis=1, keepdims=True)
    weights = jnp.exp(tops - highest)
    denominator = jnp.sum(mine[:, blocks : 2 * blocks] * weights, axis=1, keepdims=True)
    numerator = jnp.zeros((tokens, columns), jnp.float32)
    for b in range(blocks):
        numerator = numerator + got_ref[b, :tokens, :].astype(jnp.float32) * weights[:, b : b + 1]
    attention = (numerator / denominator).astype(jnp.bfloat16)
    own = w_refs[0].shape[1]
    weights = [(0, w_refs[0][...])]
    for j, w_ref in enumerate(w_refs[1:]):
        width = w_ref.shape[1]
        for piece in range(own // width):
            rows = slice(piece * columns, (piece + 1) * columns)
            weights.append(((j + 1) * own + piece * width, w_ref[rows, :]))
    for first, values in weights:
        part = jnp.dot(attention, values, preferred_element_type=jnp.float32)
        part = part.astype(jnp.bfloat16)
        for i in range(copies):
            out_ref[i, :, first : first + values.shape[1]] = part[i * steps : (i + 1) * steps]


def summed(req_count, where_ref, got_ref):
    width = got_ref.shape[2] // req_count
    blocks = []
    for i in range(req_count):
        j = lax.rem(where_ref[1] - i + req_count, req_count)
        cols = pl.ds(pl.multiple_of(j * width, width), width)
        blocks.append(jnp.sum(got_ref[:, :, cols].astype(jnp.float32), axis=0))
    return jnp.concatenate(blocks, axis=1)


def residual_kernel(
    req_count, where_ref, got_ref, hidden_ref, post_gain_ref, ffn_gain_ref, out_ref, residual_ref
):
    attn_out = summed(req_count, where_ref, got_ref)
    residual = hidden_ref[...].astype(jnp.float32) + normalize(attn_out) * post_gain_ref[...]
    residual_ref[...] = residual
    ffn_in = (normalize(residual) * ffn_gain_ref[...]).astype(jnp.bfloat16)
    for i in range(out_ref.shape[0]):
        out_ref[i] = ffn_in


def last_kernel(req_count, where_ref, got_ref, residual_ref, gain_ref, out_ref):
    down_out = summed(req_count, where_ref, got_ref)
    layer = (residual_ref[...] + normalize(down_out) * gain_ref[...]).astype(jnp.bfloat16)
    for i in range(out_ref.shape[0]):
        out_ref[i] = layer


def ffn_kernel(req_count, where_ref, x_ref, gate_ref, up_ref, down_ref, *refs):
    others = req_count - 1
    early_refs, packed_refs = refs[:others], refs[others : 2 * others]
    out_ref, pairs, downs, sem_ref = refs[2 * others :]
    rows, width = gate_ref.shape
    down_rows = down_ref.shape[0]
    piece_count = downs.shape[1]
    some = rows // 4
    copies = []

    def load(source, target):
        copies.append(pltpu.make_async_copy(source, target, sem_ref.at[len(copies)]))
        copies[-1].start()

    load(gate_ref, pairs.at[0, 0])
    load(up_ref, pairs.at[0, 1])
    for j in range(others):
        early_ref, packed_ref = early_refs[j], packed_refs[j]
        gate, up = pairs.at[j + 1, 0], pairs.at[j + 1, 1]
        load(early_ref.at[pl.ds(early_ref.shape[0] - some, some), :], gate.at[pl.ds(0, some), :])
        load(packed_ref.at[pl.ds(0, rows - some), :], gate.at[pl.ds(some, rows - some), :])
        load(packed_ref.at[pl.ds(rows - some, rows), :], up)
    for piece in range(piece_count):
        load(down_ref.at[:, pl.ds(piece * width, width)], downs.at[0, piece])
    for j in range(others):
        for piece in range(piece_count):
            first = 2 * rows - some + piece * down_rows
            load(packed_refs[j].at[pl.ds(first, down_rows), :], downs.at[j + 1, piece])
    waits = iter(copies)
    blocks, steps, _ = x_ref.shape
    tokens = blocks * steps
    gate_out = up_out = None
    for j in range(req_count):
        start = lax.rem(where_ref[1] - j + req_count, req_count) * rows
        part = x_ref[:, :, pl.ds(pl.multiple_of(start, rows), rows)].reshape(tokens, rows)
        next(waits).wait()
        if j > 0:
            next(waits).wait()
        gate = jnp.dot(part, pairs[j, 0], preferred_element_type=jnp.float32)
        next(waits).wait()
        up = jnp.dot(part, pairs[j, 1], preferred_element_type=jnp.float32)
        gate_out = gate if j == 0 else gate_out + gate
        up_out = up if j == 0 else up_out + up
    activated = (jax.nn.gelu(gate_out, approximate=True) * up_out).astype(jnp.bfloat16)
    for j in range(req_count):
        for piece in range(piece_count):
            next(waits).wait()
            part = jnp.dot(activated, downs[j, piece], preferred_element_type=jnp.float32)
            part = part.astype(jnp.bfloat16)
            first = (j * piece_count + piece) * width
            for i in range(blocks):
                out_ref[i, :, first : first + width] = part[i * steps : (i + 1) * steps]


def live_rows(
    seq_index, prompt_shape, pool_rows, group_of, prompt_lengths, tail_lengths, page_table
):
    group_count, prompt_span = prompt_shape
    rows_req = group_of.shape[0]
    member = (group_of % group_count)[:, None] == jnp.arange(group_count, dtype=jnp.int32)[None, :]
    prompt_pos = seq_index * prompt_span + jnp.arange(prompt_span, dtype=jnp.int32)
    prompt_live = prompt_pos[None, :] < prompt_lengths[:, None]
    prompt_mask = (member[:, :, None] & prompt_live[None, :, :]).reshape(
        rows_req, group_count * prompt_span
    )
    slot_count = pool_rows // PAGE
    table_row = page_table[0]
    table_len = table_row.shape[0]
    tail_pages = table_len // rows_req
    slot_ids = seq_index * slot_count + jnp.arange(slot_count, dtype=jnp.int32)
    matches = table_row[None, :] == slot_ids[:, None]
    entries = jnp.sum(
        jnp.where(matches, jnp.arange(table_len, dtype=jnp.int32)[None, :], 0), axis=1
    )
    owners = jnp.repeat(entries // tail_pages, PAGE)
    tail_pos = jnp.repeat(entries % tail_pages, PAGE) * PAGE + jnp.tile(
        jnp.arange(PAGE, dtype=jnp.int32), slot_count
    )
    tail_mask = (owners[None, :] == jnp.arange(rows_req, dtype=jnp.int32)[:, None]) & (
        tail_pos[None, :] < tail_lengths[:, None]
    )
    return jnp.concatenate([prompt_mask, tail_mask], axis=1)


def general_attention(
    seq_index,
    seq_count,
    rows_req,
    step_count,
    out_rows,
    projected,
    q_gain,
    k_gain,
    live,
    prompt_keys,
    prompt_values,
    tail_keys,
    tail_values,
):
    group_size = H // KV
    share = projected.shape[0]
    tokens = rows_req * step_count
    heads = normalize(projected.reshape(share, QKV // HD, HD))
    gains = jnp.concatenate(
        [
            jnp.broadcast_to(q_gain, (H, HD)),
            jnp.broadcast_to(k_gain, (KV, HD)),
            jnp.ones((KV, HD), jnp.float32),
        ]
    )
    mine = (heads * gains).astype(jnp.bfloat16).reshape(share, QKV)
    qkv = gather_rows(mine, seq_count)
    queries = qkv[:, : H * HD]
    keys_new = qkv[:, H * HD : (H + KV) * HD]
    values_new = qkv[:, (H + KV) * HD :]

    query_groups = queries.reshape(rows_req, step_count, KV, group_size, HD)
    mask = live[:, None, None, None, :]
    keys = jnp.concatenate([prompt_keys, tail_keys]).reshape(-1, KV, HD)
    values = jnp.concatenate([prompt_values, tail_values]).reshape(-1, KV, HD)
    scores = jnp.einsum("rskgd,pkd->rskgp", query_groups, keys, preferred_element_type=jnp.float32)
    scores = jnp.where(mask, scores, NEGATIVE)
    block_top = jnp.max(scores, axis=4)
    probs = jnp.where(mask, jnp.exp(scores - block_top[..., None]), 0.0)
    block_total = jnp.sum(probs, axis=4)
    block_accum = jnp.einsum(
        "rskgp,pkd->rskgd",
        probs.astype(jnp.bfloat16),
        values,
        preferred_element_type=jnp.float32,
    )

    stats = split_three(jnp.stack([block_top, block_total])).reshape(6, tokens, H)
    per_head = seq_count // H
    stats = jnp.repeat(stats.transpose(2, 0, 1).reshape(H, -1, out_rows), per_head, axis=0)
    accum_blocks = (
        block_accum.astype(jnp.bfloat16).reshape(tokens, seq_count, out_rows).transpose(1, 0, 2)
    )
    got = exchange(jnp.concatenate([accum_blocks, stats], axis=1), "seq")
    got_accum = got[:, :tokens].astype(jnp.float32)
    got_stats = got[:, tokens:].astype(jnp.float32).reshape(seq_count, 2 * 3, tokens)
    got_top = got_stats[:, 0] + got_stats[:, 2] + got_stats[:, 4]
    got_total = got_stats[:, 1] + got_stats[:, 3] + got_stats[:, 5]

    first_col = seq_index * out_rows
    head = first_col // HD
    kv_head = head // group_size
    head_queries = lax.dynamic_slice_in_dim(queries, head * HD, HD, 1)
    head_keys = lax.dynamic_slice_in_dim(keys_new, kv_head * HD, HD, 1)
    head_values = lax.dynamic_slice_in_dim(
        values_new, kv_head * HD + first_col % HD, out_rows, 1
    ).astype(jnp.float32)
    new_scores = jnp.dot(head_queries, head_keys.T, preferred_element_type=jnp.float32)
    token_ids = jnp.arange(tokens, dtype=jnp.int32)
    causal = (token_ids[:, None] // step_count == token_ids[None, :] // step_count) & (
        token_ids[:, None] >= token_ids[None, :]
    )
    new_scores = jnp.where(causal, new_scores, NEGATIVE)
    highest = jnp.maximum(jnp.max(got_top, axis=0), jnp.max(new_scores, axis=1))
    weights = jnp.exp(got_top - highest[None])
    new_probs = jnp.where(causal, jnp.exp(new_scores - highest[:, None]), 0.0)
    denominator = jnp.sum(got_total * weights, axis=0) + jnp.sum(new_probs, axis=1)
    numerator = jnp.sum(got_accum * weights[..., None], axis=0) + jnp.dot(
        new_probs, head_values, precision=lax.Precision.HIGHEST
    )
    return (numerator / denominator[:, None]).astype(jnp.bfloat16)


def on_device(
    req_count,
    seq_count,
    hidden_in,
    attn_gain,
    q_gain,
    k_gain,
    post_attn_gain,
    ffn_gain,
    post_ffn_gain,
    w_qkv,
    w_out,
    w_gate,
    w_up,
    w_down,
    prompt_keys,
    prompt_values,
    tail_keys,
    tail_values,
    group_of,
    prompt_lengths,
    tail_lengths,
    page_table,
):
    seq_index = lax.axis_index("seq")
    req_index = lax.axis_index("req")
    rows_req, step_count, _ = hidden_in.shape
    group_size = H // KV
    tokens = rows_req * step_count
    share = tokens // seq_count

    def shifted(values):
        return [values] + [
            lax.ppermute(values, "req", [(i, (i + j) % req_count) for i in range(req_count)])
            for j in range(1, req_count)
        ]

    where = jnp.stack([seq_index, req_index]).astype(jnp.int32)
    in_rows = w_qkv.shape[0]
    out_rows = w_out.shape[0]
    if in_rows % 128 == 0:
        normed_cols = call(
            norm_columns_kernel,
            "norm_columns",
            jax.ShapeDtypeStruct((tokens, in_rows), jnp.bfloat16),
            seq_index.astype(jnp.int32).reshape(1),
            hidden_in,
            attn_gain.reshape(1, D),
            limit=56,
        )
    else:
        normed = (normalize(hidden_in.astype(jnp.float32)) * attn_gain).astype(jnp.bfloat16)
        normed_cols = lax.dynamic_slice_in_dim(normed, seq_index * in_rows, in_rows, 2)
        normed_cols = normed_cols.reshape(tokens, in_rows)
    normed_all = lax.all_gather(normed_cols, "req", axis=0, tiled=True)
    width = w_gate.shape[1]
    first_rows = w_gate.shape[0] // 4

    def pieces(weights):
        return [weights[:, c : c + width] for c in range(0, weights.shape[1], width)]

    normed_all, w_out_late = tie(normed_all, w_out)
    early = shifted(jnp.concatenate(pieces(w_out_late) + [w_gate[:first_rows]]))[1:]
    packed = shifted(jnp.concatenate([w_gate[first_rows:], w_up] + pieces(w_down)))[1:]

    qkv_part = jnp.dot(normed_all, w_qkv, preferred_element_type=jnp.float32)
    qkv_cols = w_qkv.shape[1]
    qkv_blocks = (
        (qkv_part * LINK_SCALE)
        .astype(jnp.float16)
        .reshape(req_count * seq_count, share, qkv_cols)
    )
    qkv_got = exchange(qkv_blocks, ("req", "seq"))
    qkv_got = qkv_got.reshape(req_count, seq_count, share, qkv_cols)
    projected = jnp.sum(qkv_got.astype(jnp.float32), axis=1) * (1.0 / LINK_SCALE)
    projected, early = tie(projected, early)
    live = live_rows(
        seq_index, prompt_keys.shape[:2], tail_keys.shape[1], group_of, prompt_lengths,
        tail_lengths, page_table,
    )
    caches = [
        array.reshape(-1, KV * HD) for array in (prompt_keys, prompt_values, tail_keys, tail_values)
    ]
    direct = share == step_count and out_rows % 128 == 0 and tokens == 64 and qkv_cols % HD == 0
    if direct:
        q_blocks, new_keys, new_values = call(
            head_norm_kernel,
            "head_norm",
            (
                jax.ShapeDtypeStruct((seq_count, share, H * HD), jnp.bfloat16),
                jax.ShapeDtypeStruct((8, KV * HD), jnp.float32),
                jax.ShapeDtypeStruct((8, KV * HD), jnp.float32),
            ),
            where,
            projected,
            jnp.stack([q_gain, k_gain]),
        )
        live = jnp.repeat(live.astype(jnp.float32), step_count, axis=0)
        sent = call(
            functools.partial(block_kernel, step_count),
            "block_attention",
            jax.ShapeDtypeStruct((seq_count, tokens + 16, out_rows), jnp.bfloat16),
            where,
            exchange(q_blocks, "seq"),
            live,
            new_keys,
            new_values,
            jnp.concatenate([caches[0], caches[2]]),
            jnp.concatenate([caches[1], caches[3]]),
        )
        got = exchange(sent, "seq")
        out_part = call(
            functools.partial(out_kernel, req_count),
            "combine_out",
            jax.ShapeDtypeStruct((seq_count, share, D), jnp.bfloat16),
            where,
            got,
            w_out,
            *early,
            scratch=[pltpu.VMEM((128, 128), jnp.float32)],
        )
    else:
        projected = projected.transpose(1, 0, 2).reshape(share, QKV)
        attention_cols = general_attention(
            seq_index, seq_count, rows_req, step_count, out_rows, projected, q_gain, k_gain,
            live, *caches,
        )
        out_part = jnp.concatenate(
            [
                jnp.dot(attention_cols, w, preferred_element_type=jnp.float32)
                for w in pieces(w_out)
                + [block[i : i + out_rows] for block in early for i in range(0, out_rows * (w_out.shape[1] // width), out_rows)]
            ],
            axis=1,
        )
        out_part = out_part.astype(jnp.bfloat16).reshape(seq_count, share, D)
    hidden_mine = lax.dynamic_index_in_dim(
        hidden_in.reshape(seq_count, share, D), seq_index, 0, keepdims=False
    )
    ffn_blocks, residual = call(
        functools.partial(residual_kernel, req_count),
        "residual_norms",
        (
            jax.ShapeDtypeStruct((seq_count, share, D), jnp.bfloat16),
            jax.ShapeDtypeStruct((share, D), jnp.float32),
        ),
        where,
        exchange(out_part, "seq"),
        hidden_mine,
        post_attn_gain.reshape(1, D),
        ffn_gain.reshape(1, D),
    )
    down_part = call(
        functools.partial(ffn_kernel, req_count),
        "feed_forward",
        jax.ShapeDtypeStruct((seq_count, share, D), jnp.bfloat16),
        where,
        exchange(ffn_blocks, "seq"),
        w_gate,
        w_up,
        w_down,
        *early,
        *packed,
        scratch=[
            pltpu.VMEM((req_count, 2) + w_gate.shape, jnp.bfloat16),
            pltpu.VMEM((req_count, w_down.shape[1] // width, w_down.shape[0], width), jnp.bfloat16),
            pltpu.SemaphoreType.DMA((5 * req_count * (w_down.shape[1] // width),)),
        ],
        hbm_from=2,
        limit=56,
    )
    layer_blocks = call(
        functools.partial(last_kernel, req_count),
        "last_norm",
        jax.ShapeDtypeStruct((seq_count, share, D), jnp.bfloat16),
        where,
        exchange(down_part, "seq"),
        residual,
        post_ffn_gain.reshape(1, D),
    )
    return exchange(layer_blocks, "seq").reshape(rows_req, step_count, D)


def solution(mesh):
    return jax.shard_map(
        functools.partial(on_device, mesh.shape["req"], mesh.shape["seq"]),
        mesh=mesh,
        in_specs=(
            P("req", None, None),
            P(),
            P(),
            P(),
            P(),
            P(),
            P(),
            P("seq", "req"),
            P("seq", "req"),
            P("req", "seq"),
            P("req", "seq"),
            P("seq", "req"),
            P("req", "seq", None),
            P("req", "seq", None),
            P("req", "seq", None),
            P("req", "seq", None),
            P("req"),
            P("req"),
            P("req"),
            P("req", None),
        ),
        out_specs=P("req", None, None),
        check_vma=False,
    )
```

```python
import functools

import jax
import jax.numpy as jnp
from jax import lax
from jax.experimental import pallas as pl
from jax.experimental.pallas import tpu as pltpu
from jax.sharding import PartitionSpec as P

D = 2048
H = 8
KV = 2
HD = 256
PAGE = 16
QKV = 3072


EPSILON = 1e-06
NEGATIVE = -1e30
LINK_SCALE = 512.0


def normalize(values):
    return values * lax.rsqrt(jnp.mean(values * values, axis=-1, keepdims=True) + EPSILON)


def split_three(values):
    high = values.astype(jnp.bfloat16)
    rest = values - high.astype(jnp.float32)
    middle = rest.astype(jnp.bfloat16)
    low = (rest - middle.astype(jnp.float32)).astype(jnp.bfloat16)
    return jnp.stack([high, middle, low])


def exchange(blocks, axes, groups=None):
    return lax.all_to_all(
        blocks, axes, split_axis=0, concat_axis=0, tiled=True, axis_index_groups=groups
    )


def tie(*arrays):
    return lax.optimization_barrier(arrays)


def spread(block, copies):
    return jnp.broadcast_to(block[None], (copies,) + block.shape)


def gather_rows(rows, count):
    return exchange(spread(rows, count), "seq").reshape(count * rows.shape[0], rows.shape[1])


def call(
    kernel, name, out_shape, *operands, scratch=(), hbm_from=None, out_space=pltpu.VMEM, limit=16
):
    in_specs = [pl.BlockSpec(memory_space=pltpu.SMEM)]
    for i in range(1, len(operands)):
        space = pltpu.HBM if hbm_from is not None and i >= hbm_from else pltpu.VMEM
        in_specs.append(pl.BlockSpec(memory_space=space))
    return pl.pallas_call(
        kernel,
        name=name,
        out_shape=out_shape,
        in_specs=in_specs,
        out_specs=jax.tree.map(lambda _: pl.BlockSpec(memory_space=out_space), out_shape),
        scratch_shapes=scratch,
        compiler_params=pltpu.CompilerParams(vmem_limit_bytes=limit * 1024 * 1024),
    )(*operands)


def norm_columns_kernel(where_ref, hidden_ref, gain_ref, out_ref):
    columns = out_ref.shape[1]
    hidden = hidden_ref[...].astype(jnp.float32)
    scale = lax.rsqrt(jnp.mean(hidden * hidden, axis=-1, keepdims=True) + EPSILON)
    cols = pl.ds(pl.multiple_of(where_ref[0] * columns, columns), columns)
    normed = hidden_ref[:, :, cols].astype(jnp.float32) * scale * gain_ref[:, cols]
    out_ref[...] = normed.reshape(out_ref.shape).astype(jnp.bfloat16)


def head_norm_kernel(where_ref, projected_ref, gains_ref, q_ref, k_ref, v_ref):
    width = projected_ref.shape[2]
    copies, rows, _ = q_ref.shape
    fill = jnp.zeros((k_ref.shape[0] - rows, HD), jnp.float32)
    for head in range(H + 2 * KV):
        half, first = divmod(head * HD, width)
        values = normalize(projected_ref[half, :, first : first + HD])
        if head < H:
            values = (values * gains_ref[0:1, :]).astype(jnp.bfloat16)
            for i in range(copies):
                q_ref[i, :, head * HD : (head + 1) * HD] = values
        else:
            if head < H + KV:
                values = values * gains_ref[1:2, :]
            values = values.astype(jnp.bfloat16).astype(jnp.float32)
            target, slot = (k_ref, head - H) if head < H + KV else (v_ref, head - H - KV)
            target[:, slot * HD : (slot + 1) * HD] = jnp.concatenate([values, fill])


def dot_last(a, b):
    return lax.dot_general(a, b, (((1,), (1,)), ((), ())), preferred_element_type=jnp.float32)


def block_kernel(
    step_count,
    where_ref,
    q_ref,
    live_ref,
    new_k_ref,
    new_v_ref,
    keys_ref,
    values_ref,
    out_ref,
):
    copies, steps, _ = q_ref.shape
    tokens = copies * steps
    columns = out_ref.shape[2]
    group = H // KV
    queries = q_ref[...].reshape(tokens, H * HD)
    live = jnp.concatenate([live_ref[...]] * group) > 0.5
    first_token = where_ref[0] * step_count
    shape = (group * tokens, new_k_ref.shape[0])
    step = lax.broadcasted_iota(jnp.int32, shape, 0) % tokens - first_token
    new_index = lax.broadcasted_iota(jnp.int32, shape, 1)
    new_live = (step >= new_index) & (step < step_count)
    for kv in range(KV):
        span = slice(kv * HD, (kv + 1) * HD)
        q = jnp.concatenate(
            [queries[:, (kv * group + g) * HD : (kv * group + g + 1) * HD] for g in range(group)]
        )
        scores = jnp.where(live, dot_last(q, keys_ref[:, span]), NEGATIVE)
        top = jnp.max(scores, axis=1, keepdims=True)
        probs = jnp.where(live, jnp.exp(scores - top), 0.0)
        total = jnp.sum(probs, axis=1, keepdims=True)
        accum = jnp.dot(
            probs.astype(jnp.bfloat16), values_ref[:, span], preferred_element_type=jnp.float32
        )
        new_scores = dot_last(q, new_k_ref[:, span].astype(jnp.bfloat16))
        new_scores = jnp.where(new_live, new_scores, NEGATIVE)
        both = jnp.maximum(top, jnp.max(new_scores, axis=1, keepdims=True))
        carried = jnp.exp(top - both)
        new_probs = jnp.where(new_live, jnp.exp(new_scores - both), 0.0)
        total = total * carried + jnp.sum(new_probs, axis=1, keepdims=True)
        accum = accum * carried
        for u in range(step_count):
            accum = accum + new_probs[:, u : u + 1] * new_v_ref[u : u + 1, span]
        sent = accum.astype(jnp.bfloat16)
        parts = []
        for value in (both, total):
            for _ in range(3):
                part = value.astype(jnp.bfloat16).astype(jnp.float32)
                parts.append(part)
                value = value - part
        lane = lax.broadcasted_iota(jnp.int32, (group * tokens, 128), 1)
        wide = jnp.zeros((group * tokens, 128), jnp.float32)
        for i, part in enumerate(parts):
            wide = jnp.where(lane == i, part, wide)
        turned = jnp.transpose(wide)[:16].astype(jnp.bfloat16)
        for g in range(group):
            pair = turned[:, g // 2 * 128 : (g // 2 + 1) * 128]
            for part in range(HD // columns):
                target = (kv * group + g) * (HD // columns) + part
                out_ref[target, :tokens, :] = sent[
                    g * tokens : (g + 1) * tokens, part * columns : (part + 1) * columns
                ]
                out_ref[target, tokens:, :] = pair


def out_kernel(req_count, where_ref, got_ref, *refs):
    w_refs = refs[:req_count]
    out_ref, turned_ref = refs[req_count:]
    blocks = got_ref.shape[0]
    copies, steps, _ = out_ref.shape
    tokens = copies * steps
    columns = got_ref.shape[2]
    head = where_ref[0] * columns // HD
    stats = got_ref[:, tokens:, :].astype(jnp.float32)
    tops = stats[:, 0, :] + stats[:, 1, :] + stats[:, 2, :]
    totals = stats[:, 3, :] + stats[:, 4, :] + stats[:, 5, :]
    rest = jnp.zeros((128 - 2 * blocks, 128), jnp.float32)
    turned_ref[...] = jnp.transpose(jnp.concatenate([tops, totals, rest]))
    mine = turned_ref[pl.ds(pl.multiple_of(head % 2 * tokens, tokens), tokens), :]
    tops = mine[:, :blocks]
    highest = jnp.max(tops, axis=1, keepdims=True)
    weights = jnp.exp(tops - highest)
    denominator = jnp.sum(mine[:, blocks : 2 * blocks] * weights, axis=1, keepdims=True)
    numerator = jnp.zeros((tokens, columns), jnp.float32)
    for b in range(blocks):
        numerator = numerator + got_ref[b, :tokens, :].astype(jnp.float32) * weights[:, b : b + 1]
    attention = (numerator / denominator).astype(jnp.bfloat16)
    for j, w_ref in enumerate(w_refs):
        width = w_ref.shape[1]
        part = jnp.dot(attention, w_ref[...], preferred_element_type=jnp.float32)
        part = part.astype(jnp.bfloat16)
        for i in range(copies):
            out_ref[i, :, j * width : (j + 1) * width] = part[i * steps : (i + 1) * steps]


def summed(req_count, where_ref, got_ref):
    width = got_ref.shape[2] // req_count
    blocks = []
    for i in range(req_count):
        j = lax.rem(where_ref[1] - i + req_count, req_count)
        cols = pl.ds(pl.multiple_of(j * width, width), width)
        blocks.append(jnp.sum(got_ref[:, :, cols].astype(jnp.float32), axis=0))
    return jnp.concatenate(blocks, axis=1)


def residual_kernel(
    req_count, where_ref, got_ref, hidden_ref, post_gain_ref, ffn_gain_ref, out_ref, residual_ref
):
    attn_out = summed(req_count, where_ref, got_ref)
    residual = hidden_ref[...].astype(jnp.float32) + normalize(attn_out) * post_gain_ref[...]
    residual_ref[...] = residual
    ffn_in = (normalize(residual) * ffn_gain_ref[...]).astype(jnp.bfloat16)
    for i in range(out_ref.shape[0]):
        out_ref[i] = ffn_in


def last_kernel(req_count, where_ref, got_ref, residual_ref, gain_ref, out_ref):
    down_out = summed(req_count, where_ref, got_ref)
    layer = (residual_ref[...] + normalize(down_out) * gain_ref[...]).astype(jnp.bfloat16)
    for i in range(out_ref.shape[0]):
        out_ref[i] = layer


def start_copies(moves, sem_ref):
    copies = [
        pltpu.make_async_copy(source, target, sem_ref.at[i])
        for i, (source, target) in enumerate(moves)
    ]
    for copy in copies:
        copy.start()
    return copies


def own_kernel(req_count, where_ref, x_ref, gate_ref, up_ref, out_ref, x_held, held, sem_ref):
    copies = start_copies(
        [(x_ref, x_held), (gate_ref, held.at[0]), (up_ref, held.at[1])], sem_ref
    )
    rows = gate_ref.shape[0]
    blocks, steps, _ = x_held.shape
    copies[0].wait()
    start = where_ref[1] * rows
    part = x_held[:, :, pl.ds(pl.multiple_of(start, rows), rows)].reshape(blocks * steps, rows)
    for i in range(2):
        copies[i + 1].wait()
        out_ref[i] = jnp.dot(part, held[i], preferred_element_type=jnp.float32)


def ffn_kernel(req_count, gate_rows, where_ref, x_ref, own_ref, down_ref, *refs):
    others = req_count - 1
    packed_refs = refs[:others]
    out_ref, x_held, own_held, down_held, parts_ref = refs[others : others + 5]
    held, sem_ref = refs[others + 5 : -1], refs[-1]
    down_rows, down_width = down_ref.shape
    packed_rows, width = packed_refs[0].shape
    moves = [(x_ref, x_held), (own_ref, own_held)]
    spans = [(0, gate_rows), (gate_rows, gate_rows), (2 * gate_rows, packed_rows - 2 * gate_rows)]
    for j in range(others):
        for first, rows in spans:
            span = pl.ds(first, rows)
            moves.append((packed_refs[j].at[span, :], held[j].at[span, :]))
    moves.append((down_ref, down_held))
    copies = start_copies(moves, sem_ref)
    blocks, steps, _ = x_held.shape
    tokens = blocks * steps
    copies[0].wait()
    gates, ups = [], []
    for j in range(others):
        start = lax.rem(where_ref[1] - j - 1 + req_count, req_count) * gate_rows
        part = x_held[:, :, pl.ds(pl.multiple_of(start, gate_rows), gate_rows)]
        part = part.reshape(tokens, gate_rows)
        copies[3 * j + 2].wait()
        gates.append(jnp.dot(part, held[j][:gate_rows, :], preferred_element_type=jnp.float32))
        copies[3 * j + 3].wait()
        up_w = held[j][gate_rows : 2 * gate_rows, :]
        ups.append(jnp.dot(part, up_w, preferred_element_type=jnp.float32))
    copies[1].wait()
    gate_out, up_out = own_held[0], own_held[1]
    for gate, up in zip(gates, ups):
        gate_out = gate_out + gate
        up_out = up_out + up
    activated = (jax.nn.gelu(gate_out, approximate=True) * up_out).astype(jnp.bfloat16)
    sends = []
    for j in range(req_count):
        copies[-1 if j == 0 else 3 * j + 1].wait()
        for piece in range(down_width // width):
            if j == 0:
                down_w = down_held[:, piece * width : (piece + 1) * width]
            else:
                row = 2 * gate_rows + piece * down_rows
                down_w = held[j - 1][row : row + down_rows, :]
            part = jnp.dot(activated, down_w, preferred_element_type=jnp.float32)
            part = part.astype(jnp.bfloat16)
            index = j * (down_width // width) + piece
            for i in range(blocks):
                parts_ref[index, i] = part[i * steps : (i + 1) * steps]
            sends.append(
                pltpu.make_async_copy(
                    parts_ref.at[index],
                    out_ref.at[:, :, pl.ds(index * width, width)],
                    sem_ref.at[len(copies) + index],
                )
            )
            sends[-1].start()
    for send in sends:
        send.wait()


def live_rows(
    seq_index, prompt_shape, pool_rows, group_of, prompt_lengths, tail_lengths, page_table
):
    group_count, prompt_span = prompt_shape
    rows_req = group_of.shape[0]
    member = (group_of % group_count)[:, None] == jnp.arange(group_count, dtype=jnp.int32)[None, :]
    prompt_pos = seq_index * prompt_span + jnp.arange(prompt_span, dtype=jnp.int32)
    prompt_live = prompt_pos[None, :] < prompt_lengths[:, None]
    prompt_mask = (member[:, :, None] & prompt_live[None, :, :]).reshape(
        rows_req, group_count * prompt_span
    )
    slot_count = pool_rows // PAGE
    table_row = page_table[0]
    table_len = table_row.shape[0]
    tail_pages = table_len // rows_req
    slot_ids = seq_index * slot_count + jnp.arange(slot_count, dtype=jnp.int32)
    matches = table_row[None, :] == slot_ids[:, None]
    entries = jnp.sum(
        jnp.where(matches, jnp.arange(table_len, dtype=jnp.int32)[None, :], 0), axis=1
    )
    owners = jnp.repeat(entries // tail_pages, PAGE)
    tail_pos = jnp.repeat(entries % tail_pages, PAGE) * PAGE + jnp.tile(
        jnp.arange(PAGE, dtype=jnp.int32), slot_count
    )
    tail_mask = (owners[None, :] == jnp.arange(rows_req, dtype=jnp.int32)[:, None]) & (
        tail_pos[None, :] < tail_lengths[:, None]
    )
    return jnp.concatenate([prompt_mask, tail_mask], axis=1)


def general_attention(
    seq_index,
    seq_count,
    rows_req,
    step_count,
    out_rows,
    projected,
    q_gain,
    k_gain,
    live,
    prompt_keys,
    prompt_values,
    tail_keys,
    tail_values,
):
    group_size = H // KV
    share = projected.shape[0]
    tokens = rows_req * step_count
    heads = normalize(projected.reshape(share, QKV // HD, HD))
    gains = jnp.concatenate(
        [
            jnp.broadcast_to(q_gain, (H, HD)),
            jnp.broadcast_to(k_gain, (KV, HD)),
            jnp.ones((KV, HD), jnp.float32),
        ]
    )
    mine = (heads * gains).astype(jnp.bfloat16).reshape(share, QKV)
    qkv = gather_rows(mine, seq_count)
    queries = qkv[:, : H * HD]
    keys_new = qkv[:, H * HD : (H + KV) * HD]
    values_new = qkv[:, (H + KV) * HD :]

    query_groups = queries.reshape(rows_req, step_count, KV, group_size, HD)
    mask = live[:, None, None, None, :]
    keys = jnp.concatenate([prompt_keys, tail_keys]).reshape(-1, KV, HD)
    values = jnp.concatenate([prompt_values, tail_values]).reshape(-1, KV, HD)
    scores = jnp.einsum("rskgd,pkd->rskgp", query_groups, keys, preferred_element_type=jnp.float32)
    scores = jnp.where(mask, scores, NEGATIVE)
    block_top = jnp.max(scores, axis=4)
    probs = jnp.where(mask, jnp.exp(scores - block_top[..., None]), 0.0)
    block_total = jnp.sum(probs, axis=4)
    block_accum = jnp.einsum(
        "rskgp,pkd->rskgd",
        probs.astype(jnp.bfloat16),
        values,
        preferred_element_type=jnp.float32,
    )

    stats = split_three(jnp.stack([block_top, block_total])).reshape(6, tokens, H)
    per_head = seq_count // H
    stats = jnp.repeat(stats.transpose(2, 0, 1).reshape(H, -1, out_rows), per_head, axis=0)
    accum_blocks = (
        block_accum.astype(jnp.bfloat16).reshape(tokens, seq_count, out_rows).transpose(1, 0, 2)
    )
    got = exchange(jnp.concatenate([accum_blocks, stats], axis=1), "seq")
    got_accum = got[:, :tokens].astype(jnp.float32)
    got_stats = got[:, tokens:].astype(jnp.float32).reshape(seq_count, 2 * 3, tokens)
    got_top = got_stats[:, 0] + got_stats[:, 2] + got_stats[:, 4]
    got_total = got_stats[:, 1] + got_stats[:, 3] + got_stats[:, 5]

    first_col = seq_index * out_rows
    head = first_col // HD
    kv_head = head // group_size
    head_queries = lax.dynamic_slice_in_dim(queries, head * HD, HD, 1)
    head_keys = lax.dynamic_slice_in_dim(keys_new, kv_head * HD, HD, 1)
    head_values = lax.dynamic_slice_in_dim(
        values_new, kv_head * HD + first_col % HD, out_rows, 1
    ).astype(jnp.float32)
    new_scores = jnp.dot(head_queries, head_keys.T, preferred_element_type=jnp.float32)
    token_ids = jnp.arange(tokens, dtype=jnp.int32)
    causal = (token_ids[:, None] // step_count == token_ids[None, :] // step_count) & (
        token_ids[:, None] >= token_ids[None, :]
    )
    new_scores = jnp.where(causal, new_scores, NEGATIVE)
    highest = jnp.maximum(jnp.max(got_top, axis=0), jnp.max(new_scores, axis=1))
    weights = jnp.exp(got_top - highest[None])
    new_probs = jnp.where(causal, jnp.exp(new_scores - highest[:, None]), 0.0)
    denominator = jnp.sum(got_total * weights, axis=0) + jnp.sum(new_probs, axis=1)
    numerator = jnp.sum(got_accum * weights[..., None], axis=0) + jnp.dot(
        new_probs, head_values, precision=lax.Precision.HIGHEST
    )
    return (numerator / denominator[:, None]).astype(jnp.bfloat16)


def on_device(
    req_count,
    seq_count,
    hidden_in,
    attn_gain,
    q_gain,
    k_gain,
    post_attn_gain,
    ffn_gain,
    post_ffn_gain,
    w_qkv,
    w_out,
    w_gate,
    w_up,
    w_down,
    prompt_keys,
    prompt_values,
    tail_keys,
    tail_values,
    group_of,
    prompt_lengths,
    tail_lengths,
    page_table,
):
    seq_index = lax.axis_index("seq")
    req_index = lax.axis_index("req")
    rows_req, step_count, _ = hidden_in.shape
    group_size = H // KV
    tokens = rows_req * step_count
    share = tokens // seq_count

    def shifted(values):
        return [values] + [
            lax.ppermute(values, "req", [(i, (i + j) % req_count) for i in range(req_count)])
            for j in range(1, req_count)
        ]

    where = jnp.stack([seq_index, req_index]).astype(jnp.int32)
    in_rows = w_qkv.shape[0]
    out_rows = w_out.shape[0]
    if in_rows % 128 == 0:
        normed_cols = call(
            norm_columns_kernel,
            "norm_columns",
            jax.ShapeDtypeStruct((tokens, in_rows), jnp.bfloat16),
            seq_index.astype(jnp.int32).reshape(1),
            hidden_in,
            attn_gain.reshape(1, D),
            limit=56,
        )
    else:
        normed = (normalize(hidden_in.astype(jnp.float32)) * attn_gain).astype(jnp.bfloat16)
        normed_cols = lax.dynamic_slice_in_dim(normed, seq_index * in_rows, in_rows, 2)
        normed_cols = normed_cols.reshape(tokens, in_rows)
    normed_all = lax.all_gather(normed_cols, "req", axis=0, tiled=True)
    out_blocks = shifted(w_out)
    width = w_gate.shape[1]
    pieces = [w_down[:, c : c + width] for c in range(0, w_down.shape[1], width)]
    packed = shifted(jnp.concatenate([w_gate, w_up] + pieces))[1:]

    qkv_part = jnp.dot(normed_all, w_qkv, preferred_element_type=jnp.float32)
    qkv_cols = w_qkv.shape[1]
    qkv_blocks = (
        (qkv_part * LINK_SCALE)
        .astype(jnp.float16)
        .reshape(req_count * seq_count, share, qkv_cols)
    )
    qkv_got = exchange(qkv_blocks, ("req", "seq"))
    qkv_got = qkv_got.reshape(req_count, seq_count, share, qkv_cols)
    projected = jnp.sum(qkv_got.astype(jnp.float32), axis=1) * (1.0 / LINK_SCALE)
    live = live_rows(
        seq_index, prompt_keys.shape[:2], tail_keys.shape[1], group_of, prompt_lengths,
        tail_lengths, page_table,
    )
    caches = [
        array.reshape(-1, KV * HD) for array in (prompt_keys, prompt_values, tail_keys, tail_values)
    ]
    direct = share == step_count and out_rows % 128 == 0 and tokens == 64 and qkv_cols % HD == 0
    if direct:
        q_blocks, new_keys, new_values = call(
            head_norm_kernel,
            "head_norm",
            (
                jax.ShapeDtypeStruct((seq_count, share, H * HD), jnp.bfloat16),
                jax.ShapeDtypeStruct((8, KV * HD), jnp.float32),
                jax.ShapeDtypeStruct((8, KV * HD), jnp.float32),
            ),
            where,
            projected,
            jnp.stack([q_gain, k_gain]),
        )
        q_got, out_blocks = tie(exchange(q_blocks, "seq"), out_blocks)
        live = jnp.repeat(live.astype(jnp.float32), step_count, axis=0)
        sent = call(
            functools.partial(block_kernel, step_count),
            "block_attention",
            jax.ShapeDtypeStruct((seq_count, tokens + 16, out_rows), jnp.bfloat16),
            where,
            q_got,
            live,
            new_keys,
            new_values,
            jnp.concatenate([caches[0], caches[2]]),
            jnp.concatenate([caches[1], caches[3]]),
        )
        got = exchange(sent, "seq")
        out_part = call(
            functools.partial(out_kernel, req_count),
            "combine_out",
            jax.ShapeDtypeStruct((seq_count, share, D), jnp.bfloat16),
            where,
            got,
            *out_blocks,
            scratch=[pltpu.VMEM((128, 128), jnp.float32)],
        )
    else:
        projected = projected.transpose(1, 0, 2).reshape(share, QKV)
        attention_cols = general_attention(
            seq_index, seq_count, rows_req, step_count, out_rows, projected, q_gain, k_gain,
            live, *caches,
        )
        out_part = jnp.concatenate(
            [jnp.dot(attention_cols, w, preferred_element_type=jnp.float32) for w in out_blocks],
            axis=1,
        )
        out_part = out_part.astype(jnp.bfloat16).reshape(seq_count, share, D)
    hidden_mine = lax.dynamic_index_in_dim(
        hidden_in.reshape(seq_count, share, D), seq_index, 0, keepdims=False
    )
    ffn_blocks, residual = call(
        functools.partial(residual_kernel, req_count),
        "residual_norms",
        (
            jax.ShapeDtypeStruct((seq_count, share, D), jnp.bfloat16),
            jax.ShapeDtypeStruct((share, D), jnp.float32),
        ),
        where,
        exchange(out_part, "seq"),
        hidden_mine,
        post_attn_gain.reshape(1, D),
        ffn_gain.reshape(1, D),
    )
    ffn_in = exchange(ffn_blocks, "seq")
    x_space = pltpu.VMEM((seq_count, share, D), jnp.bfloat16)
    own_part = call(
        functools.partial(own_kernel, req_count),
        "own_gate_up",
        jax.ShapeDtypeStruct((2, tokens, width), jnp.float32),
        where,
        ffn_in,
        w_gate,
        w_up,
        scratch=[
            x_space,
            pltpu.VMEM((2,) + w_gate.shape, jnp.bfloat16),
            pltpu.SemaphoreType.DMA((3,)),
        ],
        hbm_from=1,
        limit=56,
    )
    down_part = call(
        functools.partial(ffn_kernel, req_count, w_gate.shape[0]),
        "feed_forward",
        jax.ShapeDtypeStruct((seq_count, share, D), jnp.bfloat16),
        where,
        ffn_in,
        own_part,
        w_down,
        *packed,
        scratch=[
            x_space,
            pltpu.VMEM((2, tokens, width), jnp.float32),
            pltpu.VMEM(w_down.shape, jnp.bfloat16),
            pltpu.VMEM((D // width, seq_count, share, width), jnp.bfloat16),
        ]
        + [pltpu.VMEM(w.shape, w.dtype) for w in packed]
        + [pltpu.SemaphoreType.DMA((3 * req_count + D // width,))],
        hbm_from=1,
        out_space=pltpu.HBM,
        limit=56,
    )
    layer_blocks = call(
        functools.partial(last_kernel, req_count),
        "last_norm",
        jax.ShapeDtypeStruct((seq_count, share, D), jnp.bfloat16),
        where,
        exchange(down_part, "seq"),
        residual,
        post_ffn_gain.reshape(1, D),
    )
    return exchange(layer_blocks, "seq").reshape(rows_req, step_count, D)


def solution(mesh):
    return jax.shard_map(
        functools.partial(on_device, mesh.shape["req"], mesh.shape["seq"]),
        mesh=mesh,
        in_specs=(
            P("req", None, None),
            P(),
            P(),
            P(),
            P(),
            P(),
            P(),
            P("seq", "req"),
            P("seq", "req"),
            P("req", "seq"),
            P("req", "seq"),
            P("seq", "req"),
            P("req", "seq", None),
            P("req", "seq", None),
            P("req", "seq", None),
            P("req", "seq", None),
            P("req"),
            P("req"),
            P("req"),
            P("req", None),
        ),
        out_specs=P("req", None, None),
        check_vma=False,
    )
```

```python
import functools

import jax
import jax.numpy as jnp
from jax import lax
from jax.experimental import pallas as pl
from jax.experimental.pallas import tpu as pltpu
from jax.sharding import PartitionSpec as P

D = 2048
H = 8
KV = 2
HD = 256
PAGE = 16
QKV = 3072


EPSILON = 1e-06
NEGATIVE = -1e30
LINK_SCALE = 512.0


def normalize(values):
    return values * lax.rsqrt(jnp.mean(values * values, axis=-1, keepdims=True) + EPSILON)


def split_three(values):
    high = values.astype(jnp.bfloat16)
    rest = values - high.astype(jnp.float32)
    middle = rest.astype(jnp.bfloat16)
    low = (rest - middle.astype(jnp.float32)).astype(jnp.bfloat16)
    return jnp.stack([high, middle, low])


def exchange(blocks, axes, groups=None):
    return lax.all_to_all(
        blocks, axes, split_axis=0, concat_axis=0, tiled=True, axis_index_groups=groups
    )


def tie(*arrays):
    return lax.optimization_barrier(arrays)


def spread(block, copies):
    return jnp.broadcast_to(block[None], (copies,) + block.shape)


def gather_rows(rows, count):
    return exchange(spread(rows, count), "seq").reshape(count * rows.shape[0], rows.shape[1])


def call(
    kernel, name, out_shape, *operands, scratch=(), hbm_from=None, out_space=pltpu.VMEM, limit=16
):
    in_specs = [pl.BlockSpec(memory_space=pltpu.SMEM)]
    for i in range(1, len(operands)):
        space = pltpu.HBM if hbm_from is not None and i >= hbm_from else pltpu.VMEM
        in_specs.append(pl.BlockSpec(memory_space=space))
    return pl.pallas_call(
        kernel,
        name=name,
        out_shape=out_shape,
        in_specs=in_specs,
        out_specs=jax.tree.map(lambda _: pl.BlockSpec(memory_space=out_space), out_shape),
        scratch_shapes=scratch,
        compiler_params=pltpu.CompilerParams(vmem_limit_bytes=limit * 1024 * 1024),
    )(*operands)


def norm_columns_kernel(where_ref, hidden_ref, gain_ref, out_ref):
    columns = out_ref.shape[1]
    hidden = hidden_ref[...].astype(jnp.float32)
    scale = lax.rsqrt(jnp.mean(hidden * hidden, axis=-1, keepdims=True) + EPSILON)
    cols = pl.ds(pl.multiple_of(where_ref[0] * columns, columns), columns)
    normed = hidden_ref[:, :, cols].astype(jnp.float32) * scale * gain_ref[:, cols]
    out_ref[...] = normed.reshape(out_ref.shape).astype(jnp.bfloat16)


def head_norm_kernel(where_ref, projected_ref, gains_ref, q_ref, k_ref, v_ref):
    width = projected_ref.shape[2]
    copies, rows, _ = q_ref.shape
    fill = jnp.zeros((k_ref.shape[0] - rows, HD), jnp.float32)
    for head in range(H + 2 * KV):
        half, first = divmod(head * HD, width)
        values = normalize(projected_ref[half, :, first : first + HD])
        if head < H:
            values = (values * gains_ref[0:1, :]).astype(jnp.bfloat16)
            for i in range(copies):
                q_ref[i, :, head * HD : (head + 1) * HD] = values
        else:
            if head < H + KV:
                values = values * gains_ref[1:2, :]
            values = values.astype(jnp.bfloat16).astype(jnp.float32)
            target, slot = (k_ref, head - H) if head < H + KV else (v_ref, head - H - KV)
            target[:, slot * HD : (slot + 1) * HD] = jnp.concatenate([values, fill])


def dot_last(a, b):
    return lax.dot_general(a, b, (((1,), (1,)), ((), ())), preferred_element_type=jnp.float32)


def block_kernel(
    step_count,
    where_ref,
    q_ref,
    live_ref,
    new_k_ref,
    new_v_ref,
    keys_ref,
    values_ref,
    out_ref,
):
    copies, steps, _ = q_ref.shape
    tokens = copies * steps
    columns = out_ref.shape[2]
    group = H // KV
    queries = q_ref[...].reshape(tokens, H * HD)
    live = jnp.concatenate([live_ref[...]] * group) > 0.5
    first_token = where_ref[0] * step_count
    shape = (group * tokens, new_k_ref.shape[0])
    step = lax.broadcasted_iota(jnp.int32, shape, 0) % tokens - first_token
    new_index = lax.broadcasted_iota(jnp.int32, shape, 1)
    new_live = (step >= new_index) & (step < step_count)
    for kv in range(KV):
        span = slice(kv * HD, (kv + 1) * HD)
        q = jnp.concatenate(
            [queries[:, (kv * group + g) * HD : (kv * group + g + 1) * HD] for g in range(group)]
        )
        scores = jnp.where(live, dot_last(q, keys_ref[:, span]), NEGATIVE)
        top = jnp.max(scores, axis=1, keepdims=True)
        probs = jnp.where(live, jnp.exp(scores - top), 0.0)
        total = jnp.sum(probs, axis=1, keepdims=True)
        accum = jnp.dot(
            probs.astype(jnp.bfloat16), values_ref[:, span], preferred_element_type=jnp.float32
        )
        new_scores = dot_last(q, new_k_ref[:, span].astype(jnp.bfloat16))
        new_scores = jnp.where(new_live, new_scores, NEGATIVE)
        both = jnp.maximum(top, jnp.max(new_scores, axis=1, keepdims=True))
        carried = jnp.exp(top - both)
        new_probs = jnp.where(new_live, jnp.exp(new_scores - both), 0.0)
        total = total * carried + jnp.sum(new_probs, axis=1, keepdims=True)
        accum = accum * carried
        for u in range(step_count):
            accum = accum + new_probs[:, u : u + 1] * new_v_ref[u : u + 1, span]
        sent = accum.astype(jnp.bfloat16)
        parts = []
        for value in (both, total):
            for _ in range(3):
                part = value.astype(jnp.bfloat16).astype(jnp.float32)
                parts.append(part)
                value = value - part
        lane = lax.broadcasted_iota(jnp.int32, (group * tokens, 128), 1)
        wide = jnp.zeros((group * tokens, 128), jnp.float32)
        for i, part in enumerate(parts):
            wide = jnp.where(lane == i, part, wide)
        turned = jnp.transpose(wide)[:16].astype(jnp.bfloat16)
        for g in range(group):
            pair = turned[:, g // 2 * 128 : (g // 2 + 1) * 128]
            for part in range(HD // columns):
                target = (kv * group + g) * (HD // columns) + part
                out_ref[target, :tokens, :] = sent[
                    g * tokens : (g + 1) * tokens, part * columns : (part + 1) * columns
                ]
                out_ref[target, tokens:, :] = pair


def out_kernel(req_count, where_ref, got_ref, *refs):
    w_refs = refs[:req_count]
    out_ref, turned_ref = refs[req_count:]
    blocks = got_ref.shape[0]
    copies, steps, _ = out_ref.shape
    tokens = copies * steps
    columns = got_ref.shape[2]
    head = where_ref[0] * columns // HD
    stats = got_ref[:, tokens:, :].astype(jnp.float32)
    tops = stats[:, 0, :] + stats[:, 1, :] + stats[:, 2, :]
    totals = stats[:, 3, :] + stats[:, 4, :] + stats[:, 5, :]
    rest = jnp.zeros((128 - 2 * blocks, 128), jnp.float32)
    turned_ref[...] = jnp.transpose(jnp.concatenate([tops, totals, rest]))
    mine = turned_ref[pl.ds(pl.multiple_of(head % 2 * tokens, tokens), tokens), :]
    tops = mine[:, :blocks]
    highest = jnp.max(tops, axis=1, keepdims=True)
    weights = jnp.exp(tops - highest)
    denominator = jnp.sum(mine[:, blocks : 2 * blocks] * weights, axis=1, keepdims=True)
    numerator = jnp.zeros((tokens, columns), jnp.float32)
    for b in range(blocks):
        numerator = numerator + got_ref[b, :tokens, :].astype(jnp.float32) * weights[:, b : b + 1]
    attention = (numerator / denominator).astype(jnp.bfloat16)
    for j, w_ref in enumerate(w_refs):
        width = w_ref.shape[1]
        part = jnp.dot(attention, w_ref[...], preferred_element_type=jnp.float32)
        part = part.astype(jnp.bfloat16)
        for i in range(copies):
            out_ref[i, :, j * width : (j + 1) * width] = part[i * steps : (i + 1) * steps]


def summed(req_count, where_ref, got_ref):
    width = got_ref.shape[2] // req_count
    blocks = []
    for i in range(req_count):
        j = lax.rem(where_ref[1] - i + req_count, req_count)
        cols = pl.ds(pl.multiple_of(j * width, width), width)
        blocks.append(jnp.sum(got_ref[:, :, cols].astype(jnp.float32), axis=0))
    return jnp.concatenate(blocks, axis=1)


def residual_kernel(
    req_count, where_ref, got_ref, hidden_ref, post_gain_ref, ffn_gain_ref, out_ref, residual_ref
):
    attn_out = summed(req_count, where_ref, got_ref)
    hidden = hidden_ref[where_ref[0]].astype(jnp.float32)
    residual = hidden + normalize(attn_out) * post_gain_ref[...]
    residual_ref[...] = residual
    ffn_in = (normalize(residual) * ffn_gain_ref[...]).astype(jnp.bfloat16)
    for i in range(out_ref.shape[0]):
        out_ref[i] = ffn_in


def last_kernel(req_count, where_ref, got_ref, residual_ref, gain_ref, out_ref):
    down_out = summed(req_count, where_ref, got_ref)
    layer = (residual_ref[...] + normalize(down_out) * gain_ref[...]).astype(jnp.bfloat16)
    for i in range(out_ref.shape[0]):
        out_ref[i] = layer


def start_copies(moves, sem_ref):
    copies = [
        pltpu.make_async_copy(source, target, sem_ref.at[i])
        for i, (source, target) in enumerate(moves)
    ]
    for copy in copies:
        copy.start()
    return copies


def own_kernel(req_count, where_ref, x_ref, gate_ref, up_ref, out_ref, x_held, held, sem_ref):
    copies = start_copies(
        [(x_ref, x_held), (gate_ref, held.at[0]), (up_ref, held.at[1])], sem_ref
    )
    rows = gate_ref.shape[0]
    blocks, steps, _ = x_held.shape
    copies[0].wait()
    start = where_ref[1] * rows
    part = x_held[:, :, pl.ds(pl.multiple_of(start, rows), rows)].reshape(blocks * steps, rows)
    for i in range(2):
        copies[i + 1].wait()
        out_ref[i] = jnp.dot(part, held[i], preferred_element_type=jnp.float32)


def ffn_kernel(req_count, gate_rows, where_ref, x_ref, own_ref, down_ref, *refs):
    others = req_count - 1
    packed_refs = refs[:others]
    out_ref, x_held, own_held, down_held, parts_ref = refs[others : others + 5]
    held, sem_ref = refs[others + 5 : -1], refs[-1]
    down_rows, down_width = down_ref.shape
    packed_rows, width = packed_refs[0].shape
    moves = [(x_ref, x_held), (own_ref, own_held)]
    spans = [(0, gate_rows), (gate_rows, gate_rows), (2 * gate_rows, packed_rows - 2 * gate_rows)]
    for j in range(others):
        for first, rows in spans:
            span = pl.ds(first, rows)
            moves.append((packed_refs[j].at[span, :], held[j].at[span, :]))
    moves.append((down_ref, down_held))
    copies = start_copies(moves, sem_ref)
    blocks, steps, _ = x_held.shape
    tokens = blocks * steps
    copies[0].wait()
    gates, ups = [], []
    for j in range(others):
        start = lax.rem(where_ref[1] - j - 1 + req_count, req_count) * gate_rows
        part = x_held[:, :, pl.ds(pl.multiple_of(start, gate_rows), gate_rows)]
        part = part.reshape(tokens, gate_rows)
        copies[3 * j + 2].wait()
        gates.append(jnp.dot(part, held[j][:gate_rows, :], preferred_element_type=jnp.float32))
        copies[3 * j + 3].wait()
        up_w = held[j][gate_rows : 2 * gate_rows, :]
        ups.append(jnp.dot(part, up_w, preferred_element_type=jnp.float32))
    copies[1].wait()
    gate_out, up_out = own_held[0], own_held[1]
    for gate, up in zip(gates, ups):
        gate_out = gate_out + gate
        up_out = up_out + up
    activated = (jax.nn.gelu(gate_out, approximate=True) * up_out).astype(jnp.bfloat16)
    sends = []
    for j in range(req_count):
        copies[-1 if j == 0 else 3 * j + 1].wait()
        for piece in range(down_width // width):
            if j == 0:
                down_w = down_held[:, piece * width : (piece + 1) * width]
            else:
                row = 2 * gate_rows + piece * down_rows
                down_w = held[j - 1][row : row + down_rows, :]
            part = jnp.dot(activated, down_w, preferred_element_type=jnp.float32)
            part = part.astype(jnp.bfloat16)
            index = j * (down_width // width) + piece
            for i in range(blocks):
                parts_ref[index, i] = part[i * steps : (i + 1) * steps]
            sends.append(
                pltpu.make_async_copy(
                    parts_ref.at[index],
                    out_ref.at[:, :, pl.ds(index * width, width)],
                    sem_ref.at[len(copies) + index],
                )
            )
            sends[-1].start()
    for send in sends:
        send.wait()


def live_rows(
    seq_index, prompt_shape, pool_rows, group_of, prompt_lengths, tail_lengths, page_table
):
    group_count, prompt_span = prompt_shape
    rows_req = group_of.shape[0]
    member = (group_of % group_count)[:, None] == jnp.arange(group_count, dtype=jnp.int32)[None, :]
    prompt_pos = seq_index * prompt_span + jnp.arange(prompt_span, dtype=jnp.int32)
    prompt_live = prompt_pos[None, :] < prompt_lengths[:, None]
    prompt_mask = (member[:, :, None] & prompt_live[None, :, :]).reshape(
        rows_req, group_count * prompt_span
    )
    slot_count = pool_rows // PAGE
    table_row = page_table[0]
    table_len = table_row.shape[0]
    tail_pages = table_len // rows_req
    slot_ids = seq_index * slot_count + jnp.arange(slot_count, dtype=jnp.int32)
    matches = table_row[None, :] == slot_ids[:, None]
    entries = jnp.sum(
        jnp.where(matches, jnp.arange(table_len, dtype=jnp.int32)[None, :], 0), axis=1
    )
    owners = jnp.repeat(entries // tail_pages, PAGE)
    tail_pos = jnp.repeat(entries % tail_pages, PAGE) * PAGE + jnp.tile(
        jnp.arange(PAGE, dtype=jnp.int32), slot_count
    )
    tail_mask = (owners[None, :] == jnp.arange(rows_req, dtype=jnp.int32)[:, None]) & (
        tail_pos[None, :] < tail_lengths[:, None]
    )
    return jnp.concatenate([prompt_mask, tail_mask], axis=1)


def general_attention(
    seq_index,
    seq_count,
    rows_req,
    step_count,
    out_rows,
    projected,
    q_gain,
    k_gain,
    live,
    prompt_keys,
    prompt_values,
    tail_keys,
    tail_values,
):
    group_size = H // KV
    share = projected.shape[0]
    tokens = rows_req * step_count
    heads = normalize(projected.reshape(share, QKV // HD, HD))
    gains = jnp.concatenate(
        [
            jnp.broadcast_to(q_gain, (H, HD)),
            jnp.broadcast_to(k_gain, (KV, HD)),
            jnp.ones((KV, HD), jnp.float32),
        ]
    )
    mine = (heads * gains).astype(jnp.bfloat16).reshape(share, QKV)
    qkv = gather_rows(mine, seq_count)
    queries = qkv[:, : H * HD]
    keys_new = qkv[:, H * HD : (H + KV) * HD]
    values_new = qkv[:, (H + KV) * HD :]

    query_groups = queries.reshape(rows_req, step_count, KV, group_size, HD)
    mask = live[:, None, None, None, :]
    keys = jnp.concatenate([prompt_keys, tail_keys]).reshape(-1, KV, HD)
    values = jnp.concatenate([prompt_values, tail_values]).reshape(-1, KV, HD)
    scores = jnp.einsum("rskgd,pkd->rskgp", query_groups, keys, preferred_element_type=jnp.float32)
    scores = jnp.where(mask, scores, NEGATIVE)
    block_top = jnp.max(scores, axis=4)
    probs = jnp.where(mask, jnp.exp(scores - block_top[..., None]), 0.0)
    block_total = jnp.sum(probs, axis=4)
    block_accum = jnp.einsum(
        "rskgp,pkd->rskgd",
        probs.astype(jnp.bfloat16),
        values,
        preferred_element_type=jnp.float32,
    )

    stats = split_three(jnp.stack([block_top, block_total])).reshape(6, tokens, H)
    per_head = seq_count // H
    stats = jnp.repeat(stats.transpose(2, 0, 1).reshape(H, -1, out_rows), per_head, axis=0)
    accum_blocks = (
        block_accum.astype(jnp.bfloat16).reshape(tokens, seq_count, out_rows).transpose(1, 0, 2)
    )
    got = exchange(jnp.concatenate([accum_blocks, stats], axis=1), "seq")
    got_accum = got[:, :tokens].astype(jnp.float32)
    got_stats = got[:, tokens:].astype(jnp.float32).reshape(seq_count, 2 * 3, tokens)
    got_top = got_stats[:, 0] + got_stats[:, 2] + got_stats[:, 4]
    got_total = got_stats[:, 1] + got_stats[:, 3] + got_stats[:, 5]

    first_col = seq_index * out_rows
    head = first_col // HD
    kv_head = head // group_size
    head_queries = lax.dynamic_slice_in_dim(queries, head * HD, HD, 1)
    head_keys = lax.dynamic_slice_in_dim(keys_new, kv_head * HD, HD, 1)
    head_values = lax.dynamic_slice_in_dim(
        values_new, kv_head * HD + first_col % HD, out_rows, 1
    ).astype(jnp.float32)
    new_scores = jnp.dot(head_queries, head_keys.T, preferred_element_type=jnp.float32)
    token_ids = jnp.arange(tokens, dtype=jnp.int32)
    causal = (token_ids[:, None] // step_count == token_ids[None, :] // step_count) & (
        token_ids[:, None] >= token_ids[None, :]
    )
    new_scores = jnp.where(causal, new_scores, NEGATIVE)
    highest = jnp.maximum(jnp.max(got_top, axis=0), jnp.max(new_scores, axis=1))
    weights = jnp.exp(got_top - highest[None])
    new_probs = jnp.where(causal, jnp.exp(new_scores - highest[:, None]), 0.0)
    denominator = jnp.sum(got_total * weights, axis=0) + jnp.sum(new_probs, axis=1)
    numerator = jnp.sum(got_accum * weights[..., None], axis=0) + jnp.dot(
        new_probs, head_values, precision=lax.Precision.HIGHEST
    )
    return (numerator / denominator[:, None]).astype(jnp.bfloat16)


def on_device(
    req_count,
    seq_count,
    hidden_in,
    attn_gain,
    q_gain,
    k_gain,
    post_attn_gain,
    ffn_gain,
    post_ffn_gain,
    w_qkv,
    w_out,
    w_gate,
    w_up,
    w_down,
    prompt_keys,
    prompt_values,
    tail_keys,
    tail_values,
    group_of,
    prompt_lengths,
    tail_lengths,
    page_table,
):
    seq_index = lax.axis_index("seq")
    req_index = lax.axis_index("req")
    rows_req, step_count, _ = hidden_in.shape
    group_size = H // KV
    tokens = rows_req * step_count
    share = tokens // seq_count

    def shifted(values):
        return [values] + [
            lax.ppermute(values, "req", [(i, (i + j) % req_count) for i in range(req_count)])
            for j in range(1, req_count)
        ]

    where = jnp.stack([seq_index, req_index]).astype(jnp.int32)
    in_rows = w_qkv.shape[0]
    out_rows = w_out.shape[0]
    if in_rows % 128 == 0:
        normed_cols = call(
            norm_columns_kernel,
            "norm_columns",
            jax.ShapeDtypeStruct((tokens, in_rows), jnp.bfloat16),
            seq_index.astype(jnp.int32).reshape(1),
            hidden_in,
            attn_gain.reshape(1, D),
            limit=56,
        )
    else:
        normed = (normalize(hidden_in.astype(jnp.float32)) * attn_gain).astype(jnp.bfloat16)
        normed_cols = lax.dynamic_slice_in_dim(normed, seq_index * in_rows, in_rows, 2)
        normed_cols = normed_cols.reshape(tokens, in_rows)
    normed_all = lax.all_gather(normed_cols, "req", axis=0, tiled=True)
    normed_all, out_blocks = tie(normed_all, shifted(w_out))
    width = w_gate.shape[1]
    pieces = [w_down[:, c : c + width] for c in range(0, w_down.shape[1], width)]
    packed = shifted(jnp.concatenate([w_gate, w_up] + pieces))[1:]

    qkv_part = jnp.dot(normed_all, w_qkv, preferred_element_type=jnp.float32)
    qkv_cols = w_qkv.shape[1]
    qkv_blocks = (
        (qkv_part * LINK_SCALE)
        .astype(jnp.float16)
        .reshape(req_count * seq_count, share, qkv_cols)
    )
    qkv_got = exchange(qkv_blocks, ("req", "seq"))
    qkv_got = qkv_got.reshape(req_count, seq_count, share, qkv_cols)
    projected = jnp.sum(qkv_got.astype(jnp.float32), axis=1) * (1.0 / LINK_SCALE)
    live = live_rows(
        seq_index, prompt_keys.shape[:2], tail_keys.shape[1], group_of, prompt_lengths,
        tail_lengths, page_table,
    )
    caches = [
        array.reshape(-1, KV * HD) for array in (prompt_keys, prompt_values, tail_keys, tail_values)
    ]
    direct = share == step_count and out_rows % 128 == 0 and tokens == 64 and qkv_cols % HD == 0
    if direct:
        live = jnp.repeat(live.astype(jnp.float32), step_count, axis=0)
        keys = jnp.concatenate([caches[0], caches[2]])
        values = jnp.concatenate([caches[1], caches[3]])
        projected, live, keys, values = tie(projected, live, keys, values)
        q_blocks, new_keys, new_values = call(
            head_norm_kernel,
            "head_norm",
            (
                jax.ShapeDtypeStruct((seq_count, share, H * HD), jnp.bfloat16),
                jax.ShapeDtypeStruct((8, KV * HD), jnp.float32),
                jax.ShapeDtypeStruct((8, KV * HD), jnp.float32),
            ),
            where,
            projected,
            jnp.stack([q_gain, k_gain]),
        )
        sent = call(
            functools.partial(block_kernel, step_count),
            "block_attention",
            jax.ShapeDtypeStruct((seq_count, tokens + 16, out_rows), jnp.bfloat16),
            where,
            exchange(q_blocks, "seq"),
            live,
            new_keys,
            new_values,
            keys,
            values,
        )
        got = exchange(sent, "seq")
        out_part = call(
            functools.partial(out_kernel, req_count),
            "combine_out",
            jax.ShapeDtypeStruct((seq_count, share, D), jnp.bfloat16),
            where,
            got,
            *out_blocks,
            scratch=[pltpu.VMEM((128, 128), jnp.float32)],
        )
    else:
        projected = projected.transpose(1, 0, 2).reshape(share, QKV)
        attention_cols = general_attention(
            seq_index, seq_count, rows_req, step_count, out_rows, projected, q_gain, k_gain,
            live, *caches,
        )
        out_part = jnp.concatenate(
            [jnp.dot(attention_cols, w, preferred_element_type=jnp.float32) for w in out_blocks],
            axis=1,
        )
        out_part = out_part.astype(jnp.bfloat16).reshape(seq_count, share, D)
    ffn_blocks, residual = call(
        functools.partial(residual_kernel, req_count),
        "residual_norms",
        (
            jax.ShapeDtypeStruct((seq_count, share, D), jnp.bfloat16),
            jax.ShapeDtypeStruct((share, D), jnp.float32),
        ),
        where,
        exchange(out_part, "seq"),
        hidden_in.reshape(seq_count, share, D),
        post_attn_gain.reshape(1, D),
        ffn_gain.reshape(1, D),
    )
    ffn_in = exchange(ffn_blocks, "seq")
    x_space = pltpu.VMEM((seq_count, share, D), jnp.bfloat16)
    own_part = call(
        functools.partial(own_kernel, req_count),
        "own_gate_up",
        jax.ShapeDtypeStruct((2, tokens, width), jnp.float32),
        where,
        ffn_in,
        w_gate,
        w_up,
        scratch=[
            x_space,
            pltpu.VMEM((2,) + w_gate.shape, jnp.bfloat16),
            pltpu.SemaphoreType.DMA((3,)),
        ],
        hbm_from=1,
        limit=56,
    )
    down_part = call(
        functools.partial(ffn_kernel, req_count, w_gate.shape[0]),
        "feed_forward",
        jax.ShapeDtypeStruct((seq_count, share, D), jnp.bfloat16),
        where,
        ffn_in,
        own_part,
        w_down,
        *packed,
        scratch=[
            x_space,
            pltpu.VMEM((2, tokens, width), jnp.float32),
            pltpu.VMEM(w_down.shape, jnp.bfloat16),
            pltpu.VMEM((D // width, seq_count, share, width), jnp.bfloat16),
        ]
        + [pltpu.VMEM(w.shape, w.dtype) for w in packed]
        + [pltpu.SemaphoreType.DMA((3 * req_count + D // width,))],
        hbm_from=1,
        out_space=pltpu.HBM,
        limit=56,
    )
    layer_blocks = call(
        functools.partial(last_kernel, req_count),
        "last_norm",
        jax.ShapeDtypeStruct((seq_count, share, D), jnp.bfloat16),
        where,
        exchange(down_part, "seq"),
        residual,
        post_ffn_gain.reshape(1, D),
    )
    return exchange(layer_blocks, "seq").reshape(rows_req, step_count, D)


def solution(mesh):
    return jax.shard_map(
        functools.partial(on_device, mesh.shape["req"], mesh.shape["seq"]),
        mesh=mesh,
        in_specs=(
            P("req", None, None),
            P(),
            P(),
            P(),
            P(),
            P(),
            P(),
            P("seq", "req"),
            P("seq", "req"),
            P("req", "seq"),
            P("req", "seq"),
            P("seq", "req"),
            P("req", "seq", None),
            P("req", "seq", None),
            P("req", "seq", None),
            P("req", "seq", None),
            P("req"),
            P("req"),
            P("req"),
            P("req", None),
        ),
        out_specs=P("req", None, None),
        check_vma=False,
    )
```

```python
import functools

import jax
import jax.numpy as jnp
from jax import lax
from jax.experimental import pallas as pl
from jax.experimental.pallas import tpu as pltpu
from jax.sharding import PartitionSpec as P

D = 2048
H = 8
KV = 2
HD = 256
PAGE = 16
QKV = 3072


EPSILON = 1e-06
NEGATIVE = -1e30
LINK_SCALE = 512.0


def normalize(values):
    return values * lax.rsqrt(jnp.mean(values * values, axis=-1, keepdims=True) + EPSILON)


def split_three(values):
    high = values.astype(jnp.bfloat16)
    rest = values - high.astype(jnp.float32)
    middle = rest.astype(jnp.bfloat16)
    low = (rest - middle.astype(jnp.float32)).astype(jnp.bfloat16)
    return jnp.stack([high, middle, low])


def exchange(blocks, axes, groups=None):
    return lax.all_to_all(
        blocks, axes, split_axis=0, concat_axis=0, tiled=True, axis_index_groups=groups
    )


def tie(*arrays):
    return lax.optimization_barrier(arrays)


def spread(block, copies):
    return jnp.broadcast_to(block[None], (copies,) + block.shape)


def gather_rows(rows, count):
    return exchange(spread(rows, count), "seq").reshape(count * rows.shape[0], rows.shape[1])


def call(
    kernel, name, out_shape, *operands, scratch=(), hbm_from=None, out_space=pltpu.VMEM, limit=16
):
    in_specs = [pl.BlockSpec(memory_space=pltpu.SMEM)]
    for i in range(1, len(operands)):
        space = pltpu.HBM if hbm_from is not None and i >= hbm_from else pltpu.VMEM
        in_specs.append(pl.BlockSpec(memory_space=space))
    return pl.pallas_call(
        kernel,
        name=name,
        out_shape=out_shape,
        in_specs=in_specs,
        out_specs=jax.tree.map(lambda _: pl.BlockSpec(memory_space=out_space), out_shape),
        scratch_shapes=scratch,
        compiler_params=pltpu.CompilerParams(vmem_limit_bytes=limit * 1024 * 1024),
    )(*operands)


def norm_columns_kernel(where_ref, hidden_ref, gain_ref, out_ref):
    columns = out_ref.shape[1]
    hidden = hidden_ref[...].astype(jnp.float32)
    scale = lax.rsqrt(jnp.mean(hidden * hidden, axis=-1, keepdims=True) + EPSILON)
    cols = pl.ds(pl.multiple_of(where_ref[0] * columns, columns), columns)
    normed = hidden_ref[:, :, cols].astype(jnp.float32) * scale * gain_ref[:, cols]
    out_ref[...] = normed.reshape(out_ref.shape).astype(jnp.bfloat16)


def head_norm_kernel(where_ref, projected_ref, gains_ref, q_ref, k_ref, v_ref):
    width = projected_ref.shape[2]
    copies, rows, _ = q_ref.shape
    fill = jnp.zeros((k_ref.shape[0] - rows, HD), jnp.float32)
    for head in range(H + 2 * KV):
        half, first = divmod(head * HD, width)
        values = normalize(projected_ref[half, :, first : first + HD])
        if head < H:
            values = (values * gains_ref[0:1, :]).astype(jnp.bfloat16)
            for i in range(copies):
                q_ref[i, :, head * HD : (head + 1) * HD] = values
        else:
            if head < H + KV:
                values = values * gains_ref[1:2, :]
            values = values.astype(jnp.bfloat16).astype(jnp.float32)
            target, slot = (k_ref, head - H) if head < H + KV else (v_ref, head - H - KV)
            target[:, slot * HD : (slot + 1) * HD] = jnp.concatenate([values, fill])


def dot_last(a, b):
    return lax.dot_general(a, b, (((1,), (1,)), ((), ())), preferred_element_type=jnp.float32)


def block_kernel(
    step_count,
    where_ref,
    q_ref,
    live_ref,
    new_k_ref,
    new_v_ref,
    keys_ref,
    values_ref,
    out_ref,
):
    copies, steps, _ = q_ref.shape
    tokens = copies * steps
    columns = out_ref.shape[2]
    group = H // KV
    queries = q_ref[...].reshape(tokens, H * HD)
    live = jnp.concatenate([live_ref[...]] * group) > 0.5
    first_token = where_ref[0] * step_count
    shape = (group * tokens, new_k_ref.shape[0])
    step = lax.broadcasted_iota(jnp.int32, shape, 0) % tokens - first_token
    new_index = lax.broadcasted_iota(jnp.int32, shape, 1)
    new_live = (step >= new_index) & (step < step_count)
    for kv in range(KV):
        span = slice(kv * HD, (kv + 1) * HD)
        q = jnp.concatenate(
            [queries[:, (kv * group + g) * HD : (kv * group + g + 1) * HD] for g in range(group)]
        )
        scores = jnp.where(live, dot_last(q, keys_ref[:, span]), NEGATIVE)
        top = jnp.max(scores, axis=1, keepdims=True)
        probs = jnp.where(live, jnp.exp(scores - top), 0.0)
        total = jnp.sum(probs, axis=1, keepdims=True)
        accum = jnp.dot(
            probs.astype(jnp.bfloat16), values_ref[:, span], preferred_element_type=jnp.float32
        )
        new_scores = dot_last(q, new_k_ref[:, span].astype(jnp.bfloat16))
        new_scores = jnp.where(new_live, new_scores, NEGATIVE)
        both = jnp.maximum(top, jnp.max(new_scores, axis=1, keepdims=True))
        carried = jnp.exp(top - both)
        new_probs = jnp.where(new_live, jnp.exp(new_scores - both), 0.0)
        total = total * carried + jnp.sum(new_probs, axis=1, keepdims=True)
        accum = accum * carried
        for u in range(step_count):
            accum = accum + new_probs[:, u : u + 1] * new_v_ref[u : u + 1, span]
        sent = accum.astype(jnp.bfloat16)
        parts = []
        for value in (both, total):
            for _ in range(3):
                part = value.astype(jnp.bfloat16).astype(jnp.float32)
                parts.append(part)
                value = value - part
        lane = lax.broadcasted_iota(jnp.int32, (group * tokens, 128), 1)
        wide = jnp.zeros((group * tokens, 128), jnp.float32)
        for i, part in enumerate(parts):
            wide = jnp.where(lane == i, part, wide)
        turned = jnp.transpose(wide)[:16].astype(jnp.bfloat16)
        for g in range(group):
            pair = turned[:, g // 2 * 128 : (g // 2 + 1) * 128]
            for part in range(HD // columns):
                target = (kv * group + g) * (HD // columns) + part
                out_ref[target, :tokens, :] = sent[
                    g * tokens : (g + 1) * tokens, part * columns : (part + 1) * columns
                ]
                out_ref[target, tokens:, :] = pair


def out_kernel(req_count, where_ref, got_ref, *refs):
    w_refs = refs[:req_count]
    out_ref, turned_ref = refs[req_count:]
    blocks = got_ref.shape[0]
    copies, steps, _ = out_ref.shape
    tokens = copies * steps
    columns = got_ref.shape[2]
    head = where_ref[0] * columns // HD
    stats = got_ref[:, tokens:, :].astype(jnp.float32)
    tops = stats[:, 0, :] + stats[:, 1, :] + stats[:, 2, :]
    totals = stats[:, 3, :] + stats[:, 4, :] + stats[:, 5, :]
    rest = jnp.zeros((128 - 2 * blocks, 128), jnp.float32)
    turned_ref[...] = jnp.transpose(jnp.concatenate([tops, totals, rest]))
    mine = turned_ref[pl.ds(pl.multiple_of(head % 2 * tokens, tokens), tokens), :]
    tops = mine[:, :blocks]
    highest = jnp.max(tops, axis=1, keepdims=True)
    weights = jnp.exp(tops - highest)
    denominator = jnp.sum(mine[:, blocks : 2 * blocks] * weights, axis=1, keepdims=True)
    numerator = jnp.zeros((tokens, columns), jnp.float32)
    for b in range(blocks):
        numerator = numerator + got_ref[b, :tokens, :].astype(jnp.float32) * weights[:, b : b + 1]
    attention = (numerator / denominator).astype(jnp.bfloat16)
    for j, w_ref in enumerate(w_refs):
        width = w_ref.shape[1]
        part = jnp.dot(attention, w_ref[...], preferred_element_type=jnp.float32)
        part = part.astype(jnp.bfloat16)
        for i in range(copies):
            out_ref[i, :, j * width : (j + 1) * width] = part[i * steps : (i + 1) * steps]


def summed(req_count, where_ref, got_ref):
    width = got_ref.shape[2] // req_count
    blocks = []
    for i in range(req_count):
        j = lax.rem(where_ref[1] - i + req_count, req_count)
        cols = pl.ds(pl.multiple_of(j * width, width), width)
        blocks.append(jnp.sum(got_ref[:, :, cols].astype(jnp.float32), axis=0))
    return jnp.concatenate(blocks, axis=1)


def residual_kernel(
    req_count, where_ref, got_ref, hidden_ref, post_gain_ref, ffn_gain_ref, out_ref, residual_ref
):
    attn_out = summed(req_count, where_ref, got_ref)
    hidden = hidden_ref[where_ref[0]].astype(jnp.float32)
    residual = hidden + normalize(attn_out) * post_gain_ref[...]
    residual_ref[...] = residual
    ffn_in = (normalize(residual) * ffn_gain_ref[...]).astype(jnp.bfloat16)
    for i in range(out_ref.shape[0]):
        out_ref[i] = ffn_in


def last_kernel(req_count, where_ref, got_ref, residual_ref, gain_ref, out_ref):
    down_out = summed(req_count, where_ref, got_ref)
    layer = (residual_ref[...] + normalize(down_out) * gain_ref[...]).astype(jnp.bfloat16)
    for i in range(out_ref.shape[0]):
        out_ref[i] = layer


def start_copies(moves, sem_ref):
    copies = [
        pltpu.make_async_copy(source, target, sem_ref.at[i])
        for i, (source, target) in enumerate(moves)
    ]
    for copy in copies:
        copy.start()
    return copies


def own_kernel(req_count, where_ref, x_ref, gate_ref, up_ref, out_ref, x_held, held, sem_ref):
    copies = start_copies(
        [(x_ref, x_held), (gate_ref, held.at[0]), (up_ref, held.at[1])], sem_ref
    )
    rows = gate_ref.shape[0]
    blocks, steps, _ = x_held.shape
    copies[0].wait()
    start = where_ref[1] * rows
    part = x_held[:, :, pl.ds(pl.multiple_of(start, rows), rows)].reshape(blocks * steps, rows)
    for i in range(2):
        copies[i + 1].wait()
        out_ref[i] = jnp.dot(part, held[i], preferred_element_type=jnp.float32)


def ffn_kernel(req_count, gate_rows, where_ref, x_ref, own_ref, down_ref, *refs):
    others = req_count - 1
    packed_refs = refs[:others]
    out_ref, x_held, own_held, down_held, parts_ref = refs[others : others + 5]
    held, sem_ref = refs[others + 5 : -1], refs[-1]
    down_rows, down_width = down_ref.shape
    packed_rows, width = packed_refs[0].shape
    moves = [(x_ref, x_held), (own_ref, own_held)]
    spans = [(0, gate_rows), (gate_rows, gate_rows), (2 * gate_rows, packed_rows - 2 * gate_rows)]
    for j in range(others):
        for first, rows in spans:
            span = pl.ds(first, rows)
            moves.append((packed_refs[j].at[span, :], held[j].at[span, :]))
    moves.append((down_ref, down_held))
    copies = start_copies(moves, sem_ref)
    blocks, steps, _ = x_held.shape
    tokens = blocks * steps
    copies[0].wait()
    gates, ups = [], []
    for j in range(others):
        start = lax.rem(where_ref[1] - j - 1 + req_count, req_count) * gate_rows
        part = x_held[:, :, pl.ds(pl.multiple_of(start, gate_rows), gate_rows)]
        part = part.reshape(tokens, gate_rows)
        copies[3 * j + 2].wait()
        gates.append(jnp.dot(part, held[j][:gate_rows, :], preferred_element_type=jnp.float32))
        copies[3 * j + 3].wait()
        up_w = held[j][gate_rows : 2 * gate_rows, :]
        ups.append(jnp.dot(part, up_w, preferred_element_type=jnp.float32))
    copies[1].wait()
    gate_out, up_out = own_held[0], own_held[1]
    for gate, up in zip(gates, ups):
        gate_out = gate_out + gate
        up_out = up_out + up
    activated = (jax.nn.gelu(gate_out, approximate=True) * up_out).astype(jnp.bfloat16)
    sends = []
    for j in range(req_count):
        copies[-1 if j == 0 else 3 * j + 1].wait()
        for piece in range(down_width // width):
            if j == 0:
                down_w = down_held[:, piece * width : (piece + 1) * width]
            else:
                row = 2 * gate_rows + piece * down_rows
                down_w = held[j - 1][row : row + down_rows, :]
            part = jnp.dot(activated, down_w, preferred_element_type=jnp.float32)
            part = part.astype(jnp.bfloat16)
            index = j * (down_width // width) + piece
            for i in range(blocks):
                parts_ref[index, i] = part[i * steps : (i + 1) * steps]
            sends.append(
                pltpu.make_async_copy(
                    parts_ref.at[index],
                    out_ref.at[:, :, pl.ds(index * width, width)],
                    sem_ref.at[len(copies) + index],
                )
            )
            sends[-1].start()
    for send in sends:
        send.wait()


def live_rows(
    seq_index, prompt_shape, pool_rows, group_of, prompt_lengths, tail_lengths, page_table
):
    group_count, prompt_span = prompt_shape
    rows_req = group_of.shape[0]
    member = (group_of % group_count)[:, None] == jnp.arange(group_count, dtype=jnp.int32)[None, :]
    prompt_pos = seq_index * prompt_span + jnp.arange(prompt_span, dtype=jnp.int32)
    prompt_live = prompt_pos[None, :] < prompt_lengths[:, None]
    prompt_mask = (member[:, :, None] & prompt_live[None, :, :]).reshape(
        rows_req, group_count * prompt_span
    )
    slot_count = pool_rows // PAGE
    table_row = page_table[0]
    table_len = table_row.shape[0]
    tail_pages = table_len // rows_req
    slot_ids = seq_index * slot_count + jnp.arange(slot_count, dtype=jnp.int32)
    matches = table_row[None, :] == slot_ids[:, None]
    entries = jnp.sum(
        jnp.where(matches, jnp.arange(table_len, dtype=jnp.int32)[None, :], 0), axis=1
    )
    owners = jnp.repeat(entries // tail_pages, PAGE)
    tail_pos = jnp.repeat(entries % tail_pages, PAGE) * PAGE + jnp.tile(
        jnp.arange(PAGE, dtype=jnp.int32), slot_count
    )
    tail_mask = (owners[None, :] == jnp.arange(rows_req, dtype=jnp.int32)[:, None]) & (
        tail_pos[None, :] < tail_lengths[:, None]
    )
    return jnp.concatenate([prompt_mask, tail_mask], axis=1)


def general_attention(
    seq_index,
    seq_count,
    rows_req,
    step_count,
    out_rows,
    projected,
    q_gain,
    k_gain,
    live,
    prompt_keys,
    prompt_values,
    tail_keys,
    tail_values,
):
    group_size = H // KV
    share = projected.shape[0]
    tokens = rows_req * step_count
    heads = normalize(projected.reshape(share, QKV // HD, HD))
    gains = jnp.concatenate(
        [
            jnp.broadcast_to(q_gain, (H, HD)),
            jnp.broadcast_to(k_gain, (KV, HD)),
            jnp.ones((KV, HD), jnp.float32),
        ]
    )
    mine = (heads * gains).astype(jnp.bfloat16).reshape(share, QKV)
    qkv = gather_rows(mine, seq_count)
    queries = qkv[:, : H * HD]
    keys_new = qkv[:, H * HD : (H + KV) * HD]
    values_new = qkv[:, (H + KV) * HD :]

    query_groups = queries.reshape(rows_req, step_count, KV, group_size, HD)
    mask = live[:, None, None, None, :]
    keys = jnp.concatenate([prompt_keys, tail_keys]).reshape(-1, KV, HD)
    values = jnp.concatenate([prompt_values, tail_values]).reshape(-1, KV, HD)
    scores = jnp.einsum("rskgd,pkd->rskgp", query_groups, keys, preferred_element_type=jnp.float32)
    scores = jnp.where(mask, scores, NEGATIVE)
    block_top = jnp.max(scores, axis=4)
    probs = jnp.where(mask, jnp.exp(scores - block_top[..., None]), 0.0)
    block_total = jnp.sum(probs, axis=4)
    block_accum = jnp.einsum(
        "rskgp,pkd->rskgd",
        probs.astype(jnp.bfloat16),
        values,
        preferred_element_type=jnp.float32,
    )

    stats = split_three(jnp.stack([block_top, block_total])).reshape(6, tokens, H)
    per_head = seq_count // H
    stats = jnp.repeat(stats.transpose(2, 0, 1).reshape(H, -1, out_rows), per_head, axis=0)
    accum_blocks = (
        block_accum.astype(jnp.bfloat16).reshape(tokens, seq_count, out_rows).transpose(1, 0, 2)
    )
    got = exchange(jnp.concatenate([accum_blocks, stats], axis=1), "seq")
    got_accum = got[:, :tokens].astype(jnp.float32)
    got_stats = got[:, tokens:].astype(jnp.float32).reshape(seq_count, 2 * 3, tokens)
    got_top = got_stats[:, 0] + got_stats[:, 2] + got_stats[:, 4]
    got_total = got_stats[:, 1] + got_stats[:, 3] + got_stats[:, 5]

    first_col = seq_index * out_rows
    head = first_col // HD
    kv_head = head // group_size
    head_queries = lax.dynamic_slice_in_dim(queries, head * HD, HD, 1)
    head_keys = lax.dynamic_slice_in_dim(keys_new, kv_head * HD, HD, 1)
    head_values = lax.dynamic_slice_in_dim(
        values_new, kv_head * HD + first_col % HD, out_rows, 1
    ).astype(jnp.float32)
    new_scores = jnp.dot(head_queries, head_keys.T, preferred_element_type=jnp.float32)
    token_ids = jnp.arange(tokens, dtype=jnp.int32)
    causal = (token_ids[:, None] // step_count == token_ids[None, :] // step_count) & (
        token_ids[:, None] >= token_ids[None, :]
    )
    new_scores = jnp.where(causal, new_scores, NEGATIVE)
    highest = jnp.maximum(jnp.max(got_top, axis=0), jnp.max(new_scores, axis=1))
    weights = jnp.exp(got_top - highest[None])
    new_probs = jnp.where(causal, jnp.exp(new_scores - highest[:, None]), 0.0)
    denominator = jnp.sum(got_total * weights, axis=0) + jnp.sum(new_probs, axis=1)
    numerator = jnp.sum(got_accum * weights[..., None], axis=0) + jnp.dot(
        new_probs, head_values, precision=lax.Precision.HIGHEST
    )
    return (numerator / denominator[:, None]).astype(jnp.bfloat16)


def on_device(
    req_count,
    seq_count,
    hidden_in,
    attn_gain,
    q_gain,
    k_gain,
    post_attn_gain,
    ffn_gain,
    post_ffn_gain,
    w_qkv,
    w_out,
    w_gate,
    w_up,
    w_down,
    prompt_keys,
    prompt_values,
    tail_keys,
    tail_values,
    group_of,
    prompt_lengths,
    tail_lengths,
    page_table,
):
    seq_index = lax.axis_index("seq")
    req_index = lax.axis_index("req")
    rows_req, step_count, _ = hidden_in.shape
    group_size = H // KV
    tokens = rows_req * step_count
    share = tokens // seq_count

    def shifted(values):
        return [values] + [
            lax.ppermute(values, "req", [(i, (i + j) % req_count) for i in range(req_count)])
            for j in range(1, req_count)
        ]

    where = jnp.stack([seq_index, req_index]).astype(jnp.int32)
    in_rows = w_qkv.shape[0]
    out_rows = w_out.shape[0]
    if in_rows % 128 == 0:
        normed_cols = call(
            norm_columns_kernel,
            "norm_columns",
            jax.ShapeDtypeStruct((tokens, in_rows), jnp.bfloat16),
            seq_index.astype(jnp.int32).reshape(1),
            hidden_in,
            attn_gain.reshape(1, D),
            limit=56,
        )
    else:
        normed = (normalize(hidden_in.astype(jnp.float32)) * attn_gain).astype(jnp.bfloat16)
        normed_cols = lax.dynamic_slice_in_dim(normed, seq_index * in_rows, in_rows, 2)
        normed_cols = normed_cols.reshape(tokens, in_rows)
    normed_all = lax.all_gather(normed_cols, "req", axis=0, tiled=True)
    out_blocks = shifted(w_out)
    width = w_gate.shape[1]
    pieces = [w_down[:, c : c + width] for c in range(0, w_down.shape[1], width)]
    packed = shifted(jnp.concatenate([w_gate, w_up] + pieces))[1:]

    qkv_part = jnp.dot(normed_all, w_qkv, preferred_element_type=jnp.float32)
    qkv_cols = w_qkv.shape[1]
    qkv_blocks = (
        (qkv_part * LINK_SCALE)
        .astype(jnp.float16)
        .reshape(req_count * seq_count, share, qkv_cols)
    )
    qkv_got = exchange(qkv_blocks, ("req", "seq"))
    qkv_got = qkv_got.reshape(req_count, seq_count, share, qkv_cols)
    projected = jnp.sum(qkv_got.astype(jnp.float32), axis=1) * (1.0 / LINK_SCALE)
    live = live_rows(
        seq_index, prompt_keys.shape[:2], tail_keys.shape[1], group_of, prompt_lengths,
        tail_lengths, page_table,
    )
    caches = [
        array.reshape(-1, KV * HD) for array in (prompt_keys, prompt_values, tail_keys, tail_values)
    ]
    direct = share == step_count and out_rows % 128 == 0 and tokens == 64 and qkv_cols % HD == 0
    if direct:
        q_blocks, new_keys, new_values = call(
            head_norm_kernel,
            "head_norm",
            (
                jax.ShapeDtypeStruct((seq_count, share, H * HD), jnp.bfloat16),
                jax.ShapeDtypeStruct((8, KV * HD), jnp.float32),
                jax.ShapeDtypeStruct((8, KV * HD), jnp.float32),
            ),
            where,
            projected,
            jnp.stack([q_gain, k_gain]),
        )
        q_got, out_blocks = tie(exchange(q_blocks, "seq"), out_blocks)
        live = jnp.repeat(live.astype(jnp.float32), step_count, axis=0)
        sent = call(
            functools.partial(block_kernel, step_count),
            "block_attention",
            jax.ShapeDtypeStruct((seq_count, tokens + 16, out_rows), jnp.bfloat16),
            where,
            q_got,
            live,
            new_keys,
            new_values,
            jnp.concatenate([caches[0], caches[2]]),
            jnp.concatenate([caches[1], caches[3]]),
        )
        got = exchange(sent, "seq")
        out_part = call(
            functools.partial(out_kernel, req_count),
            "combine_out",
            jax.ShapeDtypeStruct((seq_count, share, D), jnp.bfloat16),
            where,
            got,
            *out_blocks,
            scratch=[pltpu.VMEM((128, 128), jnp.float32)],
        )
    else:
        projected = projected.transpose(1, 0, 2).reshape(share, QKV)
        attention_cols = general_attention(
            seq_index, seq_count, rows_req, step_count, out_rows, projected, q_gain, k_gain,
            live, *caches,
        )
        out_part = jnp.concatenate(
            [jnp.dot(attention_cols, w, preferred_element_type=jnp.float32) for w in out_blocks],
            axis=1,
        )
        out_part = out_part.astype(jnp.bfloat16).reshape(seq_count, share, D)
    ffn_blocks, residual = call(
        functools.partial(residual_kernel, req_count),
        "residual_norms",
        (
            jax.ShapeDtypeStruct((seq_count, share, D), jnp.bfloat16),
            jax.ShapeDtypeStruct((share, D), jnp.float32),
        ),
        where,
        exchange(out_part, "seq"),
        hidden_in.reshape(seq_count, share, D),
        post_attn_gain.reshape(1, D),
        ffn_gain.reshape(1, D),
    )
    ffn_in = exchange(ffn_blocks, "seq")
    x_space = pltpu.VMEM((seq_count, share, D), jnp.bfloat16)
    own_part = call(
        functools.partial(own_kernel, req_count),
        "own_gate_up",
        jax.ShapeDtypeStruct((2, tokens, width), jnp.float32),
        where,
        ffn_in,
        w_gate,
        w_up,
        scratch=[
            x_space,
            pltpu.VMEM((2,) + w_gate.shape, jnp.bfloat16),
            pltpu.SemaphoreType.DMA((3,)),
        ],
        hbm_from=1,
        limit=56,
    )
    down_part = call(
        functools.partial(ffn_kernel, req_count, w_gate.shape[0]),
        "feed_forward",
        jax.ShapeDtypeStruct((seq_count, share, D), jnp.bfloat16),
        where,
        ffn_in,
        own_part,
        w_down,
        *packed,
        scratch=[
            x_space,
            pltpu.VMEM((2, tokens, width), jnp.float32),
            pltpu.VMEM(w_down.shape, jnp.bfloat16),
            pltpu.VMEM((D // width, seq_count, share, width), jnp.bfloat16),
        ]
        + [pltpu.VMEM(w.shape, w.dtype) for w in packed]
        + [pltpu.SemaphoreType.DMA((3 * req_count + D // width,))],
        hbm_from=1,
        out_space=pltpu.HBM,
        limit=56,
    )
    layer_blocks = call(
        functools.partial(last_kernel, req_count),
        "last_norm",
        jax.ShapeDtypeStruct((seq_count, share, D), jnp.bfloat16),
        where,
        exchange(down_part, "seq"),
        residual,
        post_ffn_gain.reshape(1, D),
    )
    return exchange(layer_blocks, "seq").reshape(rows_req, step_count, D)


def solution(mesh):
    return jax.shard_map(
        functools.partial(on_device, mesh.shape["req"], mesh.shape["seq"]),
        mesh=mesh,
        in_specs=(
            P("req", None, None),
            P(),
            P(),
            P(),
            P(),
            P(),
            P(),
            P("seq", "req"),
            P("seq", "req"),
            P("req", "seq"),
            P("req", "seq"),
            P("seq", "req"),
            P("req", "seq", None),
            P("req", "seq", None),
            P("req", "seq", None),
            P("req", "seq", None),
            P("req"),
            P("req"),
            P("req"),
            P("req", None),
        ),
        out_specs=P("req", None, None),
        check_vma=False,
    )
```

```python
import functools

import jax
import jax.numpy as jnp
from jax import lax
from jax.experimental import pallas as pl
from jax.experimental.pallas import tpu as pltpu
from jax.sharding import PartitionSpec as P

D = 2048
H = 8
KV = 2
HD = 256
PAGE = 16
QKV = 3072


EPSILON = 1e-06
NEGATIVE = -1e30
LINK_SCALE = 512.0


def normalize(values):
    return values * lax.rsqrt(jnp.mean(values * values, axis=-1, keepdims=True) + EPSILON)


def split_three(values):
    high = values.astype(jnp.bfloat16)
    rest = values - high.astype(jnp.float32)
    middle = rest.astype(jnp.bfloat16)
    low = (rest - middle.astype(jnp.float32)).astype(jnp.bfloat16)
    return jnp.stack([high, middle, low])


def exchange(blocks, axes, groups=None):
    return lax.all_to_all(
        blocks, axes, split_axis=0, concat_axis=0, tiled=True, axis_index_groups=groups
    )


def tie(*arrays):
    return lax.optimization_barrier(arrays)


def spread(block, copies):
    return jnp.broadcast_to(block[None], (copies,) + block.shape)


def gather_rows(rows, count):
    return exchange(spread(rows, count), "seq").reshape(count * rows.shape[0], rows.shape[1])


def call(
    kernel, name, out_shape, *operands, scratch=(), hbm_from=None, out_space=pltpu.VMEM, limit=16
):
    in_specs = [pl.BlockSpec(memory_space=pltpu.SMEM)]
    for i in range(1, len(operands)):
        space = pltpu.HBM if hbm_from is not None and i >= hbm_from else pltpu.VMEM
        in_specs.append(pl.BlockSpec(memory_space=space))
    return pl.pallas_call(
        kernel,
        name=name,
        out_shape=out_shape,
        in_specs=in_specs,
        out_specs=jax.tree.map(lambda _: pl.BlockSpec(memory_space=out_space), out_shape),
        scratch_shapes=scratch,
        compiler_params=pltpu.CompilerParams(vmem_limit_bytes=limit * 1024 * 1024),
    )(*operands)


def norm_columns_kernel(where_ref, hidden_ref, gain_ref, out_ref):
    columns = out_ref.shape[1]
    hidden = hidden_ref[...].astype(jnp.float32)
    scale = lax.rsqrt(jnp.mean(hidden * hidden, axis=-1, keepdims=True) + EPSILON)
    cols = pl.ds(pl.multiple_of(where_ref[0] * columns, columns), columns)
    normed = hidden_ref[:, :, cols].astype(jnp.float32) * scale * gain_ref[:, cols]
    out_ref[...] = normed.reshape(out_ref.shape).astype(jnp.bfloat16)


def head_norm_kernel(where_ref, projected_ref, gains_ref, q_ref, k_ref, v_ref):
    width = projected_ref.shape[2]
    copies, rows, _ = q_ref.shape
    fill = jnp.zeros((k_ref.shape[0] - rows, HD), jnp.float32)
    for head in range(H + 2 * KV):
        half, first = divmod(head * HD, width)
        values = normalize(projected_ref[half, :, first : first + HD])
        if head < H:
            values = (values * gains_ref[0:1, :]).astype(jnp.bfloat16)
            for i in range(copies):
                q_ref[i, :, head * HD : (head + 1) * HD] = values
        else:
            if head < H + KV:
                values = values * gains_ref[1:2, :]
            values = values.astype(jnp.bfloat16).astype(jnp.float32)
            target, slot = (k_ref, head - H) if head < H + KV else (v_ref, head - H - KV)
            target[:, slot * HD : (slot + 1) * HD] = jnp.concatenate([values, fill])


def dot_last(a, b):
    return lax.dot_general(a, b, (((1,), (1,)), ((), ())), preferred_element_type=jnp.float32)


def block_kernel(
    step_count,
    where_ref,
    q_ref,
    live_ref,
    new_k_ref,
    new_v_ref,
    keys_ref,
    values_ref,
    out_ref,
):
    copies, steps, _ = q_ref.shape
    tokens = copies * steps
    columns = out_ref.shape[2]
    group = H // KV
    queries = q_ref[...].reshape(tokens, H * HD)
    live = jnp.concatenate([live_ref[...]] * group) > 0.5
    first_token = where_ref[0] * step_count
    shape = (group * tokens, new_k_ref.shape[0])
    step = lax.broadcasted_iota(jnp.int32, shape, 0) % tokens - first_token
    new_index = lax.broadcasted_iota(jnp.int32, shape, 1)
    new_live = (step >= new_index) & (step < step_count)
    for kv in range(KV):
        span = slice(kv * HD, (kv + 1) * HD)
        q = jnp.concatenate(
            [queries[:, (kv * group + g) * HD : (kv * group + g + 1) * HD] for g in range(group)]
        )
        scores = jnp.where(live, dot_last(q, keys_ref[:, span]), NEGATIVE)
        top = jnp.max(scores, axis=1, keepdims=True)
        probs = jnp.where(live, jnp.exp(scores - top), 0.0)
        total = jnp.sum(probs, axis=1, keepdims=True)
        accum = jnp.dot(
            probs.astype(jnp.bfloat16), values_ref[:, span], preferred_element_type=jnp.float32
        )
        new_scores = dot_last(q, new_k_ref[:, span].astype(jnp.bfloat16))
        new_scores = jnp.where(new_live, new_scores, NEGATIVE)
        both = jnp.maximum(top, jnp.max(new_scores, axis=1, keepdims=True))
        carried = jnp.exp(top - both)
        new_probs = jnp.where(new_live, jnp.exp(new_scores - both), 0.0)
        total = total * carried + jnp.sum(new_probs, axis=1, keepdims=True)
        accum = accum * carried
        for u in range(step_count):
            accum = accum + new_probs[:, u : u + 1] * new_v_ref[u : u + 1, span]
        sent = accum.astype(jnp.bfloat16)
        parts = []
        for value in (both, total):
            for _ in range(3):
                part = value.astype(jnp.bfloat16).astype(jnp.float32)
                parts.append(part)
                value = value - part
        lane = lax.broadcasted_iota(jnp.int32, (group * tokens, 128), 1)
        wide = jnp.zeros((group * tokens, 128), jnp.float32)
        for i, part in enumerate(parts):
            wide = jnp.where(lane == i, part, wide)
        turned = jnp.transpose(wide)[:16].astype(jnp.bfloat16)
        for g in range(group):
            pair = turned[:, g // 2 * 128 : (g // 2 + 1) * 128]
            for part in range(HD // columns):
                target = (kv * group + g) * (HD // columns) + part
                out_ref[target, :tokens, :] = sent[
                    g * tokens : (g + 1) * tokens, part * columns : (part + 1) * columns
                ]
                out_ref[target, tokens:, :] = pair


def out_kernel(req_count, where_ref, got_ref, *refs):
    w_refs = refs[:req_count]
    out_ref, turned_ref = refs[req_count:]
    blocks = got_ref.shape[0]
    copies, steps, _ = out_ref.shape
    tokens = copies * steps
    columns = got_ref.shape[2]
    head = where_ref[0] * columns // HD
    stats = got_ref[:, tokens:, :].astype(jnp.float32)
    tops = stats[:, 0, :] + stats[:, 1, :] + stats[:, 2, :]
    totals = stats[:, 3, :] + stats[:, 4, :] + stats[:, 5, :]
    rest = jnp.zeros((128 - 2 * blocks, 128), jnp.float32)
    turned_ref[...] = jnp.transpose(jnp.concatenate([tops, totals, rest]))
    mine = turned_ref[pl.ds(pl.multiple_of(head % 2 * tokens, tokens), tokens), :]
    tops = mine[:, :blocks]
    highest = jnp.max(tops, axis=1, keepdims=True)
    weights = jnp.exp(tops - highest)
    denominator = jnp.sum(mine[:, blocks : 2 * blocks] * weights, axis=1, keepdims=True)
    numerator = jnp.zeros((tokens, columns), jnp.float32)
    for b in range(blocks):
        numerator = numerator + got_ref[b, :tokens, :].astype(jnp.float32) * weights[:, b : b + 1]
    attention = (numerator / denominator).astype(jnp.bfloat16)
    for j, w_ref in enumerate(w_refs):
        width = w_ref.shape[1]
        part = jnp.dot(attention, w_ref[...], preferred_element_type=jnp.float32)
        part = part.astype(jnp.bfloat16)
        for i in range(copies):
            out_ref[i, :, j * width : (j + 1) * width] = part[i * steps : (i + 1) * steps]


def summed(req_count, where_ref, got_ref):
    width = got_ref.shape[2] // req_count
    blocks = []
    for i in range(req_count):
        j = lax.rem(where_ref[1] - i + req_count, req_count)
        cols = pl.ds(pl.multiple_of(j * width, width), width)
        blocks.append(jnp.sum(got_ref[:, :, cols].astype(jnp.float32), axis=0))
    return jnp.concatenate(blocks, axis=1)


def residual_kernel(
    req_count, where_ref, got_ref, hidden_ref, post_gain_ref, ffn_gain_ref, out_ref, residual_ref
):
    attn_out = summed(req_count, where_ref, got_ref)
    hidden = hidden_ref[where_ref[0]].astype(jnp.float32)
    residual = hidden + normalize(attn_out) * post_gain_ref[...]
    residual_ref[...] = residual
    ffn_in = (normalize(residual) * ffn_gain_ref[...]).astype(jnp.bfloat16)
    for i in range(out_ref.shape[0]):
        out_ref[i] = ffn_in


def last_kernel(req_count, where_ref, got_ref, residual_ref, gain_ref, out_ref):
    down_out = summed(req_count, where_ref, got_ref)
    layer = (residual_ref[...] + normalize(down_out) * gain_ref[...]).astype(jnp.bfloat16)
    for i in range(out_ref.shape[0]):
        out_ref[i] = layer


def start_copies(moves, sem_ref):
    copies = [
        pltpu.make_async_copy(source, target, sem_ref.at[i])
        for i, (source, target) in enumerate(moves)
    ]
    for copy in copies:
        copy.start()
    return copies


def chunks_of(rows):
    size = min(rows, 256)
    return [(first, size) for first in range(0, rows, size)]


def x_columns(x_ref, where_ref, req_count, j, rows):
    start = lax.rem(where_ref[1] - j + req_count, req_count) * rows
    return x_ref.at[:, :, pl.ds(pl.multiple_of(start, rows), rows)]


def chunked_dot(x, held, chunks, waits):
    total = None
    for first, size in chunks:
        next(waits).wait()
        part = jnp.dot(
            x[:, first : first + size],
            held[first : first + size, :],
            preferred_element_type=jnp.float32,
        )
        total = part if total is None else total + part
    return total


def own_kernel(req_count, where_ref, x_ref, gate_ref, up_ref, out_ref, x_held, held, sem_ref):
    rows = gate_ref.shape[0]
    chunks = chunks_of(rows)
    moves = [(x_columns(x_ref, where_ref, req_count, 0, rows), x_held)]
    for i, w_ref in enumerate((gate_ref, up_ref)):
        for first, size in chunks:
            span = pl.ds(first, size)
            moves.append((w_ref.at[span, :], held.at[i, span, :]))
    waits = iter(start_copies(moves, sem_ref))
    blocks, steps, _ = x_held.shape
    next(waits).wait()
    x = x_held[...].reshape(blocks * steps, rows)
    for i in range(2):
        out_ref[i] = chunked_dot(x, held.at[i], chunks, waits)


def ffn_kernel(req_count, gate_rows, where_ref, x_ref, own_ref, down_ref, *refs):
    others = req_count - 1
    packed_refs = refs[:others]
    out_ref, x_held, own_held, downs, parts_ref, held, sem_ref = refs[others:]
    down_rows, width = downs.shape[1:]
    piece_count = down_ref.shape[1] // width
    chunks = chunks_of(gate_rows)
    moves = []
    for j in range(others):
        moves.append((x_columns(x_ref, where_ref, req_count, j + 1, gate_rows), x_held.at[j]))
        for i in range(2):
            for first, size in chunks:
                span = pl.ds(i * gate_rows + first, size)
                moves.append((packed_refs[j].at[span, :], held.at[j, span, :]))
    moves.append((own_ref, own_held))
    for piece in range(piece_count):
        moves.append((down_ref.at[:, pl.ds(piece * width, width)], downs.at[piece]))
    for j in range(others):
        for piece in range(piece_count):
            span = pl.ds(2 * gate_rows + piece * down_rows, down_rows)
            moves.append((packed_refs[j].at[span, :], downs.at[(j + 1) * piece_count + piece]))
    copies = start_copies(moves, sem_ref)
    waits = iter(copies)
    _, blocks, steps, _ = x_held.shape
    gates, ups = [], []
    for j in range(others):
        next(waits).wait()
        x = x_held[j].reshape(blocks * steps, gate_rows)
        gates.append(chunked_dot(x, held.at[j, pl.ds(0, gate_rows)], chunks, waits))
        ups.append(chunked_dot(x, held.at[j, pl.ds(gate_rows, gate_rows)], chunks, waits))
    next(waits).wait()
    gate_out, up_out = own_held[0], own_held[1]
    for gate, up in zip(gates, ups):
        gate_out = gate_out + gate
        up_out = up_out + up
    activated = (jax.nn.gelu(gate_out, approximate=True) * up_out).astype(jnp.bfloat16)
    sends = []
    for index in range(req_count * piece_count):
        next(waits).wait()
        part = jnp.dot(activated, downs[index], preferred_element_type=jnp.float32)
        part = part.astype(jnp.bfloat16)
        for i in range(blocks):
            parts_ref[index, i] = part[i * steps : (i + 1) * steps]
        sends.append(
            pltpu.make_async_copy(
                parts_ref.at[index],
                out_ref.at[:, :, pl.ds(index * width, width)],
                sem_ref.at[len(copies) + index],
            )
        )
        sends[-1].start()
    for send in sends:
        send.wait()


def live_rows(
    seq_index, prompt_shape, pool_rows, group_of, prompt_lengths, tail_lengths, page_table
):
    group_count, prompt_span = prompt_shape
    rows_req = group_of.shape[0]
    member = (group_of % group_count)[:, None] == jnp.arange(group_count, dtype=jnp.int32)[None, :]
    prompt_pos = seq_index * prompt_span + jnp.arange(prompt_span, dtype=jnp.int32)
    prompt_live = prompt_pos[None, :] < prompt_lengths[:, None]
    prompt_mask = (member[:, :, None] & prompt_live[None, :, :]).reshape(
        rows_req, group_count * prompt_span
    )
    slot_count = pool_rows // PAGE
    table_row = page_table[0]
    table_len = table_row.shape[0]
    tail_pages = table_len // rows_req
    slot_ids = seq_index * slot_count + jnp.arange(slot_count, dtype=jnp.int32)
    matches = table_row[None, :] == slot_ids[:, None]
    entries = jnp.sum(
        jnp.where(matches, jnp.arange(table_len, dtype=jnp.int32)[None, :], 0), axis=1
    )
    owners = jnp.repeat(entries // tail_pages, PAGE)
    tail_pos = jnp.repeat(entries % tail_pages, PAGE) * PAGE + jnp.tile(
        jnp.arange(PAGE, dtype=jnp.int32), slot_count
    )
    tail_mask = (owners[None, :] == jnp.arange(rows_req, dtype=jnp.int32)[:, None]) & (
        tail_pos[None, :] < tail_lengths[:, None]
    )
    return jnp.concatenate([prompt_mask, tail_mask], axis=1)


def general_attention(
    seq_index,
    seq_count,
    rows_req,
    step_count,
    out_rows,
    projected,
    q_gain,
    k_gain,
    live,
    prompt_keys,
    prompt_values,
    tail_keys,
    tail_values,
):
    group_size = H // KV
    share = projected.shape[0]
    tokens = rows_req * step_count
    heads = normalize(projected.reshape(share, QKV // HD, HD))
    gains = jnp.concatenate(
        [
            jnp.broadcast_to(q_gain, (H, HD)),
            jnp.broadcast_to(k_gain, (KV, HD)),
            jnp.ones((KV, HD), jnp.float32),
        ]
    )
    mine = (heads * gains).astype(jnp.bfloat16).reshape(share, QKV)
    qkv = gather_rows(mine, seq_count)
    queries = qkv[:, : H * HD]
    keys_new = qkv[:, H * HD : (H + KV) * HD]
    values_new = qkv[:, (H + KV) * HD :]

    query_groups = queries.reshape(rows_req, step_count, KV, group_size, HD)
    mask = live[:, None, None, None, :]
    keys = jnp.concatenate([prompt_keys, tail_keys]).reshape(-1, KV, HD)
    values = jnp.concatenate([prompt_values, tail_values]).reshape(-1, KV, HD)
    scores = jnp.einsum("rskgd,pkd->rskgp", query_groups, keys, preferred_element_type=jnp.float32)
    scores = jnp.where(mask, scores, NEGATIVE)
    block_top = jnp.max(scores, axis=4)
    probs = jnp.where(mask, jnp.exp(scores - block_top[..., None]), 0.0)
    block_total = jnp.sum(probs, axis=4)
    block_accum = jnp.einsum(
        "rskgp,pkd->rskgd",
        probs.astype(jnp.bfloat16),
        values,
        preferred_element_type=jnp.float32,
    )

    stats = split_three(jnp.stack([block_top, block_total])).reshape(6, tokens, H)
    per_head = seq_count // H
    stats = jnp.repeat(stats.transpose(2, 0, 1).reshape(H, -1, out_rows), per_head, axis=0)
    accum_blocks = (
        block_accum.astype(jnp.bfloat16).reshape(tokens, seq_count, out_rows).transpose(1, 0, 2)
    )
    got = exchange(jnp.concatenate([accum_blocks, stats], axis=1), "seq")
    got_accum = got[:, :tokens].astype(jnp.float32)
    got_stats = got[:, tokens:].astype(jnp.float32).reshape(seq_count, 2 * 3, tokens)
    got_top = got_stats[:, 0] + got_stats[:, 2] + got_stats[:, 4]
    got_total = got_stats[:, 1] + got_stats[:, 3] + got_stats[:, 5]

    first_col = seq_index * out_rows
    head = first_col // HD
    kv_head = head // group_size
    head_queries = lax.dynamic_slice_in_dim(queries, head * HD, HD, 1)
    head_keys = lax.dynamic_slice_in_dim(keys_new, kv_head * HD, HD, 1)
    head_values = lax.dynamic_slice_in_dim(
        values_new, kv_head * HD + first_col % HD, out_rows, 1
    ).astype(jnp.float32)
    new_scores = jnp.dot(head_queries, head_keys.T, preferred_element_type=jnp.float32)
    token_ids = jnp.arange(tokens, dtype=jnp.int32)
    causal = (token_ids[:, None] // step_count == token_ids[None, :] // step_count) & (
        token_ids[:, None] >= token_ids[None, :]
    )
    new_scores = jnp.where(causal, new_scores, NEGATIVE)
    highest = jnp.maximum(jnp.max(got_top, axis=0), jnp.max(new_scores, axis=1))
    weights = jnp.exp(got_top - highest[None])
    new_probs = jnp.where(causal, jnp.exp(new_scores - highest[:, None]), 0.0)
    denominator = jnp.sum(got_total * weights, axis=0) + jnp.sum(new_probs, axis=1)
    numerator = jnp.sum(got_accum * weights[..., None], axis=0) + jnp.dot(
        new_probs, head_values, precision=lax.Precision.HIGHEST
    )
    return (numerator / denominator[:, None]).astype(jnp.bfloat16)


def on_device(
    req_count,
    seq_count,
    hidden_in,
    attn_gain,
    q_gain,
    k_gain,
    post_attn_gain,
    ffn_gain,
    post_ffn_gain,
    w_qkv,
    w_out,
    w_gate,
    w_up,
    w_down,
    prompt_keys,
    prompt_values,
    tail_keys,
    tail_values,
    group_of,
    prompt_lengths,
    tail_lengths,
    page_table,
):
    seq_index = lax.axis_index("seq")
    req_index = lax.axis_index("req")
    rows_req, step_count, _ = hidden_in.shape
    group_size = H // KV
    tokens = rows_req * step_count
    share = tokens // seq_count

    def shifted(values):
        return [values] + [
            lax.ppermute(values, "req", [(i, (i + j) % req_count) for i in range(req_count)])
            for j in range(1, req_count)
        ]

    where = jnp.stack([seq_index, req_index]).astype(jnp.int32)
    in_rows = w_qkv.shape[0]
    out_rows = w_out.shape[0]
    if in_rows % 128 == 0:
        normed_cols = call(
            norm_columns_kernel,
            "norm_columns",
            jax.ShapeDtypeStruct((tokens, in_rows), jnp.bfloat16),
            seq_index.astype(jnp.int32).reshape(1),
            hidden_in,
            attn_gain.reshape(1, D),
            limit=56,
        )
    else:
        normed = (normalize(hidden_in.astype(jnp.float32)) * attn_gain).astype(jnp.bfloat16)
        normed_cols = lax.dynamic_slice_in_dim(normed, seq_index * in_rows, in_rows, 2)
        normed_cols = normed_cols.reshape(tokens, in_rows)
    normed_all = lax.all_gather(normed_cols, "req", axis=0, tiled=True)
    out_blocks = shifted(w_out)
    width = w_gate.shape[1]
    pieces = [w_down[:, c : c + width] for c in range(0, w_down.shape[1], width)]
    packed = shifted(jnp.concatenate([w_gate, w_up] + pieces))[1:]

    qkv_part = jnp.dot(normed_all, w_qkv, preferred_element_type=jnp.float32)
    qkv_cols = w_qkv.shape[1]
    qkv_blocks = (
        (qkv_part * LINK_SCALE)
        .astype(jnp.float16)
        .reshape(req_count * seq_count, share, qkv_cols)
    )
    qkv_got = exchange(qkv_blocks, ("req", "seq"))
    qkv_got = qkv_got.reshape(req_count, seq_count, share, qkv_cols)
    projected = jnp.sum(qkv_got.astype(jnp.float32), axis=1) * (1.0 / LINK_SCALE)
    live = live_rows(
        seq_index, prompt_keys.shape[:2], tail_keys.shape[1], group_of, prompt_lengths,
        tail_lengths, page_table,
    )
    caches = [
        array.reshape(-1, KV * HD) for array in (prompt_keys, prompt_values, tail_keys, tail_values)
    ]
    direct = share == step_count and out_rows % 128 == 0 and tokens == 64 and qkv_cols % HD == 0
    if direct:
        q_blocks, new_keys, new_values = call(
            head_norm_kernel,
            "head_norm",
            (
                jax.ShapeDtypeStruct((seq_count, share, H * HD), jnp.bfloat16),
                jax.ShapeDtypeStruct((8, KV * HD), jnp.float32),
                jax.ShapeDtypeStruct((8, KV * HD), jnp.float32),
            ),
            where,
            projected,
            jnp.stack([q_gain, k_gain]),
        )
        q_got, out_blocks = tie(exchange(q_blocks, "seq"), out_blocks)
        live = jnp.repeat(live.astype(jnp.float32), step_count, axis=0)
        sent = call(
            functools.partial(block_kernel, step_count),
            "block_attention",
            jax.ShapeDtypeStruct((seq_count, tokens + 16, out_rows), jnp.bfloat16),
            where,
            q_got,
            live,
            new_keys,
            new_values,
            jnp.concatenate([caches[0], caches[2]]),
            jnp.concatenate([caches[1], caches[3]]),
        )
        got = exchange(sent, "seq")
        out_part = call(
            functools.partial(out_kernel, req_count),
            "combine_out",
            jax.ShapeDtypeStruct((seq_count, share, D), jnp.bfloat16),
            where,
            got,
            *out_blocks,
            scratch=[pltpu.VMEM((128, 128), jnp.float32)],
        )
    else:
        projected = projected.transpose(1, 0, 2).reshape(share, QKV)
        attention_cols = general_attention(
            seq_index, seq_count, rows_req, step_count, out_rows, projected, q_gain, k_gain,
            live, *caches,
        )
        out_part = jnp.concatenate(
            [jnp.dot(attention_cols, w, preferred_element_type=jnp.float32) for w in out_blocks],
            axis=1,
        )
        out_part = out_part.astype(jnp.bfloat16).reshape(seq_count, share, D)
    ffn_blocks, residual = call(
        functools.partial(residual_kernel, req_count),
        "residual_norms",
        (
            jax.ShapeDtypeStruct((seq_count, share, D), jnp.bfloat16),
            jax.ShapeDtypeStruct((share, D), jnp.float32),
        ),
        where,
        exchange(out_part, "seq"),
        hidden_in.reshape(seq_count, share, D),
        post_attn_gain.reshape(1, D),
        ffn_gain.reshape(1, D),
    )
    ffn_in = exchange(ffn_blocks, "seq")
    gate_rows = w_gate.shape[0]
    chunk_count = 2 * len(chunks_of(gate_rows))
    x_shape = (seq_count, share, gate_rows)
    own_part = call(
        functools.partial(own_kernel, req_count),
        "own_gate_up",
        jax.ShapeDtypeStruct((2, tokens, width), jnp.float32),
        where,
        ffn_in,
        w_gate,
        w_up,
        scratch=[
            pltpu.VMEM(x_shape, jnp.bfloat16),
            pltpu.VMEM((2,) + w_gate.shape, jnp.bfloat16),
            pltpu.SemaphoreType.DMA((1 + chunk_count,)),
        ],
        hbm_from=1,
        limit=56,
    )
    copy_count = (req_count - 1) * (1 + chunk_count) + 1 + D // width
    down_part = call(
        functools.partial(ffn_kernel, req_count, gate_rows),
        "feed_forward",
        jax.ShapeDtypeStruct((seq_count, share, D), jnp.bfloat16),
        where,
        ffn_in,
        own_part,
        w_down,
        *packed,
        scratch=[
            pltpu.VMEM((req_count - 1,) + x_shape, jnp.bfloat16),
            pltpu.VMEM((2, tokens, width), jnp.float32),
            pltpu.VMEM((D // width, w_down.shape[0], width), jnp.bfloat16),
            pltpu.VMEM((D // width, seq_count, share, width), jnp.bfloat16),
            pltpu.VMEM((req_count - 1, 2 * gate_rows, width), jnp.bfloat16),
            pltpu.SemaphoreType.DMA((copy_count + D // width,)),
        ],
        hbm_from=1,
        out_space=pltpu.HBM,
        limit=56,
    )
    layer_blocks = call(
        functools.partial(last_kernel, req_count),
        "last_norm",
        jax.ShapeDtypeStruct((seq_count, share, D), jnp.bfloat16),
        where,
        exchange(down_part, "seq"),
        residual,
        post_ffn_gain.reshape(1, D),
    )
    return exchange(layer_blocks, "seq").reshape(rows_req, step_count, D)


def solution(mesh):
    return jax.shard_map(
        functools.partial(on_device, mesh.shape["req"], mesh.shape["seq"]),
        mesh=mesh,
        in_specs=(
            P("req", None, None),
            P(),
            P(),
            P(),
            P(),
            P(),
            P(),
            P("seq", "req"),
            P("seq", "req"),
            P("req", "seq"),
            P("req", "seq"),
            P("seq", "req"),
            P("req", "seq", None),
            P("req", "seq", None),
            P("req", "seq", None),
            P("req", "seq", None),
            P("req"),
            P("req"),
            P("req"),
            P("req", None),
        ),
        out_specs=P("req", None, None),
        check_vma=False,
    )
```

```python
import functools

import jax
import jax.numpy as jnp
from jax import lax
from jax.experimental import pallas as pl
from jax.experimental.pallas import tpu as pltpu
from jax.sharding import PartitionSpec as P

D = 2048
H = 8
KV = 2
HD = 256
PAGE = 16
QKV = 3072


EPSILON = 1e-06
NEGATIVE = -1e30
LINK_SCALE = 512.0


def normalize(values):
    return values * lax.rsqrt(jnp.mean(values * values, axis=-1, keepdims=True) + EPSILON)


def split_three(values):
    high = values.astype(jnp.bfloat16)
    rest = values - high.astype(jnp.float32)
    middle = rest.astype(jnp.bfloat16)
    low = (rest - middle.astype(jnp.float32)).astype(jnp.bfloat16)
    return jnp.stack([high, middle, low])


def exchange(blocks, axes, groups=None):
    return lax.all_to_all(
        blocks, axes, split_axis=0, concat_axis=0, tiled=True, axis_index_groups=groups
    )


def tie(*arrays):
    return lax.optimization_barrier(arrays)


def spread(block, copies):
    return jnp.broadcast_to(block[None], (copies,) + block.shape)


def gather_rows(rows, count):
    return exchange(spread(rows, count), "seq").reshape(count * rows.shape[0], rows.shape[1])


def call(
    kernel, name, out_shape, *operands, scratch=(), hbm_from=None, out_space=pltpu.VMEM, limit=16
):
    in_specs = [pl.BlockSpec(memory_space=pltpu.SMEM)]
    for i in range(1, len(operands)):
        space = pltpu.HBM if hbm_from is not None and i >= hbm_from else pltpu.VMEM
        in_specs.append(pl.BlockSpec(memory_space=space))
    return pl.pallas_call(
        kernel,
        name=name,
        out_shape=out_shape,
        in_specs=in_specs,
        out_specs=jax.tree.map(lambda _: pl.BlockSpec(memory_space=out_space), out_shape),
        scratch_shapes=scratch,
        compiler_params=pltpu.CompilerParams(vmem_limit_bytes=limit * 1024 * 1024),
    )(*operands)


def norm_columns_kernel(where_ref, hidden_ref, gain_ref, out_ref):
    columns = out_ref.shape[1]
    hidden = hidden_ref[...].astype(jnp.float32)
    scale = lax.rsqrt(jnp.mean(hidden * hidden, axis=-1, keepdims=True) + EPSILON)
    cols = pl.ds(pl.multiple_of(where_ref[0] * columns, columns), columns)
    normed = hidden_ref[:, :, cols].astype(jnp.float32) * scale * gain_ref[:, cols]
    out_ref[...] = normed.reshape(out_ref.shape).astype(jnp.bfloat16)


def head_norm_kernel(where_ref, projected_ref, gains_ref, q_ref, k_ref, v_ref):
    width = projected_ref.shape[2]
    copies, rows, _ = q_ref.shape
    fill = jnp.zeros((k_ref.shape[0] - rows, HD), jnp.float32)
    for head in range(H + 2 * KV):
        half, first = divmod(head * HD, width)
        values = normalize(projected_ref[half, :, first : first + HD])
        if head < H:
            values = (values * gains_ref[0:1, :]).astype(jnp.bfloat16)
            for i in range(copies):
                q_ref[i, :, head * HD : (head + 1) * HD] = values
        else:
            if head < H + KV:
                values = values * gains_ref[1:2, :]
            values = values.astype(jnp.bfloat16).astype(jnp.float32)
            target, slot = (k_ref, head - H) if head < H + KV else (v_ref, head - H - KV)
            target[:, slot * HD : (slot + 1) * HD] = jnp.concatenate([values, fill])


def dot_last(a, b):
    return lax.dot_general(a, b, (((1,), (1,)), ((), ())), preferred_element_type=jnp.float32)


def block_kernel(
    step_count,
    where_ref,
    q_ref,
    live_ref,
    new_k_ref,
    new_v_ref,
    keys_ref,
    values_ref,
    out_ref,
):
    copies, steps, _ = q_ref.shape
    tokens = copies * steps
    columns = out_ref.shape[2]
    group = H // KV
    queries = q_ref[...].reshape(tokens, H * HD)
    live = jnp.concatenate([live_ref[...]] * group) > 0.5
    first_token = where_ref[0] * step_count
    shape = (group * tokens, new_k_ref.shape[0])
    step = lax.broadcasted_iota(jnp.int32, shape, 0) % tokens - first_token
    new_index = lax.broadcasted_iota(jnp.int32, shape, 1)
    new_live = (step >= new_index) & (step < step_count)
    for kv in range(KV):
        span = slice(kv * HD, (kv + 1) * HD)
        q = jnp.concatenate(
            [queries[:, (kv * group + g) * HD : (kv * group + g + 1) * HD] for g in range(group)]
        )
        scores = jnp.where(live, dot_last(q, keys_ref[:, span]), NEGATIVE)
        top = jnp.max(scores, axis=1, keepdims=True)
        probs = jnp.where(live, jnp.exp(scores - top), 0.0)
        total = jnp.sum(probs, axis=1, keepdims=True)
        accum = jnp.dot(
            probs.astype(jnp.bfloat16), values_ref[:, span], preferred_element_type=jnp.float32
        )
        new_scores = dot_last(q, new_k_ref[:, span].astype(jnp.bfloat16))
        new_scores = jnp.where(new_live, new_scores, NEGATIVE)
        both = jnp.maximum(top, jnp.max(new_scores, axis=1, keepdims=True))
        carried = jnp.exp(top - both)
        new_probs = jnp.where(new_live, jnp.exp(new_scores - both), 0.0)
        total = total * carried + jnp.sum(new_probs, axis=1, keepdims=True)
        accum = accum * carried
        for u in range(step_count):
            accum = accum + new_probs[:, u : u + 1] * new_v_ref[u : u + 1, span]
        sent = accum.astype(jnp.bfloat16)
        parts = []
        for value in (both, total):
            for _ in range(3):
                part = value.astype(jnp.bfloat16).astype(jnp.float32)
                parts.append(part)
                value = value - part
        lane = lax.broadcasted_iota(jnp.int32, (group * tokens, 128), 1)
        wide = jnp.zeros((group * tokens, 128), jnp.float32)
        for i, part in enumerate(parts):
            wide = jnp.where(lane == i, part, wide)
        turned = jnp.transpose(wide)[:16].astype(jnp.bfloat16)
        for g in range(group):
            pair = turned[:, g // 2 * 128 : (g // 2 + 1) * 128]
            for part in range(HD // columns):
                target = (kv * group + g) * (HD // columns) + part
                out_ref[target, :tokens, :] = sent[
                    g * tokens : (g + 1) * tokens, part * columns : (part + 1) * columns
                ]
                out_ref[target, tokens:, :] = pair


def out_kernel(req_count, where_ref, got_ref, *refs):
    w_refs = refs[:req_count]
    out_ref, turned_ref = refs[req_count:]
    blocks = got_ref.shape[0]
    copies, steps, _ = out_ref.shape
    tokens = copies * steps
    columns = got_ref.shape[2]
    head = where_ref[0] * columns // HD
    stats = got_ref[:, tokens:, :].astype(jnp.float32)
    tops = stats[:, 0, :] + stats[:, 1, :] + stats[:, 2, :]
    totals = stats[:, 3, :] + stats[:, 4, :] + stats[:, 5, :]
    rest = jnp.zeros((128 - 2 * blocks, 128), jnp.float32)
    turned_ref[...] = jnp.transpose(jnp.concatenate([tops, totals, rest]))
    mine = turned_ref[pl.ds(pl.multiple_of(head % 2 * tokens, tokens), tokens), :]
    tops = mine[:, :blocks]
    highest = jnp.max(tops, axis=1, keepdims=True)
    weights = jnp.exp(tops - highest)
    denominator = jnp.sum(mine[:, blocks : 2 * blocks] * weights, axis=1, keepdims=True)
    numerator = jnp.zeros((tokens, columns), jnp.float32)
    for b in range(blocks):
        numerator = numerator + got_ref[b, :tokens, :].astype(jnp.float32) * weights[:, b : b + 1]
    attention = (numerator / denominator).astype(jnp.bfloat16)
    for j, w_ref in enumerate(w_refs):
        width = w_ref.shape[1]
        part = jnp.dot(attention, w_ref[...], preferred_element_type=jnp.float32)
        part = part.astype(jnp.bfloat16)
        for i in range(copies):
            out_ref[i, :, j * width : (j + 1) * width] = part[i * steps : (i + 1) * steps]


def summed(req_count, where_ref, got_ref):
    width = got_ref.shape[2] // req_count
    blocks = []
    for i in range(req_count):
        j = lax.rem(where_ref[1] - i + req_count, req_count)
        cols = pl.ds(pl.multiple_of(j * width, width), width)
        blocks.append(jnp.sum(got_ref[:, :, cols].astype(jnp.float32), axis=0))
    return jnp.concatenate(blocks, axis=1)


def residual_kernel(
    req_count, where_ref, got_ref, hidden_ref, post_gain_ref, ffn_gain_ref, out_ref, residual_ref
):
    attn_out = summed(req_count, where_ref, got_ref)
    hidden = hidden_ref[where_ref[0]].astype(jnp.float32)
    residual = hidden + normalize(attn_out) * post_gain_ref[...]
    residual_ref[...] = residual
    ffn_in = (normalize(residual) * ffn_gain_ref[...]).astype(jnp.bfloat16)
    for i in range(out_ref.shape[0]):
        out_ref[i] = ffn_in


def last_kernel(req_count, where_ref, got_ref, residual_ref, gain_ref, out_ref):
    down_out = summed(req_count, where_ref, got_ref)
    layer = (residual_ref[...] + normalize(down_out) * gain_ref[...]).astype(jnp.bfloat16)
    for i in range(out_ref.shape[0]):
        out_ref[i] = layer


def start_copies(moves, sem_ref):
    copies = [
        pltpu.make_async_copy(source, target, sem_ref.at[i])
        for i, (source, target) in enumerate(moves)
    ]
    for copy in copies:
        copy.start()
    return copies


def chunks_of(rows):
    size = min(rows, 256)
    return [(first, size) for first in range(0, rows, size)]


def x_columns(x_ref, where_ref, req_count, j, rows):
    start = lax.rem(where_ref[1] - j + req_count, req_count) * rows
    return x_ref.at[:, :, pl.ds(pl.multiple_of(start, rows), rows)]


def chunked_dot(x, held, chunks, waits):
    total = None
    for first, size in chunks:
        next(waits).wait()
        part = jnp.dot(
            x[:, first : first + size],
            held[first : first + size, :],
            preferred_element_type=jnp.float32,
        )
        total = part if total is None else total + part
    return total


def own_kernel(req_count, where_ref, x_ref, gate_ref, up_ref, out_ref, x_held, held, sem_ref):
    rows = gate_ref.shape[0]
    chunks = chunks_of(rows)
    moves = [(x_columns(x_ref, where_ref, req_count, 0, rows), x_held)]
    for i, w_ref in enumerate((gate_ref, up_ref)):
        for first, size in chunks:
            span = pl.ds(first, size)
            moves.append((w_ref.at[span, :], held.at[i, span, :]))
    waits = iter(start_copies(moves, sem_ref))
    blocks, steps, _ = x_held.shape
    next(waits).wait()
    x = x_held[...].reshape(blocks * steps, rows)
    for i in range(2):
        out_ref[i] = chunked_dot(x, held.at[i], chunks, waits)


def ffn_kernel(req_count, gate_rows, where_ref, x_ref, own_ref, down_ref, *refs):
    others = req_count - 1
    packed_refs = refs[:others]
    out_ref, x_held, own_held, downs, parts_ref, held, sem_ref = refs[others:]
    down_rows, width = downs.shape[1:]
    piece_count = down_ref.shape[1] // width
    chunks = chunks_of(gate_rows)
    moves = []
    for j in range(others):
        moves.append((x_columns(x_ref, where_ref, req_count, j + 1, gate_rows), x_held.at[j]))
        for i in range(2):
            for first, size in chunks:
                span = pl.ds(i * gate_rows + first, size)
                moves.append((packed_refs[j].at[span, :], held.at[j, span, :]))
    moves.append((own_ref, own_held))
    for piece in range(piece_count):
        moves.append((down_ref.at[:, pl.ds(piece * width, width)], downs.at[piece]))
    for j in range(others):
        for piece in range(piece_count):
            span = pl.ds(2 * gate_rows + piece * down_rows, down_rows)
            moves.append((packed_refs[j].at[span, :], downs.at[(j + 1) * piece_count + piece]))
    copies = start_copies(moves, sem_ref)
    waits = iter(copies)
    _, blocks, steps, _ = x_held.shape
    gates, ups = [], []
    for j in range(others):
        next(waits).wait()
        x = x_held[j].reshape(blocks * steps, gate_rows)
        gates.append(chunked_dot(x, held.at[j, pl.ds(0, gate_rows)], chunks, waits))
        ups.append(chunked_dot(x, held.at[j, pl.ds(gate_rows, gate_rows)], chunks, waits))
    next(waits).wait()
    gate_out, up_out = own_held[0], own_held[1]
    for gate, up in zip(gates, ups):
        gate_out = gate_out + gate
        up_out = up_out + up
    activated = (jax.nn.gelu(gate_out, approximate=True) * up_out).astype(jnp.bfloat16)
    sends = []
    for index in range(req_count * piece_count):
        next(waits).wait()
        part = jnp.dot(activated, downs[index], preferred_element_type=jnp.float32)
        part = part.astype(jnp.bfloat16)
        for i in range(blocks):
            parts_ref[index, i] = part[i * steps : (i + 1) * steps]
        sends.append(
            pltpu.make_async_copy(
                parts_ref.at[index],
                out_ref.at[:, :, pl.ds(index * width, width)],
                sem_ref.at[len(copies) + index],
            )
        )
        sends[-1].start()
    for send in sends:
        send.wait()


def live_rows(
    seq_index, prompt_shape, pool_rows, group_of, prompt_lengths, tail_lengths, page_table
):
    group_count, prompt_span = prompt_shape
    rows_req = group_of.shape[0]
    member = (group_of % group_count)[:, None] == jnp.arange(group_count, dtype=jnp.int32)[None, :]
    prompt_pos = seq_index * prompt_span + jnp.arange(prompt_span, dtype=jnp.int32)
    prompt_live = prompt_pos[None, :] < prompt_lengths[:, None]
    prompt_mask = (member[:, :, None] & prompt_live[None, :, :]).reshape(
        rows_req, group_count * prompt_span
    )
    slot_count = pool_rows // PAGE
    table_row = page_table[0]
    table_len = table_row.shape[0]
    tail_pages = table_len // rows_req
    slot_ids = seq_index * slot_count + jnp.arange(slot_count, dtype=jnp.int32)
    matches = table_row[None, :] == slot_ids[:, None]
    entries = jnp.sum(
        jnp.where(matches, jnp.arange(table_len, dtype=jnp.int32)[None, :], 0), axis=1
    )
    owners = jnp.repeat(entries // tail_pages, PAGE)
    tail_pos = jnp.repeat(entries % tail_pages, PAGE) * PAGE + jnp.tile(
        jnp.arange(PAGE, dtype=jnp.int32), slot_count
    )
    tail_mask = (owners[None, :] == jnp.arange(rows_req, dtype=jnp.int32)[:, None]) & (
        tail_pos[None, :] < tail_lengths[:, None]
    )
    return jnp.concatenate([prompt_mask, tail_mask], axis=1)


def general_attention(
    seq_index,
    seq_count,
    rows_req,
    step_count,
    out_rows,
    projected,
    q_gain,
    k_gain,
    live,
    prompt_keys,
    prompt_values,
    tail_keys,
    tail_values,
):
    group_size = H // KV
    share = projected.shape[0]
    tokens = rows_req * step_count
    heads = normalize(projected.reshape(share, QKV // HD, HD))
    gains = jnp.concatenate(
        [
            jnp.broadcast_to(q_gain, (H, HD)),
            jnp.broadcast_to(k_gain, (KV, HD)),
            jnp.ones((KV, HD), jnp.float32),
        ]
    )
    mine = (heads * gains).astype(jnp.bfloat16).reshape(share, QKV)
    qkv = gather_rows(mine, seq_count)
    queries = qkv[:, : H * HD]
    keys_new = qkv[:, H * HD : (H + KV) * HD]
    values_new = qkv[:, (H + KV) * HD :]

    query_groups = queries.reshape(rows_req, step_count, KV, group_size, HD)
    mask = live[:, None, None, None, :]
    keys = jnp.concatenate([prompt_keys, tail_keys]).reshape(-1, KV, HD)
    values = jnp.concatenate([prompt_values, tail_values]).reshape(-1, KV, HD)
    scores = jnp.einsum("rskgd,pkd->rskgp", query_groups, keys, preferred_element_type=jnp.float32)
    scores = jnp.where(mask, scores, NEGATIVE)
    block_top = jnp.max(scores, axis=4)
    probs = jnp.where(mask, jnp.exp(scores - block_top[..., None]), 0.0)
    block_total = jnp.sum(probs, axis=4)
    block_accum = jnp.einsum(
        "rskgp,pkd->rskgd",
        probs.astype(jnp.bfloat16),
        values,
        preferred_element_type=jnp.float32,
    )

    stats = split_three(jnp.stack([block_top, block_total])).reshape(6, tokens, H)
    per_head = seq_count // H
    stats = jnp.repeat(stats.transpose(2, 0, 1).reshape(H, -1, out_rows), per_head, axis=0)
    accum_blocks = (
        block_accum.astype(jnp.bfloat16).reshape(tokens, seq_count, out_rows).transpose(1, 0, 2)
    )
    got = exchange(jnp.concatenate([accum_blocks, stats], axis=1), "seq")
    got_accum = got[:, :tokens].astype(jnp.float32)
    got_stats = got[:, tokens:].astype(jnp.float32).reshape(seq_count, 2 * 3, tokens)
    got_top = got_stats[:, 0] + got_stats[:, 2] + got_stats[:, 4]
    got_total = got_stats[:, 1] + got_stats[:, 3] + got_stats[:, 5]

    first_col = seq_index * out_rows
    head = first_col // HD
    kv_head = head // group_size
    head_queries = lax.dynamic_slice_in_dim(queries, head * HD, HD, 1)
    head_keys = lax.dynamic_slice_in_dim(keys_new, kv_head * HD, HD, 1)
    head_values = lax.dynamic_slice_in_dim(
        values_new, kv_head * HD + first_col % HD, out_rows, 1
    ).astype(jnp.float32)
    new_scores = jnp.dot(head_queries, head_keys.T, preferred_element_type=jnp.float32)
    token_ids = jnp.arange(tokens, dtype=jnp.int32)
    causal = (token_ids[:, None] // step_count == token_ids[None, :] // step_count) & (
        token_ids[:, None] >= token_ids[None, :]
    )
    new_scores = jnp.where(causal, new_scores, NEGATIVE)
    highest = jnp.maximum(jnp.max(got_top, axis=0), jnp.max(new_scores, axis=1))
    weights = jnp.exp(got_top - highest[None])
    new_probs = jnp.where(causal, jnp.exp(new_scores - highest[:, None]), 0.0)
    denominator = jnp.sum(got_total * weights, axis=0) + jnp.sum(new_probs, axis=1)
    numerator = jnp.sum(got_accum * weights[..., None], axis=0) + jnp.dot(
        new_probs, head_values, precision=lax.Precision.HIGHEST
    )
    return (numerator / denominator[:, None]).astype(jnp.bfloat16)


def on_device(
    req_count,
    seq_count,
    hidden_in,
    attn_gain,
    q_gain,
    k_gain,
    post_attn_gain,
    ffn_gain,
    post_ffn_gain,
    w_qkv,
    w_out,
    w_gate,
    w_up,
    w_down,
    prompt_keys,
    prompt_values,
    tail_keys,
    tail_values,
    group_of,
    prompt_lengths,
    tail_lengths,
    page_table,
):
    seq_index = lax.axis_index("seq")
    req_index = lax.axis_index("req")
    rows_req, step_count, _ = hidden_in.shape
    group_size = H // KV
    tokens = rows_req * step_count
    share = tokens // seq_count

    def shifted(values):
        return [values] + [
            lax.ppermute(values, "req", [(i, (i + j) % req_count) for i in range(req_count)])
            for j in range(1, req_count)
        ]

    where = jnp.stack([seq_index, req_index]).astype(jnp.int32)
    in_rows = w_qkv.shape[0]
    out_rows = w_out.shape[0]
    if in_rows % 128 == 0:
        normed_cols = call(
            norm_columns_kernel,
            "norm_columns",
            jax.ShapeDtypeStruct((tokens, in_rows), jnp.bfloat16),
            seq_index.astype(jnp.int32).reshape(1),
            hidden_in,
            attn_gain.reshape(1, D),
            limit=56,
        )
    else:
        normed = (normalize(hidden_in.astype(jnp.float32)) * attn_gain).astype(jnp.bfloat16)
        normed_cols = lax.dynamic_slice_in_dim(normed, seq_index * in_rows, in_rows, 2)
        normed_cols = normed_cols.reshape(tokens, in_rows)
    normed_cols, w_out_late = tie(normed_cols, w_out)
    normed_blocks = shifted(normed_cols)
    ordered = []
    for i in range(req_count):
        chosen = normed_blocks[0]
        for j in range(1, req_count):
            chosen = jnp.where((req_index - i) % req_count == j, normed_blocks[j], chosen)
        ordered.append(chosen)
    normed_all = jnp.concatenate(ordered)
    out_blocks = shifted(w_out_late)
    width = w_gate.shape[1]
    pieces = [w_down[:, c : c + width] for c in range(0, w_down.shape[1], width)]
    packed = shifted(jnp.concatenate([w_gate, w_up] + pieces))[1:]

    qkv_part = jnp.dot(normed_all, w_qkv, preferred_element_type=jnp.float32)
    qkv_cols = w_qkv.shape[1]
    qkv_blocks = (
        (qkv_part * LINK_SCALE)
        .astype(jnp.float16)
        .reshape(req_count * seq_count, share, qkv_cols)
    )
    qkv_got = exchange(qkv_blocks, ("req", "seq"))
    qkv_got = qkv_got.reshape(req_count, seq_count, share, qkv_cols)
    projected = jnp.sum(qkv_got.astype(jnp.float32), axis=1) * (1.0 / LINK_SCALE)
    live = live_rows(
        seq_index, prompt_keys.shape[:2], tail_keys.shape[1], group_of, prompt_lengths,
        tail_lengths, page_table,
    )
    caches = [
        array.reshape(-1, KV * HD) for array in (prompt_keys, prompt_values, tail_keys, tail_values)
    ]
    direct = share == step_count and out_rows % 128 == 0 and tokens == 64 and qkv_cols % HD == 0
    if direct:
        q_blocks, new_keys, new_values = call(
            head_norm_kernel,
            "head_norm",
            (
                jax.ShapeDtypeStruct((seq_count, share, H * HD), jnp.bfloat16),
                jax.ShapeDtypeStruct((8, KV * HD), jnp.float32),
                jax.ShapeDtypeStruct((8, KV * HD), jnp.float32),
            ),
            where,
            projected,
            jnp.stack([q_gain, k_gain]),
        )
        q_got, out_blocks = tie(exchange(q_blocks, "seq"), out_blocks)
        live = jnp.repeat(live.astype(jnp.float32), step_count, axis=0)
        sent = call(
            functools.partial(block_kernel, step_count),
            "block_attention",
            jax.ShapeDtypeStruct((seq_count, tokens + 16, out_rows), jnp.bfloat16),
            where,
            q_got,
            live,
            new_keys,
            new_values,
            jnp.concatenate([caches[0], caches[2]]),
            jnp.concatenate([caches[1], caches[3]]),
        )
        got = exchange(sent, "seq")
        out_part = call(
            functools.partial(out_kernel, req_count),
            "combine_out",
            jax.ShapeDtypeStruct((seq_count, share, D), jnp.bfloat16),
            where,
            got,
            *out_blocks,
            scratch=[pltpu.VMEM((128, 128), jnp.float32)],
        )
    else:
        projected = projected.transpose(1, 0, 2).reshape(share, QKV)
        attention_cols = general_attention(
            seq_index, seq_count, rows_req, step_count, out_rows, projected, q_gain, k_gain,
            live, *caches,
        )
        out_part = jnp.concatenate(
            [jnp.dot(attention_cols, w, preferred_element_type=jnp.float32) for w in out_blocks],
            axis=1,
        )
        out_part = out_part.astype(jnp.bfloat16).reshape(seq_count, share, D)
    ffn_blocks, residual = call(
        functools.partial(residual_kernel, req_count),
        "residual_norms",
        (
            jax.ShapeDtypeStruct((seq_count, share, D), jnp.bfloat16),
            jax.ShapeDtypeStruct((share, D), jnp.float32),
        ),
        where,
        exchange(out_part, "seq"),
        hidden_in.reshape(seq_count, share, D),
        post_attn_gain.reshape(1, D),
        ffn_gain.reshape(1, D),
    )
    ffn_in = exchange(ffn_blocks, "seq")
    gate_rows = w_gate.shape[0]
    chunk_count = 2 * len(chunks_of(gate_rows))
    x_shape = (seq_count, share, gate_rows)
    own_part = call(
        functools.partial(own_kernel, req_count),
        "own_gate_up",
        jax.ShapeDtypeStruct((2, tokens, width), jnp.float32),
        where,
        ffn_in,
        w_gate,
        w_up,
        scratch=[
            pltpu.VMEM(x_shape, jnp.bfloat16),
            pltpu.VMEM((2,) + w_gate.shape, jnp.bfloat16),
            pltpu.SemaphoreType.DMA((1 + chunk_count,)),
        ],
        hbm_from=1,
        limit=56,
    )
    copy_count = (req_count - 1) * (1 + chunk_count) + 1 + D // width
    down_part = call(
        functools.partial(ffn_kernel, req_count, gate_rows),
        "feed_forward",
        jax.ShapeDtypeStruct((seq_count, share, D), jnp.bfloat16),
        where,
        ffn_in,
        own_part,
        w_down,
        *packed,
        scratch=[
            pltpu.VMEM((req_count - 1,) + x_shape, jnp.bfloat16),
            pltpu.VMEM((2, tokens, width), jnp.float32),
            pltpu.VMEM((D // width, w_down.shape[0], width), jnp.bfloat16),
            pltpu.VMEM((D // width, seq_count, share, width), jnp.bfloat16),
            pltpu.VMEM((req_count - 1, 2 * gate_rows, width), jnp.bfloat16),
            pltpu.SemaphoreType.DMA((copy_count + D // width,)),
        ],
        hbm_from=1,
        out_space=pltpu.HBM,
        limit=56,
    )
    layer_blocks = call(
        functools.partial(last_kernel, req_count),
        "last_norm",
        jax.ShapeDtypeStruct((seq_count, share, D), jnp.bfloat16),
        where,
        exchange(down_part, "seq"),
        residual,
        post_ffn_gain.reshape(1, D),
    )
    return exchange(layer_blocks, "seq").reshape(rows_req, step_count, D)


def solution(mesh):
    return jax.shard_map(
        functools.partial(on_device, mesh.shape["req"], mesh.shape["seq"]),
        mesh=mesh,
        in_specs=(
            P("req", None, None),
            P(),
            P(),
            P(),
            P(),
            P(),
            P(),
            P("seq", "req"),
            P("seq", "req"),
            P("req", "seq"),
            P("req", "seq"),
            P("seq", "req"),
            P("req", "seq", None),
            P("req", "seq", None),
            P("req", "seq", None),
            P("req", "seq", None),
            P("req"),
            P("req"),
            P("req"),
            P("req", None),
        ),
        out_specs=P("req", None, None),
        check_vma=False,
    )
```

```python
import functools

import jax
import jax.numpy as jnp
from jax import lax
from jax.experimental import pallas as pl
from jax.experimental.pallas import tpu as pltpu
from jax.sharding import PartitionSpec as P

D = 2048
H = 8
KV = 2
HD = 256
PAGE = 16
QKV = 3072


EPSILON = 1e-06
NEGATIVE = -1e30
LINK_SCALE = 512.0


def normalize(values):
    return values * lax.rsqrt(jnp.mean(values * values, axis=-1, keepdims=True) + EPSILON)


def split_three(values):
    high = values.astype(jnp.bfloat16)
    rest = values - high.astype(jnp.float32)
    middle = rest.astype(jnp.bfloat16)
    low = (rest - middle.astype(jnp.float32)).astype(jnp.bfloat16)
    return jnp.stack([high, middle, low])


def exchange(blocks, axes, groups=None):
    return lax.all_to_all(
        blocks, axes, split_axis=0, concat_axis=0, tiled=True, axis_index_groups=groups
    )


def tie(*arrays):
    return lax.optimization_barrier(arrays)


def spread(block, copies):
    return jnp.broadcast_to(block[None], (copies,) + block.shape)


def gather_rows(rows, count):
    return exchange(spread(rows, count), "seq").reshape(count * rows.shape[0], rows.shape[1])


def call(
    kernel, name, out_shape, *operands, scratch=(), hbm_from=None, out_space=pltpu.VMEM, limit=16
):
    in_specs = [pl.BlockSpec(memory_space=pltpu.SMEM)]
    for i in range(1, len(operands)):
        space = pltpu.HBM if hbm_from is not None and i >= hbm_from else pltpu.VMEM
        in_specs.append(pl.BlockSpec(memory_space=space))
    return pl.pallas_call(
        kernel,
        name=name,
        out_shape=out_shape,
        in_specs=in_specs,
        out_specs=jax.tree.map(lambda _: pl.BlockSpec(memory_space=out_space), out_shape),
        scratch_shapes=scratch,
        compiler_params=pltpu.CompilerParams(vmem_limit_bytes=limit * 1024 * 1024),
    )(*operands)


def norm_columns_kernel(where_ref, hidden_ref, gain_ref, out_ref):
    columns = out_ref.shape[1]
    hidden = hidden_ref[...].astype(jnp.float32)
    scale = lax.rsqrt(jnp.mean(hidden * hidden, axis=-1, keepdims=True) + EPSILON)
    cols = pl.ds(pl.multiple_of(where_ref[0] * columns, columns), columns)
    normed = hidden_ref[:, :, cols].astype(jnp.float32) * scale * gain_ref[:, cols]
    out_ref[...] = normed.reshape(out_ref.shape).astype(jnp.bfloat16)


def head_norm_kernel(where_ref, projected_ref, gains_ref, q_ref, k_ref, v_ref):
    width = projected_ref.shape[2]
    copies, rows, _ = q_ref.shape
    fill = jnp.zeros((k_ref.shape[0] - rows, HD), jnp.float32)
    for head in range(H + 2 * KV):
        half, first = divmod(head * HD, width)
        values = normalize(projected_ref[half, :, first : first + HD])
        if head < H:
            values = (values * gains_ref[0:1, :]).astype(jnp.bfloat16)
            for i in range(copies):
                q_ref[i, :, head * HD : (head + 1) * HD] = values
        else:
            if head < H + KV:
                values = values * gains_ref[1:2, :]
            values = values.astype(jnp.bfloat16).astype(jnp.float32)
            target, slot = (k_ref, head - H) if head < H + KV else (v_ref, head - H - KV)
            target[:, slot * HD : (slot + 1) * HD] = jnp.concatenate([values, fill])


def dot_last(a, b):
    return lax.dot_general(a, b, (((1,), (1,)), ((), ())), preferred_element_type=jnp.float32)


def block_kernel(
    step_count,
    where_ref,
    q_ref,
    live_ref,
    new_k_ref,
    new_v_ref,
    keys_ref,
    values_ref,
    out_ref,
):
    copies, steps, _ = q_ref.shape
    tokens = copies * steps
    columns = out_ref.shape[2]
    group = H // KV
    queries = q_ref[...].reshape(tokens, H * HD)
    live = jnp.concatenate([live_ref[...]] * group) > 0.5
    first_token = where_ref[0] * step_count
    shape = (group * tokens, new_k_ref.shape[0])
    step = lax.broadcasted_iota(jnp.int32, shape, 0) % tokens - first_token
    new_index = lax.broadcasted_iota(jnp.int32, shape, 1)
    new_live = (step >= new_index) & (step < step_count)
    for kv in range(KV):
        span = slice(kv * HD, (kv + 1) * HD)
        q = jnp.concatenate(
            [queries[:, (kv * group + g) * HD : (kv * group + g + 1) * HD] for g in range(group)]
        )
        scores = jnp.where(live, dot_last(q, keys_ref[:, span]), NEGATIVE)
        top = jnp.max(scores, axis=1, keepdims=True)
        probs = jnp.where(live, jnp.exp(scores - top), 0.0)
        total = jnp.sum(probs, axis=1, keepdims=True)
        accum = jnp.dot(
            probs.astype(jnp.bfloat16), values_ref[:, span], preferred_element_type=jnp.float32
        )
        new_scores = dot_last(q, new_k_ref[:, span].astype(jnp.bfloat16))
        new_scores = jnp.where(new_live, new_scores, NEGATIVE)
        both = jnp.maximum(top, jnp.max(new_scores, axis=1, keepdims=True))
        carried = jnp.exp(top - both)
        new_probs = jnp.where(new_live, jnp.exp(new_scores - both), 0.0)
        total = total * carried + jnp.sum(new_probs, axis=1, keepdims=True)
        accum = accum * carried
        for u in range(step_count):
            accum = accum + new_probs[:, u : u + 1] * new_v_ref[u : u + 1, span]
        sent = accum.astype(jnp.bfloat16)
        parts = []
        for value in (both, total):
            for _ in range(3):
                part = value.astype(jnp.bfloat16).astype(jnp.float32)
                parts.append(part)
                value = value - part
        lane = lax.broadcasted_iota(jnp.int32, (group * tokens, 128), 1)
        wide = jnp.zeros((group * tokens, 128), jnp.float32)
        for i, part in enumerate(parts):
            wide = jnp.where(lane == i, part, wide)
        turned = jnp.transpose(wide)[:16].astype(jnp.bfloat16)
        for g in range(group):
            pair = turned[:, g // 2 * 128 : (g // 2 + 1) * 128]
            for part in range(HD // columns):
                target = (kv * group + g) * (HD // columns) + part
                out_ref[target, :tokens, :] = sent[
                    g * tokens : (g + 1) * tokens, part * columns : (part + 1) * columns
                ]
                out_ref[target, tokens:, :] = pair


def out_kernel(req_count, where_ref, got_ref, *refs):
    w_refs = refs[:req_count]
    out_ref, turned_ref = refs[req_count:]
    blocks = got_ref.shape[0]
    copies, steps, _ = out_ref.shape
    tokens = copies * steps
    columns = got_ref.shape[2]
    head = where_ref[0] * columns // HD
    stats = got_ref[:, tokens:, :].astype(jnp.float32)
    tops = stats[:, 0, :] + stats[:, 1, :] + stats[:, 2, :]
    totals = stats[:, 3, :] + stats[:, 4, :] + stats[:, 5, :]
    rest = jnp.zeros((128 - 2 * blocks, 128), jnp.float32)
    turned_ref[...] = jnp.transpose(jnp.concatenate([tops, totals, rest]))
    mine = turned_ref[pl.ds(pl.multiple_of(head % 2 * tokens, tokens), tokens), :]
    tops = mine[:, :blocks]
    highest = jnp.max(tops, axis=1, keepdims=True)
    weights = jnp.exp(tops - highest)
    denominator = jnp.sum(mine[:, blocks : 2 * blocks] * weights, axis=1, keepdims=True)
    numerator = jnp.zeros((tokens, columns), jnp.float32)
    for b in range(blocks):
        numerator = numerator + got_ref[b, :tokens, :].astype(jnp.float32) * weights[:, b : b + 1]
    attention = (numerator / denominator).astype(jnp.bfloat16)
    for j, w_ref in enumerate(w_refs):
        width = w_ref.shape[1]
        part = jnp.dot(attention, w_ref[...], preferred_element_type=jnp.float32)
        part = part.astype(jnp.bfloat16)
        for i in range(copies):
            out_ref[i, :, j * width : (j + 1) * width] = part[i * steps : (i + 1) * steps]


def summed(req_count, where_ref, got_ref):
    width = got_ref.shape[2] // req_count
    blocks = []
    for i in range(req_count):
        j = lax.rem(where_ref[1] - i + req_count, req_count)
        cols = pl.ds(pl.multiple_of(j * width, width), width)
        blocks.append(jnp.sum(got_ref[:, :, cols].astype(jnp.float32), axis=0))
    return jnp.concatenate(blocks, axis=1)


def residual_kernel(
    req_count, where_ref, got_ref, hidden_ref, post_gain_ref, ffn_gain_ref, out_ref, residual_ref
):
    attn_out = summed(req_count, where_ref, got_ref)
    hidden = hidden_ref[where_ref[0]].astype(jnp.float32)
    residual = hidden + normalize(attn_out) * post_gain_ref[...]
    residual_ref[...] = residual
    ffn_in = (normalize(residual) * ffn_gain_ref[...]).astype(jnp.bfloat16)
    for i in range(out_ref.shape[0]):
        out_ref[i] = ffn_in


def last_kernel(req_count, where_ref, got_ref, residual_ref, gain_ref, out_ref):
    down_out = summed(req_count, where_ref, got_ref)
    layer = (residual_ref[...] + normalize(down_out) * gain_ref[...]).astype(jnp.bfloat16)
    for i in range(out_ref.shape[0]):
        out_ref[i] = layer


def start_copies(moves, sem_ref):
    copies = [
        pltpu.make_async_copy(source, target, sem_ref.at[i])
        for i, (source, target) in enumerate(moves)
    ]
    for copy in copies:
        copy.start()
    return copies


def chunks_of(rows):
    size = min(rows, 256)
    return [(first, size) for first in range(0, rows, size)]


def x_columns(x_ref, where_ref, req_count, j, rows):
    start = lax.rem(where_ref[1] - j + req_count, req_count) * rows
    return x_ref.at[:, :, pl.ds(pl.multiple_of(start, rows), rows)]


def chunked_dot(x, held, chunks, waits):
    total = None
    for first, size in chunks:
        next(waits).wait()
        part = jnp.dot(
            x[:, first : first + size],
            held[first : first + size, :],
            preferred_element_type=jnp.float32,
        )
        total = part if total is None else total + part
    return total


def own_kernel(req_count, where_ref, x_ref, gate_ref, up_ref, out_ref, x_held, held, sem_ref):
    rows = gate_ref.shape[0]
    chunks = chunks_of(rows)
    moves = [(x_columns(x_ref, where_ref, req_count, 0, rows), x_held)]
    for i, w_ref in enumerate((gate_ref, up_ref)):
        for first, size in chunks:
            span = pl.ds(first, size)
            moves.append((w_ref.at[span, :], held.at[i, span, :]))
    waits = iter(start_copies(moves, sem_ref))
    blocks, steps, _ = x_held.shape
    next(waits).wait()
    x = x_held[...].reshape(blocks * steps, rows)
    for i in range(2):
        out_ref[i] = chunked_dot(x, held.at[i], chunks, waits)


def ffn_kernel(req_count, gate_rows, where_ref, x_ref, own_ref, down_ref, *refs):
    others = req_count - 1
    packed_refs = refs[:others]
    out_ref, x_held, own_held, downs, parts_ref, held, sem_ref = refs[others:]
    down_rows, width = downs.shape[1:]
    piece_count = down_ref.shape[1] // width
    chunks = chunks_of(gate_rows)
    moves = []
    for j in range(others):
        moves.append((x_columns(x_ref, where_ref, req_count, j + 1, gate_rows), x_held.at[j]))
        for i in range(2):
            for first, size in chunks:
                span = pl.ds(i * gate_rows + first, size)
                moves.append((packed_refs[j].at[span, :], held.at[j, span, :]))
    moves.append((own_ref, own_held))
    for piece in range(piece_count):
        moves.append((down_ref.at[:, pl.ds(piece * width, width)], downs.at[piece]))
    for j in range(others):
        for piece in range(piece_count):
            span = pl.ds(2 * gate_rows + piece * down_rows, down_rows)
            moves.append((packed_refs[j].at[span, :], downs.at[(j + 1) * piece_count + piece]))
    copies = start_copies(moves, sem_ref)
    waits = iter(copies)
    _, blocks, steps, _ = x_held.shape
    gates, ups = [], []
    for j in range(others):
        next(waits).wait()
        x = x_held[j].reshape(blocks * steps, gate_rows)
        gates.append(chunked_dot(x, held.at[j, pl.ds(0, gate_rows)], chunks, waits))
        ups.append(chunked_dot(x, held.at[j, pl.ds(gate_rows, gate_rows)], chunks, waits))
    next(waits).wait()
    gate_out, up_out = own_held[0], own_held[1]
    for gate, up in zip(gates, ups):
        gate_out = gate_out + gate
        up_out = up_out + up
    activated = (jax.nn.gelu(gate_out, approximate=True) * up_out).astype(jnp.bfloat16)
    sends = []
    for index in range(req_count * piece_count):
        next(waits).wait()
        part = jnp.dot(activated, downs[index], preferred_element_type=jnp.float32)
        part = part.astype(jnp.bfloat16)
        for i in range(blocks):
            parts_ref[index, i] = part[i * steps : (i + 1) * steps]
        sends.append(
            pltpu.make_async_copy(
                parts_ref.at[index],
                out_ref.at[:, :, pl.ds(index * width, width)],
                sem_ref.at[len(copies) + index],
            )
        )
        sends[-1].start()
    for send in sends:
        send.wait()


def live_rows(
    seq_index, prompt_shape, pool_rows, group_of, prompt_lengths, tail_lengths, page_table
):
    group_count, prompt_span = prompt_shape
    rows_req = group_of.shape[0]
    member = (group_of % group_count)[:, None] == jnp.arange(group_count, dtype=jnp.int32)[None, :]
    prompt_pos = seq_index * prompt_span + jnp.arange(prompt_span, dtype=jnp.int32)
    prompt_live = prompt_pos[None, :] < prompt_lengths[:, None]
    prompt_mask = (member[:, :, None] & prompt_live[None, :, :]).reshape(
        rows_req, group_count * prompt_span
    )
    slot_count = pool_rows // PAGE
    table_row = page_table[0]
    table_len = table_row.shape[0]
    tail_pages = table_len // rows_req
    slot_ids = seq_index * slot_count + jnp.arange(slot_count, dtype=jnp.int32)
    matches = table_row[None, :] == slot_ids[:, None]
    entries = jnp.sum(
        jnp.where(matches, jnp.arange(table_len, dtype=jnp.int32)[None, :], 0), axis=1
    )
    owners = jnp.repeat(entries // tail_pages, PAGE)
    tail_pos = jnp.repeat(entries % tail_pages, PAGE) * PAGE + jnp.tile(
        jnp.arange(PAGE, dtype=jnp.int32), slot_count
    )
    tail_mask = (owners[None, :] == jnp.arange(rows_req, dtype=jnp.int32)[:, None]) & (
        tail_pos[None, :] < tail_lengths[:, None]
    )
    return jnp.concatenate([prompt_mask, tail_mask], axis=1)


def general_attention(
    seq_index,
    seq_count,
    rows_req,
    step_count,
    out_rows,
    projected,
    q_gain,
    k_gain,
    live,
    prompt_keys,
    prompt_values,
    tail_keys,
    tail_values,
):
    group_size = H // KV
    share = projected.shape[0]
    tokens = rows_req * step_count
    heads = normalize(projected.reshape(share, QKV // HD, HD))
    gains = jnp.concatenate(
        [
            jnp.broadcast_to(q_gain, (H, HD)),
            jnp.broadcast_to(k_gain, (KV, HD)),
            jnp.ones((KV, HD), jnp.float32),
        ]
    )
    mine = (heads * gains).astype(jnp.bfloat16).reshape(share, QKV)
    qkv = gather_rows(mine, seq_count)
    queries = qkv[:, : H * HD]
    keys_new = qkv[:, H * HD : (H + KV) * HD]
    values_new = qkv[:, (H + KV) * HD :]

    query_groups = queries.reshape(rows_req, step_count, KV, group_size, HD)
    mask = live[:, None, None, None, :]
    keys = jnp.concatenate([prompt_keys, tail_keys]).reshape(-1, KV, HD)
    values = jnp.concatenate([prompt_values, tail_values]).reshape(-1, KV, HD)
    scores = jnp.einsum("rskgd,pkd->rskgp", query_groups, keys, preferred_element_type=jnp.float32)
    scores = jnp.where(mask, scores, NEGATIVE)
    block_top = jnp.max(scores, axis=4)
    probs = jnp.where(mask, jnp.exp(scores - block_top[..., None]), 0.0)
    block_total = jnp.sum(probs, axis=4)
    block_accum = jnp.einsum(
        "rskgp,pkd->rskgd",
        probs.astype(jnp.bfloat16),
        values,
        preferred_element_type=jnp.float32,
    )

    stats = split_three(jnp.stack([block_top, block_total])).reshape(6, tokens, H)
    per_head = seq_count // H
    stats = jnp.repeat(stats.transpose(2, 0, 1).reshape(H, -1, out_rows), per_head, axis=0)
    accum_blocks = (
        block_accum.astype(jnp.bfloat16).reshape(tokens, seq_count, out_rows).transpose(1, 0, 2)
    )
    got = exchange(jnp.concatenate([accum_blocks, stats], axis=1), "seq")
    got_accum = got[:, :tokens].astype(jnp.float32)
    got_stats = got[:, tokens:].astype(jnp.float32).reshape(seq_count, 2 * 3, tokens)
    got_top = got_stats[:, 0] + got_stats[:, 2] + got_stats[:, 4]
    got_total = got_stats[:, 1] + got_stats[:, 3] + got_stats[:, 5]

    first_col = seq_index * out_rows
    head = first_col // HD
    kv_head = head // group_size
    head_queries = lax.dynamic_slice_in_dim(queries, head * HD, HD, 1)
    head_keys = lax.dynamic_slice_in_dim(keys_new, kv_head * HD, HD, 1)
    head_values = lax.dynamic_slice_in_dim(
        values_new, kv_head * HD + first_col % HD, out_rows, 1
    ).astype(jnp.float32)
    new_scores = jnp.dot(head_queries, head_keys.T, preferred_element_type=jnp.float32)
    token_ids = jnp.arange(tokens, dtype=jnp.int32)
    causal = (token_ids[:, None] // step_count == token_ids[None, :] // step_count) & (
        token_ids[:, None] >= token_ids[None, :]
    )
    new_scores = jnp.where(causal, new_scores, NEGATIVE)
    highest = jnp.maximum(jnp.max(got_top, axis=0), jnp.max(new_scores, axis=1))
    weights = jnp.exp(got_top - highest[None])
    new_probs = jnp.where(causal, jnp.exp(new_scores - highest[:, None]), 0.0)
    denominator = jnp.sum(got_total * weights, axis=0) + jnp.sum(new_probs, axis=1)
    numerator = jnp.sum(got_accum * weights[..., None], axis=0) + jnp.dot(
        new_probs, head_values, precision=lax.Precision.HIGHEST
    )
    return (numerator / denominator[:, None]).astype(jnp.bfloat16)


def on_device(
    req_count,
    seq_count,
    hidden_in,
    attn_gain,
    q_gain,
    k_gain,
    post_attn_gain,
    ffn_gain,
    post_ffn_gain,
    w_qkv,
    w_out,
    w_gate,
    w_up,
    w_down,
    prompt_keys,
    prompt_values,
    tail_keys,
    tail_values,
    group_of,
    prompt_lengths,
    tail_lengths,
    page_table,
):
    seq_index = lax.axis_index("seq")
    req_index = lax.axis_index("req")
    rows_req, step_count, _ = hidden_in.shape
    group_size = H // KV
    tokens = rows_req * step_count
    share = tokens // seq_count

    def shifted(values):
        return [values] + [
            lax.ppermute(values, "req", [(i, (i + j) % req_count) for i in range(req_count)])
            for j in range(1, req_count)
        ]

    where = jnp.stack([seq_index, req_index]).astype(jnp.int32)
    in_rows = w_qkv.shape[0]
    out_rows = w_out.shape[0]
    if in_rows % 128 == 0:
        normed_cols = call(
            norm_columns_kernel,
            "norm_columns",
            jax.ShapeDtypeStruct((tokens, in_rows), jnp.bfloat16),
            seq_index.astype(jnp.int32).reshape(1),
            hidden_in,
            attn_gain.reshape(1, D),
            limit=56,
        )
    else:
        normed = (normalize(hidden_in.astype(jnp.float32)) * attn_gain).astype(jnp.bfloat16)
        normed_cols = lax.dynamic_slice_in_dim(normed, seq_index * in_rows, in_rows, 2)
        normed_cols = normed_cols.reshape(tokens, in_rows)
    normed_cols, w_out_late = tie(normed_cols, w_out)
    normed_blocks = shifted(normed_cols)
    ordered = []
    for i in range(req_count):
        chosen = normed_blocks[0]
        for j in range(1, req_count):
            chosen = jnp.where((req_index - i) % req_count == j, normed_blocks[j], chosen)
        ordered.append(chosen)
    normed_all = jnp.concatenate(ordered)
    normed_all, gate_late, up_late, down_late = tie(normed_all, w_gate, w_up, w_down)
    out_blocks = shifted(w_out_late)
    width = w_gate.shape[1]
    pieces = [down_late[:, c : c + width] for c in range(0, w_down.shape[1], width)]
    packed = shifted(jnp.concatenate([gate_late, up_late] + pieces))[1:]

    qkv_part = jnp.dot(normed_all, w_qkv, preferred_element_type=jnp.float32)
    qkv_cols = w_qkv.shape[1]
    qkv_blocks = (
        (qkv_part * LINK_SCALE)
        .astype(jnp.float16)
        .reshape(req_count * seq_count, share, qkv_cols)
    )
    qkv_got = exchange(qkv_blocks, ("req", "seq"))
    qkv_got = qkv_got.reshape(req_count, seq_count, share, qkv_cols)
    projected = jnp.sum(qkv_got.astype(jnp.float32), axis=1) * (1.0 / LINK_SCALE)
    live = live_rows(
        seq_index, prompt_keys.shape[:2], tail_keys.shape[1], group_of, prompt_lengths,
        tail_lengths, page_table,
    )
    caches = [
        array.reshape(-1, KV * HD) for array in (prompt_keys, prompt_values, tail_keys, tail_values)
    ]
    direct = share == step_count and out_rows % 128 == 0 and tokens == 64 and qkv_cols % HD == 0
    if direct:
        q_blocks, new_keys, new_values = call(
            head_norm_kernel,
            "head_norm",
            (
                jax.ShapeDtypeStruct((seq_count, share, H * HD), jnp.bfloat16),
                jax.ShapeDtypeStruct((8, KV * HD), jnp.float32),
                jax.ShapeDtypeStruct((8, KV * HD), jnp.float32),
            ),
            where,
            projected,
            jnp.stack([q_gain, k_gain]),
        )
        q_got, out_blocks = tie(exchange(q_blocks, "seq"), out_blocks)
        live = jnp.repeat(live.astype(jnp.float32), step_count, axis=0)
        sent = call(
            functools.partial(block_kernel, step_count),
            "block_attention",
            jax.ShapeDtypeStruct((seq_count, tokens + 16, out_rows), jnp.bfloat16),
            where,
            q_got,
            live,
            new_keys,
            new_values,
            jnp.concatenate([caches[0], caches[2]]),
            jnp.concatenate([caches[1], caches[3]]),
        )
        got = exchange(sent, "seq")
        out_part = call(
            functools.partial(out_kernel, req_count),
            "combine_out",
            jax.ShapeDtypeStruct((seq_count, share, D), jnp.bfloat16),
            where,
            got,
            *out_blocks,
            scratch=[pltpu.VMEM((128, 128), jnp.float32)],
        )
    else:
        projected = projected.transpose(1, 0, 2).reshape(share, QKV)
        attention_cols = general_attention(
            seq_index, seq_count, rows_req, step_count, out_rows, projected, q_gain, k_gain,
            live, *caches,
        )
        out_part = jnp.concatenate(
            [jnp.dot(attention_cols, w, preferred_element_type=jnp.float32) for w in out_blocks],
            axis=1,
        )
        out_part = out_part.astype(jnp.bfloat16).reshape(seq_count, share, D)
    ffn_blocks, residual = call(
        functools.partial(residual_kernel, req_count),
        "residual_norms",
        (
            jax.ShapeDtypeStruct((seq_count, share, D), jnp.bfloat16),
            jax.ShapeDtypeStruct((share, D), jnp.float32),
        ),
        where,
        exchange(out_part, "seq"),
        hidden_in.reshape(seq_count, share, D),
        post_attn_gain.reshape(1, D),
        ffn_gain.reshape(1, D),
    )
    ffn_in = exchange(ffn_blocks, "seq")
    gate_rows = w_gate.shape[0]
    chunk_count = 2 * len(chunks_of(gate_rows))
    x_shape = (seq_count, share, gate_rows)
    own_part = call(
        functools.partial(own_kernel, req_count),
        "own_gate_up",
        jax.ShapeDtypeStruct((2, tokens, width), jnp.float32),
        where,
        ffn_in,
        w_gate,
        w_up,
        scratch=[
            pltpu.VMEM(x_shape, jnp.bfloat16),
            pltpu.VMEM((2,) + w_gate.shape, jnp.bfloat16),
            pltpu.SemaphoreType.DMA((1 + chunk_count,)),
        ],
        hbm_from=1,
        limit=56,
    )
    copy_count = (req_count - 1) * (1 + chunk_count) + 1 + D // width
    down_part = call(
        functools.partial(ffn_kernel, req_count, gate_rows),
        "feed_forward",
        jax.ShapeDtypeStruct((seq_count, share, D), jnp.bfloat16),
        where,
        ffn_in,
        own_part,
        w_down,
        *packed,
        scratch=[
            pltpu.VMEM((req_count - 1,) + x_shape, jnp.bfloat16),
            pltpu.VMEM((2, tokens, width), jnp.float32),
            pltpu.VMEM((D // width, w_down.shape[0], width), jnp.bfloat16),
            pltpu.VMEM((D // width, seq_count, share, width), jnp.bfloat16),
            pltpu.VMEM((req_count - 1, 2 * gate_rows, width), jnp.bfloat16),
            pltpu.SemaphoreType.DMA((copy_count + D // width,)),
        ],
        hbm_from=1,
        out_space=pltpu.HBM,
        limit=56,
    )
    layer_blocks = call(
        functools.partial(last_kernel, req_count),
        "last_norm",
        jax.ShapeDtypeStruct((seq_count, share, D), jnp.bfloat16),
        where,
        exchange(down_part, "seq"),
        residual,
        post_ffn_gain.reshape(1, D),
    )
    return exchange(layer_blocks, "seq").reshape(rows_req, step_count, D)


def solution(mesh):
    return jax.shard_map(
        functools.partial(on_device, mesh.shape["req"], mesh.shape["seq"]),
        mesh=mesh,
        in_specs=(
            P("req", None, None),
            P(),
            P(),
            P(),
            P(),
            P(),
            P(),
            P("seq", "req"),
            P("seq", "req"),
            P("req", "seq"),
            P("req", "seq"),
            P("seq", "req"),
            P("req", "seq", None),
            P("req", "seq", None),
            P("req", "seq", None),
            P("req", "seq", None),
            P("req"),
            P("req"),
            P("req"),
            P("req", None),
        ),
        out_specs=P("req", None, None),
        check_vma=False,
    )
```

```python
import functools

import jax
import jax.numpy as jnp
from jax import lax
from jax.experimental import pallas as pl
from jax.experimental.pallas import tpu as pltpu
from jax.sharding import PartitionSpec as P

D = 2048
H = 8
KV = 2
HD = 256
PAGE = 16
QKV = 3072


EPSILON = 1e-06
NEGATIVE = -1e30
LINK_SCALE = 512.0


def normalize(values):
    return values * lax.rsqrt(jnp.mean(values * values, axis=-1, keepdims=True) + EPSILON)


def split_three(values):
    high = values.astype(jnp.bfloat16)
    rest = values - high.astype(jnp.float32)
    middle = rest.astype(jnp.bfloat16)
    low = (rest - middle.astype(jnp.float32)).astype(jnp.bfloat16)
    return jnp.stack([high, middle, low])


def exchange(blocks, axes, groups=None):
    return lax.all_to_all(
        blocks, axes, split_axis=0, concat_axis=0, tiled=True, axis_index_groups=groups
    )


def tie(*arrays):
    return lax.optimization_barrier(arrays)


def spread(block, copies):
    return jnp.broadcast_to(block[None], (copies,) + block.shape)


def gather_rows(rows, count):
    return exchange(spread(rows, count), "seq").reshape(count * rows.shape[0], rows.shape[1])


def call(
    kernel, name, out_shape, *operands, scratch=(), hbm_from=None, out_space=pltpu.VMEM, limit=16
):
    in_specs = [pl.BlockSpec(memory_space=pltpu.SMEM)]
    for i in range(1, len(operands)):
        space = pltpu.HBM if hbm_from is not None and i >= hbm_from else pltpu.VMEM
        in_specs.append(pl.BlockSpec(memory_space=space))
    return pl.pallas_call(
        kernel,
        name=name,
        out_shape=out_shape,
        in_specs=in_specs,
        out_specs=jax.tree.map(lambda _: pl.BlockSpec(memory_space=out_space), out_shape),
        scratch_shapes=scratch,
        compiler_params=pltpu.CompilerParams(vmem_limit_bytes=limit * 1024 * 1024),
    )(*operands)


def norm_columns_kernel(where_ref, hidden_ref, gain_ref, out_ref):
    columns = out_ref.shape[1]
    hidden = hidden_ref[...].astype(jnp.float32)
    scale = lax.rsqrt(jnp.mean(hidden * hidden, axis=-1, keepdims=True) + EPSILON)
    cols = pl.ds(pl.multiple_of(where_ref[0] * columns, columns), columns)
    normed = hidden_ref[:, :, cols].astype(jnp.float32) * scale * gain_ref[:, cols]
    out_ref[...] = normed.reshape(out_ref.shape).astype(jnp.bfloat16)


def head_norm_kernel(where_ref, projected_ref, gains_ref, q_ref, k_ref, v_ref):
    width = projected_ref.shape[2]
    copies, rows, _ = q_ref.shape
    fill = jnp.zeros((k_ref.shape[0] - rows, HD), jnp.float32)
    for head in range(H + 2 * KV):
        half, first = divmod(head * HD, width)
        values = normalize(projected_ref[half, :, first : first + HD])
        if head < H:
            values = (values * gains_ref[0:1, :]).astype(jnp.bfloat16)
            for i in range(copies):
                q_ref[i, :, head * HD : (head + 1) * HD] = values
        else:
            if head < H + KV:
                values = values * gains_ref[1:2, :]
            values = values.astype(jnp.bfloat16).astype(jnp.float32)
            target, slot = (k_ref, head - H) if head < H + KV else (v_ref, head - H - KV)
            target[:, slot * HD : (slot + 1) * HD] = jnp.concatenate([values, fill])


def dot_last(a, b):
    return lax.dot_general(a, b, (((1,), (1,)), ((), ())), preferred_element_type=jnp.float32)


def block_kernel(
    step_count,
    where_ref,
    q_ref,
    live_ref,
    new_k_ref,
    new_v_ref,
    keys_ref,
    values_ref,
    out_ref,
):
    copies, steps, _ = q_ref.shape
    tokens = copies * steps
    columns = out_ref.shape[2]
    group = H // KV
    queries = q_ref[...].reshape(tokens, H * HD)
    live = jnp.concatenate([live_ref[...]] * group) > 0.5
    first_token = where_ref[0] * step_count
    shape = (group * tokens, new_k_ref.shape[0])
    step = lax.broadcasted_iota(jnp.int32, shape, 0) % tokens - first_token
    new_index = lax.broadcasted_iota(jnp.int32, shape, 1)
    new_live = (step >= new_index) & (step < step_count)
    for kv in range(KV):
        span = slice(kv * HD, (kv + 1) * HD)
        q = jnp.concatenate(
            [queries[:, (kv * group + g) * HD : (kv * group + g + 1) * HD] for g in range(group)]
        )
        scores = jnp.where(live, dot_last(q, keys_ref[:, span]), NEGATIVE)
        top = jnp.max(scores, axis=1, keepdims=True)
        probs = jnp.where(live, jnp.exp(scores - top), 0.0)
        total = jnp.sum(probs, axis=1, keepdims=True)
        accum = jnp.dot(
            probs.astype(jnp.bfloat16), values_ref[:, span], preferred_element_type=jnp.float32
        )
        new_scores = dot_last(q, new_k_ref[:, span].astype(jnp.bfloat16))
        new_scores = jnp.where(new_live, new_scores, NEGATIVE)
        both = jnp.maximum(top, jnp.max(new_scores, axis=1, keepdims=True))
        carried = jnp.exp(top - both)
        new_probs = jnp.where(new_live, jnp.exp(new_scores - both), 0.0)
        total = total * carried + jnp.sum(new_probs, axis=1, keepdims=True)
        accum = accum * carried
        for u in range(step_count):
            accum = accum + new_probs[:, u : u + 1] * new_v_ref[u : u + 1, span]
        sent = accum.astype(jnp.bfloat16)
        parts = []
        for value in (both, total):
            for _ in range(3):
                part = value.astype(jnp.bfloat16).astype(jnp.float32)
                parts.append(part)
                value = value - part
        lane = lax.broadcasted_iota(jnp.int32, (group * tokens, 128), 1)
        wide = jnp.zeros((group * tokens, 128), jnp.float32)
        for i, part in enumerate(parts):
            wide = jnp.where(lane == i, part, wide)
        turned = jnp.transpose(wide)[:16].astype(jnp.bfloat16)
        for g in range(group):
            pair = turned[:, g // 2 * 128 : (g // 2 + 1) * 128]
            for part in range(HD // columns):
                target = (kv * group + g) * (HD // columns) + part
                out_ref[target, :tokens, :] = sent[
                    g * tokens : (g + 1) * tokens, part * columns : (part + 1) * columns
                ]
                out_ref[target, tokens:, :] = pair


def out_kernel(req_count, where_ref, got_ref, *refs):
    w_refs = refs[:req_count]
    out_ref, turned_ref = refs[req_count:]
    blocks = got_ref.shape[0]
    copies, steps, _ = out_ref.shape
    tokens = copies * steps
    columns = got_ref.shape[2]
    head = where_ref[0] * columns // HD
    stats = got_ref[:, tokens:, :].astype(jnp.float32)
    tops = stats[:, 0, :] + stats[:, 1, :] + stats[:, 2, :]
    totals = stats[:, 3, :] + stats[:, 4, :] + stats[:, 5, :]
    rest = jnp.zeros((128 - 2 * blocks, 128), jnp.float32)
    turned_ref[...] = jnp.transpose(jnp.concatenate([tops, totals, rest]))
    mine = turned_ref[pl.ds(pl.multiple_of(head % 2 * tokens, tokens), tokens), :]
    tops = mine[:, :blocks]
    highest = jnp.max(tops, axis=1, keepdims=True)
    weights = jnp.exp(tops - highest)
    denominator = jnp.sum(mine[:, blocks : 2 * blocks] * weights, axis=1, keepdims=True)
    numerator = jnp.zeros((tokens, columns), jnp.float32)
    for b in range(blocks):
        numerator = numerator + got_ref[b, :tokens, :].astype(jnp.float32) * weights[:, b : b + 1]
    attention = (numerator / denominator).astype(jnp.bfloat16)
    for j, w_ref in enumerate(w_refs):
        width = w_ref.shape[1]
        part = jnp.dot(attention, w_ref[...], preferred_element_type=jnp.float32)
        part = part.astype(jnp.bfloat16)
        for i in range(copies):
            out_ref[i, :, j * width : (j + 1) * width] = part[i * steps : (i + 1) * steps]


def summed(req_count, where_ref, got_ref):
    width = got_ref.shape[2] // req_count
    blocks = []
    for i in range(req_count):
        j = lax.rem(where_ref[1] - i + req_count, req_count)
        cols = pl.ds(pl.multiple_of(j * width, width), width)
        blocks.append(jnp.sum(got_ref[:, :, cols].astype(jnp.float32), axis=0))
    return jnp.concatenate(blocks, axis=1)


def residual_kernel(
    req_count, where_ref, got_ref, hidden_ref, post_gain_ref, ffn_gain_ref, out_ref, residual_ref
):
    attn_out = summed(req_count, where_ref, got_ref)
    hidden = hidden_ref[where_ref[0]].astype(jnp.float32)
    residual = hidden + normalize(attn_out) * post_gain_ref[...]
    residual_ref[...] = residual
    ffn_in = (normalize(residual) * ffn_gain_ref[...]).astype(jnp.bfloat16)
    for i in range(out_ref.shape[0]):
        out_ref[i] = ffn_in


def last_kernel(req_count, where_ref, got_ref, residual_ref, gain_ref, out_ref):
    down_out = summed(req_count, where_ref, got_ref)
    layer = (residual_ref[...] + normalize(down_out) * gain_ref[...]).astype(jnp.bfloat16)
    for i in range(out_ref.shape[0]):
        out_ref[i] = layer


def start_copies(moves, sem_ref):
    copies = [
        pltpu.make_async_copy(source, target, sem_ref.at[i])
        for i, (source, target) in enumerate(moves)
    ]
    for copy in copies:
        copy.start()
    return copies


def chunks_of(rows):
    size = min(rows, 256)
    return [(first, size) for first in range(0, rows, size)]


def x_columns(x_ref, where_ref, req_count, j, rows):
    start = lax.rem(where_ref[1] - j + req_count, req_count) * rows
    return x_ref.at[:, :, pl.ds(pl.multiple_of(start, rows), rows)]


def chunked_dot(x, held, chunks, waits):
    total = None
    for first, size in chunks:
        next(waits).wait()
        part = jnp.dot(
            x[:, first : first + size],
            held[first : first + size, :],
            preferred_element_type=jnp.float32,
        )
        total = part if total is None else total + part
    return total


def own_kernel(req_count, where_ref, x_ref, gate_ref, up_ref, out_ref, x_held, held, sem_ref):
    rows = gate_ref.shape[0]
    chunks = chunks_of(rows)
    moves = [(x_columns(x_ref, where_ref, req_count, 0, rows), x_held)]
    for i, w_ref in enumerate((gate_ref, up_ref)):
        for first, size in chunks:
            span = pl.ds(first, size)
            moves.append((w_ref.at[span, :], held.at[i, span, :]))
    waits = iter(start_copies(moves, sem_ref))
    blocks, steps, _ = x_held.shape
    next(waits).wait()
    x = x_held[...].reshape(blocks * steps, rows)
    for i in range(2):
        out_ref[i] = chunked_dot(x, held.at[i], chunks, waits)


def ffn_kernel(req_count, gate_rows, where_ref, x_ref, own_ref, down_ref, *refs):
    others = req_count - 1
    packed_refs = refs[:others]
    out_ref, x_held, own_held, downs, parts_ref, held, sem_ref = refs[others:]
    down_rows, width = downs.shape[1:]
    piece_count = down_ref.shape[1] // width
    chunks = chunks_of(gate_rows)
    moves = []
    for j in range(others):
        moves.append((x_columns(x_ref, where_ref, req_count, j + 1, gate_rows), x_held.at[j]))
        for i in range(2):
            for first, size in chunks:
                span = pl.ds(i * gate_rows + first, size)
                moves.append((packed_refs[j].at[span, :], held.at[j, span, :]))
    moves.append((own_ref, own_held))
    for piece in range(piece_count):
        moves.append((down_ref.at[:, pl.ds(piece * width, width)], downs.at[piece]))
    for j in range(others):
        for piece in range(piece_count):
            span = pl.ds(2 * gate_rows + piece * down_rows, down_rows)
            moves.append((packed_refs[j].at[span, :], downs.at[(j + 1) * piece_count + piece]))
    copies = start_copies(moves, sem_ref)
    waits = iter(copies)
    _, blocks, steps, _ = x_held.shape
    gates, ups = [], []
    for j in range(others):
        next(waits).wait()
        x = x_held[j].reshape(blocks * steps, gate_rows)
        gates.append(chunked_dot(x, held.at[j, pl.ds(0, gate_rows)], chunks, waits))
        ups.append(chunked_dot(x, held.at[j, pl.ds(gate_rows, gate_rows)], chunks, waits))
    next(waits).wait()
    gate_out, up_out = own_held[0], own_held[1]
    for gate, up in zip(gates, ups):
        gate_out = gate_out + gate
        up_out = up_out + up
    activated = (jax.nn.gelu(gate_out, approximate=True) * up_out).astype(jnp.bfloat16)
    sends = []
    for index in range(req_count * piece_count):
        next(waits).wait()
        part = jnp.dot(activated, downs[index], preferred_element_type=jnp.float32)
        part = part.astype(jnp.bfloat16)
        for i in range(blocks):
            parts_ref[index, i] = part[i * steps : (i + 1) * steps]
        sends.append(
            pltpu.make_async_copy(
                parts_ref.at[index],
                out_ref.at[:, :, pl.ds(index * width, width)],
                sem_ref.at[len(copies) + index],
            )
        )
        sends[-1].start()
    for send in sends:
        send.wait()


def live_rows(
    seq_index, prompt_shape, pool_rows, group_of, prompt_lengths, tail_lengths, page_table
):
    group_count, prompt_span = prompt_shape
    rows_req = group_of.shape[0]
    member = (group_of % group_count)[:, None] == jnp.arange(group_count, dtype=jnp.int32)[None, :]
    prompt_pos = seq_index * prompt_span + jnp.arange(prompt_span, dtype=jnp.int32)
    prompt_live = prompt_pos[None, :] < prompt_lengths[:, None]
    prompt_mask = (member[:, :, None] & prompt_live[None, :, :]).reshape(
        rows_req, group_count * prompt_span
    )
    slot_count = pool_rows // PAGE
    table_row = page_table[0]
    table_len = table_row.shape[0]
    tail_pages = table_len // rows_req
    slot_ids = seq_index * slot_count + jnp.arange(slot_count, dtype=jnp.int32)
    matches = table_row[None, :] == slot_ids[:, None]
    entries = jnp.sum(
        jnp.where(matches, jnp.arange(table_len, dtype=jnp.int32)[None, :], 0), axis=1
    )
    owners = jnp.repeat(entries // tail_pages, PAGE)
    tail_pos = jnp.repeat(entries % tail_pages, PAGE) * PAGE + jnp.tile(
        jnp.arange(PAGE, dtype=jnp.int32), slot_count
    )
    tail_mask = (owners[None, :] == jnp.arange(rows_req, dtype=jnp.int32)[:, None]) & (
        tail_pos[None, :] < tail_lengths[:, None]
    )
    return jnp.concatenate([prompt_mask, tail_mask], axis=1)


def general_attention(
    seq_index,
    seq_count,
    rows_req,
    step_count,
    out_rows,
    projected,
    q_gain,
    k_gain,
    live,
    prompt_keys,
    prompt_values,
    tail_keys,
    tail_values,
):
    group_size = H // KV
    share = projected.shape[0]
    tokens = rows_req * step_count
    heads = normalize(projected.reshape(share, QKV // HD, HD))
    gains = jnp.concatenate(
        [
            jnp.broadcast_to(q_gain, (H, HD)),
            jnp.broadcast_to(k_gain, (KV, HD)),
            jnp.ones((KV, HD), jnp.float32),
        ]
    )
    mine = (heads * gains).astype(jnp.bfloat16).reshape(share, QKV)
    qkv = gather_rows(mine, seq_count)
    queries = qkv[:, : H * HD]
    keys_new = qkv[:, H * HD : (H + KV) * HD]
    values_new = qkv[:, (H + KV) * HD :]

    query_groups = queries.reshape(rows_req, step_count, KV, group_size, HD)
    mask = live[:, None, None, None, :]
    keys = jnp.concatenate([prompt_keys, tail_keys]).reshape(-1, KV, HD)
    values = jnp.concatenate([prompt_values, tail_values]).reshape(-1, KV, HD)
    scores = jnp.einsum("rskgd,pkd->rskgp", query_groups, keys, preferred_element_type=jnp.float32)
    scores = jnp.where(mask, scores, NEGATIVE)
    block_top = jnp.max(scores, axis=4)
    probs = jnp.where(mask, jnp.exp(scores - block_top[..., None]), 0.0)
    block_total = jnp.sum(probs, axis=4)
    block_accum = jnp.einsum(
        "rskgp,pkd->rskgd",
        probs.astype(jnp.bfloat16),
        values,
        preferred_element_type=jnp.float32,
    )

    stats = split_three(jnp.stack([block_top, block_total])).reshape(6, tokens, H)
    per_head = seq_count // H
    stats = jnp.repeat(stats.transpose(2, 0, 1).reshape(H, -1, out_rows), per_head, axis=0)
    accum_blocks = (
        block_accum.astype(jnp.bfloat16).reshape(tokens, seq_count, out_rows).transpose(1, 0, 2)
    )
    got = exchange(jnp.concatenate([accum_blocks, stats], axis=1), "seq")
    got_accum = got[:, :tokens].astype(jnp.float32)
    got_stats = got[:, tokens:].astype(jnp.float32).reshape(seq_count, 2 * 3, tokens)
    got_top = got_stats[:, 0] + got_stats[:, 2] + got_stats[:, 4]
    got_total = got_stats[:, 1] + got_stats[:, 3] + got_stats[:, 5]

    first_col = seq_index * out_rows
    head = first_col // HD
    kv_head = head // group_size
    head_queries = lax.dynamic_slice_in_dim(queries, head * HD, HD, 1)
    head_keys = lax.dynamic_slice_in_dim(keys_new, kv_head * HD, HD, 1)
    head_values = lax.dynamic_slice_in_dim(
        values_new, kv_head * HD + first_col % HD, out_rows, 1
    ).astype(jnp.float32)
    new_scores = jnp.dot(head_queries, head_keys.T, preferred_element_type=jnp.float32)
    token_ids = jnp.arange(tokens, dtype=jnp.int32)
    causal = (token_ids[:, None] // step_count == token_ids[None, :] // step_count) & (
        token_ids[:, None] >= token_ids[None, :]
    )
    new_scores = jnp.where(causal, new_scores, NEGATIVE)
    highest = jnp.maximum(jnp.max(got_top, axis=0), jnp.max(new_scores, axis=1))
    weights = jnp.exp(got_top - highest[None])
    new_probs = jnp.where(causal, jnp.exp(new_scores - highest[:, None]), 0.0)
    denominator = jnp.sum(got_total * weights, axis=0) + jnp.sum(new_probs, axis=1)
    numerator = jnp.sum(got_accum * weights[..., None], axis=0) + jnp.dot(
        new_probs, head_values, precision=lax.Precision.HIGHEST
    )
    return (numerator / denominator[:, None]).astype(jnp.bfloat16)


def on_device(
    req_count,
    seq_count,
    hidden_in,
    attn_gain,
    q_gain,
    k_gain,
    post_attn_gain,
    ffn_gain,
    post_ffn_gain,
    w_qkv,
    w_out,
    w_gate,
    w_up,
    w_down,
    prompt_keys,
    prompt_values,
    tail_keys,
    tail_values,
    group_of,
    prompt_lengths,
    tail_lengths,
    page_table,
):
    seq_index = lax.axis_index("seq")
    req_index = lax.axis_index("req")
    rows_req, step_count, _ = hidden_in.shape
    group_size = H // KV
    tokens = rows_req * step_count
    share = tokens // seq_count

    def shifted(values):
        return [values] + [
            lax.ppermute(values, "req", [(i, (i + j) % req_count) for i in range(req_count)])
            for j in range(1, req_count)
        ]

    where = jnp.stack([seq_index, req_index]).astype(jnp.int32)
    in_rows = w_qkv.shape[0]
    out_rows = w_out.shape[0]
    if in_rows % 128 == 0:
        normed_cols = call(
            norm_columns_kernel,
            "norm_columns",
            jax.ShapeDtypeStruct((tokens, in_rows), jnp.bfloat16),
            seq_index.astype(jnp.int32).reshape(1),
            hidden_in,
            attn_gain.reshape(1, D),
            limit=56,
        )
    else:
        normed = (normalize(hidden_in.astype(jnp.float32)) * attn_gain).astype(jnp.bfloat16)
        normed_cols = lax.dynamic_slice_in_dim(normed, seq_index * in_rows, in_rows, 2)
        normed_cols = normed_cols.reshape(tokens, in_rows)
    normed_cols, w_out_late = tie(normed_cols, w_out)
    normed_blocks = shifted(normed_cols)
    ordered = []
    for i in range(req_count):
        chosen = normed_blocks[0]
        for j in range(1, req_count):
            chosen = jnp.where((req_index - i) % req_count == j, normed_blocks[j], chosen)
        ordered.append(chosen)
    normed_all = jnp.concatenate(ordered)
    normed_all, gate_late, up_late, down_late, group_of, tail_lengths, page_table, q_gain, k_gain = (
        tie(normed_all, w_gate, w_up, w_down, group_of, tail_lengths, page_table, q_gain, k_gain)
    )
    out_blocks = shifted(w_out_late)
    width = w_gate.shape[1]
    pieces = [down_late[:, c : c + width] for c in range(0, w_down.shape[1], width)]
    packed = shifted(jnp.concatenate([gate_late, up_late] + pieces))[1:]

    qkv_part = jnp.dot(normed_all, w_qkv, preferred_element_type=jnp.float32)
    qkv_cols = w_qkv.shape[1]
    qkv_blocks = (
        (qkv_part * LINK_SCALE)
        .astype(jnp.float16)
        .reshape(req_count * seq_count, share, qkv_cols)
    )
    qkv_got = exchange(qkv_blocks, ("req", "seq"))
    qkv_got = qkv_got.reshape(req_count, seq_count, share, qkv_cols)
    projected = jnp.sum(qkv_got.astype(jnp.float32), axis=1) * (1.0 / LINK_SCALE)
    live = live_rows(
        seq_index, prompt_keys.shape[:2], tail_keys.shape[1], group_of, prompt_lengths,
        tail_lengths, page_table,
    )
    caches = [
        array.reshape(-1, KV * HD) for array in (prompt_keys, prompt_values, tail_keys, tail_values)
    ]
    direct = share == step_count and out_rows % 128 == 0 and tokens == 64 and qkv_cols % HD == 0
    if direct:
        q_blocks, new_keys, new_values = call(
            head_norm_kernel,
            "head_norm",
            (
                jax.ShapeDtypeStruct((seq_count, share, H * HD), jnp.bfloat16),
                jax.ShapeDtypeStruct((8, KV * HD), jnp.float32),
                jax.ShapeDtypeStruct((8, KV * HD), jnp.float32),
            ),
            where,
            projected,
            jnp.stack([q_gain, k_gain]),
        )
        q_got, out_blocks = tie(exchange(q_blocks, "seq"), out_blocks)
        live = jnp.repeat(live.astype(jnp.float32), step_count, axis=0)
        sent = call(
            functools.partial(block_kernel, step_count),
            "block_attention",
            jax.ShapeDtypeStruct((seq_count, tokens + 16, out_rows), jnp.bfloat16),
            where,
            q_got,
            live,
            new_keys,
            new_values,
            jnp.concatenate([caches[0], caches[2]]),
            jnp.concatenate([caches[1], caches[3]]),
        )
        got = exchange(sent, "seq")
        out_part = call(
            functools.partial(out_kernel, req_count),
            "combine_out",
            jax.ShapeDtypeStruct((seq_count, share, D), jnp.bfloat16),
            where,
            got,
            *out_blocks,
            scratch=[pltpu.VMEM((128, 128), jnp.float32)],
        )
    else:
        projected = projected.transpose(1, 0, 2).reshape(share, QKV)
        attention_cols = general_attention(
            seq_index, seq_count, rows_req, step_count, out_rows, projected, q_gain, k_gain,
            live, *caches,
        )
        out_part = jnp.concatenate(
            [jnp.dot(attention_cols, w, preferred_element_type=jnp.float32) for w in out_blocks],
            axis=1,
        )
        out_part = out_part.astype(jnp.bfloat16).reshape(seq_count, share, D)
    ffn_blocks, residual = call(
        functools.partial(residual_kernel, req_count),
        "residual_norms",
        (
            jax.ShapeDtypeStruct((seq_count, share, D), jnp.bfloat16),
            jax.ShapeDtypeStruct((share, D), jnp.float32),
        ),
        where,
        exchange(out_part, "seq"),
        hidden_in.reshape(seq_count, share, D),
        post_attn_gain.reshape(1, D),
        ffn_gain.reshape(1, D),
    )
    ffn_in = exchange(ffn_blocks, "seq")
    gate_rows = w_gate.shape[0]
    chunk_count = 2 * len(chunks_of(gate_rows))
    x_shape = (seq_count, share, gate_rows)
    own_part = call(
        functools.partial(own_kernel, req_count),
        "own_gate_up",
        jax.ShapeDtypeStruct((2, tokens, width), jnp.float32),
        where,
        ffn_in,
        w_gate,
        w_up,
        scratch=[
            pltpu.VMEM(x_shape, jnp.bfloat16),
            pltpu.VMEM((2,) + w_gate.shape, jnp.bfloat16),
            pltpu.SemaphoreType.DMA((1 + chunk_count,)),
        ],
        hbm_from=1,
        limit=56,
    )
    copy_count = (req_count - 1) * (1 + chunk_count) + 1 + D // width
    down_part = call(
        functools.partial(ffn_kernel, req_count, gate_rows),
        "feed_forward",
        jax.ShapeDtypeStruct((seq_count, share, D), jnp.bfloat16),
        where,
        ffn_in,
        own_part,
        w_down,
        *packed,
        scratch=[
            pltpu.VMEM((req_count - 1,) + x_shape, jnp.bfloat16),
            pltpu.VMEM((2, tokens, width), jnp.float32),
            pltpu.VMEM((D // width, w_down.shape[0], width), jnp.bfloat16),
            pltpu.VMEM((D // width, seq_count, share, width), jnp.bfloat16),
            pltpu.VMEM((req_count - 1, 2 * gate_rows, width), jnp.bfloat16),
            pltpu.SemaphoreType.DMA((copy_count + D // width,)),
        ],
        hbm_from=1,
        out_space=pltpu.HBM,
        limit=56,
    )
    layer_blocks = call(
        functools.partial(last_kernel, req_count),
        "last_norm",
        jax.ShapeDtypeStruct((seq_count, share, D), jnp.bfloat16),
        where,
        exchange(down_part, "seq"),
        residual,
        post_ffn_gain.reshape(1, D),
    )
    return exchange(layer_blocks, "seq").reshape(rows_req, step_count, D)


def solution(mesh):
    return jax.shard_map(
        functools.partial(on_device, mesh.shape["req"], mesh.shape["seq"]),
        mesh=mesh,
        in_specs=(
            P("req", None, None),
            P(),
            P(),
            P(),
            P(),
            P(),
            P(),
            P("seq", "req"),
            P("seq", "req"),
            P("req", "seq"),
            P("req", "seq"),
            P("seq", "req"),
            P("req", "seq", None),
            P("req", "seq", None),
            P("req", "seq", None),
            P("req", "seq", None),
            P("req"),
            P("req"),
            P("req"),
            P("req", None),
        ),
        out_specs=P("req", None, None),
        check_vma=False,
    )
```

```python
import functools

import jax
import jax.numpy as jnp
from jax import lax
from jax.experimental import pallas as pl
from jax.experimental.pallas import tpu as pltpu
from jax.sharding import PartitionSpec as P

D = 2048
H = 8
KV = 2
HD = 256
PAGE = 16
QKV = 3072


EPSILON = 1e-06
NEGATIVE = -1e30
LINK_SCALE = 512.0


def normalize(values):
    return values * lax.rsqrt(jnp.mean(values * values, axis=-1, keepdims=True) + EPSILON)


def split_three(values):
    high = values.astype(jnp.bfloat16)
    rest = values - high.astype(jnp.float32)
    middle = rest.astype(jnp.bfloat16)
    low = (rest - middle.astype(jnp.float32)).astype(jnp.bfloat16)
    return jnp.stack([high, middle, low])


def exchange(blocks, axes, groups=None):
    return lax.all_to_all(
        blocks, axes, split_axis=0, concat_axis=0, tiled=True, axis_index_groups=groups
    )


def tie(*arrays):
    return lax.optimization_barrier(arrays)


def spread(block, copies):
    return jnp.broadcast_to(block[None], (copies,) + block.shape)


def gather_rows(rows, count):
    return exchange(spread(rows, count), "seq").reshape(count * rows.shape[0], rows.shape[1])


def call(
    kernel, name, out_shape, *operands, scratch=(), hbm_from=None, out_space=pltpu.VMEM, limit=16
):
    in_specs = [pl.BlockSpec(memory_space=pltpu.SMEM)]
    for i in range(1, len(operands)):
        space = pltpu.HBM if hbm_from is not None and i >= hbm_from else pltpu.VMEM
        in_specs.append(pl.BlockSpec(memory_space=space))
    return pl.pallas_call(
        kernel,
        name=name,
        out_shape=out_shape,
        in_specs=in_specs,
        out_specs=(
            tuple(pl.BlockSpec(memory_space=space) for space in out_space)
            if isinstance(out_space, tuple)
            else jax.tree.map(lambda _: pl.BlockSpec(memory_space=out_space), out_shape)
        ),
        scratch_shapes=scratch,
        compiler_params=pltpu.CompilerParams(vmem_limit_bytes=limit * 1024 * 1024),
    )(*operands)


def norm_columns_kernel(where_ref, hidden_ref, gain_ref, out_ref):
    columns = out_ref.shape[1]
    hidden = hidden_ref[...].astype(jnp.float32)
    scale = lax.rsqrt(jnp.mean(hidden * hidden, axis=-1, keepdims=True) + EPSILON)
    cols = pl.ds(pl.multiple_of(where_ref[0] * columns, columns), columns)
    normed = hidden_ref[:, :, cols].astype(jnp.float32) * scale * gain_ref[:, cols]
    out_ref[...] = normed.reshape(out_ref.shape).astype(jnp.bfloat16)


def head_norm_kernel(where_ref, projected_ref, gains_ref, q_ref, k_ref, v_ref, held_ref, sem_ref):
    width = projected_ref.shape[2]
    copies, rows, _ = q_ref.shape
    fill = jnp.zeros((k_ref.shape[0] - rows, HD), jnp.float32)
    for head in range(H + 2 * KV):
        half, first = divmod(head * HD, width)
        values = normalize(projected_ref[half, :, first : first + HD])
        if head < H:
            values = (values * gains_ref[0:1, :]).astype(jnp.bfloat16)
            held_ref[:, head * HD : (head + 1) * HD] = values
            if head == H - 1:
                sends = [
                    pltpu.make_async_copy(held_ref, q_ref.at[i], sem_ref.at[i])
                    for i in range(copies)
                ]
                for send in sends:
                    send.start()
        else:
            if head < H + KV:
                values = values * gains_ref[1:2, :]
            values = values.astype(jnp.bfloat16).astype(jnp.float32)
            target, slot = (k_ref, head - H) if head < H + KV else (v_ref, head - H - KV)
            target[:, slot * HD : (slot + 1) * HD] = jnp.concatenate([values, fill])
    for send in sends:
        send.wait()


def dot_last(a, b):
    return lax.dot_general(a, b, (((1,), (1,)), ((), ())), preferred_element_type=jnp.float32)


def block_kernel(
    step_count,
    where_ref,
    q_ref,
    live_ref,
    new_k_ref,
    new_v_ref,
    keys_ref,
    values_ref,
    out_ref,
):
    copies, steps, _ = q_ref.shape
    tokens = copies * steps
    columns = out_ref.shape[2]
    group = H // KV
    queries = q_ref[...].reshape(tokens, H * HD)
    live = jnp.concatenate([live_ref[...]] * group) > 0.5
    first_token = where_ref[0] * step_count
    shape = (group * tokens, new_k_ref.shape[0])
    step = lax.broadcasted_iota(jnp.int32, shape, 0) % tokens - first_token
    new_index = lax.broadcasted_iota(jnp.int32, shape, 1)
    new_live = (step >= new_index) & (step < step_count)
    for kv in range(KV):
        span = slice(kv * HD, (kv + 1) * HD)
        q = jnp.concatenate(
            [queries[:, (kv * group + g) * HD : (kv * group + g + 1) * HD] for g in range(group)]
        )
        scores = jnp.where(live, dot_last(q, keys_ref[:, span]), NEGATIVE)
        top = jnp.max(scores, axis=1, keepdims=True)
        probs = jnp.where(live, jnp.exp(scores - top), 0.0)
        total = jnp.sum(probs, axis=1, keepdims=True)
        accum = jnp.dot(
            probs.astype(jnp.bfloat16), values_ref[:, span], preferred_element_type=jnp.float32
        )
        new_scores = dot_last(q, new_k_ref[:, span].astype(jnp.bfloat16))
        new_scores = jnp.where(new_live, new_scores, NEGATIVE)
        both = jnp.maximum(top, jnp.max(new_scores, axis=1, keepdims=True))
        carried = jnp.exp(top - both)
        new_probs = jnp.where(new_live, jnp.exp(new_scores - both), 0.0)
        total = total * carried + jnp.sum(new_probs, axis=1, keepdims=True)
        accum = accum * carried
        for u in range(step_count):
            accum = accum + new_probs[:, u : u + 1] * new_v_ref[u : u + 1, span]
        sent = accum.astype(jnp.bfloat16)
        parts = []
        for value in (both, total):
            for _ in range(3):
                part = value.astype(jnp.bfloat16).astype(jnp.float32)
                parts.append(part)
                value = value - part
        lane = lax.broadcasted_iota(jnp.int32, (group * tokens, 128), 1)
        wide = jnp.zeros((group * tokens, 128), jnp.float32)
        for i, part in enumerate(parts):
            wide = jnp.where(lane == i, part, wide)
        turned = jnp.transpose(wide)[:16].astype(jnp.bfloat16)
        for g in range(group):
            pair = turned[:, g // 2 * 128 : (g // 2 + 1) * 128]
            for part in range(HD // columns):
                target = (kv * group + g) * (HD // columns) + part
                out_ref[target, :tokens, :] = sent[
                    g * tokens : (g + 1) * tokens, part * columns : (part + 1) * columns
                ]
                out_ref[target, tokens:, :] = pair


def out_kernel(req_count, where_ref, got_ref, *refs):
    w_refs = refs[:req_count]
    out_ref, turned_ref = refs[req_count:]
    blocks = got_ref.shape[0]
    copies, steps, _ = out_ref.shape
    tokens = copies * steps
    columns = got_ref.shape[2]
    head = where_ref[0] * columns // HD
    stats = got_ref[:, tokens:, :].astype(jnp.float32)
    tops = stats[:, 0, :] + stats[:, 1, :] + stats[:, 2, :]
    totals = stats[:, 3, :] + stats[:, 4, :] + stats[:, 5, :]
    rest = jnp.zeros((128 - 2 * blocks, 128), jnp.float32)
    turned_ref[...] = jnp.transpose(jnp.concatenate([tops, totals, rest]))
    mine = turned_ref[pl.ds(pl.multiple_of(head % 2 * tokens, tokens), tokens), :]
    tops = mine[:, :blocks]
    highest = jnp.max(tops, axis=1, keepdims=True)
    weights = jnp.exp(tops - highest)
    denominator = jnp.sum(mine[:, blocks : 2 * blocks] * weights, axis=1, keepdims=True)
    numerator = jnp.zeros((tokens, columns), jnp.float32)
    for b in range(blocks):
        numerator = numerator + got_ref[b, :tokens, :].astype(jnp.float32) * weights[:, b : b + 1]
    attention = (numerator / denominator).astype(jnp.bfloat16)
    for j, w_ref in enumerate(w_refs):
        width = w_ref.shape[1]
        part = jnp.dot(attention, w_ref[...], preferred_element_type=jnp.float32)
        part = part.astype(jnp.bfloat16)
        for i in range(copies):
            out_ref[i, :, j * width : (j + 1) * width] = part[i * steps : (i + 1) * steps]


def summed(req_count, where_ref, got_ref):
    width = got_ref.shape[2] // req_count
    blocks = []
    for i in range(req_count):
        j = lax.rem(where_ref[1] - i + req_count, req_count)
        cols = pl.ds(pl.multiple_of(j * width, width), width)
        blocks.append(jnp.sum(got_ref[:, :, cols].astype(jnp.float32), axis=0))
    return jnp.concatenate(blocks, axis=1)


def residual_kernel(
    req_count, where_ref, got_ref, hidden_ref, post_gain_ref, ffn_gain_ref, out_ref, residual_ref
):
    attn_out = summed(req_count, where_ref, got_ref)
    hidden = hidden_ref[where_ref[0]].astype(jnp.float32)
    residual = hidden + normalize(attn_out) * post_gain_ref[...]
    residual_ref[...] = residual
    ffn_in = (normalize(residual) * ffn_gain_ref[...]).astype(jnp.bfloat16)
    for i in range(out_ref.shape[0]):
        out_ref[i] = ffn_in


def last_kernel(req_count, where_ref, got_ref, residual_ref, gain_ref, out_ref):
    down_out = summed(req_count, where_ref, got_ref)
    layer = (residual_ref[...] + normalize(down_out) * gain_ref[...]).astype(jnp.bfloat16)
    for i in range(out_ref.shape[0]):
        out_ref[i] = layer


def start_copies(moves, sem_ref):
    copies = [
        pltpu.make_async_copy(source, target, sem_ref.at[i])
        for i, (source, target) in enumerate(moves)
    ]
    for copy in copies:
        copy.start()
    return copies


def chunks_of(rows):
    size = min(rows, 256)
    return [(first, size) for first in range(0, rows, size)]


def x_columns(x_ref, where_ref, req_count, j, rows):
    start = lax.rem(where_ref[1] - j + req_count, req_count) * rows
    return x_ref.at[:, :, pl.ds(pl.multiple_of(start, rows), rows)]


def chunked_dot(x, held, chunks, waits):
    total = None
    for first, size in chunks:
        next(waits).wait()
        part = jnp.dot(
            x[:, first : first + size],
            held[first : first + size, :],
            preferred_element_type=jnp.float32,
        )
        total = part if total is None else total + part
    return total


def own_kernel(req_count, where_ref, x_ref, gate_ref, up_ref, out_ref, x_held, held, parts_ref, sem_ref):
    rows = gate_ref.shape[0]
    chunks = chunks_of(rows)
    moves = [(x_columns(x_ref, where_ref, req_count, 0, rows), x_held)]
    for i, w_ref in enumerate((gate_ref, up_ref)):
        for first, size in chunks:
            span = pl.ds(first, size)
            moves.append((w_ref.at[span, :], held.at[i, span, :]))
    waits = iter(start_copies(moves, sem_ref))
    blocks, steps, _ = x_held.shape
    next(waits).wait()
    x = x_held[...].reshape(blocks * steps, rows)
    sends = []
    for i in range(2):
        parts_ref[i] = chunked_dot(x, held.at[i], chunks, waits)
        sends.append(
            pltpu.make_async_copy(parts_ref.at[i], out_ref.at[i], sem_ref.at[len(moves) + i])
        )
        sends[-1].start()
    for send in sends:
        send.wait()


def ffn_kernel(req_count, gate_rows, where_ref, x_ref, own_ref, down_ref, *refs):
    others = req_count - 1
    packed_refs = refs[:others]
    out_ref, x_held, own_held, downs, parts_ref, held, sem_ref = refs[others:]
    down_rows, width = downs.shape[1:]
    piece_count = down_ref.shape[1] // width
    chunks = chunks_of(gate_rows)
    moves = []
    for j in range(others):
        moves.append((x_columns(x_ref, where_ref, req_count, j + 1, gate_rows), x_held.at[j]))
        for i in range(2):
            for first, size in chunks:
                span = pl.ds(i * gate_rows + first, size)
                moves.append((packed_refs[j].at[span, :], held.at[j, span, :]))
    moves.append((own_ref, own_held))
    for piece in range(piece_count):
        moves.append((down_ref.at[:, pl.ds(piece * width, width)], downs.at[piece]))
    for j in range(others):
        for piece in range(piece_count):
            span = pl.ds(2 * gate_rows + piece * down_rows, down_rows)
            moves.append((packed_refs[j].at[span, :], downs.at[(j + 1) * piece_count + piece]))
    copies = start_copies(moves, sem_ref)
    waits = iter(copies)
    _, blocks, steps, _ = x_held.shape
    gates, ups = [], []
    for j in range(others):
        next(waits).wait()
        x = x_held[j].reshape(blocks * steps, gate_rows)
        gates.append(chunked_dot(x, held.at[j, pl.ds(0, gate_rows)], chunks, waits))
        ups.append(chunked_dot(x, held.at[j, pl.ds(gate_rows, gate_rows)], chunks, waits))
    next(waits).wait()
    gate_out, up_out = own_held[0], own_held[1]
    for gate, up in zip(gates, ups):
        gate_out = gate_out + gate
        up_out = up_out + up
    activated = (jax.nn.gelu(gate_out, approximate=True) * up_out).astype(jnp.bfloat16)
    sends = []
    for index in range(req_count * piece_count):
        next(waits).wait()
        part = jnp.dot(activated, downs[index], preferred_element_type=jnp.float32)
        part = part.astype(jnp.bfloat16)
        for i in range(blocks):
            parts_ref[index, i] = part[i * steps : (i + 1) * steps]
        sends.append(
            pltpu.make_async_copy(
                parts_ref.at[index],
                out_ref.at[:, :, pl.ds(index * width, width)],
                sem_ref.at[len(copies) + index],
            )
        )
        sends[-1].start()
    for send in sends:
        send.wait()


def live_rows(
    seq_index, prompt_shape, pool_rows, group_of, prompt_lengths, tail_lengths, page_table
):
    group_count, prompt_span = prompt_shape
    rows_req = group_of.shape[0]
    member = (group_of % group_count)[:, None] == jnp.arange(group_count, dtype=jnp.int32)[None, :]
    prompt_pos = seq_index * prompt_span + jnp.arange(prompt_span, dtype=jnp.int32)
    prompt_live = prompt_pos[None, :] < prompt_lengths[:, None]
    prompt_mask = (member[:, :, None] & prompt_live[None, :, :]).reshape(
        rows_req, group_count * prompt_span
    )
    slot_count = pool_rows // PAGE
    table_row = page_table[0]
    table_len = table_row.shape[0]
    tail_pages = table_len // rows_req
    slot_ids = seq_index * slot_count + jnp.arange(slot_count, dtype=jnp.int32)
    matches = table_row[None, :] == slot_ids[:, None]
    entries = jnp.sum(
        jnp.where(matches, jnp.arange(table_len, dtype=jnp.int32)[None, :], 0), axis=1
    )
    owners = jnp.repeat(entries // tail_pages, PAGE)
    tail_pos = jnp.repeat(entries % tail_pages, PAGE) * PAGE + jnp.tile(
        jnp.arange(PAGE, dtype=jnp.int32), slot_count
    )
    tail_mask = (owners[None, :] == jnp.arange(rows_req, dtype=jnp.int32)[:, None]) & (
        tail_pos[None, :] < tail_lengths[:, None]
    )
    return jnp.concatenate([prompt_mask, tail_mask], axis=1)


def general_attention(
    seq_index,
    seq_count,
    rows_req,
    step_count,
    out_rows,
    projected,
    q_gain,
    k_gain,
    live,
    prompt_keys,
    prompt_values,
    tail_keys,
    tail_values,
):
    group_size = H // KV
    share = projected.shape[0]
    tokens = rows_req * step_count
    heads = normalize(projected.reshape(share, QKV // HD, HD))
    gains = jnp.concatenate(
        [
            jnp.broadcast_to(q_gain, (H, HD)),
            jnp.broadcast_to(k_gain, (KV, HD)),
            jnp.ones((KV, HD), jnp.float32),
        ]
    )
    mine = (heads * gains).astype(jnp.bfloat16).reshape(share, QKV)
    qkv = gather_rows(mine, seq_count)
    queries = qkv[:, : H * HD]
    keys_new = qkv[:, H * HD : (H + KV) * HD]
    values_new = qkv[:, (H + KV) * HD :]

    query_groups = queries.reshape(rows_req, step_count, KV, group_size, HD)
    mask = live[:, None, None, None, :]
    keys = jnp.concatenate([prompt_keys, tail_keys]).reshape(-1, KV, HD)
    values = jnp.concatenate([prompt_values, tail_values]).reshape(-1, KV, HD)
    scores = jnp.einsum("rskgd,pkd->rskgp", query_groups, keys, preferred_element_type=jnp.float32)
    scores = jnp.where(mask, scores, NEGATIVE)
    block_top = jnp.max(scores, axis=4)
    probs = jnp.where(mask, jnp.exp(scores - block_top[..., None]), 0.0)
    block_total = jnp.sum(probs, axis=4)
    block_accum = jnp.einsum(
        "rskgp,pkd->rskgd",
        probs.astype(jnp.bfloat16),
        values,
        preferred_element_type=jnp.float32,
    )

    stats = split_three(jnp.stack([block_top, block_total])).reshape(6, tokens, H)
    per_head = seq_count // H
    stats = jnp.repeat(stats.transpose(2, 0, 1).reshape(H, -1, out_rows), per_head, axis=0)
    accum_blocks = (
        block_accum.astype(jnp.bfloat16).reshape(tokens, seq_count, out_rows).transpose(1, 0, 2)
    )
    got = exchange(jnp.concatenate([accum_blocks, stats], axis=1), "seq")
    got_accum = got[:, :tokens].astype(jnp.float32)
    got_stats = got[:, tokens:].astype(jnp.float32).reshape(seq_count, 2 * 3, tokens)
    got_top = got_stats[:, 0] + got_stats[:, 2] + got_stats[:, 4]
    got_total = got_stats[:, 1] + got_stats[:, 3] + got_stats[:, 5]

    first_col = seq_index * out_rows
    head = first_col // HD
    kv_head = head // group_size
    head_queries = lax.dynamic_slice_in_dim(queries, head * HD, HD, 1)
    head_keys = lax.dynamic_slice_in_dim(keys_new, kv_head * HD, HD, 1)
    head_values = lax.dynamic_slice_in_dim(
        values_new, kv_head * HD + first_col % HD, out_rows, 1
    ).astype(jnp.float32)
    new_scores = jnp.dot(head_queries, head_keys.T, preferred_element_type=jnp.float32)
    token_ids = jnp.arange(tokens, dtype=jnp.int32)
    causal = (token_ids[:, None] // step_count == token_ids[None, :] // step_count) & (
        token_ids[:, None] >= token_ids[None, :]
    )
    new_scores = jnp.where(causal, new_scores, NEGATIVE)
    highest = jnp.maximum(jnp.max(got_top, axis=0), jnp.max(new_scores, axis=1))
    weights = jnp.exp(got_top - highest[None])
    new_probs = jnp.where(causal, jnp.exp(new_scores - highest[:, None]), 0.0)
    denominator = jnp.sum(got_total * weights, axis=0) + jnp.sum(new_probs, axis=1)
    numerator = jnp.sum(got_accum * weights[..., None], axis=0) + jnp.dot(
        new_probs, head_values, precision=lax.Precision.HIGHEST
    )
    return (numerator / denominator[:, None]).astype(jnp.bfloat16)


def on_device(
    req_count,
    seq_count,
    hidden_in,
    attn_gain,
    q_gain,
    k_gain,
    post_attn_gain,
    ffn_gain,
    post_ffn_gain,
    w_qkv,
    w_out,
    w_gate,
    w_up,
    w_down,
    prompt_keys,
    prompt_values,
    tail_keys,
    tail_values,
    group_of,
    prompt_lengths,
    tail_lengths,
    page_table,
):
    seq_index = lax.axis_index("seq")
    req_index = lax.axis_index("req")
    rows_req, step_count, _ = hidden_in.shape
    group_size = H // KV
    tokens = rows_req * step_count
    share = tokens // seq_count

    def shifted(values):
        return [values] + [
            lax.ppermute(values, "req", [(i, (i + j) % req_count) for i in range(req_count)])
            for j in range(1, req_count)
        ]

    where = jnp.stack([seq_index, req_index]).astype(jnp.int32)
    in_rows = w_qkv.shape[0]
    out_rows = w_out.shape[0]
    if in_rows % 128 == 0:
        normed_cols = call(
            norm_columns_kernel,
            "norm_columns",
            jax.ShapeDtypeStruct((tokens, in_rows), jnp.bfloat16),
            seq_index.astype(jnp.int32).reshape(1),
            hidden_in,
            attn_gain.reshape(1, D),
            limit=56,
        )
    else:
        normed = (normalize(hidden_in.astype(jnp.float32)) * attn_gain).astype(jnp.bfloat16)
        normed_cols = lax.dynamic_slice_in_dim(normed, seq_index * in_rows, in_rows, 2)
        normed_cols = normed_cols.reshape(tokens, in_rows)
    normed_cols, w_out_late = tie(normed_cols, w_out)
    normed_blocks = shifted(normed_cols)
    ordered = []
    for i in range(req_count):
        chosen = normed_blocks[0]
        for j in range(1, req_count):
            chosen = jnp.where((req_index - i) % req_count == j, normed_blocks[j], chosen)
        ordered.append(chosen)
    normed_all = jnp.concatenate(ordered)
    normed_all, gate_late, up_late, down_late = tie(normed_all, w_gate, w_up, w_down)
    out_blocks = shifted(w_out_late)
    width = w_gate.shape[1]
    pieces = [down_late[:, c : c + width] for c in range(0, w_down.shape[1], width)]
    packed = shifted(jnp.concatenate([gate_late, up_late] + pieces))[1:]

    qkv_part = jnp.dot(normed_all, w_qkv, preferred_element_type=jnp.float32)
    qkv_cols = w_qkv.shape[1]
    qkv_blocks = (
        (qkv_part * LINK_SCALE)
        .astype(jnp.float16)
        .reshape(req_count * seq_count, share, qkv_cols)
    )
    qkv_got = exchange(qkv_blocks, ("req", "seq"))
    qkv_got = qkv_got.reshape(req_count, seq_count, share, qkv_cols)
    projected = jnp.sum(qkv_got.astype(jnp.float32), axis=1) * (1.0 / LINK_SCALE)
    live = live_rows(
        seq_index, prompt_keys.shape[:2], tail_keys.shape[1], group_of, prompt_lengths,
        tail_lengths, page_table,
    )
    caches = [
        array.reshape(-1, KV * HD) for array in (prompt_keys, prompt_values, tail_keys, tail_values)
    ]
    direct = share == step_count and out_rows % 128 == 0 and tokens == 64 and qkv_cols % HD == 0
    if direct:
        q_blocks, new_keys, new_values = call(
            head_norm_kernel,
            "head_norm",
            (
                jax.ShapeDtypeStruct((seq_count, share, H * HD), jnp.bfloat16),
                jax.ShapeDtypeStruct((8, KV * HD), jnp.float32),
                jax.ShapeDtypeStruct((8, KV * HD), jnp.float32),
            ),
            where,
            projected,
            jnp.stack([q_gain, k_gain]),
            scratch=[
                pltpu.VMEM((share, H * HD), jnp.bfloat16),
                pltpu.SemaphoreType.DMA((seq_count,)),
            ],
            out_space=(pltpu.HBM, pltpu.VMEM, pltpu.VMEM),
        )
        q_got, out_blocks = tie(exchange(q_blocks, "seq"), out_blocks)
        live = jnp.repeat(live.astype(jnp.float32), step_count, axis=0)
        sent = call(
            functools.partial(block_kernel, step_count),
            "block_attention",
            jax.ShapeDtypeStruct((seq_count, tokens + 16, out_rows), jnp.bfloat16),
            where,
            q_got,
            live,
            new_keys,
            new_values,
            jnp.concatenate([caches[0], caches[2]]),
            jnp.concatenate([caches[1], caches[3]]),
        )
        got = exchange(sent, "seq")
        out_part = call(
            functools.partial(out_kernel, req_count),
            "combine_out",
            jax.ShapeDtypeStruct((seq_count, share, D), jnp.bfloat16),
            where,
            got,
            *out_blocks,
            scratch=[pltpu.VMEM((128, 128), jnp.float32)],
        )
    else:
        projected = projected.transpose(1, 0, 2).reshape(share, QKV)
        attention_cols = general_attention(
            seq_index, seq_count, rows_req, step_count, out_rows, projected, q_gain, k_gain,
            live, *caches,
        )
        out_part = jnp.concatenate(
            [jnp.dot(attention_cols, w, preferred_element_type=jnp.float32) for w in out_blocks],
            axis=1,
        )
        out_part = out_part.astype(jnp.bfloat16).reshape(seq_count, share, D)
    ffn_blocks, residual = call(
        functools.partial(residual_kernel, req_count),
        "residual_norms",
        (
            jax.ShapeDtypeStruct((seq_count, share, D), jnp.bfloat16),
            jax.ShapeDtypeStruct((share, D), jnp.float32),
        ),
        where,
        exchange(out_part, "seq"),
        hidden_in.reshape(seq_count, share, D),
        post_attn_gain.reshape(1, D),
        ffn_gain.reshape(1, D),
    )
    ffn_in = exchange(ffn_blocks, "seq")
    gate_rows = w_gate.shape[0]
    chunk_count = 2 * len(chunks_of(gate_rows))
    x_shape = (seq_count, share, gate_rows)
    own_part = call(
        functools.partial(own_kernel, req_count),
        "own_gate_up",
        jax.ShapeDtypeStruct((2, tokens, width), jnp.float32),
        where,
        ffn_in,
        w_gate,
        w_up,
        scratch=[
            pltpu.VMEM(x_shape, jnp.bfloat16),
            pltpu.VMEM((2,) + w_gate.shape, jnp.bfloat16),
            pltpu.VMEM((2, tokens, width), jnp.float32),
            pltpu.SemaphoreType.DMA((3 + chunk_count,)),
        ],
        hbm_from=1,
        out_space=pltpu.HBM,
        limit=56,
    )
    copy_count = (req_count - 1) * (1 + chunk_count) + 1 + D // width
    down_part = call(
        functools.partial(ffn_kernel, req_count, gate_rows),
        "feed_forward",
        jax.ShapeDtypeStruct((seq_count, share, D), jnp.bfloat16),
        where,
        ffn_in,
        own_part,
        w_down,
        *packed,
        scratch=[
            pltpu.VMEM((req_count - 1,) + x_shape, jnp.bfloat16),
            pltpu.VMEM((2, tokens, width), jnp.float32),
            pltpu.VMEM((D // width, w_down.shape[0], width), jnp.bfloat16),
            pltpu.VMEM((D // width, seq_count, share, width), jnp.bfloat16),
            pltpu.VMEM((req_count - 1, 2 * gate_rows, width), jnp.bfloat16),
            pltpu.SemaphoreType.DMA((copy_count + D // width,)),
        ],
        hbm_from=1,
        out_space=pltpu.HBM,
        limit=56,
    )
    layer_blocks = call(
        functools.partial(last_kernel, req_count),
        "last_norm",
        jax.ShapeDtypeStruct((seq_count, share, D), jnp.bfloat16),
        where,
        exchange(down_part, "seq"),
        residual,
        post_ffn_gain.reshape(1, D),
    )
    return exchange(layer_blocks, "seq").reshape(rows_req, step_count, D)


def solution(mesh):
    return jax.shard_map(
        functools.partial(on_device, mesh.shape["req"], mesh.shape["seq"]),
        mesh=mesh,
        in_specs=(
            P("req", None, None),
            P(),
            P(),
            P(),
            P(),
            P(),
            P(),
            P("seq", "req"),
            P("seq", "req"),
            P("req", "seq"),
            P("req", "seq"),
            P("seq", "req"),
            P("req", "seq", None),
            P("req", "seq", None),
            P("req", "seq", None),
            P("req", "seq", None),
            P("req"),
            P("req"),
            P("req"),
            P("req", None),
        ),
        out_specs=P("req", None, None),
        check_vma=False,
    )
```
